32 devices in a mesh: dom: 8 (over z, x), grp: 4 (over y, core).
Axes of the slice: x: 2, y: 2, z: 4, core: 2. Of those that a mesh axis runs over, the one named last changes fastest.
Arguments:
- adjoint_state: float32 [16, 16, 256, 256], P('grp', None, 'dom'), may hold values from -6 to 6
- east_wind: float32 [16, 256, 256], P(None, 'dom'), may hold values from -0.2 to 0.2
- north_wind: float32 [16, 256, 256], P(None, 'dom'), may hold values from -0.2 to 0.2
- east_diff: float32 [16, 256, 256], P(None, 'dom'), may hold values from 0.01 to 0.05
- north_diff: float32 [16, 256, 256], P(None, 'dom'), may hold values from 0.01 to 0.05
- mass_flux: float32 [16, 256, 256], P(None, 'dom'), may hold values from 0.05 to 0.45
- region_map: int32 [256, 256], P('dom'), may hold values from 0 to 15
- cloud_top: int32 [256, 256], P('dom'), may hold values from 1 to 15
Outputs:
- final_adjoint: float32 [16, 16, 256, 256], P('grp', None, 'dom')
- flux_gradient: float32 [256, 256], P('dom')
The draws below stay inside these ranges and needn't reach their ends.
Inputs may be any that keep to these rules, and one draw needn't show every extreme that they name: `region_map`: tag k of the whole set of 16 tags belongs to region k.
All inputs are finite; a program needn't handle non-finite values.
Results may differ from the reference program's by a relative error of at most 0.00002.
Values sent between devices are 32-bit elements; how exact they have to be, the bound alone decides.
No kernel may reach another device: no remote copies, remote signals or barrier semaphores. Data moves between devices by JAX's collectives and lax.ppermute only.
A program may use at most 64 MiB of HBM per device.

```python
import math
import jax
import jax.numpy as jnp
from jax import lax

LEV = 16
NLAT = 256
ITERS = 4
NTAG = 16
NLON = 256


def touch_ends(array, own_key, low, largest):
    index_at = [jax.random.randint(jax.random.fold_in(own_key, axis), (), 0, length) for axis, length in enumerate(array.shape)]
    main_axis = array.shape.index(max(array.shape))
    beside = index_at[:main_axis] + [(index_at[main_axis] + 1) % array.shape[main_axis]] + index_at[main_axis + 1:]
    return array.at[tuple(index_at)].set(low).at[tuple(beside)].set(largest)


def steps_of(stream_key, dims, split, least, top_value):
    factor_of = 1.0
    for dim, blocks in split:
        steps = jax.random.uniform(jax.random.fold_in(jax.random.fold_in(stream_key, 6), dim), (blocks,), jnp.float32, least / len(split), top_value / len(split))
        factor_of = factor_of * jnp.repeat(jnp.exp(steps), dims[dim] // blocks).reshape((-1,) + (1,) * (len(dims) - 1 - dim))
    return factor_of


def gaussian(own_key, dims, scale, reach, shards=(), kind=jnp.bfloat16):
    level = steps_of(own_key, dims, shards, -0.22, 0.18) if shards else 1.0
    entries = jax.random.normal(own_key, dims, jnp.float32) * scale * level
    return jnp.minimum(jnp.maximum(entries, -reach), reach).astype(kind)


def setup_inputs(seed: int = 0) -> dict:
    keys = jax.random.split(jax.random.key(seed), 9)
    return {
        "adjoint_state": gaussian(keys[0], (NTAG, LEV, NLON, NLAT), 1.0, 6.0, ((0, 4), (2, 8)), jnp.float32),
        "east_wind": jnp.clip(jax.random.uniform(keys[1], (LEV, NLON, NLAT), jnp.float32, -0.2, 0.2) * steps_of(keys[1], (LEV, NLON, NLAT), ((1, 8),), -0.4, 0.0), -0.2, 0.2),
        "north_wind": jnp.clip(jax.random.uniform(keys[2], (LEV, NLON, NLAT), jnp.float32, -0.2, 0.2) * steps_of(keys[2], (LEV, NLON, NLAT), ((1, 8),), -0.4, 0.0), -0.2, 0.2),
        "east_diff": jnp.clip(jnp.exp(math.log(0.05) - 1.609438 * jax.random.uniform(keys[3], (LEV, NLON, NLAT), jnp.float32) ** steps_of(keys[3], (LEV, NLON, NLAT), ((1, 8),), -0.2, 0.2)), 0.01, 0.05),
        "north_diff": jnp.clip(jnp.exp(math.log(0.05) - 1.609438 * jax.random.uniform(keys[4], (LEV, NLON, NLAT), jnp.float32) ** steps_of(keys[4], (LEV, NLON, NLAT), ((1, 8),), -0.2, 0.2)), 0.01, 0.05),
        "mass_flux": jnp.clip(0.05 + 0.39999999 * jax.random.uniform(keys[5], (LEV, NLON, NLAT), jnp.float32) ** steps_of(keys[5], (LEV, NLON, NLAT), ((1, 8),), -0.2, 0.2), 0.05, 0.45),
        "region_map": touch_ends(jax.random.randint(keys[6], (NLON, NLAT), 0, NTAG), jax.random.fold_in(keys[6], 1), 0, NTAG - 1).astype(jnp.int32),
        "cloud_top": touch_ends(jax.random.randint(keys[7], (NLON, NLAT), 1, LEV), jax.random.fold_in(keys[7], 1), 1, LEV - 1).astype(jnp.int32),
    }


def reference(adjoint_state, east_wind, north_wind, east_diff, north_diff, mass_flux, region_map, cloud_top):
    east_coef = jnp.maximum(east_wind, 0.0) + east_diff
    west_prime = jnp.maximum(-east_wind, 0.0) + east_diff
    west_coef = jnp.roll(west_prime, 1, axis=1)
    row_ids = lax.broadcasted_iota(jnp.int32, east_wind.shape, 2)
    north_coef = (jnp.maximum(north_wind, 0.0) + north_diff) * (row_ids < NLAT - 1).astype(jnp.float32)
    south_prime = jnp.maximum(-north_wind, 0.0) + north_diff
    south_coef = jnp.concatenate([jnp.zeros_like(south_prime[..., :1]), south_prime[..., :-1]], axis=-1)
    level_ids = lax.broadcasted_iota(jnp.int32, mass_flux.shape, 0)
    updraft = mass_flux * (level_ids < cloud_top[None]).astype(jnp.float32)
    lam = adjoint_state
    accum = jnp.zeros((NTAG, NLON, NLAT), jnp.float32)
    for step in range(ITERS):
        east = jnp.roll(lam, -1, axis=2)
        west = jnp.roll(lam, 1, axis=2)
        north = jnp.concatenate([lam[..., 1:], lam[..., -1:]], axis=-1)
        south = jnp.concatenate([lam[..., :1], lam[..., :-1]], axis=-1)
        h = lam + east_coef * (east - lam) + west_coef * (west - lam) + north_coef * (north - lam) + south_coef * (south - lam)
        above = jnp.concatenate([h[:, 1:], h[:, -1:]], axis=1)
        lam = h + updraft * (above - h)
        accum = accum + lam[:, 0]
    tag_ids = lax.broadcasted_iota(jnp.int32, (NTAG, NLON, NLAT), 0)
    select = (region_map[None] == tag_ids).astype(jnp.float32)
    flux_gradient = jnp.sum(select * accum, axis=0)
    return lam, flux_gradient
```

```python
import functools

import jax
import jax.numpy as jnp
from jax import lax
from jax.experimental import pallas as pl
from jax.experimental.pallas import tpu as pltpu
from jax.sharding import PartitionSpec as P

ITERS = 4
EDGE = ITERS
PAD = 8


def shifted(value, axis, by):
    size = lax.axis_size(axis)
    return lax.ppermute(value, axis, [(i, (i + by) % size) for i in range(size)])


def faces(ew, ed, nw, nd):
    lats = ew.shape[-1]
    lat = lax.broadcasted_iota(jnp.int32, ew.shape, ew.ndim - 1)
    east = jnp.maximum(ew, 0.0) + ed
    west_next = jnp.maximum(-ew, 0.0) + ed
    north = jnp.where(lat < lats - 1, jnp.maximum(nw, 0.0) + nd, 0.0)
    south = jnp.maximum(-nw, 0.0) + nd
    south = jnp.where(lat > 0, pltpu.roll(south, 1, ew.ndim - 1), 0.0)
    return east, west_next, north, south


def pack_kernel(grp_ref, lam_lo, lam_hi, *refs):
    fields_lo, fields_hi = refs[0:6], refs[6:12]
    send_lo, send_hi, coef_lo, coef_hi = refs[12:]
    levels = lam_lo.shape[1]
    per = coef_lo.shape[1]
    send_lo[...] = lam_lo[:, :, 0:EDGE]
    send_hi[...] = lam_hi[:, :, 8 - EDGE : 8]
    base = grp_ref[0] * per
    for fields, dest, start in ((fields_lo, coef_lo, 0), (fields_hi, coef_hi, 8 - EDGE)):
        for i in range(per):
            ew, ed, nw, nd, mf = (ref[i] for ref in fields[:5])
            level = base + i
            lifted = jnp.where((level < fields[5][...]) & (level < levels - 1), mf, 0.0)
            for n, value in enumerate((*faces(ew, ed, nw, nd), lifted)):
                dest[n, i] = value[start : start + EDGE]


def pack(grp, lam, fields, top, groups):
    tags, levels, cols, lats = lam.shape
    per = levels // groups
    last = cols // 8 - 1
    lam_at = lambda c: pl.BlockSpec((tags, levels, 8, lats), lambda i, g: (0, 0, c, 0))
    field_at = lambda c: pl.BlockSpec((per, 8, lats), lambda i, g: (g[0], c, 0))
    top_at = lambda c: pl.BlockSpec((8, lats), lambda i, g: (c, 0))
    whole = lambda shape: pl.BlockSpec(shape, lambda i, g: (0,) * len(shape))
    lam_send = (tags, levels, EDGE, lats)
    coef_send = (5, per, EDGE, lats)
    shapes = [lam_send, lam_send, coef_send, coef_send]
    return pl.pallas_call(
        pack_kernel,
        grid_spec=pltpu.PrefetchScalarGridSpec(
            num_scalar_prefetch=1,
            grid=(1,),
            in_specs=[lam_at(0), lam_at(last)]
            + [field_at(0)] * 5
            + [top_at(0)]
            + [field_at(last)] * 5
            + [top_at(last)],
            out_specs=[whole(s) for s in shapes],
        ),
        out_shape=[jax.ShapeDtypeStruct(s, jnp.float32) for s in shapes],
        compiler_params=pltpu.CompilerParams(vmem_limit_bytes=24 << 20),
        name="pack_edges",
    )(grp, lam, lam, *fields, top, *fields, top)


def steps_kernel(groups, grp_ref, lam_ref, ew, ed, nw, nd, mf, top, region, from_west, from_east, *refs):
    gathered = refs[:groups]
    out_ref, grad_ref = refs[groups : groups + 2]
    coef, above, done, sems = refs[groups + 2 :]
    tags, levels, cols, lats = lam_ref.shape
    wide = cols + 2 * PAD
    per = levels // groups
    mine = grp_ref[0]
    gap = jnp.zeros((PAD - EDGE, lats), jnp.float32)

    def widen(west, own, east):
        return jnp.concatenate([gap, west, own, east, gap], axis=0)

    def prepare(source, piece):
        base = lax.rem(mine - source + groups, groups) * per

        @pl.loop(0, per)
        def _(i):
            level = base + i
            lifted = jnp.where((level < top[...]) & (level < levels - 1), mf[level], 0.0)
            own = (*faces(ew[level], ed[level], nw[level], nd[level]), lifted)
            e, w, n, s, u = (widen(piece[0, j, i], own[j], piece[1, j, i]) for j in range(5))
            w = pltpu.roll(w, 1, 0)
            for j, value in enumerate((1.0 - e - w - n - s, e, w, n, s, u)):
                coef[level, j] = value

    for source in range(groups):
        prepare(source, gathered[source])

    def column(tag, level, total):
        lam = widen(from_west[tag, level], lam_ref[tag, level], from_east[tag, level])
        for t in range(ITERS):
            h = (
                coef[level, 0] * lam
                + coef[level, 1] * pltpu.roll(lam, wide - 1, 0)
                + coef[level, 2] * pltpu.roll(lam, 1, 0)
                + coef[level, 3] * pltpu.roll(lam, lats - 1, 1)
                + coef[level, 4] * pltpu.roll(lam, 1, 1)
            )
            lam = h + coef[level, 5] * (above[t] - h)
            above[t] = h
            if total is not None:
                total = total + lam[PAD : PAD + cols]
        done[tag, level] = lam[PAD : PAD + cols]
        return total

    grad_ref[...] = jnp.zeros_like(grad_ref)

    @pl.loop(0, tags)
    def _(tag):
        above[...] = jnp.zeros_like(above)

        @pl.loop(0, levels - 1)
        def _(i):
            column(tag, levels - 1 - i, None)

        total = column(tag, 0, jnp.zeros((cols, lats), jnp.float32))
        grad_ref[...] += jnp.where(region[...] == mine * tags + tag, total, 0.0)
        pltpu.make_async_copy(done.at[tag], out_ref.at[tag], sems.at[tag]).start()

    @pl.loop(0, tags)
    def _(tag):
        pltpu.make_async_copy(done.at[tag], out_ref.at[tag], sems.at[tag]).wait()


def steps(groups, grp, lam, fields, top, region, from_west, from_east, gathered):
    tags, levels, cols, lats = lam.shape
    wide = cols + 2 * PAD
    vmem = pl.BlockSpec(memory_space=pltpu.VMEM)
    operands = [lam, *fields, top, region, from_west, from_east, *gathered]
    return pl.pallas_call(
        functools.partial(steps_kernel, groups),
        in_specs=[pl.BlockSpec(memory_space=pltpu.SMEM)] + [vmem] * len(operands),
        out_specs=[pl.BlockSpec(memory_space=pl.ANY), vmem],
        out_shape=[
            jax.ShapeDtypeStruct(lam.shape, jnp.float32),
            jax.ShapeDtypeStruct((cols, lats), jnp.float32),
        ],
        scratch_shapes=[
            pltpu.VMEM((levels, 6, wide, lats), jnp.float32),
            pltpu.VMEM((ITERS, wide, lats), jnp.float32),
            pltpu.VMEM(lam.shape, jnp.float32),
            pltpu.SemaphoreType.DMA((tags,)),
        ],
        compiler_params=pltpu.CompilerParams(vmem_limit_bytes=32 << 20),
        name="adjoint_steps",
    )(grp, *operands)


def local(lam, east_wind, north_wind, east_diff, north_diff, mass_flux, region, top):
    groups = lax.axis_size("grp")
    grp = lax.axis_index("grp").astype(jnp.int32).reshape(1)
    fields = (east_wind, east_diff, north_wind, north_diff, mass_flux)
    lam_lo, lam_hi, coef_lo, coef_hi = pack(grp, lam, fields, top, groups)
    coef_west = shifted(coef_hi, "dom", 1)
    coef_east = shifted(coef_lo, "dom", -1)
    from_west = shifted(lam_hi, "dom", 1)
    from_east = shifted(lam_lo, "dom", -1)
    mine = jnp.stack([coef_west, coef_east])
    gathered = [mine] + [shifted(mine, "grp", by) for by in range(1, groups)]
    final, grad = steps(groups, grp, lam, fields, top, region, from_west, from_east, gathered)
    share = grad
    for by in range(1, groups):
        grad = grad + shifted(share, "grp", by)
    return final, grad


def solution(mesh):
    return jax.shard_map(
        local,
        mesh=mesh,
        in_specs=(
            P("grp", None, "dom", None),
            P(None, "dom", None),
            P(None, "dom", None),
            P(None, "dom", None),
            P(None, "dom", None),
            P(None, "dom", None),
            P("dom", None),
            P("dom", None),
        ),
        out_specs=(P("grp", None, "dom", None), P("dom", None)),
        check_vma=False,
    )
```

```python
import functools

import jax
import jax.numpy as jnp
from jax import lax
from jax.experimental import pallas as pl
from jax.experimental.pallas import tpu as pltpu
from jax.sharding import PartitionSpec as P

ITERS = 4
EDGE = ITERS
ENTRIES = 16
CHUNK = 6
LANES = 128


def shifted(value, axis, by):
    size = lax.axis_size(axis)
    return lax.ppermute(value, axis, [(i, (i + by) % size) for i in range(size)])


def shifted_in_blocks(value, axis, block, by):
    size = lax.axis_size(axis)
    return lax.ppermute(
        value, axis, [(i, i - i % block + (i + by) % block) for i in range(size)]
    )


def faces(ew, ed, nw, nd):
    lats = ew.shape[1]
    lat = lax.broadcasted_iota(jnp.int32, ew.shape, 1)
    east = jnp.maximum(ew, 0.0) + ed
    west_next = jnp.maximum(-ew, 0.0) + ed
    north = jnp.where(lat < lats - 1, jnp.maximum(nw, 0.0) + nd, 0.0)
    south = jnp.maximum(-nw, 0.0) + nd
    south = jnp.where(lat > 0, pltpu.roll(south, 1, 1), 0.0)
    return east, west_next, north, south


def updraft(mf, top_row):
    levels = mf.shape[0]
    level = lax.broadcasted_iota(jnp.int32, mf.shape, 0)
    return jnp.where((level < top_row) & (level < levels - 1), mf, 0.0)


def advance(coefs, mid, east, west):
    d, e, w, n, s, u = coefs
    levels, lats = mid.shape
    h = d * mid + e * east + w * west
    h = h + n * pltpu.roll(mid, lats - 1, 1) + s * pltpu.roll(mid, 1, 1)
    return h + u * (pltpu.roll(h, levels - 1, 0) - h)


def rows_of(ref):
    size = 1
    for n in ref.shape[:-1]:
        size *= n
    return ref.reshape(size, ref.shape[-1])


def halves(ref, start, levels, stride, apart):
    parts = [ref[pl.ds(start + apart * k, levels, stride=stride), :] for k in range(2)]
    return jnp.concatenate(parts, axis=1)


def pack_kernel(parts, grp_ref, lam, ew, ed, nw, nd, mf, top, lam_lo, lam_hi, coef_lo, coef_hi, lam_s, field_s, top_s, entry, sems):
    tags, levels, cols, lats = lam.shape
    copies = []

    def copy(src, dst):
        copies.append(pltpu.make_async_copy(src, dst, sems.at[len(copies)]))
        copies[-1].start()

    for side, first in enumerate((0, cols - 8)):
        copy(top.at[pl.ds(first, 8)], top_s.at[side])
        for k in range(2):
            lane = pl.ds(k * LANES, LANES)
            for f, field in enumerate((ew, ed, nw, nd, mf)):
                copy(field.at[:, pl.ds(first, 8), lane], field_s.at[f, side, k])
    fields_copies = len(copies)
    for side, first in enumerate((0, cols - 8)):
        for k in range(2):
            lane = pl.ds(k * LANES, LANES)
            copy(lam.at[:, :, pl.ds(first, 8), lane], lam_s.at[side, k])
    for c in copies[:fields_copies]:
        c.wait()

    field_rows = rows_of(field_s)
    slab = levels * 8

    def field(f, side, c):
        return halves(field_rows, (f * 2 + side) * 2 * slab + c, levels, 8, slab)

    for side in range(2):
        slot = 0
        for c in range(EDGE - 1) if side == 0 else range(8 - EDGE, 8):
            east, west, north, south = faces(*(field(f, side, c) for f in range(4)))
            lift = updraft(field(4, side, c), top_s[side, pl.ds(c, 1), :])
            wanted = (east, west, north, south, lift)
            if side == 1 and c == 8 - EDGE:
                wanted = (west,)
            for value in wanted:
                entry[side, slot] = value
                slot += 1
        for left in range(slot, ENTRIES):
            entry[side, left] = jnp.zeros((levels, lats), jnp.float32)
    per = ENTRIES // parts
    mine = lax.rem(grp_ref[0], parts) * per
    coef_lo[...] = entry[0, pl.ds(mine, per)]
    coef_hi[...] = entry[1, pl.ds(mine, per)]

    for c in copies[fields_copies:]:
        c.wait()
    lam_rows = rows_of(lam_s)
    for side, dest in enumerate((lam_lo, lam_hi)):
        for tag in range(tags):
            for c in range(EDGE):
                at = (side * 2 * tags + tag) * slab + c + (8 - EDGE) * side
                dest[tag, c] = halves(lam_rows, at, levels, 8, tags * slab)


def pack(parts, grp, lam, fields, top):
    tags, levels, cols, lats = lam.shape
    hbm = pl.BlockSpec(memory_space=pltpu.HBM)
    lam_send = pltpu.VMEM((tags, EDGE, levels, lats), jnp.float32)
    coef_send = pltpu.VMEM((ENTRIES // parts, levels, lats), jnp.float32)
    return pl.pallas_call(
        functools.partial(pack_kernel, parts),
        in_specs=[pl.BlockSpec(memory_space=pltpu.SMEM)] + [hbm] * 7,
        out_specs=[pl.BlockSpec(memory_space=pltpu.VMEM)] * 4,
        out_shape=[lam_send, lam_send, coef_send, coef_send],
        scratch_shapes=[
            pltpu.VMEM((3, 2, tags, levels, 8, LANES), jnp.float32),
            pltpu.VMEM((6, 2, 2, levels, 8, LANES), jnp.float32),
            pltpu.VMEM((2, 8, lats), jnp.int32),
            pltpu.VMEM((2, ENTRIES, levels, lats), jnp.float32),
            pltpu.SemaphoreType.DMA((26,)),
        ],
        compiler_params=pltpu.CompilerParams(vmem_limit_bytes=24 << 20),
        cost_estimate=pl.CostEstimate(flops=10**6, bytes_accessed=3 << 20, transcendentals=0),
        name="pack_edges",
    )(grp, lam, *fields, top)


def chosen(region_row, first_tag, values):
    row = jnp.zeros(region_row.shape, jnp.float32)
    for tag, value in enumerate(values):
        row = jnp.where(region_row == first_tag + tag, value[0:1], row)
    return row


def inner_kernel(grp_ref, lam, ew, ed, nw, nd, mf, top, region, out, coef, l0, l1, l2, l3, stage, rows, lam_s, field_s, sems):
    tags, levels, cols, lats = lam.shape
    first_tag = grp_ref[0] * tags
    copies = []

    def copy(src, dst):
        copies.append(pltpu.make_async_copy(src, dst, sems.at[len(copies)]))
        copies[-1].start()

    for k in range(2):
        for f, field in enumerate((ew, ed, nw, nd, mf)):
            copy(field.at[:, :, pl.ds(k * LANES, LANES)], field_s.at[f, k])
    for k in range(2):
        copy(lam.at[:, :, :, pl.ds(k * LANES, LANES)], lam_s.at[k])
    for c in copies[:10]:
        c.wait()
    field_rows = rows_of(field_s)
    lam_rows = rows_of(lam_s)
    slab = levels * cols

    def coefficients(c, west):
        ew, ed, nw, nd, mf = (
            halves(field_rows, f * 2 * slab + c, levels, cols, slab) for f in range(5)
        )
        e, next_west, n, s = faces(ew, ed, nw, nd)
        u = updraft(mf, top[pl.ds(c, 1), :])
        for j, value in enumerate((1.0 - e - west - n - s, e, west, n, s, u)):
            coef[c, j] = value
        return next_west

    def four(i, west):
        for j in range(4):
            west = coefficients(i * 4 + j, west)
        return west

    west = lax.fori_loop(0, cols // 4, four, jnp.zeros((levels, lats), jnp.float32))
    coef[cols, 2] = west
    for c in copies[10:]:
        c.wait()

    @pl.loop(0, cols // 4)
    def _(i):
        for j in range(4):
            c = i * 4 + j
            for tag in range(tags):
                l0[c, tag] = halves(lam_rows, tag * slab + c, levels, cols, tags * slab)

    stage_rows = rows_of(stage)
    store = (
        lambda c, tag, value: l1.__setitem__((c, tag), value),
        lambda c, tag, value: l2.__setitem__((c, tag), value),
        lambda c, tag, value: l3.__setitem__((c, tag), value),
        functools.partial(to_stage, stage_rows, tags, levels, cols),
    )
    sources = (l0, l1, l2, l3)
    for t in range(ITERS):
        src = sources[t]
        low, high = t + 1, cols - t - 1

        @pl.loop(0, -(-(high - low) // CHUNK))
        def _(i):
            start = jnp.minimum(low + i * CHUNK, high - CHUNK)
            for j in range(CHUNK):
                c = start + j
                coefs = [coef[c, n] for n in range(6)]
                new = [advance(coefs, src[c, k], src[c + 1, k], src[c - 1, k]) for k in range(tags)]
                for k in range(tags):
                    store[t](c, k, new[k])
                rows[t, pl.ds(c, 1), :] = chosen(region[pl.ds(c, 1), :], first_tag, new)

    inside = pl.ds(8, cols - 16)
    writes = [
        pltpu.make_async_copy(
            stage.at[k, :, :, inside],
            out.at[:, :, inside, pl.ds(k * LANES, LANES)],
            sems.at[len(copies) + k],
        )
        for k in range(2)
    ]
    for c in writes:
        c.start()
    for c in writes:
        c.wait()


def to_stage(stage_rows, tags, levels, cols, c, tag, value):
    slab = levels * cols
    for k in range(2):
        at = (k * tags + tag) * slab + c
        stage_rows[pl.ds(at, levels, stride=cols), :] = value[:, k * LANES : (k + 1) * LANES]


def inner(grp, lam, fields, top, region):
    tags, levels, cols, lats = lam.shape
    hbm = pl.BlockSpec(memory_space=pltpu.HBM)
    vmem = pl.BlockSpec(memory_space=pltpu.VMEM)
    state = pltpu.VMEM((cols, tags, levels, lats), jnp.float32)
    return pl.pallas_call(
        inner_kernel,
        in_specs=[pl.BlockSpec(memory_space=pltpu.SMEM)] + [hbm] * 6 + [vmem] * 2,
        out_specs=[hbm] + [vmem] * 7,
        out_shape=[
            pltpu.HBM(lam.shape, jnp.float32),
            pltpu.VMEM((cols + 1, 6, levels, lats), jnp.float32),
            *[state] * 4,
            pltpu.VMEM((3, tags, levels, cols, LANES), jnp.float32),
            pltpu.VMEM((ITERS, cols, lats), jnp.float32),
        ],
        scratch_shapes=[
            pltpu.VMEM((3, tags, levels, cols, LANES), jnp.float32),
            pltpu.VMEM((6, 2, levels, cols, LANES), jnp.float32),
            pltpu.SemaphoreType.DMA((14,)),
        ],
        compiler_params=pltpu.CompilerParams(vmem_limit_bytes=32 << 20),
        cost_estimate=pl.CostEstimate(flops=40 * 10**6, bytes_accessed=8 << 20, transcendentals=0),
        name="inner_steps",
    )(grp, lam, *fields, top, region)


def border_kernel(parts, grp_ref, region, coef, l0, l1, l2, l3, west, east, *refs):
    pieces = refs[:parts]
    stage_in, out_in, rows_in, stage, out, grad, entry, wide, work, rows, sems = refs[parts:]
    cols, tags, levels, lats = l0.shape
    first_tag = grp_ref[0] * tags
    per = ENTRIES // parts
    mine = lax.rem(grp_ref[0], parts)
    for by in range(parts):
        base = lax.rem(mine - by + parts, parts) * per
        for side in range(2):
            entry[side, pl.ds(base, per)] = pieces[by][side]

    def slot(c):
        return (0, c + EDGE - 1) if c < EDGE else (1, c - (cols - EDGE))

    def outside(c):
        if c < 0:
            at = 1 + 5 * (c + EDGE - 1)
            e, _, n, s, u = (entry[0, at + j] for j in range(5))
            w = entry[0, at - 4] if c > 1 - EDGE else entry[0, 0]
        else:
            at = 5 * (c - cols)
            e, _, n, s, u = (entry[1, at + j] for j in range(5))
            w = entry[1, at - 4] if c > cols else coef[cols, 2]
        return 1.0 - e - w - n - s, e, w, n, s, u

    for c in [*range(1 - EDGE, 0), *range(cols, cols + EDGE - 1)]:
        for j, value in enumerate(outside(c)):
            wide[*slot(c), j] = value
    first_west = entry[0, 1 + 5 * (EDGE - 2) + 1]
    first_mid = 1.0 - coef[0, 1] - first_west - coef[0, 3] - coef[0, 4]

    def coefs_at(c):
        if c < 0 or c >= cols:
            return [wide[*slot(c), j] for j in range(6)]
        if c == 0:
            return [first_mid, coef[0, 1], first_west, *(coef[0, j] for j in range(3, 6))]
        return [coef[c, j] for j in range(6)]

    kept = (l0, l1, l2, l3)

    def state(t, c, tag):
        if t <= c < cols - t:
            return kept[t][c, tag]
        if t == 0:
            return west[tag, c + EDGE] if c < 0 else east[tag, c - cols]
        return work[t, *slot(c), tag]

    rows[...] = rows_in[...]
    stage_rows = rows_of(stage)
    for t in range(ITERS):
        reach = EDGE - 1 - t
        for c in [*range(-reach, t + 1), *range(cols - t - 1, cols + reach)]:
            coefs = coefs_at(c)
            new = [
                advance(coefs, state(t, c, k), state(t, c + 1, k), state(t, c - 1, k))
                for k in range(tags)
            ]
            for k in range(tags):
                if t < ITERS - 1:
                    work[t + 1, *slot(c), k] = new[k]
                else:
                    to_stage(stage_rows, tags, levels, cols, c, k, new[k])
            if 0 <= c < cols:
                rows[t, c : c + 1, :] = chosen(region[c : c + 1, :], first_tag, new)
    writes = []
    for side, first in enumerate((0, cols - 8)):
        for k in range(2):
            writes.append(
                pltpu.make_async_copy(
                    stage.at[k, :, :, pl.ds(first, 8)],
                    out.at[:, :, pl.ds(first, 8), pl.ds(k * LANES, LANES)],
                    sems.at[side * 2 + k],
                )
            )
            writes[-1].start()
    total = rows[0]
    for t in range(1, ITERS):
        total = total + rows[t]
    grad[...] = total
    for c in writes:
        c.wait()


def border(parts, grp, region, coef, states, west, east, pieces, stage, out, rows):
    cols, tags, levels, lats = states[0].shape
    hbm = pl.BlockSpec(memory_space=pltpu.HBM)
    vmem = pl.BlockSpec(memory_space=pltpu.VMEM)
    operands = [region, coef, *states, west, east, *pieces, stage]
    n = len(operands)
    return pl.pallas_call(
        functools.partial(border_kernel, parts),
        in_specs=[pl.BlockSpec(memory_space=pltpu.SMEM)] + [vmem] * n + [hbm, vmem],
        out_specs=[vmem, hbm, vmem],
        out_shape=[
            pltpu.VMEM(stage.shape, jnp.float32),
            pltpu.HBM(out.shape, jnp.float32),
            pltpu.VMEM((cols, lats), jnp.float32),
        ],
        input_output_aliases={n: 0, n + 1: 1},
        scratch_shapes=[
            pltpu.VMEM((2, ENTRIES, levels, lats), jnp.float32),
            pltpu.VMEM((2, 2 * EDGE - 1, 6, levels, lats), jnp.float32),
            pltpu.VMEM((ITERS, 2, 2 * EDGE - 1, tags, levels, lats), jnp.float32),
            pltpu.VMEM((ITERS, cols, lats), jnp.float32),
            pltpu.SemaphoreType.DMA((4,)),
        ],
        compiler_params=pltpu.CompilerParams(vmem_limit_bytes=32 << 20),
        cost_estimate=pl.CostEstimate(flops=10 * 10**6, bytes_accessed=2 << 20, transcendentals=0),
        name="border_steps",
    )(grp, *operands, out, rows)


def local(lam, east_wind, north_wind, east_diff, north_diff, mass_flux, region, top):
    groups = lax.axis_size("grp")
    parts = 4 if groups % 4 == 0 else 1
    grp = lax.axis_index("grp").astype(jnp.int32).reshape(1)
    lam, *fields = (
        pltpu.with_memory_space_constraint(value, pltpu.HBM)
        for value in (lam, east_wind, east_diff, north_wind, north_diff, mass_flux)
    )
    far_top = pltpu.with_memory_space_constraint(top, pltpu.HBM)
    lam_lo, lam_hi, coef_lo, coef_hi = pack(parts, grp, lam, fields, far_top)
    coef_west = shifted(coef_hi, "dom", 1)
    coef_east = shifted(coef_lo, "dom", -1)
    west = shifted(lam_hi, "dom", 1)
    east = shifted(lam_lo, "dom", -1)
    out, coef, *states, stage, rows = inner(grp, lam, fields, top, region)
    coef_west, coef_east, rows = lax.optimization_barrier((coef_west, coef_east, rows))
    mine = jnp.stack([coef_west, coef_east])
    pieces = [mine] + [shifted_in_blocks(mine, "grp", parts, by) for by in range(1, parts)]
    _, final, grad = border(
        parts, grp, region, coef, states, west, east, pieces, stage, out, rows
    )
    share = grad
    for by in range(1, groups):
        grad = grad + shifted(share, "grp", by)
    return final, grad


def solution(mesh):
    return jax.shard_map(
        local,
        mesh=mesh,
        in_specs=(
            P("grp", None, "dom", None),
            P(None, "dom", None),
            P(None, "dom", None),
            P(None, "dom", None),
            P(None, "dom", None),
            P(None, "dom", None),
            P("dom", None),
            P("dom", None),
        ),
        out_specs=(P("grp", None, "dom", None), P("dom", None)),
        check_vma=False,
    )
```

```python
import functools

import jax
import jax.numpy as jnp
from jax import lax
from jax.experimental import pallas as pl
from jax.experimental.pallas import tpu as pltpu
from jax.sharding import PartitionSpec as P

ITERS = 4
EDGE = ITERS
ENTRIES = 16
CHUNK = 6
LANES = 128


def shifted(value, axis, by):
    size = lax.axis_size(axis)
    return lax.ppermute(value, axis, [(i, (i + by) % size) for i in range(size)])


def swapped(value, axis, bit):
    return lax.ppermute(value, axis, [(i, i ^ bit) for i in range(lax.axis_size(axis))])


def faces(ew, ed, nw, nd):
    lats = ew.shape[1]
    lat = lax.broadcasted_iota(jnp.int32, ew.shape, 1)
    east = jnp.maximum(ew, 0.0) + ed
    west_next = jnp.maximum(-ew, 0.0) + ed
    north = jnp.where(lat < lats - 1, jnp.maximum(nw, 0.0) + nd, 0.0)
    south = jnp.maximum(-nw, 0.0) + nd
    south = jnp.where(lat > 0, pltpu.roll(south, 1, 1), 0.0)
    return east, west_next, north, south


def updraft(mf, top_row):
    levels = mf.shape[0]
    level = lax.broadcasted_iota(jnp.int32, mf.shape, 0)
    return jnp.where((level < top_row) & (level < levels - 1), mf, 0.0)


def advance(coefs, mid, east, west):
    d, e, w, n, s, u = coefs
    levels, lats = mid.shape
    h = d * mid + e * east + w * west
    h = h + n * pltpu.roll(mid, lats - 1, 1) + s * pltpu.roll(mid, 1, 1)
    return h + u * (pltpu.roll(h, levels - 1, 0) - h)


def pitched(slabs, levels, width):
    return -(-(slabs * levels * (width + 1) + width + 8) // 8) * 8


def halves(ref, start, levels, stride, apart):
    parts = [ref[pl.ds(start + apart * k, levels, stride=stride), :] for k in range(2)]
    return jnp.concatenate(parts, axis=1)


def pack_kernel(parts, grp_ref, lam, ew, ed, nw, nd, mf, top, lam_lo, lam_hi, coef_lo, coef_hi, lam_s, field_s, top_s, entry, lam_p, field_p, sems):
    tags, levels, cols, lats = lam.shape
    copies = []

    def copy(src, dst):
        copies.append(pltpu.make_async_copy(src, dst, sems.at[len(copies)]))
        copies[-1].start()

    for side, first in enumerate((0, cols - 8)):
        copy(top.at[pl.ds(first, 8)], top_s.at[side])
        for k in range(2):
            lane = pl.ds(k * LANES, LANES)
            for f, field in enumerate((ew, ed, nw, nd, mf)):
                copy(field.at[:, pl.ds(first, 8), lane], field_s.at[f, side, k])
    fields_copies = len(copies)
    for side, first in enumerate((0, cols - 8)):
        for k in range(2):
            lane = pl.ds(k * LANES, LANES)
            copy(lam.at[:, :, pl.ds(first, 8), lane], lam_s.at[side, k])
    for c in copies[:fields_copies]:
        c.wait()

    pitch = 9
    slab = levels * pitch

    @pl.loop(0, levels)
    def _(level):
        for f in range(5):
            for side in range(2):
                for k in range(2):
                    at = ((f * 2 + side) * 2 + k) * slab
                    field_p[pl.ds(at + level * pitch, 8), :] = field_s[f, side, k, level]

    def field(f, side, c):
        return halves(field_p, (f * 2 + side) * 2 * slab + c, levels, pitch, slab)

    for side in range(2):
        slot = 0
        for c in range(EDGE - 1) if side == 0 else range(8 - EDGE, 8):
            east, west, north, south = faces(*(field(f, side, c) for f in range(4)))
            lift = updraft(field(4, side, c), top_s[side, pl.ds(c, 1), :])
            wanted = (east, west, north, south, lift)
            if side == 1 and c == 8 - EDGE:
                wanted = (west,)
            for value in wanted:
                entry[side, slot] = value
                slot += 1
        for left in range(slot, ENTRIES):
            entry[side, left] = jnp.zeros((levels, lats), jnp.float32)
    per = ENTRIES // parts
    mine = lax.rem(grp_ref[0], parts) * per
    coef_lo[...] = entry[0, pl.ds(mine, per)]
    coef_hi[...] = entry[1, pl.ds(mine, per)]

    for c in copies[fields_copies:]:
        c.wait()

    @pl.loop(0, levels)
    def _(level):
        for side in range(2):
            for k in range(2):
                for tag in range(tags):
                    at = ((side * 2 + k) * tags + tag) * slab
                    lam_p[pl.ds(at + level * pitch, 8), :] = lam_s[side, k, tag, level]

    for side, dest in enumerate((lam_lo, lam_hi)):
        for tag in range(tags):
            for c in range(EDGE):
                at = (side * 2 * tags + tag) * slab + c + (8 - EDGE) * side
                dest[tag, c] = halves(lam_p, at, levels, pitch, tags * slab)


def pack(parts, grp, lam, fields, top):
    tags, levels, cols, lats = lam.shape
    hbm = pl.BlockSpec(memory_space=pltpu.HBM)
    lam_send = pltpu.VMEM((tags, EDGE, levels, lats), jnp.float32)
    coef_send = pltpu.VMEM((ENTRIES // parts, levels, lats), jnp.float32)
    return pl.pallas_call(
        functools.partial(pack_kernel, parts),
        in_specs=[pl.BlockSpec(memory_space=pltpu.SMEM)] + [hbm] * 7,
        out_specs=[pl.BlockSpec(memory_space=pltpu.VMEM)] * 4,
        out_shape=[lam_send, lam_send, coef_send, coef_send],
        scratch_shapes=[
            pltpu.VMEM((2, 2, tags, levels, 8, LANES), jnp.float32),
            pltpu.VMEM((5, 2, 2, levels, 8, LANES), jnp.float32),
            pltpu.VMEM((2, 8, lats), jnp.int32),
            pltpu.VMEM((2, ENTRIES, levels, lats), jnp.float32),
            pltpu.VMEM((pitched(4 * tags, levels, 8), LANES), jnp.float32),
            pltpu.VMEM((pitched(20, levels, 8), LANES), jnp.float32),
            pltpu.SemaphoreType.DMA((26,)),
        ],
        compiler_params=pltpu.CompilerParams(vmem_limit_bytes=24 << 20),
        cost_estimate=pl.CostEstimate(flops=10**6, bytes_accessed=3 << 20, transcendentals=0),
        name="pack_edges",
    )(grp, lam, *fields, top)


def chosen(region_row, first_tag, values):
    row = jnp.zeros(region_row.shape, jnp.float32)
    for tag, value in enumerate(values):
        row = jnp.where(region_row == first_tag + tag, value[0:1], row)
    return row


def inner_kernel(grp_ref, lam, ew, ed, nw, nd, mf, top, region, out, coef, l0, l1, l2, l3, stage, rows, lam_s, field_s, lam_p, field_p, inside, sems):
    tags, levels, cols, lats = lam.shape
    first_tag = grp_ref[0] * tags
    copies = []

    def copy(src, dst):
        copies.append(pltpu.make_async_copy(src, dst, sems.at[len(copies)]))
        copies[-1].start()

    for k in range(2):
        for f, field in enumerate((ew, ed, nw, nd, mf)):
            copy(field.at[:, :, pl.ds(k * LANES, LANES)], field_s.at[f, k])
    for k in range(2):
        copy(lam.at[:, :, :, pl.ds(k * LANES, LANES)], lam_s.at[k])
    for c in copies[:10]:
        c.wait()
    pitch = cols + 1
    slab = levels * pitch

    @pl.loop(0, levels)
    def _(level):
        for f in range(5):
            for k in range(2):
                field_p[pl.ds((f * 2 + k) * slab + level * pitch, cols), :] = field_s[f, k, level]

    def coefficients(c, west):
        ew, ed, nw, nd, mf = (
            halves(field_p, f * 2 * slab + c, levels, pitch, slab) for f in range(5)
        )
        e, next_west, n, s = faces(ew, ed, nw, nd)
        u = updraft(mf, top[pl.ds(c, 1), :])
        for j, value in enumerate((1.0 - e - west - n - s, e, west, n, s, u)):
            coef[c, j] = value
        return next_west

    def four(i, west):
        for j in range(4):
            west = coefficients(i * 4 + j, west)
        return west

    west = lax.fori_loop(0, cols // 4, four, jnp.zeros((levels, lats), jnp.float32))
    coef[cols, 2] = west
    for c in copies[10:]:
        c.wait()

    @pl.loop(0, levels)
    def _(level):
        for k in range(2):
            for tag in range(tags):
                lam_p[pl.ds((k * tags + tag) * slab + level * pitch, cols), :] = lam_s[k, tag, level]

    @pl.loop(0, cols // 4)
    def _(i):
        for j in range(4):
            c = i * 4 + j
            for tag in range(tags):
                l0[c, tag] = halves(lam_p, tag * slab + c, levels, pitch, tags * slab)

    store = (
        lambda c, tag, value: l1.__setitem__((c, tag), value),
        lambda c, tag, value: l2.__setitem__((c, tag), value),
        lambda c, tag, value: l3.__setitem__((c, tag), value),
        functools.partial(to_stage, stage, tags, levels, pitch),
    )
    sources = (l0, l1, l2, l3)
    for t in range(ITERS):
        src = sources[t]
        low, high = t + 1, cols - t - 1

        @pl.loop(0, -(-(high - low) // CHUNK))
        def _(i):
            start = jnp.minimum(low + i * CHUNK, high - CHUNK)
            for j in range(CHUNK):
                c = start + j
                coefs = [coef[c, n] for n in range(6)]
                new = [advance(coefs, src[c, k], src[c + 1, k], src[c - 1, k]) for k in range(tags)]
                for k in range(tags):
                    store[t](c, k, new[k])
                rows[t, pl.ds(c, 1), :] = chosen(region[pl.ds(c, 1), :], first_tag, new)

    @pl.loop(0, levels)
    def _(level):
        for k in range(2):
            for tag in range(tags):
                at = (k * tags + tag) * slab + level * pitch + 8
                inside[k, tag, level] = stage[pl.ds(at, cols - 16), :]

    writes = [
        pltpu.make_async_copy(
            inside.at[k],
            out.at[:, :, pl.ds(8, cols - 16), pl.ds(k * LANES, LANES)],
            sems.at[len(copies) + k],
        )
        for k in range(2)
    ]
    for c in writes:
        c.start()
    for c in writes:
        c.wait()


def to_stage(stage, tags, levels, pitch, c, tag, value):
    for k in range(2):
        at = (k * tags + tag) * levels * pitch + c
        stage[pl.ds(at, levels, stride=pitch), :] = value[:, k * LANES : (k + 1) * LANES]


def inner(grp, lam, fields, top, region):
    tags, levels, cols, lats = lam.shape
    hbm = pl.BlockSpec(memory_space=pltpu.HBM)
    vmem = pl.BlockSpec(memory_space=pltpu.VMEM)
    state = pltpu.VMEM((cols, tags, levels, lats), jnp.float32)
    return pl.pallas_call(
        inner_kernel,
        in_specs=[pl.BlockSpec(memory_space=pltpu.SMEM)] + [hbm] * 6 + [vmem] * 2,
        out_specs=[hbm] + [vmem] * 7,
        out_shape=[
            pltpu.HBM(lam.shape, jnp.float32),
            pltpu.VMEM((cols + 1, 6, levels, lats), jnp.float32),
            *[state] * 4,
            pltpu.VMEM((pitched(2 * tags, levels, cols), LANES), jnp.float32),
            pltpu.VMEM((ITERS, cols, lats), jnp.float32),
        ],
        scratch_shapes=[
            pltpu.VMEM((2, tags, levels, cols, LANES), jnp.float32),
            pltpu.VMEM((5, 2, levels, cols, LANES), jnp.float32),
            pltpu.VMEM((pitched(2 * tags, levels, cols), LANES), jnp.float32),
            pltpu.VMEM((pitched(10, levels, cols), LANES), jnp.float32),
            pltpu.VMEM((2, tags, levels, cols - 16, LANES), jnp.float32),
            pltpu.SemaphoreType.DMA((14,)),
        ],
        compiler_params=pltpu.CompilerParams(vmem_limit_bytes=32 << 20),
        cost_estimate=pl.CostEstimate(flops=40 * 10**6, bytes_accessed=8 << 20, transcendentals=0),
        name="inner_steps",
    )(grp, lam, *fields, top, region)


def border_kernel(parts, grp_ref, region, coef, l0, l1, l2, l3, west, east, *refs):
    pieces = refs[:parts]
    stage_in, out_in, rows_in, stage, out, grad, entry, wide, work, rows, sides, sems = refs[parts:]
    cols, tags, levels, lats = l0.shape
    first_tag = grp_ref[0] * tags
    per = ENTRIES // parts
    mine = lax.rem(grp_ref[0], parts)
    for by in range(parts):
        base = (mine ^ by) * per
        for side in range(2):
            entry[side, pl.ds(base, per)] = pieces[by][side]

    def slot(c):
        return (0, c + EDGE - 1) if c < EDGE else (1, c - (cols - EDGE))

    def outside(c):
        if c < 0:
            at = 1 + 5 * (c + EDGE - 1)
            e, _, n, s, u = (entry[0, at + j] for j in range(5))
            w = entry[0, at - 4] if c > 1 - EDGE else entry[0, 0]
        else:
            at = 5 * (c - cols)
            e, _, n, s, u = (entry[1, at + j] for j in range(5))
            w = entry[1, at - 4] if c > cols else coef[cols, 2]
        return 1.0 - e - w - n - s, e, w, n, s, u

    for c in [*range(1 - EDGE, 0), *range(cols, cols + EDGE - 1)]:
        for j, value in enumerate(outside(c)):
            wide[*slot(c), j] = value
    first_west = entry[0, 1 + 5 * (EDGE - 2) + 1]
    first_mid = 1.0 - coef[0, 1] - first_west - coef[0, 3] - coef[0, 4]

    def coefs_at(c):
        if c < 0 or c >= cols:
            return [wide[*slot(c), j] for j in range(6)]
        if c == 0:
            return [first_mid, coef[0, 1], first_west, *(coef[0, j] for j in range(3, 6))]
        return [coef[c, j] for j in range(6)]

    kept = (l0, l1, l2, l3)

    def state(t, c, tag):
        if t <= c < cols - t:
            return kept[t][c, tag]
        if t == 0:
            return west[tag, c + EDGE] if c < 0 else east[tag, c - cols]
        return work[t, *slot(c), tag]

    rows[...] = rows_in[...]
    pitch = cols + 1
    for t in range(ITERS):
        reach = EDGE - 1 - t
        for c in [*range(-reach, t + 1), *range(cols - t - 1, cols + reach)]:
            coefs = coefs_at(c)
            new = [
                advance(coefs, state(t, c, k), state(t, c + 1, k), state(t, c - 1, k))
                for k in range(tags)
            ]
            for k in range(tags):
                if t < ITERS - 1:
                    work[t + 1, *slot(c), k] = new[k]
                else:
                    to_stage(stage, tags, levels, pitch, c, k, new[k])
            if 0 <= c < cols:
                rows[t, c : c + 1, :] = chosen(region[c : c + 1, :], first_tag, new)

    @pl.loop(0, levels)
    def _(level):
        for side, first in enumerate((0, cols - 8)):
            for k in range(2):
                for tag in range(tags):
                    at = ((k * tags + tag) * levels + level) * pitch + first
                    sides[side, k, tag, level] = stage[pl.ds(at, 8), :]

    writes = []
    for side, first in enumerate((0, cols - 8)):
        for k in range(2):
            writes.append(
                pltpu.make_async_copy(
                    sides.at[side, k],
                    out.at[:, :, pl.ds(first, 8), pl.ds(k * LANES, LANES)],
                    sems.at[side * 2 + k],
                )
            )
            writes[-1].start()
    total = rows[0]
    for t in range(1, ITERS):
        total = total + rows[t]
    grad[...] = total
    for c in writes:
        c.wait()


def border(parts, grp, region, coef, states, west, east, pieces, stage, out, rows):
    cols, tags, levels, lats = states[0].shape
    hbm = pl.BlockSpec(memory_space=pltpu.HBM)
    vmem = pl.BlockSpec(memory_space=pltpu.VMEM)
    operands = [region, coef, *states, west, east, *pieces, stage]
    n = len(operands)
    return pl.pallas_call(
        functools.partial(border_kernel, parts),
        in_specs=[pl.BlockSpec(memory_space=pltpu.SMEM)] + [vmem] * n + [hbm, vmem],
        out_specs=[vmem, hbm, vmem],
        out_shape=[
            pltpu.VMEM(stage.shape, jnp.float32),
            pltpu.HBM(out.shape, jnp.float32),
            pltpu.VMEM((cols, lats), jnp.float32),
        ],
        input_output_aliases={n: 0, n + 1: 1},
        scratch_shapes=[
            pltpu.VMEM((2, ENTRIES, levels, lats), jnp.float32),
            pltpu.VMEM((2, 2 * EDGE - 1, 6, levels, lats), jnp.float32),
            pltpu.VMEM((ITERS, 2, 2 * EDGE - 1, tags, levels, lats), jnp.float32),
            pltpu.VMEM((ITERS, cols, lats), jnp.float32),
            pltpu.VMEM((2, 2, tags, levels, 8, LANES), jnp.float32),
            pltpu.SemaphoreType.DMA((4,)),
        ],
        compiler_params=pltpu.CompilerParams(vmem_limit_bytes=32 << 20),
        cost_estimate=pl.CostEstimate(flops=10 * 10**6, bytes_accessed=2 << 20, transcendentals=0),
        name="border_steps",
    )(grp, *operands, out, rows)


def local(lam, east_wind, north_wind, east_diff, north_diff, mass_flux, region, top):
    groups = lax.axis_size("grp")
    parts = 4 if groups % 4 == 0 else 1
    grp = lax.axis_index("grp").astype(jnp.int32).reshape(1)
    lam, *fields = (
        pltpu.with_memory_space_constraint(value, pltpu.HBM)
        for value in (lam, east_wind, east_diff, north_wind, north_diff, mass_flux)
    )
    far_top = pltpu.with_memory_space_constraint(top, pltpu.HBM)
    lam_lo, lam_hi, coef_lo, coef_hi = pack(parts, grp, lam, fields, far_top)
    coef_west = shifted(coef_hi, "dom", 1)
    west = shifted(lam_hi, "dom", 1)
    coef_east = shifted(coef_lo, "dom", -1)
    east = shifted(lam_lo, "dom", -1)
    out, coef, *states, stage, rows = inner(grp, lam, fields, top, region)
    coef_west, coef_east, rows = lax.optimization_barrier((coef_west, coef_east, rows))
    mine = jnp.stack([coef_west, coef_east])
    pieces = [mine]
    if parts == 4:
        across = swapped(mine, "grp", 2)
        pieces += [swapped(mine, "grp", 1), across, swapped(across, "grp", 1)]
    _, final, grad = border(
        parts, grp, region, coef, states, west, east, pieces, stage, out, rows
    )
    share = grad
    for by in range(1, groups):
        grad = grad + shifted(share, "grp", by)
    return final, grad


def solution(mesh):
    return jax.shard_map(
        local,
        mesh=mesh,
        in_specs=(
            P("grp", None, "dom", None),
            P(None, "dom", None),
            P(None, "dom", None),
            P(None, "dom", None),
            P(None, "dom", None),
            P(None, "dom", None),
            P("dom", None),
            P("dom", None),
        ),
        out_specs=(P("grp", None, "dom", None), P("dom", None)),
        check_vma=False,
    )
```

```python
import functools

import jax
import jax.numpy as jnp
from jax import lax
from jax.experimental import pallas as pl
from jax.experimental.pallas import tpu as pltpu
from jax.sharding import PartitionSpec as P

ITERS = 4
EDGE = ITERS
ENTRIES = 16
CHUNKS = 3
LANES = 128
SHORT = pl.CostEstimate(flops=1000, bytes_accessed=1000, transcendentals=0)
LOW, HIGH = 0, 1


def swapped(value, axis, partner):
    return lax.ppermute(value, axis, [(i, partner(i)) for i in range(lax.axis_size(axis))])


def level_of(shape):
    row = lax.broadcasted_iota(jnp.int32, shape, 0)
    half = shape[0] // 2
    return jnp.where(row < half, 2 * row, 2 * (row - half) + 1)


def place_of(level, levels):
    return (level % 2) * (levels // 2) + level // 2


def faces(ew, ed, nw, nd):
    lats = ew.shape[1]
    lat = lax.broadcasted_iota(jnp.int32, ew.shape, 1)
    east = jnp.maximum(ew, 0.0) + ed
    west_next = jnp.maximum(-ew, 0.0) + ed
    north = jnp.where(lat < lats - 1, jnp.maximum(nw, 0.0) + nd, 0.0)
    south = jnp.maximum(-nw, 0.0) + nd
    south = jnp.where(lat > 0, pltpu.roll(south, 1, 1), 0.0)
    return east, west_next, north, south


def updraft(mf, top_row):
    levels = mf.shape[0]
    level = level_of(mf.shape)
    return jnp.where((level < top_row) & (level < levels - 1), mf, 0.0)


def advance(coefs, mid, east, west):
    d, e, w, n, s, u = coefs
    levels, lats = mid.shape
    half = levels // 2
    h = d * mid + e * east + w * west
    h = h + n * pltpu.roll(mid, lats - 1, 1) + s * pltpu.roll(mid, 1, 1)
    above = jnp.concatenate([h[half:], pltpu.roll(h[:half], half - 1, 0)], axis=0)
    return h + u * (above - h)


def pitched(slabs, levels, width):
    return -(-(slabs * levels * (width + 1) + width + 8) // 8) * 8


def column_at(ref, start, levels, pitch, apart):
    parts = [ref[pl.ds(start + apart * k, levels, stride=pitch), :] for k in range(2)]
    return jnp.concatenate(parts, axis=1)


def pack_coefs_kernel(parts, place, ew, ed, nw, nd, mf, top, first, second, field_s, top_s, entry, field_p, sems):
    levels, cols, lats = ew.shape
    copies = []

    def copy(src, dst):
        copies.append(pltpu.make_async_copy(src, dst, sems.at[len(copies)]))
        copies[-1].start()

    for side, at in ((LOW, 0), (HIGH, cols - 8)):
        copy(top.at[pl.ds(at, 8)], top_s.at[side])
        for k in range(2):
            for f, field in enumerate((ew, ed, nw, nd, mf)):
                copy(field.at[:, pl.ds(at, 8), pl.ds(k * LANES, LANES)], field_s.at[f, side, k])
    for c in copies:
        c.wait()
    pitch = 9
    slab = levels * pitch

    @pl.loop(0, levels)
    def _(level):
        row = place_of(level, levels) * pitch
        for f in range(5):
            for side in range(2):
                for k in range(2):
                    at = ((f * 2 + side) * 2 + k) * slab
                    field_p[pl.ds(at + row, 8), :] = field_s[f, side, k, level]

    def field(f, side, c):
        return column_at(field_p, (f * 2 + side) * 2 * slab + c, levels, pitch, slab)

    for side in (LOW, HIGH):
        slot = 0
        for c in range(EDGE - 1) if side == LOW else range(8 - EDGE, 8):
            east, west, north, south = faces(*(field(f, side, c) for f in range(4)))
            lift = updraft(field(4, side, c), top_s[side, pl.ds(c, 1), :])
            wanted = (east, west, north, south, lift)
            if side == HIGH and c == 8 - EDGE:
                wanted = (west,)
            for value in wanted:
                entry[side, slot] = value
                slot += 1
        for left in range(slot, ENTRIES):
            entry[side, left] = jnp.zeros((levels, lats), jnp.float32)
    per = ENTRIES // parts
    mine = lax.rem(place[0], parts) * per
    odd = place[1]
    first[...] = entry[1 - odd, pl.ds(mine, per)]
    second[...] = entry[odd, pl.ds(mine, per)]


def pack_coefs(parts, place, fields, top):
    levels, cols, lats = fields[0].shape
    hbm = pl.BlockSpec(memory_space=pltpu.HBM)
    send = pltpu.VMEM((ENTRIES // parts, levels, lats), jnp.float32)
    return pl.pallas_call(
        functools.partial(pack_coefs_kernel, parts),
        in_specs=[pl.BlockSpec(memory_space=pltpu.SMEM)] + [hbm] * 6,
        out_specs=[pl.BlockSpec(memory_space=pltpu.VMEM)] * 2,
        out_shape=[send, send],
        scratch_shapes=[
            pltpu.VMEM((5, 2, 2, levels, 8, LANES), jnp.float32),
            pltpu.VMEM((2, 8, lats), jnp.int32),
            pltpu.VMEM((2, ENTRIES, levels, lats), jnp.float32),
            pltpu.VMEM((pitched(20, levels, 8), LANES), jnp.float32),
            pltpu.SemaphoreType.DMA((22,)),
        ],
        compiler_params=pltpu.CompilerParams(vmem_limit_bytes=24 << 20),
        cost_estimate=SHORT,
        name="pack_coefs",
    )(place, *fields, top)


def pack_lam_kernel(place, lam, first, second, lam_s, lam_p, sems):
    tags, levels, cols, lats = lam.shape
    copies = []
    for side, at in ((LOW, 0), (HIGH, cols - 8)):
        for k in range(2):
            copies.append(
                pltpu.make_async_copy(
                    lam.at[:, :, pl.ds(at, 8), pl.ds(k * LANES, LANES)],
                    lam_s.at[side, k],
                    sems.at[side * 2 + k],
                )
            )
            copies[-1].start()
    for c in copies:
        c.wait()
    pitch = 9
    slab = levels * pitch

    @pl.loop(0, levels)
    def _(level):
        row = place_of(level, levels) * pitch
        for side in range(2):
            for k in range(2):
                for tag in range(tags):
                    at = ((side * 2 + k) * tags + tag) * slab
                    lam_p[pl.ds(at + row, 8), :] = lam_s[side, k, tag, level]

    odd = place[1]
    for dest, side in ((first, 1 - odd), (second, odd)):
        start = side * (2 * tags * slab + 8 - EDGE)
        for tag in range(tags):
            for c in range(EDGE):
                dest[tag, c] = column_at(lam_p, start + tag * slab + c, levels, pitch, tags * slab)


def pack_lam(place, lam):
    tags, levels, cols, lats = lam.shape
    send = pltpu.VMEM((tags, EDGE, levels, lats), jnp.float32)
    return pl.pallas_call(
        pack_lam_kernel,
        in_specs=[pl.BlockSpec(memory_space=pltpu.SMEM), pl.BlockSpec(memory_space=pltpu.HBM)],
        out_specs=[pl.BlockSpec(memory_space=pltpu.VMEM)] * 2,
        out_shape=[send, send],
        scratch_shapes=[
            pltpu.VMEM((2, 2, tags, levels, 8, LANES), jnp.float32),
            pltpu.VMEM((pitched(4 * tags, levels, 8), LANES), jnp.float32),
            pltpu.SemaphoreType.DMA((4,)),
        ],
        compiler_params=pltpu.CompilerParams(vmem_limit_bytes=24 << 20),
        cost_estimate=SHORT,
        name="pack_lam",
    )(place, lam)


def chosen(region_row, first_tag, values):
    row = jnp.zeros(region_row.shape, jnp.float32)
    for tag, value in enumerate(values):
        row = jnp.where(region_row == first_tag + tag, value[0:1], row)
    return row


def sweep(t, first_tag, region, coef, src, store, rows):
    cols, tags = src.shape[:2]
    low, high = t + 1, cols - t - 1
    chunk = -(-(high - low) // CHUNKS)

    @pl.loop(0, CHUNKS)
    def _(i):
        start = jnp.minimum(low + i * chunk, high - chunk)
        for j in range(chunk):
            c = start + j
            coefs = [coef[c, n] for n in range(6)]
            new = [advance(coefs, src[c, k], src[c + 1, k], src[c - 1, k]) for k in range(tags)]
            for k in range(tags):
                store(c, k, new[k])
            rows[t, pl.ds(c, 1), :] = chosen(region[pl.ds(c, 1), :], first_tag, new)


def storing(ref):
    def store(c, tag, value):
        ref[c, tag] = value

    return store


def storing_rows(ref, tags, levels, pitch):
    def store(c, tag, value):
        for k in range(2):
            at = (k * tags + tag) * levels * pitch + c
            ref[pl.ds(at, levels, stride=pitch), :] = value[:, k * LANES : (k + 1) * LANES]

    return store


def inner_kernel(place, lam, ew, ed, nw, nd, mf, top, region, coef, l0, l1, l2, l3, final, rows, lam_p, field_p):
    tags, levels, cols, lats = lam.shape
    pitch = cols + 1
    slab = levels * pitch
    halves = [slice(k * LANES, (k + 1) * LANES) for k in range(2)]

    @pl.loop(0, levels)
    def _(level):
        row = place_of(level, levels) * pitch
        for f, field in enumerate((ew, ed, nw, nd, mf)):
            for k in range(2):
                field_p[pl.ds((f * 2 + k) * slab + row, cols), :] = field[level, :, halves[k]]
        for tag in range(tags):
            for k in range(2):
                lam_p[pl.ds((k * tags + tag) * slab + row, cols), :] = lam[tag, level, :, halves[k]]

    def coefficients(c, west):
        ew, ed, nw, nd, mf = (
            column_at(field_p, f * 2 * slab + c, levels, pitch, slab) for f in range(5)
        )
        e, next_west, n, s = faces(ew, ed, nw, nd)
        u = updraft(mf, top[pl.ds(c, 1), :])
        for j, value in enumerate((1.0 - e - west - n - s, e, west, n, s, u)):
            coef[c, j] = value
        return next_west

    def some(i, west):
        for j in range(8):
            c = i * 8 + j
            west = coefficients(c, west)
            for tag in range(tags):
                l0[c, tag] = column_at(lam_p, tag * slab + c, levels, pitch, tags * slab)
        return west

    west = lax.fori_loop(0, cols // 8, some, jnp.zeros((levels, lats), jnp.float32))
    coef[cols, 2] = west
    first_tag = place[0] * tags
    sweep(0, first_tag, region, coef, l0, storing(l1), rows)
    sweep(1, first_tag, region, coef, l1, storing(l2), rows)
    sweep(2, first_tag, region, coef, l2, storing(l3), rows)
    sweep(3, first_tag, region, coef, l3, storing_rows(final, tags, levels, pitch), rows)


def inner(place, lam, fields, top, region):
    tags, levels, cols, lats = lam.shape
    vmem = pl.BlockSpec(memory_space=pltpu.VMEM)
    state = pltpu.VMEM((cols, tags, levels, lats), jnp.float32)
    return pl.pallas_call(
        inner_kernel,
        in_specs=[pl.BlockSpec(memory_space=pltpu.SMEM)] + [vmem] * 8,
        out_specs=[vmem] * 7,
        out_shape=[
            pltpu.VMEM((cols + 1, 6, levels, lats), jnp.float32),
            *[state] * 4,
            pltpu.VMEM((pitched(2 * tags, levels, cols), LANES), jnp.float32),
            pltpu.VMEM((ITERS, cols, lats), jnp.float32),
        ],
        scratch_shapes=[
            pltpu.VMEM((pitched(2 * tags, levels, cols), LANES), jnp.float32),
            pltpu.VMEM((pitched(10, levels, cols), LANES), jnp.float32),
        ],
        compiler_params=pltpu.CompilerParams(vmem_limit_bytes=32 << 20),
        cost_estimate=SHORT,
        name="inner_steps",
    )(place, lam, *fields, top, region)


def border_kernel(parts, place, region, coef, l0, l1, l2, l3, first, second, *refs):
    pieces = refs[:parts]
    final_in, rows_in, final, grad, entry, halo, wide, work, rows = refs[parts:]
    cols, tags, levels, lats = l0.shape
    first_tag = place[0] * tags
    per = ENTRIES // parts
    mine = lax.rem(place[0], parts)
    odd = place[1]
    halo[1 - odd] = first[...]
    halo[odd] = second[...]
    for by in range(parts):
        base = (mine ^ by) * per
        entry[1 - odd, pl.ds(base, per)] = pieces[by][0]
        entry[odd, pl.ds(base, per)] = pieces[by][1]

    def slot(c):
        return (LOW, c + EDGE - 1) if c < EDGE else (HIGH, c - (cols - EDGE))

    def outside(c):
        if c < 0:
            at = 1 + 5 * (c + EDGE - 1)
            e, _, n, s, u = (entry[LOW, at + j] for j in range(5))
            w = entry[LOW, at - 4] if c > 1 - EDGE else entry[LOW, 0]
        else:
            at = 5 * (c - cols)
            e, _, n, s, u = (entry[HIGH, at + j] for j in range(5))
            w = entry[HIGH, at - 4] if c > cols else coef[cols, 2]
        return 1.0 - e - w - n - s, e, w, n, s, u

    for c in [*range(1 - EDGE, 0), *range(cols, cols + EDGE - 1)]:
        for j, value in enumerate(outside(c)):
            wide[*slot(c), j] = value
    first_west = entry[LOW, 1 + 5 * (EDGE - 2) + 1]
    first_mid = 1.0 - coef[0, 1] - first_west - coef[0, 3] - coef[0, 4]
    for j, value in enumerate((first_mid, coef[0, 1], first_west, *(coef[0, j] for j in range(3, 6)))):
        wide[*slot(0), j] = value

    def coefs_at(c):
        if 0 < c < cols:
            return [coef[c, j] for j in range(6)]
        return [wide[*slot(c), j] for j in range(6)]

    kept = (l0, l1, l2, l3)

    def state(t, c, tag):
        if t <= c < cols - t:
            return kept[t][c, tag]
        if t == 0:
            return halo[LOW, tag, c + EDGE] if c < 0 else halo[HIGH, tag, c - cols]
        return work[t, *slot(c), tag]

    rows[...] = rows_in[...]
    store = storing_rows(final, tags, levels, cols + 1)
    for t in range(ITERS):
        reach = EDGE - 1 - t
        for c in [*range(-reach, t + 1), *range(cols - t - 1, cols + reach)]:
            coefs = coefs_at(c)
            new = [
                advance(coefs, state(t, c, k), state(t, c + 1, k), state(t, c - 1, k))
                for k in range(tags)
            ]
            for k in range(tags):
                if t < ITERS - 1:
                    work[t + 1, *slot(c), k] = new[k]
                else:
                    store(c, k, new[k])
            if 0 <= c < cols:
                rows[t, c : c + 1, :] = chosen(region[c : c + 1, :], first_tag, new)
    total = rows[0]
    for t in range(1, ITERS):
        total = total + rows[t]
    grad[...] = total


def border(parts, place, region, coef, states, first, second, pieces, final, rows):
    cols, tags, levels, lats = states[0].shape
    vmem = pl.BlockSpec(memory_space=pltpu.VMEM)
    operands = [region, coef, *states, first, second, *pieces]
    return pl.pallas_call(
        functools.partial(border_kernel, parts),
        in_specs=[pl.BlockSpec(memory_space=pltpu.SMEM)] + [vmem] * (len(operands) + 2),
        out_specs=[vmem] * 2,
        out_shape=[
            pltpu.VMEM(final.shape, jnp.float32),
            pltpu.VMEM((cols, lats), jnp.float32),
        ],
        input_output_aliases={len(operands) + 1: 0},
        scratch_shapes=[
            pltpu.VMEM((2, ENTRIES, levels, lats), jnp.float32),
            pltpu.VMEM((2, tags, EDGE, levels, lats), jnp.float32),
            pltpu.VMEM((2, 2 * EDGE - 1, 6, levels, lats), jnp.float32),
            pltpu.VMEM((ITERS, 2, 2 * EDGE - 1, tags, levels, lats), jnp.float32),
            pltpu.VMEM((ITERS, cols, lats), jnp.float32),
        ],
        compiler_params=pltpu.CompilerParams(vmem_limit_bytes=32 << 20),
        cost_estimate=SHORT,
        name="border_steps",
    )(place, *operands, final, rows)


def write_kernel(final, out, block, sems):
    tags, levels, cols, _ = out.shape
    pitch = cols + 1
    copies = []
    for tag in range(tags):

        @pl.loop(0, levels)
        def _(level):
            row = place_of(level, levels) * pitch
            for k in range(2):
                at = (k * tags + tag) * levels * pitch + row
                block[tag, level, :, k * LANES : (k + 1) * LANES] = final[pl.ds(at, cols), :]

        copies.append(pltpu.make_async_copy(block.at[tag], out.at[tag], sems.at[tag]))
        copies[-1].start()
    for c in copies:
        c.wait()


def write(final, shape):
    return pl.pallas_call(
        write_kernel,
        in_specs=[pl.BlockSpec(memory_space=pltpu.VMEM)],
        out_specs=pl.BlockSpec(memory_space=pltpu.HBM),
        out_shape=pltpu.HBM(shape, jnp.float32),
        scratch_shapes=[
            pltpu.VMEM(shape, jnp.float32),
            pltpu.SemaphoreType.DMA((shape[0],)),
        ],
        compiler_params=pltpu.CompilerParams(vmem_limit_bytes=24 << 20),
        cost_estimate=SHORT,
        name="write_final",
    )(final)


def local(lam, east_wind, north_wind, east_diff, north_diff, mass_flux, region, top):
    groups, tiles = lax.axis_size("grp"), lax.axis_size("dom")
    parts = 4 if groups % 4 == 0 else 1
    grp, dom = lax.axis_index("grp"), lax.axis_index("dom")
    place = jnp.stack([grp, dom % 2]).astype(jnp.int32)
    own = (lam, east_wind, east_diff, north_wind, north_diff, mass_flux)
    far = [pltpu.with_memory_space_constraint(value, pltpu.HBM) for value in (*own, top)]

    pairs = lambda i: i ^ 1
    turn = lambda i: (((i - 1) % tiles ^ 1) + 1) % tiles
    coef_first, coef_second = pack_coefs(parts, place, far[1:6], far[6])
    coef_first, coef_second, far_lam, *own = lax.optimization_barrier(
        (coef_first, coef_second, far[0], *own)
    )
    lam_first, lam_second = pack_lam(place, far_lam)
    coef_first = swapped(coef_first, "dom", pairs)
    coef_second = swapped(coef_second, "dom", turn)
    coef_first, coef_second, _ = lax.optimization_barrier((coef_first, coef_second, lam_first))
    first = swapped(lam_first, "dom", pairs)
    second = swapped(lam_second, "dom", turn)
    pieces = [jnp.stack([coef_first, coef_second])]
    for by in range(1, parts):
        pieces.append(swapped(pieces[0], "grp", lambda i: i ^ by))
    coef, *states, final, rows = inner(place, own[0], own[1:], top, region)
    final, grad = border(parts, place, region, coef, states, first, second, pieces, final, rows)
    share = grad
    for by in range(1, groups):
        grad = grad + swapped(share, "grp", lambda i: (i + by) % groups)
    return write(final, lam.shape), grad


def solution(mesh):
    return jax.shard_map(
        local,
        mesh=mesh,
        in_specs=(
            P("grp", None, "dom", None),
            P(None, "dom", None),
            P(None, "dom", None),
            P(None, "dom", None),
            P(None, "dom", None),
            P(None, "dom", None),
            P("dom", None),
            P("dom", None),
        ),
        out_specs=(P("grp", None, "dom", None), P("dom", None)),
        check_vma=False,
    )
```

```python
import functools

import jax
import jax.numpy as jnp
from jax import lax
from jax.experimental import pallas as pl
from jax.experimental.pallas import tpu as pltpu
from jax.sharding import PartitionSpec as P

ITERS = 4
EDGE = ITERS
ENTRIES = 16
CHUNKS = 3
LANES = 128
HALVES = (slice(0, LANES), slice(LANES, 2 * LANES))
SHORT = pl.CostEstimate(flops=1000, bytes_accessed=1000, transcendentals=0)
LOW, HIGH = 0, 1


def swapped(value, axis, partner):
    return lax.ppermute(value, axis, [(i, partner(i)) for i in range(lax.axis_size(axis))])


def level_of(shape):
    row = lax.broadcasted_iota(jnp.int32, shape, 0)
    half = shape[0] // 2
    return jnp.where(row < half, 2 * row, 2 * (row - half) + 1)


def place_of(level, levels):
    return (level % 2) * (levels // 2) + level // 2


def faces(ew, ed, nw, nd):
    lats = ew.shape[1]
    lat = lax.broadcasted_iota(jnp.int32, ew.shape, 1)
    east = jnp.maximum(ew, 0.0) + ed
    west_next = jnp.maximum(-ew, 0.0) + ed
    north = jnp.where(lat < lats - 1, jnp.maximum(nw, 0.0) + nd, 0.0)
    south = jnp.maximum(-nw, 0.0) + nd
    south = jnp.where(lat > 0, pltpu.roll(south, 1, 1), 0.0)
    return east, west_next, north, south


def updraft(mf, top_row):
    levels = mf.shape[0]
    level = level_of(mf.shape)
    return jnp.where((level < top_row) & (level < levels - 1), mf, 0.0)


def advance(coefs, mid, east, west):
    d, e, w, n, s, u = coefs
    half = mid.shape[0] // 2
    h = d * mid + e * east + w * west
    lane = lax.broadcasted_iota(jnp.int32, (mid.shape[0], LANES), 1)
    north = [pltpu.roll(mid[:, part], LANES - 1, 1) for part in HALVES]
    south = [pltpu.roll(mid[:, part], 1, 1) for part in HALVES]
    north = jnp.concatenate([jnp.where(lane < LANES - 1, *north), north[1]], axis=1)
    south = jnp.concatenate([south[0], jnp.where(lane > 0, south[1], south[0])], axis=1)
    h = h + n * north + s * south
    above = jnp.concatenate([h[half:], pltpu.roll(h[:half], half - 1, 0)], axis=0)
    return h + u * (above - h)


def pitched(slabs, levels, width):
    return -(-(slabs * levels * (width + 1) + width + 8) // 8) * 8


def column_at(ref, start, levels, pitch, apart):
    parts = [ref[pl.ds(start + apart * k, levels, stride=pitch), :] for k in range(2)]
    return jnp.concatenate(parts, axis=1)


def pack_kernel(parts, place, lam, ew, ed, nw, nd, mf, top, *refs):
    coef_first, coef_second, lam_first, lam_second = refs[:4]
    field_s, top_s, lam_s, entry, field_p, lam_p, sems = refs[4:]
    tags, levels, cols, lats = lam.shape
    copies = []

    def copy(src, dst):
        copies.append(pltpu.make_async_copy(src, dst, sems.at[len(copies)]))
        copies[-1].start()

    for side, at in ((LOW, 0), (HIGH, cols - 8)):
        for f, field in enumerate((ew, ed, nw, nd, mf)):
            copy(field.at[:, pl.ds(at, 8)], field_s.at[f, side])
        copy(top.at[pl.ds(at, 8)], top_s.at[side])
    field_copies = len(copies)
    for side, at in ((LOW, 0), (HIGH, cols - 8)):
        copy(lam.at[:, :, pl.ds(at, 8)], lam_s.at[side])
    for c in copies[:field_copies]:
        c.wait()
    pitch = 9
    slab = levels * pitch

    @pl.loop(0, levels)
    def _(level):
        row = place_of(level, levels) * pitch
        for f in range(5):
            for side in range(2):
                for k in range(2):
                    at = ((f * 2 + side) * 2 + k) * slab
                    field_p[pl.ds(at + row, 8), :] = field_s[f, side, level, :, HALVES[k]]

    def field(f, side, c):
        return column_at(field_p, (f * 2 + side) * 2 * slab + c, levels, pitch, slab)

    for side in (LOW, HIGH):
        slot = 0
        for c in range(EDGE - 1) if side == LOW else range(8 - EDGE, 8):
            east, west, north, south = faces(*(field(f, side, c) for f in range(4)))
            lift = updraft(field(4, side, c), top_s[side, pl.ds(c, 1), :])
            wanted = (east, west, north, south, lift)
            if side == HIGH and c == 8 - EDGE:
                wanted = (west,)
            for value in wanted:
                entry[side, slot] = value
                slot += 1
        for left in range(slot, ENTRIES):
            entry[side, left] = jnp.zeros((levels, lats), jnp.float32)
    per = ENTRIES // parts
    mine = lax.rem(place[0], parts) * per
    odd = place[1]
    coef_first[...] = entry[1 - odd, pl.ds(mine, per)]
    coef_second[...] = entry[odd, pl.ds(mine, per)]

    for c in copies[field_copies:]:
        c.wait()

    @pl.loop(0, levels)
    def _(level):
        row = place_of(level, levels) * pitch
        for side in range(2):
            for tag in range(tags):
                for k in range(2):
                    at = ((side * 2 + k) * tags + tag) * slab
                    lam_p[pl.ds(at + row, 8), :] = lam_s[side, tag, level, :, HALVES[k]]

    for dest, side in ((lam_first, 1 - odd), (lam_second, odd)):
        start = side * (2 * tags * slab + 8 - EDGE)
        for tag in range(tags):
            for c in range(EDGE):
                dest[tag, c] = column_at(lam_p, start + tag * slab + c, levels, pitch, tags * slab)


def pack(parts, place, lam, fields, top):
    tags, levels, cols, lats = lam.shape
    hbm = pl.BlockSpec(memory_space=pltpu.HBM)
    coef_send = pltpu.VMEM((ENTRIES // parts, levels, lats), jnp.float32)
    lam_send = pltpu.VMEM((tags, EDGE, levels, lats), jnp.float32)
    return pl.pallas_call(
        functools.partial(pack_kernel, parts),
        in_specs=[pl.BlockSpec(memory_space=pltpu.SMEM)] + [hbm] * 7,
        out_specs=[pl.BlockSpec(memory_space=pltpu.VMEM)] * 4,
        out_shape=[coef_send, coef_send, lam_send, lam_send],
        scratch_shapes=[
            pltpu.VMEM((5, 2, levels, 8, lats), jnp.float32),
            pltpu.VMEM((2, 8, lats), jnp.int32),
            pltpu.VMEM((2, tags, levels, 8, lats), jnp.float32),
            pltpu.VMEM((2, ENTRIES, levels, lats), jnp.float32),
            pltpu.VMEM((pitched(20, levels, 8), LANES), jnp.float32),
            pltpu.VMEM((pitched(4 * tags, levels, 8), LANES), jnp.float32),
            pltpu.SemaphoreType.DMA((14,)),
        ],
        compiler_params=pltpu.CompilerParams(vmem_limit_bytes=24 << 20),
        cost_estimate=SHORT,
        name="pack_edges",
    )(place, lam, *fields, top)


def chosen(region_row, first_tag, values):
    row = jnp.zeros(region_row.shape, jnp.float32)
    for tag, value in enumerate(values):
        row = jnp.where(region_row == first_tag + tag, value[0:1], row)
    return row


def sweep(t, first_tag, region, coef, src, store, rows):
    cols, tags = src.shape[:2]
    low, high = t + 1, cols - t - 1
    chunk = -(-(high - low) // CHUNKS)

    @pl.loop(0, CHUNKS)
    def _(i):
        start = jnp.minimum(low + i * chunk, high - chunk)
        for j in range(chunk):
            c = start + j
            coefs = [coef[c, n] for n in range(6)]
            new = [advance(coefs, src[c, k], src[c + 1, k], src[c - 1, k]) for k in range(tags)]
            for k in range(tags):
                store(c, k, new[k])
            rows[t, pl.ds(c, 1), :] = chosen(region[pl.ds(c, 1), :], first_tag, new)


def storing(ref):
    def store(c, tag, value):
        ref[c, tag] = value

    return store


def storing_rows(ref, tags, levels, pitch):
    def store(c, tag, value):
        for k in range(2):
            at = (k * tags + tag) * levels * pitch + c
            ref[pl.ds(at, levels, stride=pitch), :] = value[:, HALVES[k]]

    return store


def inner_kernel(place, lam, ew, ed, nw, nd, mf, top, region, *refs):
    coef, l0, l1, l2, l3, final, rows, lam_s, lam_p, field_p, sems = refs
    tags, levels, cols, lats = lam.shape
    pitch = cols + 1
    slab = levels * pitch
    loads = [pltpu.make_async_copy(lam.at[k], lam_s.at[k], sems.at[k]) for k in range(tags)]
    for c in loads:
        c.start()

    @pl.loop(0, levels)
    def _(level):
        row = place_of(level, levels) * pitch
        for f, field in enumerate((ew, ed, nw, nd, mf)):
            for k in range(2):
                field_p[pl.ds((f * 2 + k) * slab + row, cols), :] = field[level, :, HALVES[k]]

    def coefficients(c, west):
        ew, ed, nw, nd, mf = (
            column_at(field_p, f * 2 * slab + c, levels, pitch, slab) for f in range(5)
        )
        e, next_west, n, s = faces(ew, ed, nw, nd)
        u = updraft(mf, top[pl.ds(c, 1), :])
        for j, value in enumerate((1.0 - e - west - n - s, e, west, n, s, u)):
            coef[c, j] = value
        return next_west

    def some(i, west):
        for j in range(8):
            c = i * 8 + j
            west = coefficients(c, west)
        return west

    west = lax.fori_loop(0, cols // 8, some, jnp.zeros((levels, lats), jnp.float32))
    coef[cols, 2] = west
    for c in loads:
        c.wait()

    @pl.loop(0, levels)
    def _(level):
        row = place_of(level, levels) * pitch
        for tag in range(tags):
            for k in range(2):
                at = (k * tags + tag) * slab + row
                lam_p[pl.ds(at, cols), :] = lam_s[tag, level, :, HALVES[k]]

    @pl.loop(0, cols // 8)
    def _(i):
        for j in range(8):
            c = i * 8 + j
            for tag in range(tags):
                l0[c, tag] = column_at(lam_p, tag * slab + c, levels, pitch, tags * slab)

    first_tag = place[0] * tags
    sweep(0, first_tag, region, coef, l0, storing(l1), rows)
    sweep(1, first_tag, region, coef, l1, storing(l2), rows)
    sweep(2, first_tag, region, coef, l2, storing(l3), rows)
    sweep(3, first_tag, region, coef, l3, storing_rows(final, tags, levels, pitch), rows)


def inner(place, lam, fields, top, region):
    tags, levels, cols, lats = lam.shape
    vmem = pl.BlockSpec(memory_space=pltpu.VMEM)
    state = pltpu.VMEM((cols, tags, levels, lats), jnp.float32)
    return pl.pallas_call(
        inner_kernel,
        in_specs=[
            pl.BlockSpec(memory_space=pltpu.SMEM),
            pl.BlockSpec(memory_space=pltpu.HBM),
            *[vmem] * 7,
        ],
        out_specs=[vmem] * 7,
        out_shape=[
            pltpu.VMEM((cols + 1, 6, levels, lats), jnp.float32),
            *[state] * 4,
            pltpu.VMEM((pitched(2 * tags, levels, cols), LANES), jnp.float32),
            pltpu.VMEM((ITERS, cols, lats), jnp.float32),
        ],
        scratch_shapes=[
            pltpu.VMEM(lam.shape, jnp.float32),
            pltpu.VMEM((pitched(2 * tags, levels, cols), LANES), jnp.float32),
            pltpu.VMEM((pitched(10, levels, cols), LANES), jnp.float32),
            pltpu.SemaphoreType.DMA((tags,)),
        ],
        compiler_params=pltpu.CompilerParams(vmem_limit_bytes=32 << 20),
        cost_estimate=SHORT,
        name="inner_steps",
    )(place, lam, *fields, top, region)


def border_kernel(parts, place, region, coef, l0, l1, l2, l3, first, second, *refs):
    pieces = refs[:parts]
    final_in, rows_in, final, grad, entry, halo, wide, work, rows = refs[parts:]
    cols, tags, levels, lats = l0.shape
    first_tag = place[0] * tags
    per = ENTRIES // parts
    mine = lax.rem(place[0], parts)
    odd = place[1]
    halo[1 - odd] = first[...]
    halo[odd] = second[...]
    for by in range(parts):
        base = (mine ^ by) * per
        entry[1 - odd, pl.ds(base, per)] = pieces[by][0]
        entry[odd, pl.ds(base, per)] = pieces[by][1]

    def slot(c):
        return (LOW, c + EDGE - 1) if c < EDGE else (HIGH, c - (cols - EDGE))

    def outside(c):
        if c < 0:
            at = 1 + 5 * (c + EDGE - 1)
            e, _, n, s, u = (entry[LOW, at + j] for j in range(5))
            w = entry[LOW, at - 4] if c > 1 - EDGE else entry[LOW, 0]
        else:
            at = 5 * (c - cols)
            e, _, n, s, u = (entry[HIGH, at + j] for j in range(5))
            w = entry[HIGH, at - 4] if c > cols else coef[cols, 2]
        return 1.0 - e - w - n - s, e, w, n, s, u

    for c in [*range(1 - EDGE, 0), *range(cols, cols + EDGE - 1)]:
        for j, value in enumerate(outside(c)):
            wide[*slot(c), j] = value
    first_west = entry[LOW, 1 + 5 * (EDGE - 2) + 1]
    first_mid = 1.0 - coef[0, 1] - first_west - coef[0, 3] - coef[0, 4]
    for j, value in enumerate((first_mid, coef[0, 1], first_west, *(coef[0, j] for j in range(3, 6)))):
        wide[*slot(0), j] = value

    def coefs_at(c):
        if 0 < c < cols:
            return [coef[c, j] for j in range(6)]
        return [wide[*slot(c), j] for j in range(6)]

    kept = (l0, l1, l2, l3)

    def state(t, c, tag):
        if t <= c < cols - t:
            return kept[t][c, tag]
        if t == 0:
            return halo[LOW, tag, c + EDGE] if c < 0 else halo[HIGH, tag, c - cols]
        return work[t, *slot(c), tag]

    rows[...] = rows_in[...]
    store = storing_rows(final, tags, levels, cols + 1)
    for t in range(ITERS):
        reach = EDGE - 1 - t
        for c in [*range(-reach, t + 1), *range(cols - t - 1, cols + reach)]:
            coefs = coefs_at(c)
            new = [
                advance(coefs, state(t, c, k), state(t, c + 1, k), state(t, c - 1, k))
                for k in range(tags)
            ]
            for k in range(tags):
                if t < ITERS - 1:
                    work[t + 1, *slot(c), k] = new[k]
                else:
                    store(c, k, new[k])
            if 0 <= c < cols:
                rows[t, c : c + 1, :] = chosen(region[c : c + 1, :], first_tag, new)
    total = rows[0]
    for t in range(1, ITERS):
        total = total + rows[t]
    grad[...] = total


def border(parts, place, region, coef, states, first, second, pieces, final, rows):
    cols, tags, levels, lats = states[0].shape
    vmem = pl.BlockSpec(memory_space=pltpu.VMEM)
    operands = [region, coef, *states, first, second, *pieces]
    return pl.pallas_call(
        functools.partial(border_kernel, parts),
        in_specs=[pl.BlockSpec(memory_space=pltpu.SMEM)] + [vmem] * (len(operands) + 2),
        out_specs=[vmem] * 2,
        out_shape=[
            pltpu.VMEM(final.shape, jnp.float32),
            pltpu.VMEM((cols, lats), jnp.float32),
        ],
        input_output_aliases={len(operands) + 1: 0},
        scratch_shapes=[
            pltpu.VMEM((2, ENTRIES, levels, lats), jnp.float32),
            pltpu.VMEM((2, tags, EDGE, levels, lats), jnp.float32),
            pltpu.VMEM((2, 2 * EDGE - 1, 6, levels, lats), jnp.float32),
            pltpu.VMEM((ITERS, 2, 2 * EDGE - 1, tags, levels, lats), jnp.float32),
            pltpu.VMEM((ITERS, cols, lats), jnp.float32),
        ],
        compiler_params=pltpu.CompilerParams(vmem_limit_bytes=32 << 20),
        cost_estimate=SHORT,
        name="border_steps",
    )(place, *operands, final, rows)


def write_kernel(final, out, block, sems):
    tags, levels, cols, _ = out.shape
    pitch = cols + 1
    copies = []
    for tag in range(tags):

        @pl.loop(0, levels)
        def _(level):
            row = place_of(level, levels) * pitch
            for k in range(2):
                at = (k * tags + tag) * levels * pitch + row
                block[tag, level, :, HALVES[k]] = final[pl.ds(at, cols), :]

        copies.append(pltpu.make_async_copy(block.at[tag], out.at[tag], sems.at[tag]))
        copies[-1].start()
    for c in copies:
        c.wait()


def write(final, shape):
    return pl.pallas_call(
        write_kernel,
        in_specs=[pl.BlockSpec(memory_space=pltpu.VMEM)],
        out_specs=pl.BlockSpec(memory_space=pltpu.HBM),
        out_shape=pltpu.HBM(shape, jnp.float32),
        scratch_shapes=[
            pltpu.VMEM(shape, jnp.float32),
            pltpu.SemaphoreType.DMA((shape[0],)),
        ],
        compiler_params=pltpu.CompilerParams(vmem_limit_bytes=24 << 20),
        cost_estimate=SHORT,
        name="write_final",
    )(final)


def local(lam, east_wind, north_wind, east_diff, north_diff, mass_flux, region, top):
    groups, tiles = lax.axis_size("grp"), lax.axis_size("dom")
    parts = 4 if groups % 4 == 0 else 1
    grp, dom = lax.axis_index("grp"), lax.axis_index("dom")
    place = jnp.stack([grp, dom % 2]).astype(jnp.int32)
    own = (lam, east_wind, east_diff, north_wind, north_diff, mass_flux)
    far = [pltpu.with_memory_space_constraint(value, pltpu.HBM) for value in (*own, top)]

    pairs = lambda i: i ^ 1
    turn = lambda i: (((i - 1) % tiles ^ 1) + 1) % tiles
    coef_first, coef_second, lam_first, lam_second = pack(parts, place, far[0], far[1:6], far[6])
    coef_first = swapped(coef_first, "dom", pairs)
    coef_second = swapped(coef_second, "dom", turn)
    first = swapped(lam_first, "dom", pairs)
    second = swapped(lam_second, "dom", turn)
    pieces = [jnp.stack([coef_first, coef_second])]
    for by in range(1, parts):
        pieces.append(swapped(pieces[0], "grp", lambda i: i ^ by))
    coef, *states, final, rows = inner(place, far[0], own[1:], top, region)
    final, grad = border(parts, place, region, coef, states, first, second, pieces, final, rows)
    share = grad
    for by in range(1, groups):
        grad = grad + swapped(share, "grp", lambda i: (i + by) % groups)
    return write(final, lam.shape), grad


def solution(mesh):
    return jax.shard_map(
        local,
        mesh=mesh,
        in_specs=(
            P("grp", None, "dom", None),
            P(None, "dom", None),
            P(None, "dom", None),
            P(None, "dom", None),
            P(None, "dom", None),
            P(None, "dom", None),
            P("dom", None),
            P("dom", None),
        ),
        out_specs=(P("grp", None, "dom", None), P("dom", None)),
        check_vma=False,
    )
```

```python
import functools

import jax
import jax.numpy as jnp
from jax import lax
from jax.experimental import pallas as pl
from jax.experimental.pallas import tpu as pltpu
from jax.sharding import PartitionSpec as P

ITERS = 4
EDGE = ITERS
ENTRIES = 16
CHUNKS = 3
LANES = 128
HALVES = (slice(0, LANES), slice(LANES, 2 * LANES))
SHORT = pl.CostEstimate(flops=1000, bytes_accessed=1000, transcendentals=0)
LOW, HIGH = 0, 1


def swapped(value, axis, partner):
    return lax.ppermute(value, axis, [(i, partner(i)) for i in range(lax.axis_size(axis))])


def level_of(shape):
    row = lax.broadcasted_iota(jnp.int32, shape, 0)
    half = shape[0] // 2
    return jnp.where(row < half, 2 * row, 2 * (row - half) + 1)


def place_of(level, levels):
    return (level % 2) * (levels // 2) + level // 2


def faces(ew, ed, nw, nd):
    lats = ew.shape[1]
    lat = lax.broadcasted_iota(jnp.int32, ew.shape, 1)
    east = jnp.maximum(ew, 0.0) + ed
    west_next = jnp.maximum(-ew, 0.0) + ed
    north = jnp.where(lat < lats - 1, jnp.maximum(nw, 0.0) + nd, 0.0)
    south = jnp.maximum(-nw, 0.0) + nd
    south = jnp.where(lat > 0, pltpu.roll(south, 1, 1), 0.0)
    return east, west_next, north, south


def updraft(mf, top_row):
    levels = mf.shape[0]
    level = level_of(mf.shape)
    return jnp.where((level < top_row) & (level < levels - 1), mf, 0.0)


def advance(coefs, mid, east, west):
    d, e, w, n, s, u = coefs
    half = mid.shape[0] // 2
    h = d * mid + e * east + w * west
    lane = lax.broadcasted_iota(jnp.int32, (mid.shape[0], LANES), 1)
    north = [pltpu.roll(mid[:, part], LANES - 1, 1) for part in HALVES]
    south = [pltpu.roll(mid[:, part], 1, 1) for part in HALVES]
    north = jnp.concatenate([jnp.where(lane < LANES - 1, *north), north[1]], axis=1)
    south = jnp.concatenate([south[0], jnp.where(lane > 0, south[1], south[0])], axis=1)
    h = h + n * north + s * south
    above = jnp.concatenate([h[half:], pltpu.roll(h[:half], half - 1, 0)], axis=0)
    return h + u * (above - h)


def pitched(slabs, levels, width):
    return -(-(slabs * levels * (width + 1) + width + 8) // 8) * 8


def column_at(ref, start, levels, pitch, apart):
    parts = [ref[pl.ds(start + apart * k, levels, stride=pitch), :] for k in range(2)]
    return jnp.concatenate(parts, axis=1)


def pack_kernel(parts, place, lam, ew, ed, nw, nd, mf, top, *refs):
    coef_first, coef_second, lam_first, lam_second = refs[:4]
    field_s, top_s, lam_s, entry, field_p, lam_p, sems = refs[4:]
    tags, levels, cols, lats = lam.shape
    copies = []

    def copy(src, dst):
        copies.append(pltpu.make_async_copy(src, dst, sems.at[len(copies)]))
        copies[-1].start()

    for side, at in ((LOW, 0), (HIGH, cols - 8)):
        for f, field in enumerate((ew, ed, nw, nd, mf)):
            copy(field.at[:, pl.ds(at, 8)], field_s.at[f, side])
        copy(top.at[pl.ds(at, 8)], top_s.at[side])
    field_copies = len(copies)
    for side, at in ((LOW, 0), (HIGH, cols - 8)):
        copy(lam.at[:, :, pl.ds(at, 8)], lam_s.at[side])
    for c in copies[:field_copies]:
        c.wait()
    pitch = 9
    slab = levels * pitch

    @pl.loop(0, levels)
    def _(level):
        row = place_of(level, levels) * pitch
        for f in range(5):
            for side in range(2):
                for k in range(2):
                    at = ((f * 2 + side) * 2 + k) * slab
                    field_p[pl.ds(at + row, 8), :] = field_s[f, side, level, :, HALVES[k]]

    def field(f, side, c):
        return column_at(field_p, (f * 2 + side) * 2 * slab + c, levels, pitch, slab)

    for side in (LOW, HIGH):
        slot = 0
        for c in range(EDGE - 1) if side == LOW else range(8 - EDGE, 8):
            east, west, north, south = faces(*(field(f, side, c) for f in range(4)))
            lift = updraft(field(4, side, c), top_s[side, pl.ds(c, 1), :])
            wanted = (east, west, north, south, lift)
            if side == HIGH and c == 8 - EDGE:
                wanted = (west,)
            for value in wanted:
                entry[side, slot] = value
                slot += 1
        for left in range(slot, ENTRIES):
            entry[side, left] = jnp.zeros((levels, lats), jnp.float32)
    per = ENTRIES // parts
    mine = lax.rem(place[0], parts) * per
    odd = place[1]
    coef_first[...] = entry[1 - odd, pl.ds(mine, per)]
    coef_second[...] = entry[odd, pl.ds(mine, per)]

    for c in copies[field_copies:]:
        c.wait()

    @pl.loop(0, levels)
    def _(level):
        row = place_of(level, levels) * pitch
        for side in range(2):
            for tag in range(tags):
                for k in range(2):
                    at = ((side * 2 + k) * tags + tag) * slab
                    lam_p[pl.ds(at + row, 8), :] = lam_s[side, tag, level, :, HALVES[k]]

    for dest, side in ((lam_first, 1 - odd), (lam_second, odd)):
        start = side * (2 * tags * slab + 8 - EDGE)
        for tag in range(tags):
            for c in range(EDGE):
                dest[tag * EDGE + c] = column_at(lam_p, start + tag * slab + c, levels, pitch, tags * slab)


def pack(parts, place, lam, fields, top):
    tags, levels, cols, lats = lam.shape
    hbm = pl.BlockSpec(memory_space=pltpu.HBM)
    send = lambda slabs: pltpu.VMEM((slabs, levels, lats), jnp.float32)
    few, many = ENTRIES // parts, tags * EDGE
    return pl.pallas_call(
        functools.partial(pack_kernel, parts),
        in_specs=[pl.BlockSpec(memory_space=pltpu.SMEM)] + [hbm] * 7,
        out_specs=[pl.BlockSpec(memory_space=pltpu.VMEM)] * 4,
        out_shape=[send(few), send(few), send(many), send(many)],
        scratch_shapes=[
            pltpu.VMEM((5, 2, levels, 8, lats), jnp.float32),
            pltpu.VMEM((2, 8, lats), jnp.int32),
            pltpu.VMEM((2, tags, levels, 8, lats), jnp.float32),
            pltpu.VMEM((2, ENTRIES, levels, lats), jnp.float32),
            pltpu.VMEM((pitched(20, levels, 8), LANES), jnp.float32),
            pltpu.VMEM((pitched(4 * tags, levels, 8), LANES), jnp.float32),
            pltpu.SemaphoreType.DMA((14,)),
        ],
        compiler_params=pltpu.CompilerParams(vmem_limit_bytes=24 << 20),
        cost_estimate=SHORT,
        name="pack_edges",
    )(place, lam, *fields, top)


def chosen(region_row, first_tag, values):
    row = jnp.zeros(region_row.shape, jnp.float32)
    for tag, value in enumerate(values):
        row = jnp.where(region_row == first_tag + tag, value[0:1], row)
    return row


def sweep(t, shape, first_tag, region, coef, load, store, rows):
    tags, _, cols, _ = shape
    low, high = t + 1, cols - t - 1
    chunk = -(-(high - low) // CHUNKS)
    column = lambda c: [load(c, k) for k in range(tags)]

    @pl.loop(0, CHUNKS)
    def _(i):
        start = jnp.minimum(low + i * chunk, high - chunk)
        west, mid = column(start - 1), column(start)
        for j in range(chunk):
            c = start + j
            east = column(c + 1)
            coefs = [coef[c, n] for n in range(6)]
            new = [advance(coefs, mid[k], east[k], west[k]) for k in range(tags)]
            for k in range(tags):
                store(c, k, new[k])
            rows[t, pl.ds(c, 1), :] = chosen(region[pl.ds(c, 1), :], first_tag, new)
            west, mid = mid, east


def loading(ref):
    return lambda c, tag: ref[c, tag]


def storing(ref):
    def store(c, tag, value):
        ref[c, tag] = value

    return store


def storing_rows(ref, tags, levels, pitch):
    def store(c, tag, value):
        for k in range(2):
            at = (k * tags + tag) * levels * pitch + c
            ref[pl.ds(at, levels, stride=pitch), :] = value[:, HALVES[k]]

    return store


def inner_kernel(place, lam, ew, ed, nw, nd, mf, top, region, *refs):
    coef, l0, l1, l2, l3, final, rows, lam_p, field_p = refs
    tags, levels, cols, lats = lam.shape
    pitch = cols + 1
    slab = levels * pitch

    @pl.loop(0, levels)
    def _(level):
        row = place_of(level, levels) * pitch
        for f, field in enumerate((ew, ed, nw, nd, mf)):
            for k in range(2):
                field_p[pl.ds((f * 2 + k) * slab + row, cols), :] = field[level, :, HALVES[k]]
        for tag in range(tags):
            for k in range(2):
                at = (k * tags + tag) * slab + row
                lam_p[pl.ds(at, cols), :] = lam[tag, level, :, HALVES[k]]

    def coefficients(c, west):
        ew, ed, nw, nd, mf = (
            column_at(field_p, f * 2 * slab + c, levels, pitch, slab) for f in range(5)
        )
        e, next_west, n, s = faces(ew, ed, nw, nd)
        u = updraft(mf, top[pl.ds(c, 1), :])
        for j, value in enumerate((1.0 - e - west - n - s, e, west, n, s, u)):
            coef[c, j] = value
        return next_west

    def some(i, west):
        for j in range(8):
            west = coefficients(i * 8 + j, west)
        return west

    west = lax.fori_loop(0, cols // 8, some, jnp.zeros((levels, lats), jnp.float32))
    coef[cols, 2] = west

    def given(c, tag):
        return column_at(lam_p, tag * slab + c, levels, pitch, tags * slab)

    for at, c in enumerate((0, 1, cols - 2, cols - 1)):
        for tag in range(tags):
            l0[at, tag] = given(c, tag)
    last = storing_rows(final, tags, levels, pitch)
    loads = (given, loading(l1), loading(l2), loading(l3))
    stores = (storing(l1), storing(l2), storing(l3), last)
    for t in range(ITERS):
        sweep(t, lam.shape, place[0] * tags, region, coef, loads[t], stores[t], rows)


def inner(place, lam, fields, top, region):
    tags, levels, cols, lats = lam.shape
    vmem = pl.BlockSpec(memory_space=pltpu.VMEM)
    state = pltpu.VMEM((cols, tags, levels, lats), jnp.float32)
    return pl.pallas_call(
        inner_kernel,
        in_specs=[pl.BlockSpec(memory_space=pltpu.SMEM)] + [vmem] * 8,
        out_specs=[vmem] * 7,
        out_shape=[
            pltpu.VMEM((cols + 1, 6, levels, lats), jnp.float32),
            pltpu.VMEM((4, tags, levels, lats), jnp.float32),
            *[state] * 3,
            pltpu.VMEM((pitched(2 * tags, levels, cols), LANES), jnp.float32),
            pltpu.VMEM((ITERS, cols, lats), jnp.float32),
        ],
        scratch_shapes=[
            pltpu.VMEM((pitched(2 * tags, levels, cols), LANES), jnp.float32),
            pltpu.VMEM((pitched(10, levels, cols), LANES), jnp.float32),
        ],
        compiler_params=pltpu.CompilerParams(vmem_limit_bytes=32 << 20),
        cost_estimate=SHORT,
        name="inner_steps",
    )(place, lam, *fields, top, region)


def slot(c, cols):
    return (LOW, c + EDGE - 1) if c < EDGE else (HIGH, c - (cols - EDGE))


def outer_kernel(parts, cols, place, coef, *refs):
    pieces, wide, entry = refs[:parts], refs[parts], refs[parts + 1]
    per = ENTRIES // parts
    mine = lax.rem(place[0], parts)
    odd = place[1]
    for by in range(parts):
        base = (mine ^ by) * per
        entry[1 - odd, pl.ds(base, per)] = pieces[by][0]
        entry[odd, pl.ds(base, per)] = pieces[by][1]

    def outside(c):
        if c < 0:
            at = 1 + 5 * (c + EDGE - 1)
            e, _, n, s, u = (entry[LOW, at + j] for j in range(5))
            w = entry[LOW, at - 4] if c > 1 - EDGE else entry[LOW, 0]
        else:
            at = 5 * (c - cols)
            e, _, n, s, u = (entry[HIGH, at + j] for j in range(5))
            w = entry[HIGH, at - 4] if c > cols else coef[cols, 2]
        return e, w, n, s, u

    first_west = entry[LOW, 1 + 5 * (EDGE - 2) + 1]
    for c in [*range(1 - EDGE, 1), *range(cols, cols + EDGE - 1)]:
        if c == 0:
            e, w, n, s, u = coef[0, 1], first_west, coef[0, 3], coef[0, 4], coef[0, 5]
        else:
            e, w, n, s, u = outside(c)
        for j, value in enumerate((1.0 - e - w - n - s, e, w, n, s, u)):
            wide[*slot(c, cols), j] = value


def outer_coefs(parts, cols, place, coef, pieces):
    _, _, levels, lats = coef.shape
    vmem = pl.BlockSpec(memory_space=pltpu.VMEM)
    return pl.pallas_call(
        functools.partial(outer_kernel, parts, cols),
        in_specs=[pl.BlockSpec(memory_space=pltpu.SMEM)] + [vmem] * (1 + parts),
        out_specs=vmem,
        out_shape=pltpu.VMEM((2, 2 * EDGE - 1, 6, levels, lats), jnp.float32),
        scratch_shapes=[pltpu.VMEM((2, ENTRIES, levels, lats), jnp.float32)],
        compiler_params=pltpu.CompilerParams(vmem_limit_bytes=24 << 20),
        cost_estimate=SHORT,
        name="outer_coefs",
    )(place, coef, *pieces)


def border_kernel(place, region, coef, wide, l0, l1, l2, l3, first, second, *refs):
    final_in, rows_in, final, grad, halo, work, rows = refs
    cols, tags, levels, lats = l1.shape
    first_tag = place[0] * tags
    odd = place[1]
    halo[1 - odd] = first[...]
    halo[odd] = second[...]

    def coefs_at(c):
        if 0 < c < cols:
            return [coef[c, j] for j in range(6)]
        return [wide[*slot(c, cols), j] for j in range(6)]

    kept = (None, l1, l2, l3)

    def state(t, c, tag):
        if t == 0:
            if c < 0:
                return halo[LOW, tag * EDGE + c + EDGE]
            if c >= cols:
                return halo[HIGH, tag * EDGE + c - cols]
            return l0[c if c < 2 else c - (cols - 4), tag]
        return kept[t][c, tag] if t <= c < cols - t else work[t, *slot(c, cols), tag]

    def column(t, c):
        return [state(t, c, tag) for tag in range(tags)]

    rows[...] = rows_in[...]
    store = storing_rows(final, tags, levels, cols + 1)
    for t in range(ITERS):
        reach = EDGE - 1 - t
        for run in (range(-reach, t + 1), range(cols - t - 1, cols + reach)):
            west, mid = column(t, run[0] - 1), column(t, run[0])
            for c in run:
                east = column(t, c + 1)
                coefs = coefs_at(c)
                new = [advance(coefs, mid[k], east[k], west[k]) for k in range(tags)]
                for k in range(tags):
                    if t < ITERS - 1:
                        work[t + 1, *slot(c, cols), k] = new[k]
                    else:
                        store(c, k, new[k])
                if 0 <= c < cols:
                    rows[t, c : c + 1, :] = chosen(region[c : c + 1, :], first_tag, new)
                west, mid = mid, east
    total = rows[0]
    for t in range(1, ITERS):
        total = total + rows[t]
    grad[...] = total


def border(place, region, coef, wide, states, first, second, final, rows):
    cols, tags, levels, lats = states[1].shape
    vmem = pl.BlockSpec(memory_space=pltpu.VMEM)
    operands = [region, coef, wide, *states, first, second]
    return pl.pallas_call(
        border_kernel,
        in_specs=[pl.BlockSpec(memory_space=pltpu.SMEM)] + [vmem] * (len(operands) + 2),
        out_specs=[vmem] * 2,
        out_shape=[
            pltpu.VMEM(final.shape, jnp.float32),
            pltpu.VMEM((cols, lats), jnp.float32),
        ],
        input_output_aliases={len(operands) + 1: 0},
        scratch_shapes=[
            pltpu.VMEM((2, tags * EDGE, levels, lats), jnp.float32),
            pltpu.VMEM((ITERS, 2, 2 * EDGE - 1, tags, levels, lats), jnp.float32),
            pltpu.VMEM((ITERS, cols, lats), jnp.float32),
        ],
        compiler_params=pltpu.CompilerParams(vmem_limit_bytes=32 << 20),
        cost_estimate=SHORT,
        name="border_steps",
    )(place, *operands, final, rows)


def write_kernel(final, out, block, sems):
    tags, levels, cols, _ = out.shape
    pitch = cols + 1
    copies = []
    for tag in range(tags):

        @pl.loop(0, levels)
        def _(level):
            row = place_of(level, levels) * pitch
            for k in range(2):
                at = (k * tags + tag) * levels * pitch + row
                block[tag, level, :, HALVES[k]] = final[pl.ds(at, cols), :]

        copies.append(pltpu.make_async_copy(block.at[tag], out.at[tag], sems.at[tag]))
        copies[-1].start()
    for c in copies:
        c.wait()


def write(final, shape):
    return pl.pallas_call(
        write_kernel,
        in_specs=[pl.BlockSpec(memory_space=pltpu.VMEM)],
        out_specs=pl.BlockSpec(memory_space=pltpu.HBM),
        out_shape=pltpu.HBM(shape, jnp.float32),
        scratch_shapes=[
            pltpu.VMEM(shape, jnp.float32),
            pltpu.SemaphoreType.DMA((shape[0],)),
        ],
        compiler_params=pltpu.CompilerParams(vmem_limit_bytes=24 << 20),
        cost_estimate=SHORT,
        name="write_final",
    )(final)


def local(lam, east_wind, north_wind, east_diff, north_diff, mass_flux, region, top):
    groups, tiles = lax.axis_size("grp"), lax.axis_size("dom")
    parts = 4 if groups % 4 == 0 else 1
    grp, dom = lax.axis_index("grp"), lax.axis_index("dom")
    place = jnp.stack([grp, dom % 2]).astype(jnp.int32)
    own = (lam, east_wind, east_diff, north_wind, north_diff, mass_flux)
    far = [pltpu.with_memory_space_constraint(value, pltpu.HBM) for value in (*own, top)]

    pairs = lambda i: i ^ 1
    turn = lambda i: (((i - 1) % tiles ^ 1) + 1) % tiles
    coef_first, coef_second, first, second = pack(parts, place, far[0], far[1:6], far[6])
    coef_first = swapped(coef_first, "dom", pairs)
    coef_second = swapped(coef_second, "dom", turn)
    first = swapped(first, "dom", pairs)
    second = swapped(second, "dom", turn)
    pieces = [jnp.stack([coef_first, coef_second])]
    for by in range(1, parts):
        pieces.append(swapped(pieces[0], "grp", lambda i: i ^ by))
    coef, *states, final, rows = inner(place, own[0], own[1:], top, region)
    wide = outer_coefs(parts, lam.shape[2], place, coef, pieces)
    final, grad = border(place, region, coef, wide, states, first, second, final, rows)
    share = grad
    for by in range(1, groups):
        grad = grad + swapped(share, "grp", lambda i: (i + by) % groups)
    return write(final, lam.shape), grad


def solution(mesh):
    return jax.shard_map(
        local,
        mesh=mesh,
        in_specs=(
            P("grp", None, "dom", None),
            P(None, "dom", None),
            P(None, "dom", None),
            P(None, "dom", None),
            P(None, "dom", None),
            P(None, "dom", None),
            P("dom", None),
            P("dom", None),
        ),
        out_specs=(P("grp", None, "dom", None), P("dom", None)),
        check_vma=False,
    )
```

```python
import functools

import jax
import jax.numpy as jnp
from jax import lax
from jax.experimental import pallas as pl
from jax.experimental.pallas import tpu as pltpu
from jax.sharding import PartitionSpec as P

ITERS = 4
EDGE = ITERS
ENTRIES = 16
CHUNKS = 5
LANES = 128
HALVES = (slice(0, LANES), slice(LANES, 2 * LANES))
SHORT = pl.CostEstimate(flops=1000, bytes_accessed=1000, transcendentals=0)
LOW, HIGH = 0, 1


def swapped(value, axis, partner):
    return lax.ppermute(value, axis, [(i, partner(i)) for i in range(lax.axis_size(axis))])


def level_of(shape):
    row = lax.broadcasted_iota(jnp.int32, shape, 0)
    half = shape[0] // 2
    return jnp.where(row < half, 2 * row, 2 * (row - half) + 1)


def place_of(level, levels):
    return (level % 2) * (levels // 2) + level // 2


def faces(ew, ed, nw, nd):
    lats = ew.shape[1]
    lat = lax.broadcasted_iota(jnp.int32, ew.shape, 1)
    east = jnp.maximum(ew, 0.0) + ed
    west_next = jnp.maximum(-ew, 0.0) + ed
    north = jnp.where(lat < lats - 1, jnp.maximum(nw, 0.0) + nd, 0.0)
    south = jnp.maximum(-nw, 0.0) + nd
    south = jnp.where(lat > 0, pltpu.roll(south, 1, 1), 0.0)
    return east, west_next, north, south


def updraft(mf, top_row):
    levels = mf.shape[0]
    level = level_of(mf.shape)
    return jnp.where((level < top_row) & (level < levels - 1), mf, 0.0)


def advance(coefs, mid, east, west):
    d, e, w, n, s, u = coefs
    half = mid.shape[0] // 2
    h = d * mid + e * east + w * west
    lane = lax.broadcasted_iota(jnp.int32, (mid.shape[0], LANES), 1)
    north = [pltpu.roll(mid[:, part], LANES - 1, 1) for part in HALVES]
    south = [pltpu.roll(mid[:, part], 1, 1) for part in HALVES]
    north = jnp.concatenate([jnp.where(lane < LANES - 1, *north), north[1]], axis=1)
    south = jnp.concatenate([south[0], jnp.where(lane > 0, south[1], south[0])], axis=1)
    h = h + n * north + s * south
    above = jnp.concatenate([h[half:], pltpu.roll(h[:half], half - 1, 0)], axis=0)
    return h + u * (above - h)


def pitched(slabs, levels, width):
    return -(-(slabs * levels * (width + 1) + width + 8) // 8) * 8


def column_at(ref, start, levels, pitch, apart):
    parts = [ref[pl.ds(start + apart * k, levels, stride=pitch), :] for k in range(2)]
    return jnp.concatenate(parts, axis=1)


def pack_kernel(parts, place, lam, ew, ed, nw, nd, mf, top, *refs):
    coef_first, coef_second, lam_first, lam_second, lam_v, field_v = refs[:6]
    top_v, entry, field_p, lam_p, sems = refs[6:]
    tags, levels, cols, lats = lam.shape
    edges = (pl.ds(0, 8), pl.ds(cols - 8, 8))
    middle = pl.ds(8, cols - 16)
    copies = []

    def copy(src, dst):
        copies.append(pltpu.make_async_copy(src, dst, sems.at[len(copies)]))
        copies[-1].start()

    copy(top, top_v)
    fields = list(enumerate((ew, ed, nw, nd, mf)))
    for part in edges:
        for f, field in fields:
            copy(field.at[:, part], field_v.at[f, :, part])
    for part in edges:
        copy(lam.at[:, :, part], lam_v.at[:, :, part])
    for f, field in fields:
        copy(field.at[:, middle], field_v.at[f, :, middle])
    copy(lam.at[:, :, middle], lam_v.at[:, :, middle])
    for c in copies[:11]:
        c.wait()
    pitch = 9
    slab = levels * pitch

    @pl.loop(0, levels)
    def _(level):
        row = place_of(level, levels) * pitch
        for f in range(5):
            for side, part in enumerate(edges):
                for k in range(2):
                    at = ((f * 2 + side) * 2 + k) * slab
                    field_p[pl.ds(at + row, 8), :] = field_v[f, level, part, HALVES[k]]

    def field(f, side, c):
        return column_at(field_p, (f * 2 + side) * 2 * slab + c, levels, pitch, slab)

    entry[LOW, 0] = jnp.zeros((levels, lats), jnp.float32)
    start = 8 - EDGE
    entry[HIGH, 0] = jnp.maximum(-field(0, HIGH, start), 0.0) + field(1, HIGH, start)

    @pl.loop(0, EDGE - 1)
    def _(j):
        for side in (LOW, HIGH):
            c = j + (start + 1) * side
            east, west, north, south = faces(*(field(f, side, c) for f in range(4)))
            row = top_v[pl.ds(c + (cols - 8) * side, 1), :]
            lift = updraft(field(4, side, c), row)
            for n, value in enumerate((east, north, south, lift, west)):
                entry[side, 5 * j + 1 + n] = value

    per = ENTRIES // parts
    mine = lax.rem(place[0], parts) * per
    odd = place[1]
    coef_first[...] = entry[1 - odd, pl.ds(mine, per)]
    coef_second[...] = entry[odd, pl.ds(mine, per)]

    for c in copies[11:13]:
        c.wait()

    @pl.loop(0, levels)
    def _(level):
        row = place_of(level, levels) * pitch
        for side, part in enumerate(edges):
            for tag in range(tags):
                for k in range(2):
                    at = ((side * 2 + k) * tags + tag) * slab
                    lam_p[pl.ds(at + row, 8), :] = lam_v[tag, level, part, HALVES[k]]

    @pl.loop(0, tags)
    def _(tag):
        for dest, side in ((lam_first, 1 - odd), (lam_second, odd)):
            at = side * (2 * tags * slab + start) + tag * slab
            for c in range(EDGE):
                dest[tag * EDGE + c] = column_at(lam_p, at + c, levels, pitch, tags * slab)

    for c in copies[13:]:
        c.wait()


def pack(parts, place, lam, fields, top):
    tags, levels, cols, lats = lam.shape
    hbm = pl.BlockSpec(memory_space=pltpu.HBM)
    send = lambda slabs: pltpu.VMEM((slabs, levels, lats), jnp.float32)
    few, many = ENTRIES // parts, tags * EDGE
    return pl.pallas_call(
        functools.partial(pack_kernel, parts),
        in_specs=[pl.BlockSpec(memory_space=pltpu.SMEM)] + [hbm] * 7,
        out_specs=[pl.BlockSpec(memory_space=pltpu.VMEM)] * 6,
        out_shape=[
            send(few),
            send(few),
            send(many),
            send(many),
            pltpu.VMEM(lam.shape, jnp.float32),
            pltpu.VMEM((5, levels, cols, lats), jnp.float32),
        ],
        scratch_shapes=[
            pltpu.VMEM((cols, lats), jnp.int32),
            pltpu.VMEM((2, ENTRIES, levels, lats), jnp.float32),
            pltpu.VMEM((pitched(20, levels, 8), LANES), jnp.float32),
            pltpu.VMEM((pitched(4 * tags, levels, 8), LANES), jnp.float32),
            pltpu.SemaphoreType.DMA((19,)),
        ],
        compiler_params=pltpu.CompilerParams(vmem_limit_bytes=24 << 20),
        cost_estimate=SHORT,
        name="pack_edges",
    )(place, lam, *fields, top)


def chosen(region_row, first_tag, values):
    row = jnp.zeros(region_row.shape, jnp.float32)
    for tag, value in enumerate(values):
        row = jnp.where(region_row == first_tag + tag, value[0:1], row)
    return row


def sweep(t, shape, first_tag, region, coef, load, store, rows):
    tags, _, cols, _ = shape
    low, high = t + 1, cols - t - 1
    chunk = -(-(high - low) // CHUNKS)
    column = lambda c: [load(c, k) for k in range(tags)]

    @pl.loop(0, CHUNKS)
    def _(i):
        start = jnp.minimum(low + i * chunk, high - chunk)
        west, mid = column(start - 1), column(start)
        for j in range(chunk):
            c = start + j
            east = column(c + 1)
            coefs = [coef[c, n] for n in range(6)]
            new = [advance(coefs, mid[k], east[k], west[k]) for k in range(tags)]
            for k in range(tags):
                store(c, k, new[k])
            rows[t, pl.ds(c, 1), :] = chosen(region[pl.ds(c, 1), :], first_tag, new)
            west, mid = mid, east


def loading(ref):
    return lambda c, tag: ref[c, tag]


def storing(ref):
    def store(c, tag, value):
        ref[c, tag] = value

    return store


def storing_rows(ref, tags, levels, pitch):
    def store(c, tag, value):
        for k in range(2):
            at = (k * tags + tag) * levels * pitch + c
            ref[pl.ds(at, levels, stride=pitch), :] = value[:, HALVES[k]]

    return store


def inner_kernel(place, lam, fields, top, region, *refs):
    coef, l0, l1, l2, l3, final, rows, lam_p, field_p = refs
    tags, levels, cols, lats = lam.shape
    pitch = cols + 1
    slab = levels * pitch

    @pl.loop(0, levels)
    def _(level):
        row = place_of(level, levels) * pitch
        for f in range(5):
            for k in range(2):
                field_p[pl.ds((f * 2 + k) * slab + row, cols), :] = fields[f, level, :, HALVES[k]]
        for tag in range(tags):
            for k in range(2):
                at = (k * tags + tag) * slab + row
                lam_p[pl.ds(at, cols), :] = lam[tag, level, :, HALVES[k]]

    def coefficients(c, west):
        ew, ed, nw, nd, mf = (
            column_at(field_p, f * 2 * slab + c, levels, pitch, slab) for f in range(5)
        )
        e, next_west, n, s = faces(ew, ed, nw, nd)
        u = updraft(mf, top[pl.ds(c, 1), :])
        for j, value in enumerate((1.0 - e - west - n - s, e, west, n, s, u)):
            coef[c, j] = value
        return next_west

    def some(i, west):
        for j in range(8):
            west = coefficients(i * 8 + j, west)
        return west

    west = lax.fori_loop(0, cols // 8, some, jnp.zeros((levels, lats), jnp.float32))
    coef[cols, 2] = west

    def given(c, tag):
        return column_at(lam_p, tag * slab + c, levels, pitch, tags * slab)

    for at, c in enumerate((0, 1, cols - 2, cols - 1)):
        for tag in range(tags):
            l0[at, tag] = given(c, tag)
    last = storing_rows(final, tags, levels, pitch)
    loads = (given, loading(l1), loading(l2), loading(l3))
    stores = (storing(l1), storing(l2), storing(l3), last)
    for t in range(ITERS):
        sweep(t, lam.shape, place[0] * tags, region, coef, loads[t], stores[t], rows)


def inner(place, lam, fields, top, region):
    tags, levels, cols, lats = lam.shape
    vmem = pl.BlockSpec(memory_space=pltpu.VMEM)
    state = pltpu.VMEM((cols, tags, levels, lats), jnp.float32)
    return pl.pallas_call(
        inner_kernel,
        in_specs=[pl.BlockSpec(memory_space=pltpu.SMEM)] + [vmem] * 4,
        out_specs=[vmem] * 7,
        out_shape=[
            pltpu.VMEM((cols + 1, 6, levels, lats), jnp.float32),
            pltpu.VMEM((4, tags, levels, lats), jnp.float32),
            *[state] * 3,
            pltpu.VMEM((pitched(2 * tags, levels, cols), LANES), jnp.float32),
            pltpu.VMEM((ITERS, cols, lats), jnp.float32),
        ],
        scratch_shapes=[
            pltpu.VMEM((pitched(2 * tags, levels, cols), LANES), jnp.float32),
            pltpu.VMEM((pitched(10, levels, cols), LANES), jnp.float32),
        ],
        compiler_params=pltpu.CompilerParams(vmem_limit_bytes=32 << 20),
        cost_estimate=SHORT,
        name="inner_steps",
    )(place, lam, fields, top, region)


def slot(c, cols):
    return (LOW, c + EDGE - 1) if c < EDGE else (HIGH, c - (cols - EDGE))


def outer_kernel(parts, cols, place, coef, *refs):
    pieces, wide, entry = refs[:parts], refs[parts], refs[parts + 1]
    per = ENTRIES // parts
    mine = lax.rem(place[0], parts)
    odd = place[1]
    for by in range(parts):
        base = (mine ^ by) * per
        entry[1 - odd, pl.ds(base, per)] = pieces[by][0]
        entry[odd, pl.ds(base, per)] = pieces[by][1]

    entry[HIGH, 0] = coef[cols, 2]

    @pl.loop(0, EDGE - 1)
    def _(j):
        for side in (LOW, HIGH):
            w, e, n, s, u = (entry[side, 5 * j + i] for i in range(5))
            for i, value in enumerate((1.0 - e - w - n - s, e, w, n, s, u)):
                wide[side, j + EDGE * side, i] = value

    first_west = entry[LOW, ENTRIES - 1]
    e, n, s, u = (coef[0, i] for i in (1, 3, 4, 5))
    for i, value in enumerate((1.0 - e - first_west - n - s, e, first_west, n, s, u)):
        wide[*slot(0, cols), i] = value


def outer_coefs(parts, cols, place, coef, pieces):
    _, _, levels, lats = coef.shape
    vmem = pl.BlockSpec(memory_space=pltpu.VMEM)
    return pl.pallas_call(
        functools.partial(outer_kernel, parts, cols),
        in_specs=[pl.BlockSpec(memory_space=pltpu.SMEM)] + [vmem] * (1 + parts),
        out_specs=vmem,
        out_shape=pltpu.VMEM((2, 2 * EDGE - 1, 6, levels, lats), jnp.float32),
        scratch_shapes=[pltpu.VMEM((2, ENTRIES, levels, lats), jnp.float32)],
        compiler_params=pltpu.CompilerParams(vmem_limit_bytes=24 << 20),
        cost_estimate=SHORT,
        name="outer_coefs",
    )(place, coef, *pieces)


def border_kernel(place, region, coef, wide, l0, l1, l2, l3, first, second, *refs):
    final_in, rows_in, final, grad, halo, work, rows = refs
    cols, tags, levels, lats = l1.shape
    first_tag = place[0] * tags
    odd = place[1]
    halo[1 - odd] = first[...]
    halo[odd] = second[...]

    def coefs_at(c):
        if 0 < c < cols:
            return [coef[c, j] for j in range(6)]
        return [wide[*slot(c, cols), j] for j in range(6)]

    kept = (None, l1, l2, l3)

    def state(t, c, tag):
        if t == 0:
            if c < 0:
                return halo[LOW, tag * EDGE + c + EDGE]
            if c >= cols:
                return halo[HIGH, tag * EDGE + c - cols]
            return l0[c if c < 2 else c - (cols - 4), tag]
        return kept[t][c, tag] if t <= c < cols - t else work[t, *slot(c, cols), tag]

    def column(t, c):
        return [state(t, c, tag) for tag in range(tags)]

    rows[...] = rows_in[...]
    store = storing_rows(final, tags, levels, cols + 1)
    for t in range(ITERS):
        reach = EDGE - 1 - t
        for run in (range(-reach, t + 1), range(cols - t - 1, cols + reach)):
            west, mid = column(t, run[0] - 1), column(t, run[0])
            for c in run:
                east = column(t, c + 1)
                coefs = coefs_at(c)
                new = [advance(coefs, mid[k], east[k], west[k]) for k in range(tags)]
                for k in range(tags):
                    if t < ITERS - 1:
                        work[t + 1, *slot(c, cols), k] = new[k]
                    else:
                        store(c, k, new[k])
                if 0 <= c < cols:
                    rows[t, c : c + 1, :] = chosen(region[c : c + 1, :], first_tag, new)
                west, mid = mid, east
    total = rows[0]
    for t in range(1, ITERS):
        total = total + rows[t]
    grad[...] = total


def border(place, region, coef, wide, states, first, second, final, rows):
    cols, tags, levels, lats = states[1].shape
    vmem = pl.BlockSpec(memory_space=pltpu.VMEM)
    operands = [region, coef, wide, *states, first, second]
    return pl.pallas_call(
        border_kernel,
        in_specs=[pl.BlockSpec(memory_space=pltpu.SMEM)] + [vmem] * (len(operands) + 2),
        out_specs=[vmem] * 2,
        out_shape=[
            pltpu.VMEM(final.shape, jnp.float32),
            pltpu.VMEM((cols, lats), jnp.float32),
        ],
        input_output_aliases={len(operands) + 1: 0},
        scratch_shapes=[
            pltpu.VMEM((2, tags * EDGE, levels, lats), jnp.float32),
            pltpu.VMEM((ITERS, 2, 2 * EDGE - 1, tags, levels, lats), jnp.float32),
            pltpu.VMEM((ITERS, cols, lats), jnp.float32),
        ],
        compiler_params=pltpu.CompilerParams(vmem_limit_bytes=32 << 20),
        cost_estimate=SHORT,
        name="border_steps",
    )(place, *operands, final, rows)


def write_kernel(final, out, block, sems):
    tags, levels, cols, _ = out.shape
    pitch = cols + 1
    copies = []
    for tag in range(tags):

        @pl.loop(0, levels)
        def _(level):
            row = place_of(level, levels) * pitch
            for k in range(2):
                at = (k * tags + tag) * levels * pitch + row
                block[tag, level, :, HALVES[k]] = final[pl.ds(at, cols), :]

        copies.append(pltpu.make_async_copy(block.at[tag], out.at[tag], sems.at[tag]))
        copies[-1].start()
    for c in copies:
        c.wait()


def write(final, shape):
    return pl.pallas_call(
        write_kernel,
        in_specs=[pl.BlockSpec(memory_space=pltpu.VMEM)],
        out_specs=pl.BlockSpec(memory_space=pltpu.HBM),
        out_shape=pltpu.HBM(shape, jnp.float32),
        scratch_shapes=[
            pltpu.VMEM(shape, jnp.float32),
            pltpu.SemaphoreType.DMA((shape[0],)),
        ],
        compiler_params=pltpu.CompilerParams(vmem_limit_bytes=24 << 20),
        cost_estimate=SHORT,
        name="write_final",
    )(final)


def local(lam, east_wind, north_wind, east_diff, north_diff, mass_flux, region, top):
    groups, tiles = lax.axis_size("grp"), lax.axis_size("dom")
    parts = 4 if groups % 4 == 0 else 1
    grp, dom = lax.axis_index("grp"), lax.axis_index("dom")
    place = jnp.stack([grp, dom % 2]).astype(jnp.int32)
    far_lam, *far = (
        pltpu.with_memory_space_constraint(value, pltpu.HBM)
        for value in (lam, east_wind, east_diff, north_wind, north_diff, mass_flux, top)
    )

    pairs = lambda i: i ^ 1
    turn = lambda i: (((i - 1) % tiles ^ 1) + 1) % tiles
    coef_first, coef_second, first, second, own_lam, own_fields = pack(
        parts, place, far_lam, far[:5], far[5]
    )
    coef_first = swapped(coef_first, "dom", pairs)
    coef_second = swapped(coef_second, "dom", turn)
    first = swapped(first, "dom", pairs)
    second = swapped(second, "dom", turn)
    pieces = [jnp.stack([coef_first, coef_second])]
    for by in range(1, parts):
        pieces.append(swapped(pieces[0], "grp", lambda i: i ^ by))
    coef, *states, final, rows = inner(place, own_lam, own_fields, top, region)
    wide = outer_coefs(parts, lam.shape[2], place, coef, pieces)
    final, grad = border(place, region, coef, wide, states, first, second, final, rows)
    share = grad
    for by in range(1, groups):
        grad = grad + swapped(share, "grp", lambda i: (i + by) % groups)
    return write(final, lam.shape), grad


def solution(mesh):
    return jax.shard_map(
        local,
        mesh=mesh,
        in_specs=(
            P("grp", None, "dom", None),
            P(None, "dom", None),
            P(None, "dom", None),
            P(None, "dom", None),
            P(None, "dom", None),
            P(None, "dom", None),
            P("dom", None),
            P("dom", None),
        ),
        out_specs=(P("grp", None, "dom", None), P("dom", None)),
        check_vma=False,
    )
```

```python
import functools

import jax
import jax.numpy as jnp
from jax import lax
from jax.experimental import pallas as pl
from jax.experimental.pallas import tpu as pltpu
from jax.sharding import PartitionSpec as P

ITERS = 4
EDGE = ITERS
ENTRIES = 16
CHUNKS = 2
LANES = 128
HALVES = (slice(0, LANES), slice(LANES, 2 * LANES))
SHORT = pl.CostEstimate(flops=1000, bytes_accessed=1000, transcendentals=0)
LOW, HIGH = 0, 1


def swapped(value, axis, partner):
    return lax.ppermute(value, axis, [(i, partner(i)) for i in range(lax.axis_size(axis))])


def level_of(shape):
    row = lax.broadcasted_iota(jnp.int32, shape, 0)
    half = shape[0] // 2
    return jnp.where(row < half, 2 * row, 2 * (row - half) + 1)


def place_of(level, levels):
    return (level % 2) * (levels // 2) + level // 2


def faces(ew, ed, nw, nd):
    lats = ew.shape[1]
    lat = lax.broadcasted_iota(jnp.int32, ew.shape, 1)
    east = jnp.maximum(ew, 0.0) + ed
    west_next = jnp.maximum(-ew, 0.0) + ed
    north = jnp.where(lat < lats - 1, jnp.maximum(nw, 0.0) + nd, 0.0)
    south = jnp.maximum(-nw, 0.0) + nd
    south = jnp.where(lat > 0, pltpu.roll(south, 1, 1), 0.0)
    return east, west_next, north, south


def updraft(mf, top_row):
    levels = mf.shape[0]
    level = level_of(mf.shape)
    return jnp.where((level < top_row) & (level < levels - 1), mf, 0.0)


def advance(coefs, mid, east, west):
    d, e, w, n, s, u = coefs
    half = mid.shape[0] // 2
    h = d * mid + e * east + w * west
    lane = lax.broadcasted_iota(jnp.int32, (mid.shape[0], LANES), 1)
    north = [pltpu.roll(mid[:, part], LANES - 1, 1) for part in HALVES]
    south = [pltpu.roll(mid[:, part], 1, 1) for part in HALVES]
    north = jnp.concatenate([jnp.where(lane < LANES - 1, *north), north[1]], axis=1)
    south = jnp.concatenate([south[0], jnp.where(lane > 0, south[1], south[0])], axis=1)
    h = h + n * north + s * south
    above = jnp.concatenate([h[half:], pltpu.roll(h[:half], half - 1, 0)], axis=0)
    return h + u * (above - h)


def pitched(slabs, levels, width):
    return -(-(slabs * levels * (width + 1) + width + 8) // 8) * 8


def column_at(ref, start, levels, pitch, apart):
    parts = [ref[pl.ds(start + apart * k, levels, stride=pitch), :] for k in range(2)]
    return jnp.concatenate(parts, axis=1)


def pack_kernel(parts, place, lam, ew, ed, nw, nd, mf, top, *refs):
    first, coef_second, lam_first, lam_second, lam_v, field_v = refs[:6]
    top_v, entry, field_p, lam_p, sems = refs[6:]
    tags, levels, cols, lats = lam.shape
    edges = (pl.ds(0, 8), pl.ds(cols - 8, 8))
    middle = pl.ds(8, cols - 16)
    copies = []

    def copy(src, dst):
        copies.append(pltpu.make_async_copy(src, dst, sems.at[len(copies)]))
        copies[-1].start()

    copy(top, top_v)
    for f, field in enumerate((ew, ed, nw, nd, mf)):
        copy(field, field_v.at[f])
    for part in (*edges, middle):
        copy(lam.at[:, :, part], lam_v.at[:, :, part])
    for c in copies[:6]:
        c.wait()
    pitch = 9
    slab = levels * pitch

    @pl.loop(0, levels)
    def _(level):
        row = place_of(level, levels) * pitch
        for f in range(5):
            for side, part in enumerate(edges):
                for k in range(2):
                    at = ((f * 2 + side) * 2 + k) * slab
                    field_p[pl.ds(at + row, 8), :] = field_v[f, level, part, HALVES[k]]

    def field(f, side, c):
        return column_at(field_p, (f * 2 + side) * 2 * slab + c, levels, pitch, slab)

    entry[LOW, 0] = jnp.zeros((levels, lats), jnp.float32)
    start = 8 - EDGE
    entry[HIGH, 0] = jnp.maximum(-field(0, HIGH, start), 0.0) + field(1, HIGH, start)

    @pl.loop(0, EDGE - 1)
    def _(j):
        for side in (LOW, HIGH):
            c = j + (start + 1) * side
            east, west, north, south = faces(*(field(f, side, c) for f in range(4)))
            row = top_v[pl.ds(c + (cols - 8) * side, 1), :]
            lift = updraft(field(4, side, c), row)
            for n, value in enumerate((east, north, south, lift, west)):
                entry[side, 5 * j + 1 + n] = value

    per = ENTRIES // parts
    mine = lax.rem(place[0], parts) * per
    odd = place[1]
    half = tags // 2 * EDGE
    first[half:] = entry[1 - odd, pl.ds(mine, per)]
    coef_second[...] = entry[odd, pl.ds(mine, per)]

    for c in copies[6:8]:
        c.wait()

    @pl.loop(0, levels)
    def _(level):
        row = place_of(level, levels) * pitch
        for side, part in enumerate(edges):
            for tag in range(tags):
                for k in range(2):
                    at = ((side * 2 + k) * tags + tag) * slab
                    lam_p[pl.ds(at + row, 8), :] = lam_v[tag, level, part, HALVES[k]]

    def columns(tag, side):
        at = side * (2 * tags * slab + start) + tag * slab
        return [column_at(lam_p, at + c, levels, pitch, tags * slab) for c in range(EDGE)]

    @pl.loop(0, tags // 2)
    def _(i):
        for c, value in enumerate(columns(i, 1 - odd)):
            first[i * EDGE + c] = value
        for c, value in enumerate(columns(tags // 2 + i, 1 - odd)):
            lam_first[i * EDGE + c] = value

    @pl.loop(0, tags)
    def _(tag):
        for c, value in enumerate(columns(tag, odd)):
            lam_second[tag * EDGE + c] = value

    for c in copies[8:]:
        c.wait()


def pack(parts, place, lam, fields, top):
    tags, levels, cols, lats = lam.shape
    hbm = pl.BlockSpec(memory_space=pltpu.HBM)
    send = lambda slabs: pltpu.VMEM((slabs, levels, lats), jnp.float32)
    few, many = ENTRIES // parts, tags * EDGE
    return pl.pallas_call(
        functools.partial(pack_kernel, parts),
        in_specs=[pl.BlockSpec(memory_space=pltpu.SMEM)] + [hbm] * 7,
        out_specs=[pl.BlockSpec(memory_space=pltpu.VMEM)] * 6,
        out_shape=[
            send(many // 2 + few),
            send(few),
            send(many // 2),
            send(many),
            pltpu.VMEM(lam.shape, jnp.float32),
            pltpu.VMEM((5, levels, cols, lats), jnp.float32),
        ],
        scratch_shapes=[
            pltpu.VMEM((cols, lats), jnp.int32),
            pltpu.VMEM((2, ENTRIES, levels, lats), jnp.float32),
            pltpu.VMEM((pitched(20, levels, 8), LANES), jnp.float32),
            pltpu.VMEM((pitched(4 * tags, levels, 8), LANES), jnp.float32),
            pltpu.SemaphoreType.DMA((9,)),
        ],
        compiler_params=pltpu.CompilerParams(vmem_limit_bytes=24 << 20),
        cost_estimate=SHORT,
        name="pack_edges",
    )(place, lam, *fields, top)


def chosen(region_row, first_tag, values):
    row = jnp.zeros(region_row.shape, jnp.float32)
    for tag, value in enumerate(values):
        row = jnp.where(region_row == first_tag + tag, value[0:1], row)
    return row


def sweep(t, shape, first_tag, region, coef, load, store, rows):
    tags, _, cols, _ = shape
    low, high = t + 1, cols - t - 1
    chunk = -(-(high - low) // CHUNKS)
    column = lambda c: [load(c, k) for k in range(tags)]

    @pl.loop(0, CHUNKS)
    def _(i):
        start = jnp.minimum(low + i * chunk, high - chunk)
        west, mid = column(start - 1), column(start)
        for j in range(chunk):
            c = start + j
            east = column(c + 1)
            coefs = [coef[c, n] for n in range(6)]
            new = [advance(coefs, mid[k], east[k], west[k]) for k in range(tags)]
            for k in range(tags):
                store(c, k, new[k])
            rows[t, pl.ds(c, 1), :] = chosen(region[pl.ds(c, 1), :], first_tag, new)
            west, mid = mid, east


def loading(ref):
    return lambda c, tag: ref[c, tag]


def storing(ref):
    def store(c, tag, value):
        ref[c, tag] = value

    return store


def storing_rows(ref, tags, levels, pitch):
    def store(c, tag, value):
        for k in range(2):
            at = (k * tags + tag) * levels * pitch + c
            ref[pl.ds(at, levels, stride=pitch), :] = value[:, HALVES[k]]

    return store


def inner_kernel(place, lam, fields, top, region, *refs):
    coef, l0, l1, l2, l3, final, rows, lam_p, field_p = refs
    tags, levels, cols, lats = lam.shape
    pitch = cols + 1
    slab = levels * pitch

    @pl.loop(0, levels)
    def _(level):
        row = place_of(level, levels) * pitch
        for f in range(5):
            for k in range(2):
                field_p[pl.ds((f * 2 + k) * slab + row, cols), :] = fields[f, level, :, HALVES[k]]
        for tag in range(tags):
            for k in range(2):
                at = (k * tags + tag) * slab + row
                lam_p[pl.ds(at, cols), :] = lam[tag, level, :, HALVES[k]]

    def coefficients(c, west):
        ew, ed, nw, nd, mf = (
            column_at(field_p, f * 2 * slab + c, levels, pitch, slab) for f in range(5)
        )
        e, next_west, n, s = faces(ew, ed, nw, nd)
        u = updraft(mf, top[pl.ds(c, 1), :])
        for j, value in enumerate((1.0 - e - west - n - s, e, west, n, s, u)):
            coef[c, j] = value
        return next_west

    def some(i, west):
        for j in range(8):
            west = coefficients(i * 8 + j, west)
        return west

    west = lax.fori_loop(0, cols // 8, some, jnp.zeros((levels, lats), jnp.float32))
    coef[cols, 2] = west

    def given(c, tag):
        return column_at(lam_p, tag * slab + c, levels, pitch, tags * slab)

    for at, c in enumerate((0, 1, cols - 2, cols - 1)):
        for tag in range(tags):
            l0[at, tag] = given(c, tag)
    last = storing_rows(final, tags, levels, pitch)
    loads = (given, loading(l1), loading(l2), loading(l3))
    stores = (storing(l1), storing(l2), storing(l3), last)
    for t in range(ITERS):
        sweep(t, lam.shape, place[0] * tags, region, coef, loads[t], stores[t], rows)


def inner(place, lam, fields, top, region):
    tags, levels, cols, lats = lam.shape
    vmem = pl.BlockSpec(memory_space=pltpu.VMEM)
    state = pltpu.VMEM((cols, tags, levels, lats), jnp.float32)
    return pl.pallas_call(
        inner_kernel,
        in_specs=[pl.BlockSpec(memory_space=pltpu.SMEM)] + [vmem] * 4,
        out_specs=[vmem] * 7,
        out_shape=[
            pltpu.VMEM((cols + 1, 6, levels, lats), jnp.float32),
            pltpu.VMEM((4, tags, levels, lats), jnp.float32),
            *[state] * 3,
            pltpu.VMEM((pitched(2 * tags, levels, cols), LANES), jnp.float32),
            pltpu.VMEM((ITERS, cols, lats), jnp.float32),
        ],
        scratch_shapes=[
            pltpu.VMEM((pitched(2 * tags, levels, cols), LANES), jnp.float32),
            pltpu.VMEM((pitched(10, levels, cols), LANES), jnp.float32),
        ],
        compiler_params=pltpu.CompilerParams(vmem_limit_bytes=32 << 20),
        cost_estimate=SHORT,
        name="inner_steps",
    )(place, lam, fields, top, region)


def slot(c, cols):
    return (LOW, c + EDGE - 1) if c < EDGE else (HIGH, c - (cols - EDGE))


def outer_kernel(parts, cols, place, coef, *refs):
    pieces, wide, entry = refs[:parts], refs[parts], refs[parts + 1]
    per = ENTRIES // parts
    mine = lax.rem(place[0], parts)
    odd = place[1]
    for by in range(parts):
        base = (mine ^ by) * per
        entry[1 - odd, pl.ds(base, per)] = pieces[by][0]
        entry[odd, pl.ds(base, per)] = pieces[by][1]

    entry[HIGH, 0] = coef[cols, 2]

    @pl.loop(0, EDGE - 1)
    def _(j):
        for side in (LOW, HIGH):
            w, e, n, s, u = (entry[side, 5 * j + i] for i in range(5))
            for i, value in enumerate((1.0 - e - w - n - s, e, w, n, s, u)):
                wide[side, j + EDGE * side, i] = value

    first_west = entry[LOW, ENTRIES - 1]
    e, n, s, u = (coef[0, i] for i in (1, 3, 4, 5))
    for i, value in enumerate((1.0 - e - first_west - n - s, e, first_west, n, s, u)):
        wide[*slot(0, cols), i] = value


def outer_coefs(parts, cols, place, coef, pieces):
    _, _, levels, lats = coef.shape
    vmem = pl.BlockSpec(memory_space=pltpu.VMEM)
    return pl.pallas_call(
        functools.partial(outer_kernel, parts, cols),
        in_specs=[pl.BlockSpec(memory_space=pltpu.SMEM)] + [vmem] * (1 + parts),
        out_specs=vmem,
        out_shape=pltpu.VMEM((2, 2 * EDGE - 1, 6, levels, lats), jnp.float32),
        scratch_shapes=[pltpu.VMEM((2, ENTRIES, levels, lats), jnp.float32)],
        compiler_params=pltpu.CompilerParams(vmem_limit_bytes=24 << 20),
        cost_estimate=SHORT,
        name="outer_coefs",
    )(place, coef, *pieces)


def border_kernel(place, region, coef, wide, l0, l1, l2, l3, first, rest, second, *refs):
    final_in, rows_in, final, grad, halo, work, rows = refs
    cols, tags, levels, lats = l1.shape
    first_tag = place[0] * tags
    odd = place[1]
    half = rest.shape[0]
    halo[1 - odd, :half] = first[:half]
    halo[1 - odd, half:] = rest[...]
    halo[odd] = second[...]

    def coefs_at(c):
        if 0 < c < cols:
            return [coef[c, j] for j in range(6)]
        return [wide[*slot(c, cols), j] for j in range(6)]

    kept = (None, l1, l2, l3)

    def state(t, c, tag):
        if t == 0:
            if c < 0:
                return halo[LOW, tag * EDGE + c + EDGE]
            if c >= cols:
                return halo[HIGH, tag * EDGE + c - cols]
            return l0[c if c < 2 else c - (cols - 4), tag]
        return kept[t][c, tag] if t <= c < cols - t else work[t, *slot(c, cols), tag]

    def column(t, c):
        return [state(t, c, tag) for tag in range(tags)]

    rows[...] = rows_in[...]
    store = storing_rows(final, tags, levels, cols + 1)
    for t in range(ITERS):
        reach = EDGE - 1 - t
        for run in (range(-reach, t + 1), range(cols - t - 1, cols + reach)):
            west, mid = column(t, run[0] - 1), column(t, run[0])
            for c in run:
                east = column(t, c + 1)
                coefs = coefs_at(c)
                new = [advance(coefs, mid[k], east[k], west[k]) for k in range(tags)]
                for k in range(tags):
                    if t < ITERS - 1:
                        work[t + 1, *slot(c, cols), k] = new[k]
                    else:
                        store(c, k, new[k])
                if 0 <= c < cols:
                    rows[t, c : c + 1, :] = chosen(region[c : c + 1, :], first_tag, new)
                west, mid = mid, east
    total = rows[0]
    for t in range(1, ITERS):
        total = total + rows[t]
    grad[...] = total


def border(place, region, coef, wide, states, halos, final, rows):
    cols, tags, levels, lats = states[1].shape
    vmem = pl.BlockSpec(memory_space=pltpu.VMEM)
    operands = [region, coef, wide, *states, *halos]
    return pl.pallas_call(
        border_kernel,
        in_specs=[pl.BlockSpec(memory_space=pltpu.SMEM)] + [vmem] * (len(operands) + 2),
        out_specs=[vmem] * 2,
        out_shape=[
            pltpu.VMEM(final.shape, jnp.float32),
            pltpu.VMEM((cols, lats), jnp.float32),
        ],
        input_output_aliases={len(operands) + 1: 0},
        scratch_shapes=[
            pltpu.VMEM((2, tags * EDGE, levels, lats), jnp.float32),
            pltpu.VMEM((ITERS, 2, 2 * EDGE - 1, tags, levels, lats), jnp.float32),
            pltpu.VMEM((ITERS, cols, lats), jnp.float32),
        ],
        compiler_params=pltpu.CompilerParams(vmem_limit_bytes=32 << 20),
        cost_estimate=SHORT,
        name="border_steps",
    )(place, *operands, final, rows)


def write_kernel(final, out, block, sems):
    tags, levels, cols, _ = out.shape
    pitch = cols + 1
    copies = []
    for tag in range(tags):

        @pl.loop(0, levels)
        def _(level):
            row = place_of(level, levels) * pitch
            for k in range(2):
                at = (k * tags + tag) * levels * pitch + row
                block[tag, level, :, HALVES[k]] = final[pl.ds(at, cols), :]

        copies.append(pltpu.make_async_copy(block.at[tag], out.at[tag], sems.at[tag]))
        copies[-1].start()
    for c in copies:
        c.wait()


def write(final, shape):
    return pl.pallas_call(
        write_kernel,
        in_specs=[pl.BlockSpec(memory_space=pltpu.VMEM)],
        out_specs=pl.BlockSpec(memory_space=pltpu.HBM),
        out_shape=pltpu.HBM(shape, jnp.float32),
        scratch_shapes=[
            pltpu.VMEM(shape, jnp.float32),
            pltpu.SemaphoreType.DMA((shape[0],)),
        ],
        compiler_params=pltpu.CompilerParams(vmem_limit_bytes=24 << 20),
        cost_estimate=SHORT,
        name="write_final",
    )(final)


def local(lam, east_wind, north_wind, east_diff, north_diff, mass_flux, region, top):
    groups, tiles = lax.axis_size("grp"), lax.axis_size("dom")
    parts = 4 if groups % 4 == 0 else 1
    grp, dom = lax.axis_index("grp"), lax.axis_index("dom")
    place = jnp.stack([grp, dom % 2]).astype(jnp.int32)
    far_lam, *far = (
        pltpu.with_memory_space_constraint(value, pltpu.HBM)
        for value in (lam, east_wind, east_diff, north_wind, north_diff, mass_flux, top)
    )

    pairs = lambda i: i ^ 1
    turn = lambda i: (((i - 1) % tiles ^ 1) + 1) % tiles
    first, coef_second, rest, second, own_lam, own_fields = pack(
        parts, place, far_lam, far[:5], far[5]
    )
    first = swapped(first, "dom", pairs)
    coef_second = swapped(coef_second, "dom", turn)
    rest = swapped(rest, "dom", pairs)
    second = swapped(second, "dom", turn)
    pieces = [jnp.stack([first[rest.shape[0] :], coef_second])]
    for by in range(1, parts):
        pieces.append(swapped(pieces[0], "grp", lambda i: i ^ by))
    coef, *states, final, rows = inner(place, own_lam, own_fields, top, region)
    wide = outer_coefs(parts, lam.shape[2], place, coef, pieces)
    final, grad = border(place, region, coef, wide, states, (first, rest, second), final, rows)
    share = grad
    for by in range(1, groups):
        grad = grad + swapped(share, "grp", lambda i: (i + by) % groups)
    return write(final, lam.shape), grad


def solution(mesh):
    return jax.shard_map(
        local,
        mesh=mesh,
        in_specs=(
            P("grp", None, "dom", None),
            P(None, "dom", None),
            P(None, "dom", None),
            P(None, "dom", None),
            P(None, "dom", None),
            P(None, "dom", None),
            P("dom", None),
            P("dom", None),
        ),
        out_specs=(P("grp", None, "dom", None), P("dom", None)),
        check_vma=False,
    )
```

```python
import functools

import jax
import jax.numpy as jnp
from jax import lax
from jax.experimental import pallas as pl
from jax.experimental.pallas import tpu as pltpu
from jax.sharding import PartitionSpec as P

ITERS = 4
EDGE = ITERS
ENTRIES = 16
CHUNKS = 2
LANES = 128
HALVES = (slice(0, LANES), slice(LANES, 2 * LANES))
SHORT = pl.CostEstimate(flops=1000, bytes_accessed=1000, transcendentals=0)
LOW, HIGH = 0, 1


def swapped(value, axis, partner):
    return lax.ppermute(value, axis, [(i, partner(i)) for i in range(lax.axis_size(axis))])


def level_of(shape):
    row = lax.broadcasted_iota(jnp.int32, shape, 0)
    half = shape[0] // 2
    return jnp.where(row < half, 2 * row, 2 * (row - half) + 1)


def place_of(level, levels):
    return (level % 2) * (levels // 2) + level // 2


def faces(ew, ed, nw, nd):
    lats = ew.shape[1]
    lat = lax.broadcasted_iota(jnp.int32, ew.shape, 1)
    east = jnp.maximum(ew, 0.0) + ed
    west_next = jnp.maximum(-ew, 0.0) + ed
    north = jnp.where(lat < lats - 1, jnp.maximum(nw, 0.0) + nd, 0.0)
    south = jnp.maximum(-nw, 0.0) + nd
    south = jnp.where(lat > 0, pltpu.roll(south, 1, 1), 0.0)
    return east, west_next, north, south


def updraft(mf, top_row):
    levels = mf.shape[0]
    level = level_of(mf.shape)
    return jnp.where((level < top_row) & (level < levels - 1), mf, 0.0)


def advance(coefs, mid, east, west):
    d, e, w, n, s, u = coefs
    half = mid.shape[0] // 2
    h = d * mid + e * east + w * west
    lane = lax.broadcasted_iota(jnp.int32, (mid.shape[0], LANES), 1)
    north = [pltpu.roll(mid[:, part], LANES - 1, 1) for part in HALVES]
    south = [pltpu.roll(mid[:, part], 1, 1) for part in HALVES]
    north = jnp.concatenate([jnp.where(lane < LANES - 1, *north), north[1]], axis=1)
    south = jnp.concatenate([south[0], jnp.where(lane > 0, south[1], south[0])], axis=1)
    h = h + n * north + s * south
    above = jnp.concatenate([h[half:], pltpu.roll(h[:half], half - 1, 0)], axis=0)
    return h + u * (above - h)


def pitched(slabs, levels, width):
    return -(-(slabs * levels * (width + 1) + width + 8) // 8) * 8


def column_at(ref, start, levels, pitch, apart):
    parts = [ref[pl.ds(start + apart * k, levels, stride=pitch), :] for k in range(2)]
    return jnp.concatenate(parts, axis=1)


def pack_kernel(parts, place, lam, ew, ed, nw, nd, mf, top, *refs):
    coef_first, coef_second, lam_first, lam_second = refs[:4]
    field_s, top_s, lam_s, entry, field_p, lam_p, sems = refs[4:]
    tags, levels, cols, lats = lam.shape
    copies = []

    def copy(src, dst):
        copies.append(pltpu.make_async_copy(src, dst, sems.at[len(copies)]))
        copies[-1].start()

    for side, at in ((LOW, 0), (HIGH, cols - 8)):
        for f, field in enumerate((ew, ed, nw, nd, mf)):
            copy(field.at[:, pl.ds(at, 8)], field_s.at[f, side])
        copy(top.at[pl.ds(at, 8)], top_s.at[side])
    for side, at in ((LOW, 0), (HIGH, cols - 8)):
        copy(lam.at[:, :, pl.ds(at, 8)], lam_s.at[side])
    for c in copies[:12]:
        c.wait()
    pitch = 9
    slab = levels * pitch

    @pl.loop(0, levels)
    def _(level):
        row = place_of(level, levels) * pitch
        for f in range(5):
            for side in (LOW, HIGH):
                for k in range(2):
                    at = ((f * 2 + side) * 2 + k) * slab
                    field_p[pl.ds(at + row, 8), :] = field_s[f, side, level, :, HALVES[k]]

    def field(f, side, c):
        return column_at(field_p, (f * 2 + side) * 2 * slab + c, levels, pitch, slab)

    entry[LOW, 0] = jnp.zeros((levels, lats), jnp.float32)
    start = 8 - EDGE
    entry[HIGH, 0] = jnp.maximum(-field(0, HIGH, start), 0.0) + field(1, HIGH, start)

    @pl.loop(0, EDGE - 1)
    def _(j):
        for side in (LOW, HIGH):
            c = j + (start + 1) * side
            east, west, north, south = faces(*(field(f, side, c) for f in range(4)))
            lift = updraft(field(4, side, c), top_s[side, pl.ds(c, 1), :])
            for n, value in enumerate((east, north, south, lift, west)):
                entry[side, 5 * j + 1 + n] = value

    per = ENTRIES // parts
    mine = lax.rem(place[0], parts) * per
    odd = place[1]
    copy(entry.at[1 - odd, pl.ds(mine, per)], coef_first)
    copy(entry.at[odd, pl.ds(mine, per)], coef_second)
    for c in copies[12:14]:
        c.wait()

    @pl.loop(0, levels)
    def _(level):
        row = place_of(level, levels) * pitch
        for side in (LOW, HIGH):
            for tag in range(tags):
                for k in range(2):
                    at = ((side * 2 + k) * tags + tag) * slab
                    lam_p[pl.ds(at + row, 8), :] = lam_s[side, tag, level, :, HALVES[k]]

    @pl.loop(0, tags)
    def _(tag):
        for dest, side in ((lam_first, 1 - odd), (lam_second, odd)):
            at = side * (2 * tags * slab + start) + tag * slab
            for c in range(EDGE):
                dest[tag * EDGE + c] = column_at(lam_p, at + c, levels, pitch, tags * slab)

    for c in copies[14:]:
        c.wait()


def pack(parts, place, lam, fields, top):
    tags, levels, cols, lats = lam.shape
    hbm = pl.BlockSpec(memory_space=pltpu.HBM)
    vmem = pl.BlockSpec(memory_space=pltpu.VMEM)
    coef_send = pltpu.HBM((ENTRIES // parts, levels, lats), jnp.float32)
    lam_send = pltpu.VMEM((tags * EDGE, levels, lats), jnp.float32)
    return pl.pallas_call(
        functools.partial(pack_kernel, parts),
        in_specs=[pl.BlockSpec(memory_space=pltpu.SMEM)] + [hbm] * 7,
        out_specs=[hbm, hbm, vmem, vmem],
        out_shape=[coef_send, coef_send, lam_send, lam_send],
        scratch_shapes=[
            pltpu.VMEM((5, 2, levels, 8, lats), jnp.float32),
            pltpu.VMEM((2, 8, lats), jnp.int32),
            pltpu.VMEM((2, tags, levels, 8, lats), jnp.float32),
            pltpu.VMEM((2, ENTRIES, levels, lats), jnp.float32),
            pltpu.VMEM((pitched(20, levels, 8), LANES), jnp.float32),
            pltpu.VMEM((pitched(4 * tags, levels, 8), LANES), jnp.float32),
            pltpu.SemaphoreType.DMA((16,)),
        ],
        compiler_params=pltpu.CompilerParams(vmem_limit_bytes=24 << 20),
        cost_estimate=SHORT,
        name="pack_edges",
    )(place, lam, *fields, top)


def chosen(region_row, first_tag, values):
    row = jnp.zeros(region_row.shape, jnp.float32)
    for tag, value in enumerate(values):
        row = jnp.where(region_row == first_tag + tag, value[0:1], row)
    return row


def sweep(t, shape, first_tag, region, coef, load, store, rows):
    tags, _, cols, _ = shape
    low, high = t + 1, cols - t - 1
    chunk = -(-(high - low) // CHUNKS)
    column = lambda c: [load(c, k) for k in range(tags)]

    @pl.loop(0, CHUNKS)
    def _(i):
        start = jnp.minimum(low + i * chunk, high - chunk)
        west, mid = column(start - 1), column(start)
        for j in range(chunk):
            c = start + j
            east = column(c + 1)
            coefs = [coef[c, n] for n in range(6)]
            new = [advance(coefs, mid[k], east[k], west[k]) for k in range(tags)]
            for k in range(tags):
                store(c, k, new[k])
            rows[t, pl.ds(c, 1), :] = chosen(region[pl.ds(c, 1), :], first_tag, new)
            west, mid = mid, east


def loading(ref):
    return lambda c, tag: ref[c, tag]


def storing(ref):
    def store(c, tag, value):
        ref[c, tag] = value

    return store


def storing_rows(ref, tags, levels, pitch):
    def store(c, tag, value):
        for k in range(2):
            at = (k * tags + tag) * levels * pitch + c
            ref[pl.ds(at, levels, stride=pitch), :] = value[:, HALVES[k]]

    return store


def inner_kernel(place, lam, ew, ed, nw, nd, mf, top, region, *refs):
    coef, l0, l1, l2, l3, final, rows, lam_s, field_s, lam_p, field_p, sems = refs
    tags, levels, cols, lats = lam.shape
    pitch = cols + 1
    slab = levels * pitch

    loads = [
        pltpu.make_async_copy(field, field_s.at[f], sems.at[f])
        for f, field in enumerate((ew, ed, nw, nd, mf))
    ]
    loads.append(pltpu.make_async_copy(lam, lam_s, sems.at[5]))
    for c in loads:
        c.start()
    for c in loads[:5]:
        c.wait()

    @pl.loop(0, levels)
    def _(level):
        row = place_of(level, levels) * pitch
        for f in range(5):
            for k in range(2):
                at = (f * 2 + k) * slab + row
                field_p[pl.ds(at, cols), :] = field_s[f, level, :, HALVES[k]]

    def coefficients(c, west):
        ew, ed, nw, nd, mf = (
            column_at(field_p, f * 2 * slab + c, levels, pitch, slab) for f in range(5)
        )
        e, next_west, n, s = faces(ew, ed, nw, nd)
        u = updraft(mf, top[pl.ds(c, 1), :])
        for j, value in enumerate((1.0 - e - west - n - s, e, west, n, s, u)):
            coef[c, j] = value
        return next_west

    def some(i, west):
        for j in range(8):
            west = coefficients(i * 8 + j, west)
        return west

    west = lax.fori_loop(0, cols // 8, some, jnp.zeros((levels, lats), jnp.float32))
    coef[cols, 2] = west
    loads[5].wait()

    @pl.loop(0, levels)
    def _(level):
        row = place_of(level, levels) * pitch
        for tag in range(tags):
            for k in range(2):
                at = (k * tags + tag) * slab + row
                lam_p[pl.ds(at, cols), :] = lam_s[tag, level, :, HALVES[k]]

    def given(c, tag):
        return column_at(lam_p, tag * slab + c, levels, pitch, tags * slab)

    for at, c in enumerate((0, 1, cols - 2, cols - 1)):
        for tag in range(tags):
            l0[at, tag] = given(c, tag)
    last = storing_rows(final, tags, levels, pitch)
    sources = (given, loading(l1), loading(l2), loading(l3))
    stores = (storing(l1), storing(l2), storing(l3), last)
    for t in range(ITERS):
        sweep(t, lam.shape, place[0] * tags, region, coef, sources[t], stores[t], rows)


def inner(place, lam, fields, top, region):
    tags, levels, cols, lats = lam.shape
    vmem = pl.BlockSpec(memory_space=pltpu.VMEM)
    hbm = pl.BlockSpec(memory_space=pltpu.HBM)
    state = pltpu.VMEM((cols, tags, levels, lats), jnp.float32)
    return pl.pallas_call(
        inner_kernel,
        in_specs=[pl.BlockSpec(memory_space=pltpu.SMEM)] + [hbm] * 6 + [vmem] * 2,
        out_specs=[vmem] * 7,
        out_shape=[
            pltpu.VMEM((cols + 1, 6, levels, lats), jnp.float32),
            pltpu.VMEM((4, tags, levels, lats), jnp.float32),
            *[state] * 3,
            pltpu.VMEM((pitched(2 * tags, levels, cols), LANES), jnp.float32),
            pltpu.VMEM((ITERS, cols, lats), jnp.float32),
        ],
        scratch_shapes=[
            pltpu.VMEM(lam.shape, jnp.float32),
            pltpu.VMEM((5, levels, cols, lats), jnp.float32),
            pltpu.VMEM((pitched(2 * tags, levels, cols), LANES), jnp.float32),
            pltpu.VMEM((pitched(10, levels, cols), LANES), jnp.float32),
            pltpu.SemaphoreType.DMA((6,)),
        ],
        compiler_params=pltpu.CompilerParams(vmem_limit_bytes=32 << 20),
        cost_estimate=SHORT,
        name="inner_steps",
    )(place, lam, *fields, top, region)


def slot(c, cols):
    return (LOW, c + EDGE - 1) if c < EDGE else (HIGH, c - (cols - EDGE))


def outer_kernel(place, coef, first, second, wide, entry, sems):
    cols = coef.shape[0] - 1
    odd, before = place[1], place[2]
    copies = [
        pltpu.make_async_copy(
            first.at[pl.ds((1 - odd) * ENTRIES, ENTRIES)], entry.at[1 - odd], sems.at[0]
        ),
        pltpu.make_async_copy(
            second.at[pl.ds(before * ENTRIES, ENTRIES)], entry.at[odd], sems.at[1]
        ),
    ]
    for c in copies:
        c.start()
    for c in copies:
        c.wait()
    entry[HIGH, 0] = coef[cols, 2]

    @pl.loop(0, EDGE - 1)
    def _(j):
        for side in (LOW, HIGH):
            w, e, n, s, u = (entry[side, 5 * j + i] for i in range(5))
            for i, value in enumerate((1.0 - e - w - n - s, e, w, n, s, u)):
                wide[side, j + EDGE * side, i] = value

    first_west = entry[LOW, ENTRIES - 1]
    e, n, s, u = (coef[0, i] for i in (1, 3, 4, 5))
    for i, value in enumerate((1.0 - e - first_west - n - s, e, first_west, n, s, u)):
        wide[*slot(0, cols), i] = value


def outer_coefs(place, coef, first, second):
    _, _, levels, lats = coef.shape
    vmem = pl.BlockSpec(memory_space=pltpu.VMEM)
    hbm = pl.BlockSpec(memory_space=pltpu.HBM)
    return pl.pallas_call(
        outer_kernel,
        in_specs=[pl.BlockSpec(memory_space=pltpu.SMEM), vmem, hbm, hbm],
        out_specs=vmem,
        out_shape=pltpu.VMEM((2, 2 * EDGE - 1, 6, levels, lats), jnp.float32),
        scratch_shapes=[
            pltpu.VMEM((2, ENTRIES, levels, lats), jnp.float32),
            pltpu.SemaphoreType.DMA((2,)),
        ],
        compiler_params=pltpu.CompilerParams(vmem_limit_bytes=24 << 20),
        cost_estimate=SHORT,
        name="outer_coefs",
    )(place, coef, first, second)


def border_kernel(place, region, coef, wide, l0, l1, l2, l3, first, second, *refs):
    final_in, rows_in, final, grad, halo, work, rows = refs
    cols, tags, levels, lats = l1.shape
    first_tag = place[0] * tags
    odd = place[1]
    halo[1 - odd] = first[...]
    halo[odd] = second[...]

    def coefs_at(c):
        if 0 < c < cols:
            return [coef[c, j] for j in range(6)]
        return [wide[*slot(c, cols), j] for j in range(6)]

    kept = (None, l1, l2, l3)

    def state(t, c, tag):
        if t == 0:
            if c < 0:
                return halo[LOW, tag * EDGE + c + EDGE]
            if c >= cols:
                return halo[HIGH, tag * EDGE + c - cols]
            return l0[c if c < 2 else c - (cols - 4), tag]
        return kept[t][c, tag] if t <= c < cols - t else work[t, *slot(c, cols), tag]

    def column(t, c):
        return [state(t, c, tag) for tag in range(tags)]

    rows[...] = rows_in[...]
    store = storing_rows(final, tags, levels, cols + 1)
    for t in range(ITERS):
        reach = EDGE - 1 - t
        for run in (range(-reach, t + 1), range(cols - t - 1, cols + reach)):
            west, mid = column(t, run[0] - 1), column(t, run[0])
            for c in run:
                east = column(t, c + 1)
                coefs = coefs_at(c)
                new = [advance(coefs, mid[k], east[k], west[k]) for k in range(tags)]
                for k in range(tags):
                    if t < ITERS - 1:
                        work[t + 1, *slot(c, cols), k] = new[k]
                    else:
                        store(c, k, new[k])
                if 0 <= c < cols:
                    rows[t, c : c + 1, :] = chosen(region[c : c + 1, :], first_tag, new)
                west, mid = mid, east
    total = rows[0]
    for t in range(1, ITERS):
        total = total + rows[t]
    grad[...] = total


def border(place, region, coef, wide, states, first, second, final, rows):
    cols, tags, levels, lats = states[1].shape
    vmem = pl.BlockSpec(memory_space=pltpu.VMEM)
    operands = [region, coef, wide, *states, first, second]
    return pl.pallas_call(
        border_kernel,
        in_specs=[pl.BlockSpec(memory_space=pltpu.SMEM)] + [vmem] * (len(operands) + 2),
        out_specs=[vmem] * 2,
        out_shape=[
            pltpu.VMEM(final.shape, jnp.float32),
            pltpu.VMEM((cols, lats), jnp.float32),
        ],
        input_output_aliases={len(operands) + 1: 0},
        scratch_shapes=[
            pltpu.VMEM((2, tags * EDGE, levels, lats), jnp.float32),
            pltpu.VMEM((ITERS, 2, 2 * EDGE - 1, tags, levels, lats), jnp.float32),
            pltpu.VMEM((ITERS, cols, lats), jnp.float32),
        ],
        compiler_params=pltpu.CompilerParams(vmem_limit_bytes=32 << 20),
        cost_estimate=SHORT,
        name="border_steps",
    )(place, *operands, final, rows)


def write_kernel(final, out, block, sems):
    tags, levels, cols, _ = out.shape
    pitch = cols + 1
    copies = []
    for tag in range(tags):

        @pl.loop(0, levels)
        def _(level):
            row = place_of(level, levels) * pitch
            for k in range(2):
                at = (k * tags + tag) * levels * pitch + row
                block[tag, level, :, HALVES[k]] = final[pl.ds(at, cols), :]

        copies.append(pltpu.make_async_copy(block.at[tag], out.at[tag], sems.at[tag]))
        copies[-1].start()
    for c in copies:
        c.wait()


def write(final, shape):
    return pl.pallas_call(
        write_kernel,
        in_specs=[pl.BlockSpec(memory_space=pltpu.VMEM)],
        out_specs=pl.BlockSpec(memory_space=pltpu.HBM),
        out_shape=pltpu.HBM(shape, jnp.float32),
        scratch_shapes=[
            pltpu.VMEM(shape, jnp.float32),
            pltpu.SemaphoreType.DMA((shape[0],)),
        ],
        compiler_params=pltpu.CompilerParams(vmem_limit_bytes=24 << 20),
        cost_estimate=SHORT,
        name="write_final",
    )(final)


def local(lam, east_wind, north_wind, east_diff, north_diff, mass_flux, region, top):
    groups, tiles = lax.axis_size("grp"), lax.axis_size("dom")
    grp, dom = lax.axis_index("grp"), lax.axis_index("dom")
    odd = dom % 2
    before = jnp.where((dom > 0) & (dom < tiles - 1), odd, 1 - odd)
    place = jnp.stack([grp, odd, before]).astype(jnp.int32)
    lam, *fields, far_top = (
        pltpu.with_memory_space_constraint(value, pltpu.HBM)
        for value in (lam, east_wind, east_diff, north_wind, north_diff, mass_flux, top)
    )
    coef_first, coef_second, first, second = pack(groups, place, lam, fields, far_top)

    pairs = lambda i: i ^ 1
    turn = lambda i: (((i - 1) % tiles ^ 1) + 1) % tiles

    def gathered(value, partner):
        sets = sorted({tuple(sorted((i, partner(i)))) for i in range(tiles)})
        members = [[i * groups + rank for i in both for rank in range(groups)] for both in sets]
        value = lax.all_gather(value, ("dom", "grp"), axis_index_groups=members, tiled=True)
        return pltpu.with_memory_space_constraint(value, pltpu.HBM)

    coef_first = gathered(coef_first, pairs)
    coef_second = gathered(coef_second, turn)
    first = swapped(first, "dom", pairs)
    second = swapped(second, "dom", turn)
    coef, *states, final, rows = inner(place, lam, fields, top, region)
    wide = outer_coefs(place, coef, coef_first, coef_second)
    final, grad = border(place, region, coef, wide, states, first, second, final, rows)
    share = grad
    for by in range(1, groups):
        grad = grad + swapped(share, "grp", lambda i: (i + by) % groups)
    return write(final, lam.shape), grad


def solution(mesh):
    return jax.shard_map(
        local,
        mesh=mesh,
        in_specs=(
            P("grp", None, "dom", None),
            P(None, "dom", None),
            P(None, "dom", None),
            P(None, "dom", None),
            P(None, "dom", None),
            P(None, "dom", None),
            P("dom", None),
            P("dom", None),
        ),
        out_specs=(P("grp", None, "dom", None), P("dom", None)),
        check_vma=False,
    )
```

```python
import functools

import jax
import jax.numpy as jnp
from jax import lax
from jax.experimental import pallas as pl
from jax.experimental.pallas import tpu as pltpu
from jax.sharding import PartitionSpec as P

ITERS = 4
EDGE = ITERS
ENTRIES = 16
CHUNKS = 2
LANES = 128
HALVES = (slice(0, LANES), slice(LANES, 2 * LANES))
SHORT = pl.CostEstimate(flops=1000, bytes_accessed=1000, transcendentals=0)
LOW, HIGH = 0, 1


def swapped(value, axis, partner):
    return lax.ppermute(value, axis, [(i, partner(i)) for i in range(lax.axis_size(axis))])


def level_of(shape):
    row = lax.broadcasted_iota(jnp.int32, shape, 0)
    half = shape[0] // 2
    return jnp.where(row < half, 2 * row, 2 * (row - half) + 1)


def place_of(level, levels):
    return (level % 2) * (levels // 2) + level // 2


def faces(ew, ed, nw, nd):
    lats = ew.shape[1]
    lat = lax.broadcasted_iota(jnp.int32, ew.shape, 1)
    east = jnp.maximum(ew, 0.0) + ed
    west_next = jnp.maximum(-ew, 0.0) + ed
    north = jnp.where(lat < lats - 1, jnp.maximum(nw, 0.0) + nd, 0.0)
    south = jnp.maximum(-nw, 0.0) + nd
    south = jnp.where(lat > 0, pltpu.roll(south, 1, 1), 0.0)
    return east, west_next, north, south


def updraft(mf, top_row):
    levels = mf.shape[0]
    level = level_of(mf.shape)
    return jnp.where((level < top_row) & (level < levels - 1), mf, 0.0)


def advance(coefs, mid, east, west):
    d, e, w, n, s, u = coefs
    half = mid.shape[0] // 2
    h = d * mid + e * east + w * west
    lane = lax.broadcasted_iota(jnp.int32, (mid.shape[0], LANES), 1)
    north = [pltpu.roll(mid[:, part], LANES - 1, 1) for part in HALVES]
    south = [pltpu.roll(mid[:, part], 1, 1) for part in HALVES]
    north = jnp.concatenate([jnp.where(lane < LANES - 1, *north), north[1]], axis=1)
    south = jnp.concatenate([south[0], jnp.where(lane > 0, south[1], south[0])], axis=1)
    h = h + n * north + s * south
    above = jnp.concatenate([h[half:], pltpu.roll(h[:half], half - 1, 0)], axis=0)
    return h + u * (above - h)


def pitched(slabs, levels, width):
    return -(-(slabs * levels * (width + 1) + width + 8) // 8) * 8


def column_at(ref, start, levels, pitch, apart):
    parts = [ref[pl.ds(start + apart * k, levels, stride=pitch), :] for k in range(2)]
    return jnp.concatenate(parts, axis=1)


def pack_kernel(parts, place, lam, ew, ed, nw, nd, mf, top, *refs):
    first, coef_second, lam_first, lam_second = refs[:4]
    field_s, top_s, lam_s, entry, field_p, lam_p, sems = refs[4:]
    tags, levels, cols, lats = lam.shape
    copies = []

    def copy(src, dst):
        copies.append(pltpu.make_async_copy(src, dst, sems.at[len(copies)]))
        copies[-1].start()

    for side, at in ((LOW, 0), (HIGH, cols - 8)):
        for f, field in enumerate((ew, ed, nw, nd, mf)):
            copy(field.at[:, pl.ds(at, 8)], field_s.at[f, side])
        copy(top.at[pl.ds(at, 8)], top_s.at[side])
    for side, at in ((LOW, 0), (HIGH, cols - 8)):
        for tag in range(tags):
            copy(lam.at[tag, :, pl.ds(at, 8)], lam_s.at[side, tag])
    for c in copies[:12]:
        c.wait()
    pitch = 9
    slab = levels * pitch

    @pl.loop(0, levels)
    def _(level):
        row = place_of(level, levels) * pitch
        for f in range(5):
            for side in (LOW, HIGH):
                for k in range(2):
                    at = ((f * 2 + side) * 2 + k) * slab
                    field_p[pl.ds(at + row, 8), :] = field_s[f, side, level, :, HALVES[k]]

    def field(f, side, c):
        return column_at(field_p, (f * 2 + side) * 2 * slab + c, levels, pitch, slab)

    entry[LOW, 0] = jnp.zeros((levels, lats), jnp.float32)
    start = 8 - EDGE
    entry[HIGH, 0] = jnp.maximum(-field(0, HIGH, start), 0.0) + field(1, HIGH, start)

    @pl.loop(0, EDGE - 1)
    def _(j):
        for side in (LOW, HIGH):
            c = j + (start + 1) * side
            east, west, north, south = faces(*(field(f, side, c) for f in range(4)))
            lift = updraft(field(4, side, c), top_s[side, pl.ds(c, 1), :])
            for n, value in enumerate((east, north, south, lift, west)):
                entry[side, 5 * j + 1 + n] = value

    per = ENTRIES // parts
    mine = lax.rem(place[0], parts) * per
    odd = place[1]
    first[EDGE:] = entry[1 - odd, pl.ds(mine, per)]
    coef_second[...] = entry[odd, pl.ds(mine, per)]

    for c in copies[12:]:
        c.wait()

    @pl.loop(0, levels)
    def _(level):
        row = place_of(level, levels) * pitch
        for side in (LOW, HIGH):
            for tag in range(tags):
                for k in range(2):
                    at = ((side * 2 + k) * tags + tag) * slab
                    lam_p[pl.ds(at + row, 8), :] = lam_s[side, tag, level, :, HALVES[k]]

    def columns(tag, side):
        at = side * (2 * tags * slab + start) + tag * slab
        return [column_at(lam_p, at + c, levels, pitch, tags * slab) for c in range(EDGE)]

    for c, value in enumerate(columns(0, 1 - odd)):
        first[c] = value

    @pl.loop(1, tags)
    def _(tag):
        for c, value in enumerate(columns(tag, 1 - odd)):
            lam_first[(tag - 1) * EDGE + c] = value

    @pl.loop(0, tags)
    def _(tag):
        for c, value in enumerate(columns(tag, odd)):
            lam_second[tag * EDGE + c] = value


def pack(parts, place, lam, fields, top):
    tags, levels, cols, lats = lam.shape
    hbm = pl.BlockSpec(memory_space=pltpu.HBM)
    send = lambda slabs: pltpu.VMEM((slabs, levels, lats), jnp.float32)
    few, many = ENTRIES // parts, tags * EDGE
    return pl.pallas_call(
        functools.partial(pack_kernel, parts),
        in_specs=[pl.BlockSpec(memory_space=pltpu.SMEM)] + [hbm] * 7,
        out_specs=[pl.BlockSpec(memory_space=pltpu.VMEM)] * 4,
        out_shape=[send(EDGE + few), send(few), send(many - EDGE), send(many)],
        scratch_shapes=[
            pltpu.VMEM((5, 2, levels, 8, lats), jnp.float32),
            pltpu.VMEM((2, 8, lats), jnp.int32),
            pltpu.VMEM((2, tags, levels, 8, lats), jnp.float32),
            pltpu.VMEM((2, ENTRIES, levels, lats), jnp.float32),
            pltpu.VMEM((pitched(20, levels, 8), LANES), jnp.float32),
            pltpu.VMEM((pitched(4 * tags, levels, 8), LANES), jnp.float32),
            pltpu.SemaphoreType.DMA((12 + 2 * tags,)),
        ],
        compiler_params=pltpu.CompilerParams(vmem_limit_bytes=24 << 20),
        cost_estimate=SHORT,
        name="pack_edges",
    )(place, lam, *fields, top)


def chosen(region_row, first_tag, values):
    row = jnp.zeros(region_row.shape, jnp.float32)
    for tag, value in enumerate(values):
        row = jnp.where(region_row == first_tag + tag, value[0:1], row)
    return row


def sweep(t, shape, first_tag, region, coef, load, store, rows):
    tags, _, cols, _ = shape
    low, high = t + 1, cols - t - 1
    chunk = -(-(high - low) // CHUNKS)
    column = lambda c: [load(c, k) for k in range(tags)]

    @pl.loop(0, CHUNKS)
    def _(i):
        start = jnp.minimum(low + i * chunk, high - chunk)
        west, mid = column(start - 1), column(start)
        for j in range(chunk):
            c = start + j
            east = column(c + 1)
            coefs = [coef[c, n] for n in range(6)]
            new = [advance(coefs, mid[k], east[k], west[k]) for k in range(tags)]
            for k in range(tags):
                store(c, k, new[k])
            rows[t, pl.ds(c, 1), :] = chosen(region[pl.ds(c, 1), :], first_tag, new)
            west, mid = mid, east


def loading(ref):
    return lambda c, tag: ref[c, tag]


def storing(ref):
    def store(c, tag, value):
        ref[c, tag] = value

    return store


def storing_rows(ref, tags, levels, pitch):
    def store(c, tag, value):
        for k in range(2):
            at = (k * tags + tag) * levels * pitch + c
            ref[pl.ds(at, levels, stride=pitch), :] = value[:, HALVES[k]]

    return store


def inner_kernel(place, lam, ew, ed, nw, nd, mf, top, region, *refs):
    coef, l0, l1, l2, l3, final, rows, lam_p, field_p = refs
    tags, levels, cols, lats = lam.shape
    pitch = cols + 1
    slab = levels * pitch

    @pl.loop(0, levels)
    def _(level):
        row = place_of(level, levels) * pitch
        for f, field in enumerate((ew, ed, nw, nd, mf)):
            for k in range(2):
                field_p[pl.ds((f * 2 + k) * slab + row, cols), :] = field[level, :, HALVES[k]]
        for tag in range(tags):
            for k in range(2):
                at = (k * tags + tag) * slab + row
                lam_p[pl.ds(at, cols), :] = lam[tag, level, :, HALVES[k]]

    def coefficients(c, west):
        ew, ed, nw, nd, mf = (
            column_at(field_p, f * 2 * slab + c, levels, pitch, slab) for f in range(5)
        )
        e, next_west, n, s = faces(ew, ed, nw, nd)
        u = updraft(mf, top[pl.ds(c, 1), :])
        for j, value in enumerate((1.0 - e - west - n - s, e, west, n, s, u)):
            coef[c, j] = value
        return next_west

    def some(i, west):
        for j in range(8):
            west = coefficients(i * 8 + j, west)
        return west

    west = lax.fori_loop(0, cols // 8, some, jnp.zeros((levels, lats), jnp.float32))
    coef[cols, 2] = west

    def given(c, tag):
        return column_at(lam_p, tag * slab + c, levels, pitch, tags * slab)

    for at, c in enumerate((0, 1, cols - 2, cols - 1)):
        for tag in range(tags):
            l0[at, tag] = given(c, tag)
    last = storing_rows(final, tags, levels, pitch)
    loads = (given, loading(l1), loading(l2), loading(l3))
    stores = (storing(l1), storing(l2), storing(l3), last)
    for t in range(ITERS):
        sweep(t, lam.shape, place[0] * tags, region, coef, loads[t], stores[t], rows)


def inner(place, lam, fields, top, region):
    tags, levels, cols, lats = lam.shape
    vmem = pl.BlockSpec(memory_space=pltpu.VMEM)
    state = pltpu.VMEM((cols, tags, levels, lats), jnp.float32)
    return pl.pallas_call(
        inner_kernel,
        in_specs=[pl.BlockSpec(memory_space=pltpu.SMEM)] + [vmem] * 8,
        out_specs=[vmem] * 7,
        out_shape=[
            pltpu.VMEM((cols + 1, 6, levels, lats), jnp.float32),
            pltpu.VMEM((4, tags, levels, lats), jnp.float32),
            *[state] * 3,
            pltpu.VMEM((pitched(2 * tags, levels, cols), LANES), jnp.float32),
            pltpu.VMEM((ITERS, cols, lats), jnp.float32),
        ],
        scratch_shapes=[
            pltpu.VMEM((pitched(2 * tags, levels, cols), LANES), jnp.float32),
            pltpu.VMEM((pitched(10, levels, cols), LANES), jnp.float32),
        ],
        compiler_params=pltpu.CompilerParams(vmem_limit_bytes=32 << 20),
        cost_estimate=SHORT,
        name="inner_steps",
    )(place, lam, *fields, top, region)


def slot(c, cols):
    return (LOW, c + EDGE - 1) if c < EDGE else (HIGH, c - (cols - EDGE))


def outer_kernel(parts, cols, place, coef, *refs):
    pieces, wide, entry = refs[:parts], refs[parts], refs[parts + 1]
    per = ENTRIES // parts
    mine = lax.rem(place[0], parts)
    odd = place[1]
    for by in range(parts):
        base = (mine ^ by) * per
        entry[1 - odd, pl.ds(base, per)] = pieces[by][0]
        entry[odd, pl.ds(base, per)] = pieces[by][1]

    entry[HIGH, 0] = coef[cols, 2]

    @pl.loop(0, EDGE - 1)
    def _(j):
        for side in (LOW, HIGH):
            w, e, n, s, u = (entry[side, 5 * j + i] for i in range(5))
            for i, value in enumerate((1.0 - e - w - n - s, e, w, n, s, u)):
                wide[side, j + EDGE * side, i] = value

    first_west = entry[LOW, ENTRIES - 1]
    e, n, s, u = (coef[0, i] for i in (1, 3, 4, 5))
    for i, value in enumerate((1.0 - e - first_west - n - s, e, first_west, n, s, u)):
        wide[*slot(0, cols), i] = value


def outer_coefs(parts, cols, place, coef, pieces):
    _, _, levels, lats = coef.shape
    vmem = pl.BlockSpec(memory_space=pltpu.VMEM)
    return pl.pallas_call(
        functools.partial(outer_kernel, parts, cols),
        in_specs=[pl.BlockSpec(memory_space=pltpu.SMEM)] + [vmem] * (1 + parts),
        out_specs=vmem,
        out_shape=pltpu.VMEM((2, 2 * EDGE - 1, 6, levels, lats), jnp.float32),
        scratch_shapes=[pltpu.VMEM((2, ENTRIES, levels, lats), jnp.float32)],
        compiler_params=pltpu.CompilerParams(vmem_limit_bytes=24 << 20),
        cost_estimate=SHORT,
        name="outer_coefs",
    )(place, coef, *pieces)


def border_kernel(place, region, coef, wide, l0, l1, l2, l3, first, rest, second, *refs):
    final_in, rows_in, final, grad, halo, work, rows = refs
    cols, tags, levels, lats = l1.shape
    first_tag = place[0] * tags
    odd = place[1]
    halo[1 - odd, :EDGE] = first[:EDGE]
    halo[1 - odd, EDGE:] = rest[...]
    halo[odd] = second[...]

    def coefs_at(c):
        if 0 < c < cols:
            return [coef[c, j] for j in range(6)]
        return [wide[*slot(c, cols), j] for j in range(6)]

    kept = (None, l1, l2, l3)

    def state(t, c, tag):
        if t == 0:
            if c < 0:
                return halo[LOW, tag * EDGE + c + EDGE]
            if c >= cols:
                return halo[HIGH, tag * EDGE + c - cols]
            return l0[c if c < 2 else c - (cols - 4), tag]
        return kept[t][c, tag] if t <= c < cols - t else work[t, *slot(c, cols), tag]

    def column(t, c):
        return [state(t, c, tag) for tag in range(tags)]

    rows[...] = rows_in[...]
    store = storing_rows(final, tags, levels, cols + 1)
    for t in range(ITERS):
        reach = EDGE - 1 - t
        for run in (range(-reach, t + 1), range(cols - t - 1, cols + reach)):
            west, mid = column(t, run[0] - 1), column(t, run[0])
            for c in run:
                east = column(t, c + 1)
                coefs = coefs_at(c)
                new = [advance(coefs, mid[k], east[k], west[k]) for k in range(tags)]
                for k in range(tags):
                    if t < ITERS - 1:
                        work[t + 1, *slot(c, cols), k] = new[k]
                    else:
                        store(c, k, new[k])
                if 0 <= c < cols:
                    rows[t, c : c + 1, :] = chosen(region[c : c + 1, :], first_tag, new)
                west, mid = mid, east
    total = rows[0]
    for t in range(1, ITERS):
        total = total + rows[t]
    grad[...] = total


def border(place, region, coef, wide, states, halos, final, rows):
    cols, tags, levels, lats = states[1].shape
    vmem = pl.BlockSpec(memory_space=pltpu.VMEM)
    operands = [region, coef, wide, *states, *halos]
    return pl.pallas_call(
        border_kernel,
        in_specs=[pl.BlockSpec(memory_space=pltpu.SMEM)] + [vmem] * (len(operands) + 2),
        out_specs=[vmem] * 2,
        out_shape=[
            pltpu.VMEM(final.shape, jnp.float32),
            pltpu.VMEM((cols, lats), jnp.float32),
        ],
        input_output_aliases={len(operands) + 1: 0},
        scratch_shapes=[
            pltpu.VMEM((2, tags * EDGE, levels, lats), jnp.float32),
            pltpu.VMEM((ITERS, 2, 2 * EDGE - 1, tags, levels, lats), jnp.float32),
            pltpu.VMEM((ITERS, cols, lats), jnp.float32),
        ],
        compiler_params=pltpu.CompilerParams(vmem_limit_bytes=32 << 20),
        cost_estimate=SHORT,
        name="border_steps",
    )(place, *operands, final, rows)


def write_kernel(final, out, block, sems):
    tags, levels, cols, _ = out.shape
    pitch = cols + 1
    copies = []
    for tag in range(tags):

        @pl.loop(0, levels)
        def _(level):
            row = place_of(level, levels) * pitch
            for k in range(2):
                at = (k * tags + tag) * levels * pitch + row
                block[tag, level, :, HALVES[k]] = final[pl.ds(at, cols), :]

        copies.append(pltpu.make_async_copy(block.at[tag], out.at[tag], sems.at[tag]))
        copies[-1].start()
    for c in copies:
        c.wait()


def write(final, shape):
    return pl.pallas_call(
        write_kernel,
        in_specs=[pl.BlockSpec(memory_space=pltpu.VMEM)],
        out_specs=pl.BlockSpec(memory_space=pltpu.HBM),
        out_shape=pltpu.HBM(shape, jnp.float32),
        scratch_shapes=[
            pltpu.VMEM(shape, jnp.float32),
            pltpu.SemaphoreType.DMA((shape[0],)),
        ],
        compiler_params=pltpu.CompilerParams(vmem_limit_bytes=24 << 20),
        cost_estimate=SHORT,
        name="write_final",
    )(final)


def local(lam, east_wind, north_wind, east_diff, north_diff, mass_flux, region, top):
    groups, tiles = lax.axis_size("grp"), lax.axis_size("dom")
    parts = 4 if groups % 4 == 0 else 1
    grp, dom = lax.axis_index("grp"), lax.axis_index("dom")
    place = jnp.stack([grp, dom % 2]).astype(jnp.int32)
    own = (lam, east_wind, east_diff, north_wind, north_diff, mass_flux)
    far_lam, *far = (
        pltpu.with_memory_space_constraint(value, pltpu.HBM) for value in (*own, top)
    )

    pairs = lambda i: i ^ 1
    turn = lambda i: (((i - 1) % tiles ^ 1) + 1) % tiles
    first, coef_second, rest, second = pack(parts, place, far_lam, far[:5], far[5])
    first = swapped(first, "dom", pairs)
    coef_second = swapped(coef_second, "dom", turn)
    rest = swapped(rest, "dom", pairs)
    second = swapped(second, "dom", turn)
    pieces = [jnp.stack([first[EDGE:], coef_second])]
    for by in range(1, parts):
        pieces.append(swapped(pieces[0], "grp", lambda i: i ^ by))
    coef, *states, final, rows = inner(place, own[0], own[1:], top, region)
    wide = outer_coefs(parts, lam.shape[2], place, coef, pieces)
    final, grad = border(place, region, coef, wide, states, (first, rest, second), final, rows)
    share = grad
    for by in range(1, groups):
        grad = grad + swapped(share, "grp", lambda i: (i + by) % groups)
    return write(final, lam.shape), grad


def solution(mesh):
    return jax.shard_map(
        local,
        mesh=mesh,
        in_specs=(
            P("grp", None, "dom", None),
            P(None, "dom", None),
            P(None, "dom", None),
            P(None, "dom", None),
            P(None, "dom", None),
            P(None, "dom", None),
            P("dom", None),
            P("dom", None),
        ),
        out_specs=(P("grp", None, "dom", None), P("dom", None)),
        check_vma=False,
    )
```

```python
import functools

import jax
import jax.numpy as jnp
from jax import lax
from jax.experimental import pallas as pl
from jax.experimental.pallas import tpu as pltpu
from jax.sharding import PartitionSpec as P

ITERS = 4
EDGE = ITERS
ENTRIES = 16
CHUNKS = 2
LANES = 128
HALVES = (slice(0, LANES), slice(LANES, 2 * LANES))
SHORT = pl.CostEstimate(flops=1000, bytes_accessed=1000, transcendentals=0)
LOW, HIGH = 0, 1

def swapped(value, axis, partner):
    return lax.ppermute(value, axis, [(i, partner(i)) for i in range(lax.axis_size(axis))])


def faces(ew, ed, nw, nd):
    lats = ew.shape[1]
    lat = lax.broadcasted_iota(jnp.int32, ew.shape, 1)
    east = jnp.maximum(ew, 0.0) + ed
    west_next = jnp.maximum(-ew, 0.0) + ed
    north = jnp.where(lat < lats - 1, jnp.maximum(nw, 0.0) + nd, 0.0)
    south = jnp.maximum(-nw, 0.0) + nd
    south = jnp.where(lat > 0, pltpu.roll(south, 1, 1), 0.0)
    return east, west_next, north, south


def updraft(mf, top_row):
    levels = mf.shape[0]
    level = lax.broadcasted_iota(jnp.int32, mf.shape, 0)
    return jnp.where((level < top_row) & (level < levels - 1), mf, 0.0)


def level_above(h):
    if h.shape[0] == 8:
        return pltpu.roll(h, 7, 0)
    parts = [pltpu.roll(h[at : at + 8], 7, 0) for at in range(0, h.shape[0], 8)]
    inside = lax.broadcasted_iota(jnp.int32, parts[0].shape, 0) < 7
    joined = [jnp.where(inside, low, high) for low, high in zip(parts, parts[1:])]
    return jnp.concatenate([*joined, parts[-1]], axis=0)


def advance(coefs, mid, east, west):
    d, e, w, n, s, u = coefs
    h = d * mid + e * east + w * west
    lane = lax.broadcasted_iota(jnp.int32, (mid.shape[0], LANES), 1)
    north = [pltpu.roll(mid[:, part], LANES - 1, 1) for part in HALVES]
    south = [pltpu.roll(mid[:, part], 1, 1) for part in HALVES]
    north = jnp.concatenate([jnp.where(lane < LANES - 1, *north), north[1]], axis=1)
    south = jnp.concatenate([south[0], jnp.where(lane > 0, south[1], south[0])], axis=1)
    h = h + n * north + s * south
    return h + u * (level_above(h) - h)


def pitched(slabs, levels, width):
    return -(-(slabs * levels * (width + 1) + width + 8) // 8) * 8


def column_at(ref, start, levels, pitch, apart):
    parts = [ref[pl.ds(start + apart * k, levels, stride=pitch), :] for k in range(2)]
    return jnp.concatenate(parts, axis=1)


def pack_kernel(parts, place, lam, ew, ed, nw, nd, mf, top, *refs):
    coef_first, coef_second, lam_first, lam_second = refs[:4]
    field_s, top_s, lam_s, entry, field_p, lam_p, sems = refs[4:]
    tags, levels, cols, lats = lam.shape
    copies = []

    def copy(src, dst):
        copies.append(pltpu.make_async_copy(src, dst, sems.at[len(copies)]))
        copies[-1].start()

    for side, at in ((LOW, 0), (HIGH, cols - 8)):
        for f, field in enumerate((ew, ed, nw, nd, mf)):
            copy(field.at[:, pl.ds(at, 8)], field_s.at[f, side])
        copy(top.at[pl.ds(at, 8)], top_s.at[side])
    field_copies = len(copies)
    for side, at in ((LOW, 0), (HIGH, cols - 8)):
        for tag in range(tags):
            copy(lam.at[tag, :, pl.ds(at, 8)], lam_s.at[side, tag])
    for c in copies[:field_copies]:
        c.wait()
    pitch = 9
    slab = levels * pitch

    @pl.loop(0, levels)
    def _(level):
        row = level * pitch
        for f in range(5):
            for side in range(2):
                for k in range(2):
                    at = ((f * 2 + side) * 2 + k) * slab
                    field_p[pl.ds(at + row, 8), :] = field_s[f, side, level, :, HALVES[k]]

    def field(f, side, c):
        return column_at(field_p, (f * 2 + side) * 2 * slab + c, levels, pitch, slab)

    for side in (LOW, HIGH):
        slot = 0
        for c in range(EDGE - 1) if side == LOW else range(8 - EDGE, 8):
            east, west, north, south = faces(*(field(f, side, c) for f in range(4)))
            lift = updraft(field(4, side, c), top_s[side, pl.ds(c, 1), :])
            wanted = (east, west, north, south, lift)
            if side == HIGH and c == 8 - EDGE:
                wanted = (west,)
            for value in wanted:
                entry[side, slot] = value
                slot += 1
        for left in range(slot, ENTRIES):
            entry[side, left] = jnp.zeros((levels, lats), jnp.float32)
    per = ENTRIES // parts
    mine = lax.rem(place[0], parts) * per
    odd = place[1]
    coef_first[...] = entry[1 - odd, pl.ds(mine, per)]
    coef_second[...] = entry[odd, pl.ds(mine, per)]

    for c in copies[field_copies:]:
        c.wait()

    @pl.loop(0, levels)
    def _(level):
        row = level * pitch
        for side in range(2):
            for tag in range(tags):
                for k in range(2):
                    at = ((side * 2 + k) * tags + tag) * slab
                    lam_p[pl.ds(at + row, 8), :] = lam_s[side, tag, level, :, HALVES[k]]

    for dest, side in ((lam_first, 1 - odd), (lam_second, odd)):
        start = side * (2 * tags * slab + 8 - EDGE)
        for tag in range(tags):
            for c in range(EDGE):
                dest[tag * EDGE + c] = column_at(lam_p, start + tag * slab + c, levels, pitch, tags * slab)


def pack(parts, place, lam, fields, top):
    tags, levels, cols, lats = lam.shape
    hbm = pl.BlockSpec(memory_space=pltpu.HBM)
    send = lambda slabs: pltpu.VMEM((slabs, levels, lats), jnp.float32)
    few, many = ENTRIES // parts, tags * EDGE
    return pl.pallas_call(
        functools.partial(pack_kernel, parts),
        in_specs=[pl.BlockSpec(memory_space=pltpu.SMEM)] + [hbm] * 7,
        out_specs=[pl.BlockSpec(memory_space=pltpu.VMEM)] * 4,
        out_shape=[send(few), send(few), send(many), send(many)],
        scratch_shapes=[
            pltpu.VMEM((5, 2, levels, 8, lats), jnp.float32),
            pltpu.VMEM((2, 8, lats), jnp.int32),
            pltpu.VMEM((2, tags, levels, 8, lats), jnp.float32),
            pltpu.VMEM((2, ENTRIES, levels, lats), jnp.float32),
            pltpu.VMEM((pitched(20, levels, 8), LANES), jnp.float32),
            pltpu.VMEM((pitched(4 * tags, levels, 8), LANES), jnp.float32),
            pltpu.SemaphoreType.DMA((12 + 2 * tags,)),
        ],
        compiler_params=pltpu.CompilerParams(vmem_limit_bytes=24 << 20),
        cost_estimate=SHORT,
        name="pack_edges",
    )(place, lam, *fields, top)


def chosen(region_row, first_tag, values):
    row = jnp.zeros(region_row.shape, jnp.float32)
    for tag, value in enumerate(values):
        row = jnp.where(region_row == first_tag + tag, value[0:1], row)
    return row


def sweep(t, shape, first_tag, region, coef, load, store, rows):
    tags, _, cols, _ = shape
    low, high = t + 1, cols - t - 1
    chunk = -(-(high - low) // CHUNKS)
    column = lambda c: [load(c, k) for k in range(tags)]

    @pl.loop(0, CHUNKS)
    def _(i):
        start = jnp.minimum(low + i * chunk, high - chunk)
        west, mid = column(start - 1), column(start)
        for j in range(chunk):
            c = start + j
            east = column(c + 1)
            coefs = [coef[c, n] for n in range(6)]
            new = [advance(coefs, mid[k], east[k], west[k]) for k in range(tags)]
            for k in range(tags):
                store(c, k, new[k])
            rows[t, pl.ds(c, 1), :] = chosen(region[pl.ds(c, 1), :], first_tag, new)
            west, mid = mid, east


def loading(ref):
    return lambda c, tag: ref[c, tag]


def storing(ref):
    def store(c, tag, value):
        ref[c, tag] = value

    return store


def storing_rows(ref, tags, levels, pitch):
    def store(c, tag, value):
        for k in range(2):
            at = (k * tags + tag) * levels * pitch + c
            ref[pl.ds(at, levels, stride=pitch), :] = value[:, HALVES[k]]

    return store


def inner_kernel(place, lam, ew, ed, nw, nd, mf, top, region, *refs):
    coef, l0, l1, l2, l3, final, rows, lam_p, field_p = refs
    tags, levels, cols, lats = lam.shape
    pitch = cols + 1
    slab = levels * pitch

    @pl.loop(0, levels)
    def _(level):
        row = level * pitch
        for f, field in enumerate((ew, ed, nw, nd, mf)):
            for k in range(2):
                field_p[pl.ds((f * 2 + k) * slab + row, cols), :] = field[level, :, HALVES[k]]
        for tag in range(tags):
            for k in range(2):
                at = (k * tags + tag) * slab + row
                lam_p[pl.ds(at, cols), :] = lam[tag, level, :, HALVES[k]]

    def coefficients(c, west):
        ew, ed, nw, nd, mf = (
            column_at(field_p, f * 2 * slab + c, levels, pitch, slab) for f in range(5)
        )
        e, next_west, n, s = faces(ew, ed, nw, nd)
        u = updraft(mf, top[pl.ds(c, 1), :])
        for j, value in enumerate((1.0 - e - west - n - s, e, west, n, s, u)):
            coef[c, j] = value
        return next_west

    def some(i, west):
        for j in range(8):
            west = coefficients(i * 8 + j, west)
        return west

    west = lax.fori_loop(0, cols // 8, some, jnp.zeros((levels, lats), jnp.float32))
    coef[cols, 2] = west

    def given(c, tag):
        return column_at(lam_p, tag * slab + c, levels, pitch, tags * slab)

    for at, c in enumerate((0, 1, cols - 2, cols - 1)):
        for tag in range(tags):
            l0[at, tag] = given(c, tag)
    last = storing_rows(final, tags, levels, pitch)
    loads = (given, loading(l1), loading(l2), loading(l3))
    stores = (storing(l1), storing(l2), storing(l3), last)
    for t in range(ITERS):
        sweep(t, lam.shape, place[0] * tags, region, coef, loads[t], stores[t], rows)


def inner(place, lam, fields, top, region):
    tags, levels, cols, lats = lam.shape
    vmem = pl.BlockSpec(memory_space=pltpu.VMEM)
    state = pltpu.VMEM((cols, tags, levels, lats), jnp.float32)
    return pl.pallas_call(
        inner_kernel,
        in_specs=[pl.BlockSpec(memory_space=pltpu.SMEM)] + [vmem] * 8,
        out_specs=[vmem] * 7,
        out_shape=[
            pltpu.VMEM((cols + 1, 6, levels, lats), jnp.float32),
            pltpu.VMEM((4, tags, levels, lats), jnp.float32),
            *[state] * 3,
            pltpu.VMEM((pitched(2 * tags, levels, cols), LANES), jnp.float32),
            pltpu.VMEM((ITERS, cols, lats), jnp.float32),
        ],
        scratch_shapes=[
            pltpu.VMEM((pitched(2 * tags, levels, cols), LANES), jnp.float32),
            pltpu.VMEM((pitched(10, levels, cols), LANES), jnp.float32),
        ],
        compiler_params=pltpu.CompilerParams(vmem_limit_bytes=32 << 20),
        cost_estimate=SHORT,
        name="inner_steps",
    )(place, lam, *fields, top, region)


def slot(c, cols):
    return (LOW, c + EDGE - 1) if c < EDGE else (HIGH, c - (cols - EDGE))


def outer_kernel(parts, cols, place, coef, *refs):
    pieces, wide, entry = refs[:parts], refs[parts], refs[parts + 1]
    per = ENTRIES // parts
    mine = lax.rem(place[0], parts)
    odd = place[1]
    for by in range(parts):
        base = (mine ^ by) * per
        entry[1 - odd, pl.ds(base, per)] = pieces[by][0]
        entry[odd, pl.ds(base, per)] = pieces[by][1]

    def outside(c):
        if c < 0:
            at = 1 + 5 * (c + EDGE - 1)
            e, _, n, s, u = (entry[LOW, at + j] for j in range(5))
            w = entry[LOW, at - 4] if c > 1 - EDGE else entry[LOW, 0]
        else:
            at = 5 * (c - cols)
            e, _, n, s, u = (entry[HIGH, at + j] for j in range(5))
            w = entry[HIGH, at - 4] if c > cols else coef[cols, 2]
        return e, w, n, s, u

    first_west = entry[LOW, 1 + 5 * (EDGE - 2) + 1]
    for c in [*range(1 - EDGE, 1), *range(cols, cols + EDGE - 1)]:
        if c == 0:
            e, w, n, s, u = coef[0, 1], first_west, coef[0, 3], coef[0, 4], coef[0, 5]
        else:
            e, w, n, s, u = outside(c)
        for j, value in enumerate((1.0 - e - w - n - s, e, w, n, s, u)):
            wide[*slot(c, cols), j] = value


def outer_coefs(parts, cols, place, coef, pieces):
    _, _, levels, lats = coef.shape
    vmem = pl.BlockSpec(memory_space=pltpu.VMEM)
    return pl.pallas_call(
        functools.partial(outer_kernel, parts, cols),
        in_specs=[pl.BlockSpec(memory_space=pltpu.SMEM)] + [vmem] * (1 + parts),
        out_specs=vmem,
        out_shape=pltpu.VMEM((2, 2 * EDGE - 1, 6, levels, lats), jnp.float32),
        scratch_shapes=[pltpu.VMEM((2, ENTRIES, levels, lats), jnp.float32)],
        compiler_params=pltpu.CompilerParams(vmem_limit_bytes=24 << 20),
        cost_estimate=SHORT,
        name="outer_coefs",
    )(place, coef, *pieces)


def border_steps(depth, place, region, coef, wide, kept, l0, halos, halo, work, store, rows):
    cols, tags, levels, lats = kept[1].shape
    first_tag = place[0] * tags
    part = slice(0, depth)
    halo[1 - place[1]] = halos[0][:, part]
    halo[place[1]] = halos[1][:, part]

    def coefs_at(c):
        if 0 < c < cols:
            return [coef[c, j, part] for j in range(6)]
        return [wide[*slot(c, cols), j, part] for j in range(6)]

    def state(t, c, tag):
        if t == 0:
            if c < 0:
                return halo[LOW, tag * EDGE + c + EDGE]
            if c >= cols:
                return halo[HIGH, tag * EDGE + c - cols]
            return l0[c if c < 2 else c - (cols - 4), tag, part]
        if t <= c < cols - t:
            return kept[t][c, tag, part]
        return work[t, *slot(c, cols), tag]

    def column(t, c):
        return [state(t, c, tag) for tag in range(tags)]

    for t in range(ITERS):
        reach = EDGE - 1 - t
        for run in (range(-reach, t + 1), range(cols - t - 1, cols + reach)):
            west, mid = column(t, run[0] - 1), column(t, run[0])
            for c in run:
                east = column(t, c + 1)
                coefs = coefs_at(c)
                new = [advance(coefs, mid[k], east[k], west[k]) for k in range(tags)]
                for k in range(tags):
                    if t < ITERS - 1:
                        work[t + 1, *slot(c, cols), k] = new[k]
                    elif store is not None:
                        store(c, k, new[k])
                if rows is not None and 0 <= c < cols:
                    rows[t, c : c + 1, :] = chosen(region[c : c + 1, :], first_tag, new)
                west, mid = mid, east


def low_kernel(place, region, coef, wide, l0, l1, l2, l3, first, second, rows_in, grad, halo, work, rows):
    rows[...] = rows_in[...]
    kept = (None, l1, l2, l3)
    border_steps(
        8, place, region, coef, wide, kept, l0, (first, second), halo, work, None, rows
    )
    total = rows[0]
    for t in range(1, ITERS):
        total = total + rows[t]
    grad[...] = total


def border_scratch(tags, depth, lats):
    return [
        pltpu.VMEM((2, tags * EDGE, depth, lats), jnp.float32),
        pltpu.VMEM((ITERS, 2, 2 * EDGE - 1, tags, depth, lats), jnp.float32),
    ]


def gradient(place, region, coef, wide, states, halos, rows):
    cols, tags, levels, lats = states[1].shape
    vmem = pl.BlockSpec(memory_space=pltpu.VMEM)
    operands = [region, coef, wide, *states, *halos, rows]
    return pl.pallas_call(
        low_kernel,
        in_specs=[pl.BlockSpec(memory_space=pltpu.SMEM)] + [vmem] * len(operands),
        out_specs=vmem,
        out_shape=pltpu.VMEM((cols, lats), jnp.float32),
        scratch_shapes=[
            *border_scratch(tags, 8, lats),
            pltpu.VMEM((ITERS, cols, lats), jnp.float32),
        ],
        compiler_params=pltpu.CompilerParams(vmem_limit_bytes=32 << 20),
        cost_estimate=SHORT,
        name="border_low_levels",
    )(place, *operands)


def border_kernel(place, coef, wide, l0, l1, l2, l3, first, second, *refs):
    final_in, out_in, final, out, halo, work, sides, sems = refs
    cols, tags, levels, lats = l1.shape
    pitch = cols + 1
    store = storing_rows(final, tags, levels, pitch)
    kept = (None, l1, l2, l3)
    border_steps(
        levels, place, None, coef, wide, kept, l0, (first, second), halo, work, store, None
    )
    edges = (0, cols - 8)

    @pl.loop(0, levels)
    def _(level):
        for tag in range(tags):
            for k in range(2):
                at = ((k * tags + tag) * levels + level) * pitch
                for side, c in enumerate(edges):
                    sides[side, tag, level, :, HALVES[k]] = final[pl.ds(at + c, 8), :]

    copies = []
    for side, c in enumerate(edges):
        for tag in range(tags):
            copies.append(
                pltpu.make_async_copy(
                    sides.at[side, tag], out.at[tag, :, pl.ds(c, 8)], sems.at[len(copies)]
                )
            )
            copies[-1].start()
    for c in copies:
        c.wait()


def border(place, coef, wide, states, halos, final, out):
    cols, tags, levels, lats = states[1].shape
    vmem = pl.BlockSpec(memory_space=pltpu.VMEM)
    hbm = pl.BlockSpec(memory_space=pltpu.HBM)
    operands = [coef, wide, *states, *halos]
    n = len(operands) + 1
    return pl.pallas_call(
        border_kernel,
        in_specs=[pl.BlockSpec(memory_space=pltpu.SMEM)] + [vmem] * n + [hbm],
        out_specs=[vmem, hbm],
        out_shape=[
            pltpu.VMEM(final.shape, jnp.float32),
            pltpu.HBM(out.shape, jnp.float32),
        ],
        input_output_aliases={n: 0, n + 1: 1},
        scratch_shapes=[
            *border_scratch(tags, levels, lats),
            pltpu.VMEM((2, tags, levels, 8, lats), jnp.float32),
            pltpu.SemaphoreType.DMA((2 * tags,)),
        ],
        compiler_params=pltpu.CompilerParams(vmem_limit_bytes=32 << 20),
        cost_estimate=SHORT,
        name="border_all_levels",
    )(place, *operands, final, out)[1]


def write_kernel(final, out, block, sems):
    tags, levels, cols, _ = out.shape
    pitch = cols + 1
    copies = []
    for tag in range(tags):

        @pl.loop(0, levels)
        def _(level):
            for k in range(2):
                at = ((k * tags + tag) * levels + level) * pitch + 8
                block[tag, level, :, HALVES[k]] = final[pl.ds(at, cols - 16), :]

        copies.append(
            pltpu.make_async_copy(
                block.at[tag], out.at[tag, :, pl.ds(8, cols - 16)], sems.at[tag]
            )
        )
        copies[-1].start()
    for c in copies:
        c.wait()


def write_inner(final, shape):
    tags, levels, cols, lats = shape
    return pl.pallas_call(
        write_kernel,
        in_specs=[pl.BlockSpec(memory_space=pltpu.VMEM)],
        out_specs=pl.BlockSpec(memory_space=pltpu.HBM),
        out_shape=pltpu.HBM(shape, jnp.float32),
        scratch_shapes=[
            pltpu.VMEM((tags, levels, cols - 16, lats), jnp.float32),
            pltpu.SemaphoreType.DMA((tags,)),
        ],
        compiler_params=pltpu.CompilerParams(vmem_limit_bytes=24 << 20),
        cost_estimate=SHORT,
        name="write_inner",
    )(final)


def local(lam, east_wind, north_wind, east_diff, north_diff, mass_flux, region, top):
    groups, tiles = lax.axis_size("grp"), lax.axis_size("dom")
    parts = 4 if groups % 4 == 0 else 1
    grp, dom = lax.axis_index("grp"), lax.axis_index("dom")
    place = jnp.stack([grp, dom % 2]).astype(jnp.int32)
    own = (lam, east_wind, east_diff, north_wind, north_diff, mass_flux)
    far = [pltpu.with_memory_space_constraint(value, pltpu.HBM) for value in (*own, top)]

    pairs = lambda i: i ^ 1
    turn = lambda i: (((i - 1) % tiles ^ 1) + 1) % tiles
    coef_first, coef_second, first, second = pack(parts, place, far[0], far[1:6], far[6])
    coef_first = swapped(coef_first, "dom", pairs)
    coef_second = swapped(coef_second, "dom", turn)
    first = swapped(first, "dom", pairs)
    second = swapped(second, "dom", turn)
    pieces = [jnp.stack([coef_first, coef_second])]
    for by in range(1, parts):
        pieces.append(swapped(pieces[0], "grp", lambda i: i ^ by))
    coef, *states, final, rows = inner(place, own[0], own[1:], top, region)
    wide = outer_coefs(parts, lam.shape[2], place, coef, pieces)
    out = write_inner(final, lam.shape)
    wide, out = lax.optimization_barrier((wide, out))
    grad = gradient(place, region, coef, wide, states, (first, second), rows)
    grad, wide = lax.optimization_barrier((grad, wide))
    out = border(place, coef, wide, states, (first, second), final, out)
    share = grad
    for by in range(1, groups):
        grad = grad + swapped(share, "grp", lambda i: (i + by) % groups)
    return out, grad


def solution(mesh):
    return jax.shard_map(
        local,
        mesh=mesh,
        in_specs=(
            P("grp", None, "dom", None),
            P(None, "dom", None),
            P(None, "dom", None),
            P(None, "dom", None),
            P(None, "dom", None),
            P(None, "dom", None),
            P("dom", None),
            P("dom", None),
        ),
        out_specs=(P("grp", None, "dom", None), P("dom", None)),
        check_vma=False,
    )
```

```python
import functools

import jax
import jax.numpy as jnp
from jax import lax
from jax.experimental import pallas as pl
from jax.experimental.pallas import tpu as pltpu
from jax.sharding import PartitionSpec as P

ITERS = 4
EDGE = ITERS
ENTRIES = 16
CHUNKS = 2
LANES = 128
HALVES = (slice(0, LANES), slice(LANES, 2 * LANES))
SHORT = pl.CostEstimate(flops=1000, bytes_accessed=1000, transcendentals=0)
LOW, HIGH = 0, 1

def swapped(value, axis, partner):
    return lax.ppermute(value, axis, [(i, partner(i)) for i in range(lax.axis_size(axis))])


def faces(ew, ed, nw, nd):
    lats = ew.shape[1]
    lat = lax.broadcasted_iota(jnp.int32, ew.shape, 1)
    east = jnp.maximum(ew, 0.0) + ed
    west_next = jnp.maximum(-ew, 0.0) + ed
    north = jnp.where(lat < lats - 1, jnp.maximum(nw, 0.0) + nd, 0.0)
    south = jnp.maximum(-nw, 0.0) + nd
    south = jnp.where(lat > 0, pltpu.roll(south, 1, 1), 0.0)
    return east, west_next, north, south


def updraft(mf, top_row):
    levels = mf.shape[0]
    level = lax.broadcasted_iota(jnp.int32, mf.shape, 0)
    return jnp.where((level < top_row) & (level < levels - 1), mf, 0.0)


def level_above(h):
    if h.shape[0] == 8:
        return pltpu.roll(h, 7, 0)
    parts = [pltpu.roll(h[at : at + 8], 7, 0) for at in range(0, h.shape[0], 8)]
    inside = lax.broadcasted_iota(jnp.int32, parts[0].shape, 0) < 7
    joined = [jnp.where(inside, low, high) for low, high in zip(parts, parts[1:])]
    return jnp.concatenate([*joined, parts[-1]], axis=0)


def advance(coefs, mid, east, west):
    d, e, w, n, s, u = coefs
    h = d * mid + e * east + w * west
    lane = lax.broadcasted_iota(jnp.int32, (mid.shape[0], LANES), 1)
    north = [pltpu.roll(mid[:, part], LANES - 1, 1) for part in HALVES]
    south = [pltpu.roll(mid[:, part], 1, 1) for part in HALVES]
    north = jnp.concatenate([jnp.where(lane < LANES - 1, *north), north[1]], axis=1)
    south = jnp.concatenate([south[0], jnp.where(lane > 0, south[1], south[0])], axis=1)
    h = h + n * north + s * south
    return h + u * (level_above(h) - h)


def pitched(slabs, levels, width):
    return -(-(slabs * levels * (width + 1) + width + 8) // 8) * 8


def column_at(ref, start, levels, pitch, apart):
    parts = [ref[pl.ds(start + apart * k, levels, stride=pitch), :] for k in range(2)]
    return jnp.concatenate(parts, axis=1)


def pack_kernel(parts, place, lam, ew, ed, nw, nd, mf, top, *refs):
    coef_first, coef_second, lam_first, lam_second = refs[:4]
    field_s, top_s, lam_s, entry, field_p, lam_p, sems = refs[4:]
    tags, levels, cols, lats = lam.shape
    copies = []

    def copy(src, dst):
        copies.append(pltpu.make_async_copy(src, dst, sems.at[len(copies)]))
        copies[-1].start()

    for side, at in ((LOW, 0), (HIGH, cols - 8)):
        for f, field in enumerate((ew, ed, nw, nd, mf)):
            copy(field.at[:, pl.ds(at, 8)], field_s.at[f, side])
        copy(top.at[pl.ds(at, 8)], top_s.at[side])
    field_copies = len(copies)
    for side, at in ((LOW, 0), (HIGH, cols - 8)):
        for tag in range(tags):
            copy(lam.at[tag, :, pl.ds(at, 8)], lam_s.at[side, tag])
    for c in copies[:field_copies]:
        c.wait()
    pitch = 9
    slab = levels * pitch

    @pl.loop(0, levels)
    def _(level):
        row = level * pitch
        for f in range(5):
            for side in range(2):
                for k in range(2):
                    at = ((f * 2 + side) * 2 + k) * slab
                    field_p[pl.ds(at + row, 8), :] = field_s[f, side, level, :, HALVES[k]]

    def field(f, side, c):
        return column_at(field_p, (f * 2 + side) * 2 * slab + c, levels, pitch, slab)

    for side in (LOW, HIGH):
        slot = 0
        for c in range(EDGE - 1) if side == LOW else range(8 - EDGE, 8):
            east, west, north, south = faces(*(field(f, side, c) for f in range(4)))
            lift = updraft(field(4, side, c), top_s[side, pl.ds(c, 1), :])
            wanted = (east, west, north, south, lift)
            if side == HIGH and c == 8 - EDGE:
                wanted = (west,)
            for value in wanted:
                entry[side, slot] = value
                slot += 1
        for left in range(slot, ENTRIES):
            entry[side, left] = jnp.zeros((levels, lats), jnp.float32)
    per = ENTRIES // parts
    mine = lax.rem(place[0], parts) * per
    odd = place[1]
    coef_first[...] = entry[1 - odd, pl.ds(mine, per)]
    coef_second[...] = entry[odd, pl.ds(mine, per)]

    for c in copies[field_copies:]:
        c.wait()

    @pl.loop(0, levels)
    def _(level):
        row = level * pitch
        for side in range(2):
            for tag in range(tags):
                for k in range(2):
                    at = ((side * 2 + k) * tags + tag) * slab
                    lam_p[pl.ds(at + row, 8), :] = lam_s[side, tag, level, :, HALVES[k]]

    for dest, side in ((lam_first, 1 - odd), (lam_second, odd)):
        start = side * (2 * tags * slab + 8 - EDGE)
        for tag in range(tags):
            for c in range(EDGE):
                dest[tag * EDGE + c] = column_at(lam_p, start + tag * slab + c, levels, pitch, tags * slab)


def pack(parts, place, lam, fields, top):
    tags, levels, cols, lats = lam.shape
    hbm = pl.BlockSpec(memory_space=pltpu.HBM)
    send = lambda slabs: pltpu.VMEM((slabs, levels, lats), jnp.float32)
    few, many = ENTRIES // parts, tags * EDGE
    return pl.pallas_call(
        functools.partial(pack_kernel, parts),
        in_specs=[pl.BlockSpec(memory_space=pltpu.SMEM)] + [hbm] * 7,
        out_specs=[pl.BlockSpec(memory_space=pltpu.VMEM)] * 4,
        out_shape=[send(few), send(few), send(many), send(many)],
        scratch_shapes=[
            pltpu.VMEM((5, 2, levels, 8, lats), jnp.float32),
            pltpu.VMEM((2, 8, lats), jnp.int32),
            pltpu.VMEM((2, tags, levels, 8, lats), jnp.float32),
            pltpu.VMEM((2, ENTRIES, levels, lats), jnp.float32),
            pltpu.VMEM((pitched(20, levels, 8), LANES), jnp.float32),
            pltpu.VMEM((pitched(4 * tags, levels, 8), LANES), jnp.float32),
            pltpu.SemaphoreType.DMA((12 + 2 * tags,)),
        ],
        compiler_params=pltpu.CompilerParams(vmem_limit_bytes=24 << 20),
        cost_estimate=SHORT,
        name="pack_edges",
    )(place, lam, *fields, top)


def chosen(region_row, first_tag, values):
    row = jnp.zeros(region_row.shape, jnp.float32)
    for tag, value in enumerate(values):
        row = jnp.where(region_row == first_tag + tag, value[0:1], row)
    return row


def sweep(t, shape, first_tag, region, coef, load, store, rows):
    tags, _, cols, _ = shape
    low, high = t + 1, cols - t - 1
    chunk = -(-(high - low) // CHUNKS)
    column = lambda c: [load(c, k) for k in range(tags)]

    @pl.loop(0, CHUNKS)
    def _(i):
        start = jnp.minimum(low + i * chunk, high - chunk)
        west, mid = column(start - 1), column(start)
        for j in range(chunk):
            c = start + j
            east = column(c + 1)
            coefs = [coef[c, n] for n in range(6)]
            new = [advance(coefs, mid[k], east[k], west[k]) for k in range(tags)]
            for k in range(tags):
                store(c, k, new[k])
            rows[t, pl.ds(c, 1), :] = chosen(region[pl.ds(c, 1), :], first_tag, new)
            west, mid = mid, east


def loading(ref):
    return lambda c, tag: ref[c, tag]


def storing(ref):
    def store(c, tag, value):
        ref[c, tag] = value

    return store


def storing_rows(ref, tags, levels, pitch):
    def store(c, tag, value):
        for k in range(2):
            at = (k * tags + tag) * levels * pitch + c
            ref[pl.ds(at, levels, stride=pitch), :] = value[:, HALVES[k]]

    return store


def inner_kernel(place, lam, ew, ed, nw, nd, mf, top, region, *refs):
    coef, l0, l1, l2, l3, final, rows, lam_p, field_p = refs
    tags, levels, cols, lats = lam.shape
    pitch = cols + 1
    slab = levels * pitch

    @pl.loop(0, levels)
    def _(level):
        row = level * pitch
        for f, field in enumerate((ew, ed, nw, nd, mf)):
            for k in range(2):
                field_p[pl.ds((f * 2 + k) * slab + row, cols), :] = field[level, :, HALVES[k]]
        for tag in range(tags):
            for k in range(2):
                at = (k * tags + tag) * slab + row
                lam_p[pl.ds(at, cols), :] = lam[tag, level, :, HALVES[k]]

    def coefficients(c, west):
        ew, ed, nw, nd, mf = (
            column_at(field_p, f * 2 * slab + c, levels, pitch, slab) for f in range(5)
        )
        e, next_west, n, s = faces(ew, ed, nw, nd)
        u = updraft(mf, top[pl.ds(c, 1), :])
        for j, value in enumerate((1.0 - e - west - n - s, e, west, n, s, u)):
            coef[c, j] = value
        return next_west

    def some(i, west):
        for j in range(8):
            west = coefficients(i * 8 + j, west)
        return west

    west = lax.fori_loop(0, cols // 8, some, jnp.zeros((levels, lats), jnp.float32))
    coef[cols, 2] = west

    def given(c, tag):
        return column_at(lam_p, tag * slab + c, levels, pitch, tags * slab)

    for at, c in enumerate((0, 1, cols - 2, cols - 1)):
        for tag in range(tags):
            l0[at, tag] = given(c, tag)
    last = storing_rows(final, tags, levels, pitch)
    loads = (given, loading(l1), loading(l2), loading(l3))
    stores = (storing(l1), storing(l2), storing(l3), last)
    for t in range(ITERS):
        sweep(t, lam.shape, place[0] * tags, region, coef, loads[t], stores[t], rows)


def inner(place, lam, fields, top, region):
    tags, levels, cols, lats = lam.shape
    vmem = pl.BlockSpec(memory_space=pltpu.VMEM)
    state = pltpu.VMEM((cols, tags, levels, lats), jnp.float32)
    return pl.pallas_call(
        inner_kernel,
        in_specs=[pl.BlockSpec(memory_space=pltpu.SMEM)] + [vmem] * 8,
        out_specs=[vmem] * 7,
        out_shape=[
            pltpu.VMEM((cols + 1, 6, levels, lats), jnp.float32),
            pltpu.VMEM((4, tags, levels, lats), jnp.float32),
            *[state] * 3,
            pltpu.VMEM((pitched(2 * tags, levels, cols), LANES), jnp.float32),
            pltpu.VMEM((ITERS, cols, lats), jnp.float32),
        ],
        scratch_shapes=[
            pltpu.VMEM((pitched(2 * tags, levels, cols), LANES), jnp.float32),
            pltpu.VMEM((pitched(10, levels, cols), LANES), jnp.float32),
        ],
        compiler_params=pltpu.CompilerParams(vmem_limit_bytes=32 << 20),
        cost_estimate=SHORT,
        name="inner_steps",
    )(place, lam, *fields, top, region)


def slot(c, cols):
    return (LOW, c + EDGE - 1) if c < EDGE else (HIGH, c - (cols - EDGE))


def outer_kernel(parts, cols, place, coef, *refs):
    pieces, wide, entry = refs[:parts], refs[parts], refs[parts + 1]
    per = ENTRIES // parts
    mine = lax.rem(place[0], parts)
    odd = place[1]
    for by in range(parts):
        base = (mine ^ by) * per
        entry[1 - odd, pl.ds(base, per)] = pieces[by][0]
        entry[odd, pl.ds(base, per)] = pieces[by][1]

    def outside(c):
        if c < 0:
            at = 1 + 5 * (c + EDGE - 1)
            e, _, n, s, u = (entry[LOW, at + j] for j in range(5))
            w = entry[LOW, at - 4] if c > 1 - EDGE else entry[LOW, 0]
        else:
            at = 5 * (c - cols)
            e, _, n, s, u = (entry[HIGH, at + j] for j in range(5))
            w = entry[HIGH, at - 4] if c > cols else coef[cols, 2]
        return e, w, n, s, u

    first_west = entry[LOW, 1 + 5 * (EDGE - 2) + 1]
    for c in [*range(1 - EDGE, 1), *range(cols, cols + EDGE - 1)]:
        if c == 0:
            e, w, n, s, u = coef[0, 1], first_west, coef[0, 3], coef[0, 4], coef[0, 5]
        else:
            e, w, n, s, u = outside(c)
        for j, value in enumerate((1.0 - e - w - n - s, e, w, n, s, u)):
            wide[*slot(c, cols), j] = value


def outer_coefs(parts, cols, place, coef, pieces):
    _, _, levels, lats = coef.shape
    vmem = pl.BlockSpec(memory_space=pltpu.VMEM)
    return pl.pallas_call(
        functools.partial(outer_kernel, parts, cols),
        in_specs=[pl.BlockSpec(memory_space=pltpu.SMEM)] + [vmem] * (1 + parts),
        out_specs=vmem,
        out_shape=pltpu.VMEM((2, 2 * EDGE - 1, 6, levels, lats), jnp.float32),
        scratch_shapes=[pltpu.VMEM((2, ENTRIES, levels, lats), jnp.float32)],
        compiler_params=pltpu.CompilerParams(vmem_limit_bytes=24 << 20),
        cost_estimate=SHORT,
        name="outer_coefs",
    )(place, coef, *pieces)


def border_steps(
    depth, place, region, coef, wide, kept, l0, halos, halo, work, rows=None, store=None, finish=None
):
    cols, tags, levels, lats = kept[1].shape
    first_tag = place[0] * tags
    part = slice(0, depth)
    halo[1 - place[1]] = halos[0][:, part]
    halo[place[1]] = halos[1][:, part]

    def coefs_at(c):
        if 0 < c < cols:
            return [coef[c, j, part] for j in range(6)]
        return [wide[*slot(c, cols), j, part] for j in range(6)]

    def state(t, c, tag):
        if t == 0:
            if c < 0:
                return halo[LOW, tag * EDGE + c + EDGE]
            if c >= cols:
                return halo[HIGH, tag * EDGE + c - cols]
            return l0[c if c < 2 else c - (cols - 4), tag, part]
        if t <= c < cols - t:
            return kept[t][c, tag, part]
        return work[t, *slot(c, cols), tag]

    def column(t, c):
        return [state(t, c, tag) for tag in range(tags)]

    for t in range(ITERS if store is None else ITERS - 1):
        reach = EDGE - 1 - t
        for run in (range(-reach, t + 1), range(cols - t - 1, cols + reach)):
            west, mid = column(t, run[0] - 1), column(t, run[0])
            for c in run:
                east = column(t, c + 1)
                coefs = coefs_at(c)
                new = [advance(coefs, mid[k], east[k], west[k]) for k in range(tags)]
                if t < ITERS - 1:
                    for k in range(tags):
                        work[t + 1, *slot(c, cols), k] = new[k]
                if rows is not None and 0 <= c < cols:
                    rows[t, c : c + 1, :] = chosen(region[c : c + 1, :], first_tag, new)
                west, mid = mid, east
    if store is None:
        return
    t = ITERS - 1
    for k in range(tags):
        for c in [*range(EDGE), *range(cols - EDGE, cols)]:
            near = [state(t, at, k) for at in (c, c + 1, c - 1)]
            store(c, k, advance(coefs_at(c), *near))
        finish(k)


def low_kernel(place, region, coef, wide, l0, l1, l2, l3, first, second, rows_in, grad, halo, work, rows):
    rows[...] = rows_in[...]
    kept = (None, l1, l2, l3)
    border_steps(8, place, region, coef, wide, kept, l0, (first, second), halo, work, rows)
    total = rows[0]
    for t in range(1, ITERS):
        total = total + rows[t]
    grad[...] = total


def border_scratch(tags, depth, lats):
    return [
        pltpu.VMEM((2, tags * EDGE, depth, lats), jnp.float32),
        pltpu.VMEM((ITERS, 2, 2 * EDGE - 1, tags, depth, lats), jnp.float32),
    ]


def gradient(place, region, coef, wide, states, halos, rows):
    cols, tags, levels, lats = states[1].shape
    vmem = pl.BlockSpec(memory_space=pltpu.VMEM)
    operands = [region, coef, wide, *states, *halos, rows]
    return pl.pallas_call(
        low_kernel,
        in_specs=[pl.BlockSpec(memory_space=pltpu.SMEM)] + [vmem] * len(operands),
        out_specs=vmem,
        out_shape=pltpu.VMEM((cols, lats), jnp.float32),
        scratch_shapes=[
            *border_scratch(tags, 8, lats),
            pltpu.VMEM((ITERS, cols, lats), jnp.float32),
        ],
        compiler_params=pltpu.CompilerParams(vmem_limit_bytes=32 << 20),
        cost_estimate=SHORT,
        name="border_low_levels",
    )(place, *operands)


def border_kernel(place, coef, wide, l0, l1, l2, l3, first, second, *refs):
    final_in, out_in, final, out, halo, work, sides, sems = refs
    cols, tags, levels, lats = l1.shape
    pitch = cols + 1
    store = storing_rows(final, tags, levels, pitch)
    kept = (None, l1, l2, l3)
    copies = []

    def finish(tag):
        @pl.loop(0, levels // 8)
        def _(i):
            for j in range(8):
                level = i * 8 + j
                for k in range(2):
                    at = ((k * tags + tag) * levels + level) * pitch
                    for side, c in enumerate((0, cols - 8)):
                        sides[side, tag, level, :, HALVES[k]] = final[pl.ds(at + c, 8), :]

        for side, c in enumerate((0, cols - 8)):
            copies.append(
                pltpu.make_async_copy(
                    sides.at[side, tag], out.at[tag, :, pl.ds(c, 8)], sems.at[len(copies)]
                )
            )
            copies[-1].start()

    border_steps(
        levels, place, None, coef, wide, kept, l0, (first, second), halo, work, None, store, finish
    )
    for c in copies:
        c.wait()


def border(place, coef, wide, states, halos, final, out):
    cols, tags, levels, lats = states[1].shape
    vmem = pl.BlockSpec(memory_space=pltpu.VMEM)
    hbm = pl.BlockSpec(memory_space=pltpu.HBM)
    operands = [coef, wide, *states, *halos]
    n = len(operands) + 1
    return pl.pallas_call(
        border_kernel,
        in_specs=[pl.BlockSpec(memory_space=pltpu.SMEM)] + [vmem] * n + [hbm],
        out_specs=[vmem, hbm],
        out_shape=[
            pltpu.VMEM(final.shape, jnp.float32),
            pltpu.HBM(out.shape, jnp.float32),
        ],
        input_output_aliases={n: 0, n + 1: 1},
        scratch_shapes=[
            *border_scratch(tags, levels, lats),
            pltpu.VMEM((2, tags, levels, 8, lats), jnp.float32),
            pltpu.SemaphoreType.DMA((2 * tags,)),
        ],
        compiler_params=pltpu.CompilerParams(vmem_limit_bytes=32 << 20),
        cost_estimate=SHORT,
        name="border_all_levels",
    )(place, *operands, final, out)[1]


def write_kernel(final, out, block, sems):
    tags, levels, cols, _ = out.shape
    pitch = cols + 1
    copies = []
    for tag in range(tags):

        @pl.loop(0, levels)
        def _(level):
            for k in range(2):
                at = ((k * tags + tag) * levels + level) * pitch + 8
                block[tag, level, :, HALVES[k]] = final[pl.ds(at, cols - 16), :]

        copies.append(
            pltpu.make_async_copy(
                block.at[tag], out.at[tag, :, pl.ds(8, cols - 16)], sems.at[tag]
            )
        )
        copies[-1].start()
    for c in copies:
        c.wait()


def write_inner(final, shape):
    tags, levels, cols, lats = shape
    return pl.pallas_call(
        write_kernel,
        in_specs=[pl.BlockSpec(memory_space=pltpu.VMEM)],
        out_specs=pl.BlockSpec(memory_space=pltpu.HBM),
        out_shape=pltpu.HBM(shape, jnp.float32),
        scratch_shapes=[
            pltpu.VMEM((tags, levels, cols - 16, lats), jnp.float32),
            pltpu.SemaphoreType.DMA((tags,)),
        ],
        compiler_params=pltpu.CompilerParams(vmem_limit_bytes=24 << 20),
        cost_estimate=SHORT,
        name="write_inner",
    )(final)


def local(lam, east_wind, north_wind, east_diff, north_diff, mass_flux, region, top):
    groups, tiles = lax.axis_size("grp"), lax.axis_size("dom")
    parts = 4 if groups % 4 == 0 else 1
    grp, dom = lax.axis_index("grp"), lax.axis_index("dom")
    place = jnp.stack([grp, dom % 2]).astype(jnp.int32)
    own = (lam, east_wind, east_diff, north_wind, north_diff, mass_flux)
    far = [pltpu.with_memory_space_constraint(value, pltpu.HBM) for value in (*own, top)]

    pairs = lambda i: i ^ 1
    turn = lambda i: (((i - 1) % tiles ^ 1) + 1) % tiles
    coef_first, coef_second, first, second = pack(parts, place, far[0], far[1:6], far[6])
    coef_first = swapped(coef_first, "dom", pairs)
    coef_second = swapped(coef_second, "dom", turn)
    first = swapped(first, "dom", pairs)
    second = swapped(second, "dom", turn)
    pieces = [jnp.stack([coef_first, coef_second])]
    for by in range(1, parts):
        pieces.append(swapped(pieces[0], "grp", lambda i: i ^ by))
    coef, *states, final, rows = inner(place, own[0], own[1:], top, region)
    wide = outer_coefs(parts, lam.shape[2], place, coef, pieces)
    out = write_inner(final, lam.shape)
    wide, out = lax.optimization_barrier((wide, out))
    grad = gradient(place, region, coef, wide, states, (first, second), rows)
    grad, wide = lax.optimization_barrier((grad, wide))
    out = border(place, coef, wide, states, (first, second), final, out)
    share = grad
    for by in range(1, groups):
        grad = grad + swapped(share, "grp", lambda i: i ^ by)
    return out, grad


def solution(mesh):
    return jax.shard_map(
        local,
        mesh=mesh,
        in_specs=(
            P("grp", None, "dom", None),
            P(None, "dom", None),
            P(None, "dom", None),
            P(None, "dom", None),
            P(None, "dom", None),
            P(None, "dom", None),
            P("dom", None),
            P("dom", None),
        ),
        out_specs=(P("grp", None, "dom", None), P("dom", None)),
        check_vma=False,
    )
```

```python
import functools

import jax
import jax.numpy as jnp
from jax import lax
from jax.experimental import pallas as pl
from jax.experimental.pallas import tpu as pltpu
from jax.sharding import PartitionSpec as P

ITERS = 4
EDGE = ITERS
ENTRIES = 16
CHUNKS = 2
LANES = 128
HALVES = (slice(0, LANES), slice(LANES, 2 * LANES))
SHORT = pl.CostEstimate(flops=1000, bytes_accessed=1000, transcendentals=0)
LOW, HIGH = 0, 1

def swapped(value, axis, partner):
    return lax.ppermute(value, axis, [(i, partner(i)) for i in range(lax.axis_size(axis))])


def faces(ew, ed, nw, nd):
    lats = ew.shape[1]
    lat = lax.broadcasted_iota(jnp.int32, ew.shape, 1)
    east = jnp.maximum(ew, 0.0) + ed
    west_next = jnp.maximum(-ew, 0.0) + ed
    north = jnp.where(lat < lats - 1, jnp.maximum(nw, 0.0) + nd, 0.0)
    south = jnp.maximum(-nw, 0.0) + nd
    south = jnp.where(lat > 0, pltpu.roll(south, 1, 1), 0.0)
    return east, west_next, north, south


def updraft(mf, top_row):
    levels = mf.shape[0]
    level = lax.broadcasted_iota(jnp.int32, mf.shape, 0)
    return jnp.where((level < top_row) & (level < levels - 1), mf, 0.0)


def level_above(h):
    if h.shape[0] == 8:
        return pltpu.roll(h, 7, 0)
    parts = [pltpu.roll(h[at : at + 8], 7, 0) for at in range(0, h.shape[0], 8)]
    inside = lax.broadcasted_iota(jnp.int32, parts[0].shape, 0) < 7
    joined = [jnp.where(inside, low, high) for low, high in zip(parts, parts[1:])]
    return jnp.concatenate([*joined, parts[-1]], axis=0)


def advance(coefs, mid, east, west):
    d, e, w, n, s, u = coefs
    h = d * mid + e * east + w * west
    lane = lax.broadcasted_iota(jnp.int32, (mid.shape[0], LANES), 1)
    north = [pltpu.roll(mid[:, part], LANES - 1, 1) for part in HALVES]
    south = [pltpu.roll(mid[:, part], 1, 1) for part in HALVES]
    north = jnp.concatenate([jnp.where(lane < LANES - 1, *north), north[1]], axis=1)
    south = jnp.concatenate([south[0], jnp.where(lane > 0, south[1], south[0])], axis=1)
    h = h + n * north + s * south
    return h + u * (level_above(h) - h)


def pitched(slabs, levels, width):
    return -(-(slabs * levels * (width + 1) + width + 8) // 8) * 8


def column_at(ref, start, levels, pitch, apart):
    parts = [ref[pl.ds(start + apart * k, levels, stride=pitch), :] for k in range(2)]
    return jnp.concatenate(parts, axis=1)


def pack_kernel(parts, place, lam, ew, ed, nw, nd, mf, top, *refs):
    coef_first, coef_second, lam_first, lam_second = refs[:4]
    field_s, top_s, lam_s, coef_p, lam_p, sems = refs[4:]
    tags, levels, cols, lats = lam.shape
    per = levels // parts
    base = lax.rem(place[0], parts) * per
    copies = []

    def copy(src, dst):
        copies.append(pltpu.make_async_copy(src, dst, sems.at[len(copies)]))
        copies[-1].start()

    for side, at in ((LOW, 0), (HIGH, cols - 8)):
        for f, field in enumerate((ew, ed, nw, nd, mf)):
            copy(field.at[pl.ds(base, per), pl.ds(at, 8)], field_s.at[f, side])
        copy(top.at[pl.ds(at, 8)], top_s.at[side])
    for side, at in ((LOW, 0), (HIGH, cols - 8)):
        for tag in range(tags):
            copy(lam.at[tag, :, pl.ds(at, 8)], lam_s.at[side, tag])
    for c in copies[:12]:
        c.wait()
    pitch = 9
    few = per * pitch

    @pl.loop(0, per)
    def _(i):
        level = base + i
        for side in (LOW, HIGH):
            ew, ed, nw, nd, mf = (field_s[f, side, i] for f in range(5))
            lift = jnp.where((level < top_s[side]) & (level < levels - 1), mf, 0.0)
            for j, value in enumerate((*faces(ew, ed, nw, nd), lift)):
                for k in range(2):
                    at = ((j * 2 + side) * 2 + k) * few + i * pitch
                    coef_p[pl.ds(at, 8), :] = value[:, HALVES[k]]

    odd = place[1]
    start = 8 - EDGE
    for dest, side in ((coef_first, 1 - odd), (coef_second, odd)):

        def column(j, c):
            return column_at(coef_p, (j * 2 + side) * 2 * few + c, per, pitch, few)

        c = side * (start + 1)
        dest[0] = column(1, jnp.maximum(c - 1, 0))
        for i in range(EDGE - 1):
            for n, j in enumerate((0, 2, 3, 4, 1)):
                dest[5 * i + 1 + n] = column(j, c + i)

    for c in copies[12:]:
        c.wait()
    slab = levels * pitch

    @pl.loop(0, levels)
    def _(level):
        for side in (LOW, HIGH):
            for tag in range(tags):
                for k in range(2):
                    at = ((side * 2 + k) * tags + tag) * slab + level * pitch
                    lam_p[pl.ds(at, 8), :] = lam_s[side, tag, level, :, HALVES[k]]

    for dest, side in ((lam_first, 1 - odd), (lam_second, odd)):
        at = side * (2 * tags * slab + start)
        for tag in range(tags):
            for c in range(EDGE):
                dest[tag * EDGE + c] = column_at(
                    lam_p, at + tag * slab + c, levels, pitch, tags * slab
                )


def pack(parts, place, lam, fields, top):
    tags, levels, cols, lats = lam.shape
    per = levels // parts
    hbm = pl.BlockSpec(memory_space=pltpu.HBM)
    coef_send = pltpu.VMEM((ENTRIES, per, lats), jnp.float32)
    lam_send = pltpu.VMEM((tags * EDGE, levels, lats), jnp.float32)
    return pl.pallas_call(
        functools.partial(pack_kernel, parts),
        in_specs=[pl.BlockSpec(memory_space=pltpu.SMEM)] + [hbm] * 7,
        out_specs=[pl.BlockSpec(memory_space=pltpu.VMEM)] * 4,
        out_shape=[coef_send, coef_send, lam_send, lam_send],
        scratch_shapes=[
            pltpu.VMEM((5, 2, per, 8, lats), jnp.float32),
            pltpu.VMEM((2, 8, lats), jnp.int32),
            pltpu.VMEM((2, tags, levels, 8, lats), jnp.float32),
            pltpu.VMEM((pitched(20, per, 8), LANES), jnp.float32),
            pltpu.VMEM((pitched(4 * tags, levels, 8), LANES), jnp.float32),
            pltpu.SemaphoreType.DMA((12 + 2 * tags,)),
        ],
        compiler_params=pltpu.CompilerParams(vmem_limit_bytes=24 << 20),
        cost_estimate=SHORT,
        name="pack_edges",
    )(place, lam, *fields, top)


def chosen(region_row, first_tag, values):
    row = jnp.zeros(region_row.shape, jnp.float32)
    for tag, value in enumerate(values):
        row = jnp.where(region_row == first_tag + tag, value[0:1], row)
    return row


def sweep(t, shape, first_tag, region, coef, load, store, rows):
    tags, _, cols, _ = shape
    low, high = t + 1, cols - t - 1
    chunk = -(-(high - low) // CHUNKS)
    column = lambda c: [load(c, k) for k in range(tags)]

    @pl.loop(0, CHUNKS)
    def _(i):
        start = jnp.minimum(low + i * chunk, high - chunk)
        west, mid = column(start - 1), column(start)
        for j in range(chunk):
            c = start + j
            east = column(c + 1)
            coefs = [coef[c, n] for n in range(6)]
            new = [advance(coefs, mid[k], east[k], west[k]) for k in range(tags)]
            for k in range(tags):
                store(c, k, new[k])
            rows[t, pl.ds(c, 1), :] = chosen(region[pl.ds(c, 1), :], first_tag, new)
            west, mid = mid, east


def loading(ref):
    return lambda c, tag: ref[c, tag]


def storing(ref):
    def store(c, tag, value):
        ref[c, tag] = value

    return store


def storing_rows(ref, tags, levels, pitch):
    def store(c, tag, value):
        for k in range(2):
            at = (k * tags + tag) * levels * pitch + c
            ref[pl.ds(at, levels, stride=pitch), :] = value[:, HALVES[k]]

    return store


def inner_kernel(place, lam, ew, ed, nw, nd, mf, top, region, *refs):
    coef, l0, l1, l2, l3, final, rows, lam_p, field_p = refs
    tags, levels, cols, lats = lam.shape
    pitch = cols + 1
    slab = levels * pitch

    @pl.loop(0, levels)
    def _(level):
        row = level * pitch
        for f, field in enumerate((ew, ed, nw, nd, mf)):
            for k in range(2):
                field_p[pl.ds((f * 2 + k) * slab + row, cols), :] = field[level, :, HALVES[k]]
        for tag in range(tags):
            for k in range(2):
                at = (k * tags + tag) * slab + row
                lam_p[pl.ds(at, cols), :] = lam[tag, level, :, HALVES[k]]

    def coefficients(c, west):
        ew, ed, nw, nd, mf = (
            column_at(field_p, f * 2 * slab + c, levels, pitch, slab) for f in range(5)
        )
        e, next_west, n, s = faces(ew, ed, nw, nd)
        u = updraft(mf, top[pl.ds(c, 1), :])
        for j, value in enumerate((1.0 - e - west - n - s, e, west, n, s, u)):
            coef[c, j] = value
        return next_west

    def some(i, west):
        for j in range(8):
            west = coefficients(i * 8 + j, west)
        return west

    west = lax.fori_loop(0, cols // 8, some, jnp.zeros((levels, lats), jnp.float32))
    coef[cols, 2] = west

    def given(c, tag):
        return column_at(lam_p, tag * slab + c, levels, pitch, tags * slab)

    for at, c in enumerate((0, 1, cols - 2, cols - 1)):
        for tag in range(tags):
            l0[at, tag] = given(c, tag)
    last = storing_rows(final, tags, levels, pitch)
    loads = (given, loading(l1), loading(l2), loading(l3))
    stores = (storing(l1), storing(l2), storing(l3), last)
    for t in range(ITERS):
        sweep(t, lam.shape, place[0] * tags, region, coef, loads[t], stores[t], rows)


def inner(place, lam, fields, top, region):
    tags, levels, cols, lats = lam.shape
    vmem = pl.BlockSpec(memory_space=pltpu.VMEM)
    state = pltpu.VMEM((cols, tags, levels, lats), jnp.float32)
    return pl.pallas_call(
        inner_kernel,
        in_specs=[pl.BlockSpec(memory_space=pltpu.SMEM)] + [vmem] * 8,
        out_specs=[vmem] * 7,
        out_shape=[
            pltpu.VMEM((cols + 1, 6, levels, lats), jnp.float32),
            pltpu.VMEM((4, tags, levels, lats), jnp.float32),
            *[state] * 3,
            pltpu.VMEM((pitched(2 * tags, levels, cols), LANES), jnp.float32),
            pltpu.VMEM((ITERS, cols, lats), jnp.float32),
        ],
        scratch_shapes=[
            pltpu.VMEM((pitched(2 * tags, levels, cols), LANES), jnp.float32),
            pltpu.VMEM((pitched(10, levels, cols), LANES), jnp.float32),
        ],
        compiler_params=pltpu.CompilerParams(vmem_limit_bytes=32 << 20),
        cost_estimate=SHORT,
        name="inner_steps",
    )(place, lam, *fields, top, region)


def slot(c, cols):
    return (LOW, c + EDGE - 1) if c < EDGE else (HIGH, c - (cols - EDGE))


def outer_kernel(parts, cols, place, coef, *refs):
    pieces, wide, entry = refs[:parts], refs[parts], refs[parts + 1]
    levels = coef.shape[2]
    per = levels // parts
    mine = lax.rem(place[0], parts)
    odd = place[1]
    for by in range(parts):
        for half, side in enumerate((1 - odd, odd)):

            @pl.loop(0, ENTRIES // 4)
            def _(i):
                for j in range(4):
                    e = i * 4 + j
                    for k in range(2):
                        at = ((side * ENTRIES + e) * 2 + k) * levels + (mine ^ by) * per
                        entry[pl.ds(at, per), :] = pieces[by][half, e, :, HALVES[k]]

    def slab(side, e):
        at = (side * ENTRIES + e) * 2 * levels
        return jnp.concatenate([entry[at + k * levels : at + (k + 1) * levels] for k in (0, 1)], 1)

    for side in (LOW, HIGH):
        for i in range(EDGE - 1):
            w, e, n, s, u = (slab(side, 5 * i + j) for j in range(5))
            if side == HIGH and i == 0:
                w = coef[cols, 2]
            for j, value in enumerate((1.0 - e - w - n - s, e, w, n, s, u)):
                wide[side, i + EDGE * side, j] = value
    first_west = slab(LOW, ENTRIES - 1)
    e, n, s, u = (coef[0, j] for j in (1, 3, 4, 5))
    for j, value in enumerate((1.0 - e - first_west - n - s, e, first_west, n, s, u)):
        wide[*slot(0, cols), j] = value


def outer_coefs(parts, cols, place, coef, pieces):
    _, _, levels, lats = coef.shape
    vmem = pl.BlockSpec(memory_space=pltpu.VMEM)
    return pl.pallas_call(
        functools.partial(outer_kernel, parts, cols),
        in_specs=[pl.BlockSpec(memory_space=pltpu.SMEM)] + [vmem] * (1 + parts),
        out_specs=vmem,
        out_shape=pltpu.VMEM((2, 2 * EDGE - 1, 6, levels, lats), jnp.float32),
        scratch_shapes=[pltpu.VMEM((2 * ENTRIES * 2 * levels, LANES), jnp.float32)],
        compiler_params=pltpu.CompilerParams(vmem_limit_bytes=24 << 20),
        cost_estimate=SHORT,
        name="outer_coefs",
    )(place, coef, *pieces)


def border_steps(
    depth, place, region, coef, wide, kept, l0, halos, halo, work, rows=None, store=None, finish=None
):
    cols, tags, levels, lats = kept[1].shape
    first_tag = place[0] * tags
    part = slice(0, depth)
    halo[1 - place[1]] = halos[0][:, part]
    halo[place[1]] = halos[1][:, part]

    def coefs_at(c):
        if 0 < c < cols:
            return [coef[c, j, part] for j in range(6)]
        return [wide[*slot(c, cols), j, part] for j in range(6)]

    def state(t, c, tag):
        if t == 0:
            if c < 0:
                return halo[LOW, tag * EDGE + c + EDGE]
            if c >= cols:
                return halo[HIGH, tag * EDGE + c - cols]
            return l0[c if c < 2 else c - (cols - 4), tag, part]
        if t <= c < cols - t:
            return kept[t][c, tag, part]
        return work[t, *slot(c, cols), tag]

    def column(t, c):
        return [state(t, c, tag) for tag in range(tags)]

    for t in range(ITERS if store is None else ITERS - 1):
        reach = EDGE - 1 - t
        for run in (range(-reach, t + 1), range(cols - t - 1, cols + reach)):
            west, mid = column(t, run[0] - 1), column(t, run[0])
            for c in run:
                east = column(t, c + 1)
                coefs = coefs_at(c)
                new = [advance(coefs, mid[k], east[k], west[k]) for k in range(tags)]
                if t < ITERS - 1:
                    for k in range(tags):
                        work[t + 1, *slot(c, cols), k] = new[k]
                if rows is not None and 0 <= c < cols:
                    rows[t, c : c + 1, :] = chosen(region[c : c + 1, :], first_tag, new)
                west, mid = mid, east
    if store is None:
        return
    t = ITERS - 1
    for k in range(tags):
        for c in [*range(EDGE), *range(cols - EDGE, cols)]:
            near = [state(t, at, k) for at in (c, c + 1, c - 1)]
            store(c, k, advance(coefs_at(c), *near))
        finish(k)


def low_kernel(place, region, coef, wide, l0, l1, l2, l3, first, second, rows_in, grad, halo, work, rows):
    rows[...] = rows_in[...]
    kept = (None, l1, l2, l3)
    border_steps(8, place, region, coef, wide, kept, l0, (first, second), halo, work, rows)
    total = rows[0]
    for t in range(1, ITERS):
        total = total + rows[t]
    grad[...] = total


def border_scratch(tags, depth, lats):
    return [
        pltpu.VMEM((2, tags * EDGE, depth, lats), jnp.float32),
        pltpu.VMEM((ITERS, 2, 2 * EDGE - 1, tags, depth, lats), jnp.float32),
    ]


def gradient(place, region, coef, wide, states, halos, rows):
    cols, tags, levels, lats = states[1].shape
    vmem = pl.BlockSpec(memory_space=pltpu.VMEM)
    operands = [region, coef, wide, *states, *halos, rows]
    return pl.pallas_call(
        low_kernel,
        in_specs=[pl.BlockSpec(memory_space=pltpu.SMEM)] + [vmem] * len(operands),
        out_specs=vmem,
        out_shape=pltpu.VMEM((cols, lats), jnp.float32),
        scratch_shapes=[
            *border_scratch(tags, 8, lats),
            pltpu.VMEM((ITERS, cols, lats), jnp.float32),
        ],
        compiler_params=pltpu.CompilerParams(vmem_limit_bytes=32 << 20),
        cost_estimate=SHORT,
        name="border_low_levels",
    )(place, *operands)


def border_kernel(place, coef, wide, l0, l1, l2, l3, first, second, *refs):
    final_in, out_in, final, out, halo, work, sides, sems = refs
    cols, tags, levels, lats = l1.shape
    pitch = cols + 1
    store = storing_rows(final, tags, levels, pitch)
    kept = (None, l1, l2, l3)
    copies = []

    def finish(tag):
        @pl.loop(0, levels // 8)
        def _(i):
            for j in range(8):
                level = i * 8 + j
                for k in range(2):
                    at = ((k * tags + tag) * levels + level) * pitch
                    for side, c in enumerate((0, cols - 8)):
                        sides[side, tag, level, :, HALVES[k]] = final[pl.ds(at + c, 8), :]

        for side, c in enumerate((0, cols - 8)):
            copies.append(
                pltpu.make_async_copy(
                    sides.at[side, tag], out.at[tag, :, pl.ds(c, 8)], sems.at[len(copies)]
                )
            )
            copies[-1].start()

    border_steps(
        levels, place, None, coef, wide, kept, l0, (first, second), halo, work, None, store, finish
    )
    for c in copies:
        c.wait()


def border(place, coef, wide, states, halos, final, out):
    cols, tags, levels, lats = states[1].shape
    vmem = pl.BlockSpec(memory_space=pltpu.VMEM)
    hbm = pl.BlockSpec(memory_space=pltpu.HBM)
    operands = [coef, wide, *states, *halos]
    n = len(operands) + 1
    return pl.pallas_call(
        border_kernel,
        in_specs=[pl.BlockSpec(memory_space=pltpu.SMEM)] + [vmem] * n + [hbm],
        out_specs=[vmem, hbm],
        out_shape=[
            pltpu.VMEM(final.shape, jnp.float32),
            pltpu.HBM(out.shape, jnp.float32),
        ],
        input_output_aliases={n: 0, n + 1: 1},
        scratch_shapes=[
            *border_scratch(tags, levels, lats),
            pltpu.VMEM((2, tags, levels, 8, lats), jnp.float32),
            pltpu.SemaphoreType.DMA((2 * tags,)),
        ],
        compiler_params=pltpu.CompilerParams(vmem_limit_bytes=32 << 20),
        cost_estimate=SHORT,
        name="border_all_levels",
    )(place, *operands, final, out)[1]


def write_kernel(final, out, block, sems):
    tags, levels, cols, _ = out.shape
    pitch = cols + 1
    copies = []
    for tag in range(tags):

        @pl.loop(0, levels)
        def _(level):
            for k in range(2):
                at = ((k * tags + tag) * levels + level) * pitch + 8
                block[tag, level, :, HALVES[k]] = final[pl.ds(at, cols - 16), :]

        copies.append(
            pltpu.make_async_copy(
                block.at[tag], out.at[tag, :, pl.ds(8, cols - 16)], sems.at[tag]
            )
        )
        copies[-1].start()
    for c in copies:
        c.wait()


def write_inner(final, shape):
    tags, levels, cols, lats = shape
    return pl.pallas_call(
        write_kernel,
        in_specs=[pl.BlockSpec(memory_space=pltpu.VMEM)],
        out_specs=pl.BlockSpec(memory_space=pltpu.HBM),
        out_shape=pltpu.HBM(shape, jnp.float32),
        scratch_shapes=[
            pltpu.VMEM((tags, levels, cols - 16, lats), jnp.float32),
            pltpu.SemaphoreType.DMA((tags,)),
        ],
        compiler_params=pltpu.CompilerParams(vmem_limit_bytes=24 << 20),
        cost_estimate=SHORT,
        name="write_inner",
    )(final)


def local(lam, east_wind, north_wind, east_diff, north_diff, mass_flux, region, top):
    groups, tiles = lax.axis_size("grp"), lax.axis_size("dom")
    parts = 4 if groups % 4 == 0 else 1
    grp, dom = lax.axis_index("grp"), lax.axis_index("dom")
    place = jnp.stack([grp, dom % 2]).astype(jnp.int32)
    own = (lam, east_wind, east_diff, north_wind, north_diff, mass_flux)
    far = [pltpu.with_memory_space_constraint(value, pltpu.HBM) for value in (*own, top)]

    pairs = lambda i: i ^ 1
    turn = lambda i: (((i - 1) % tiles ^ 1) + 1) % tiles
    coef_first, coef_second, first, second = pack(parts, place, far[0], far[1:6], far[6])
    coef_first = swapped(coef_first, "dom", pairs)
    coef_second = swapped(coef_second, "dom", turn)
    first = swapped(first, "dom", pairs)
    second = swapped(second, "dom", turn)
    pieces = [jnp.stack([coef_first, coef_second])]
    for by in range(1, parts):
        pieces.append(swapped(pieces[0], "grp", lambda i: i ^ by))
    coef, *states, final, rows = inner(place, own[0], own[1:], top, region)
    wide = outer_coefs(parts, lam.shape[2], place, coef, pieces)
    out = write_inner(final, lam.shape)
    wide, out = lax.optimization_barrier((wide, out))
    grad = gradient(place, region, coef, wide, states, (first, second), rows)
    grad, wide = lax.optimization_barrier((grad, wide))
    out = border(place, coef, wide, states, (first, second), final, out)
    share = grad
    for by in range(1, groups):
        grad = grad + swapped(share, "grp", lambda i: i ^ by)
    return out, grad


def solution(mesh):
    return jax.shard_map(
        local,
        mesh=mesh,
        in_specs=(
            P("grp", None, "dom", None),
            P(None, "dom", None),
            P(None, "dom", None),
            P(None, "dom", None),
            P(None, "dom", None),
            P(None, "dom", None),
            P("dom", None),
            P("dom", None),
        ),
        out_specs=(P("grp", None, "dom", None), P("dom", None)),
        check_vma=False,
    )
```

```python
import functools

import jax
import jax.numpy as jnp
from jax import lax
from jax.experimental import pallas as pl
from jax.experimental.pallas import tpu as pltpu
from jax.sharding import PartitionSpec as P

ITERS = 4
EDGE = ITERS
ENTRIES = 16
CHUNKS = 2
LANES = 128
HALVES = (slice(0, LANES), slice(LANES, 2 * LANES))
SHORT = pl.CostEstimate(flops=1000, bytes_accessed=1000, transcendentals=0)
LOW, HIGH = 0, 1

def swapped(value, axis, partner):
    return lax.ppermute(value, axis, [(i, partner(i)) for i in range(lax.axis_size(axis))])


def faces(ew, ed, nw, nd):
    lats = ew.shape[1]
    lat = lax.broadcasted_iota(jnp.int32, ew.shape, 1)
    east = jnp.maximum(ew, 0.0) + ed
    west_next = jnp.maximum(-ew, 0.0) + ed
    north = jnp.where(lat < lats - 1, jnp.maximum(nw, 0.0) + nd, 0.0)
    south = jnp.maximum(-nw, 0.0) + nd
    south = jnp.where(lat > 0, pltpu.roll(south, 1, 1), 0.0)
    return east, west_next, north, south


def updraft(mf, top_row):
    levels = mf.shape[0]
    level = lax.broadcasted_iota(jnp.int32, mf.shape, 0)
    return jnp.where((level < top_row) & (level < levels - 1), mf, 0.0)


def level_above(h):
    if h.shape[0] == 8:
        return pltpu.roll(h, 7, 0)
    parts = [pltpu.roll(h[at : at + 8], 7, 0) for at in range(0, h.shape[0], 8)]
    inside = lax.broadcasted_iota(jnp.int32, parts[0].shape, 0) < 7
    joined = [jnp.where(inside, low, high) for low, high in zip(parts, parts[1:])]
    return jnp.concatenate([*joined, parts[-1]], axis=0)


def advance(coefs, mid, east, west):
    d, e, w, n, s, u = coefs
    h = d * mid + e * east + w * west
    lane = lax.broadcasted_iota(jnp.int32, (mid.shape[0], LANES), 1)
    north = [pltpu.roll(mid[:, part], LANES - 1, 1) for part in HALVES]
    south = [pltpu.roll(mid[:, part], 1, 1) for part in HALVES]
    north = jnp.concatenate([jnp.where(lane < LANES - 1, *north), north[1]], axis=1)
    south = jnp.concatenate([south[0], jnp.where(lane > 0, south[1], south[0])], axis=1)
    h = h + n * north + s * south
    return h + u * (level_above(h) - h)


def pitched(slabs, levels, width):
    return -(-(slabs * levels * (width + 1) + width + 8) // 8) * 8


def column_at(ref, start, levels, pitch, apart):
    parts = [ref[pl.ds(start + apart * k, levels, stride=pitch), :] for k in range(2)]
    return jnp.concatenate(parts, axis=1)


def pack_kernel(parts, place, lam, ew, ed, nw, nd, mf, top, *refs):
    coef_first, coef_second, lam_first, lam_second = refs[:4]
    field_s, top_s, lam_s, coef_p, lam_p, sems = refs[4:]
    tags, levels, cols, lats = lam.shape
    per = levels // parts
    base = lax.rem(place[0], parts) * per
    copies = []

    def copy(src, dst):
        copies.append(pltpu.make_async_copy(src, dst, sems.at[len(copies)]))
        copies[-1].start()

    for side, at in ((LOW, 0), (HIGH, cols - 8)):
        for f, field in enumerate((ew, ed, nw, nd, mf)):
            copy(field.at[pl.ds(base, per), pl.ds(at, 8)], field_s.at[f, side])
        copy(top.at[pl.ds(at, 8)], top_s.at[side])
    for side, at in ((LOW, 0), (HIGH, cols - 8)):
        for tag in range(tags):
            copy(lam.at[tag, :, pl.ds(at, 8)], lam_s.at[side, tag])
    for c in copies[:12]:
        c.wait()
    pitch = 9
    few = per * pitch

    @pl.loop(0, per)
    def _(i):
        level = base + i
        for side in (LOW, HIGH):
            ew, ed, nw, nd, mf = (field_s[f, side, i] for f in range(5))
            lift = jnp.where((level < top_s[side]) & (level < levels - 1), mf, 0.0)
            for j, value in enumerate((*faces(ew, ed, nw, nd), lift)):
                for k in range(2):
                    at = ((j * 2 + side) * 2 + k) * few + i * pitch
                    coef_p[pl.ds(at, 8), :] = value[:, HALVES[k]]

    odd = place[1]
    start = 8 - EDGE
    for dest, side in ((coef_first, 1 - odd), (coef_second, odd)):

        def column(j, c):
            return column_at(coef_p, (j * 2 + side) * 2 * few + c, per, pitch, few)

        c = side * (start + 1)
        dest[0] = column(1, jnp.maximum(c - 1, 0))
        for i in range(EDGE - 1):
            for n, j in enumerate((0, 2, 3, 4, 1)):
                dest[5 * i + 1 + n] = column(j, c + i)

    for c in copies[12:]:
        c.wait()
    slab = levels * pitch

    @pl.loop(0, levels)
    def _(level):
        for side in (LOW, HIGH):
            for tag in range(tags):
                for k in range(2):
                    at = ((side * 2 + k) * tags + tag) * slab + level * pitch
                    lam_p[pl.ds(at, 8), :] = lam_s[side, tag, level, :, HALVES[k]]

    for dest, side in ((lam_first, 1 - odd), (lam_second, odd)):
        at = side * (2 * tags * slab + start)
        for tag in range(tags):
            for c in range(EDGE):
                dest[tag * EDGE + c] = column_at(
                    lam_p, at + tag * slab + c, levels, pitch, tags * slab
                )


def pack(parts, place, lam, fields, top):
    tags, levels, cols, lats = lam.shape
    per = levels // parts
    hbm = pl.BlockSpec(memory_space=pltpu.HBM)
    coef_send = pltpu.VMEM((ENTRIES, per, lats), jnp.float32)
    lam_send = pltpu.VMEM((tags * EDGE, levels, lats), jnp.float32)
    return pl.pallas_call(
        functools.partial(pack_kernel, parts),
        in_specs=[pl.BlockSpec(memory_space=pltpu.SMEM)] + [hbm] * 7,
        out_specs=[pl.BlockSpec(memory_space=pltpu.VMEM)] * 4,
        out_shape=[coef_send, coef_send, lam_send, lam_send],
        scratch_shapes=[
            pltpu.VMEM((5, 2, per, 8, lats), jnp.float32),
            pltpu.VMEM((2, 8, lats), jnp.int32),
            pltpu.VMEM((2, tags, levels, 8, lats), jnp.float32),
            pltpu.VMEM((pitched(20, per, 8), LANES), jnp.float32),
            pltpu.VMEM((pitched(4 * tags, levels, 8), LANES), jnp.float32),
            pltpu.SemaphoreType.DMA((12 + 2 * tags,)),
        ],
        compiler_params=pltpu.CompilerParams(vmem_limit_bytes=24 << 20),
        cost_estimate=SHORT,
        name="pack_edges",
    )(place, lam, *fields, top)


def chosen(region_row, first_tag, values):
    row = jnp.zeros(region_row.shape, jnp.float32)
    for tag, value in enumerate(values):
        row = jnp.where(region_row == first_tag + tag, value[0:1], row)
    return row


def sweep(t, shape, first_tag, region, coef, load, store, rows):
    tags, _, cols, _ = shape
    low, high = t + 1, cols - t - 1
    chunk = -(-(high - low) // CHUNKS)
    column = lambda c: [load(c, k) for k in range(tags)]

    @pl.loop(0, CHUNKS)
    def _(i):
        start = jnp.minimum(low + i * chunk, high - chunk)
        west, mid = column(start - 1), column(start)
        for j in range(chunk):
            c = start + j
            east = column(c + 1)
            coefs = [coef[c, n] for n in range(6)]
            new = [advance(coefs, mid[k], east[k], west[k]) for k in range(tags)]
            for k in range(tags):
                store(c, k, new[k])
            rows[t, pl.ds(c, 1), :] = chosen(region[pl.ds(c, 1), :], first_tag, new)
            west, mid = mid, east


def loading(ref):
    return lambda c, tag: ref[c, tag]


def storing(ref):
    def store(c, tag, value):
        ref[c, tag] = value

    return store


def storing_rows(ref, tags, levels, pitch):
    def store(c, tag, value):
        for k in range(2):
            at = (k * tags + tag) * levels * pitch + c
            ref[pl.ds(at, levels, stride=pitch), :] = value[:, HALVES[k]]

    return store


def inner_kernel(place, lam, ew, ed, nw, nd, mf, top, region, *refs):
    coef, l0, l1, l2, l3, final, grad, lam_p, field_p, rows = refs
    rows[...] = jnp.zeros_like(rows)
    tags, levels, cols, lats = lam.shape
    pitch = cols + 1
    slab = levels * pitch

    @pl.loop(0, levels)
    def _(level):
        row = level * pitch
        for f, field in enumerate((ew, ed, nw, nd, mf)):
            for k in range(2):
                field_p[pl.ds((f * 2 + k) * slab + row, cols), :] = field[level, :, HALVES[k]]
        for tag in range(tags):
            for k in range(2):
                at = (k * tags + tag) * slab + row
                lam_p[pl.ds(at, cols), :] = lam[tag, level, :, HALVES[k]]

    def coefficients(c, west):
        ew, ed, nw, nd, mf = (
            column_at(field_p, f * 2 * slab + c, levels, pitch, slab) for f in range(5)
        )
        e, next_west, n, s = faces(ew, ed, nw, nd)
        u = updraft(mf, top[pl.ds(c, 1), :])
        for j, value in enumerate((1.0 - e - west - n - s, e, west, n, s, u)):
            coef[c, j] = value
        return next_west

    def some(i, west):
        for j in range(8):
            west = coefficients(i * 8 + j, west)
        return west

    west = lax.fori_loop(0, cols // 8, some, jnp.zeros((levels, lats), jnp.float32))
    coef[cols, 2] = west

    def given(c, tag):
        return column_at(lam_p, tag * slab + c, levels, pitch, tags * slab)

    for at, c in enumerate((0, 1, cols - 2, cols - 1)):
        for tag in range(tags):
            l0[at, tag] = given(c, tag)
    last = storing_rows(final, tags, levels, pitch)
    loads = (given, loading(l1), loading(l2), loading(l3))
    stores = (storing(l1), storing(l2), storing(l3), last)
    for t in range(ITERS):
        sweep(t, lam.shape, place[0] * tags, region, coef, loads[t], stores[t], rows)
    total = rows[0]
    for t in range(1, ITERS):
        total = total + rows[t]
    grad[...] = total


def inner(place, lam, fields, top, region):
    tags, levels, cols, lats = lam.shape
    vmem = pl.BlockSpec(memory_space=pltpu.VMEM)
    state = pltpu.VMEM((cols, tags, levels, lats), jnp.float32)
    return pl.pallas_call(
        inner_kernel,
        in_specs=[pl.BlockSpec(memory_space=pltpu.SMEM)] + [vmem] * 8,
        out_specs=[vmem] * 7,
        out_shape=[
            pltpu.VMEM((cols + 1, 6, levels, lats), jnp.float32),
            pltpu.VMEM((4, tags, levels, lats), jnp.float32),
            *[state] * 3,
            pltpu.VMEM((pitched(2 * tags, levels, cols), LANES), jnp.float32),
            pltpu.VMEM((cols, lats), jnp.float32),
        ],
        scratch_shapes=[
            pltpu.VMEM((pitched(2 * tags, levels, cols), LANES), jnp.float32),
            pltpu.VMEM((pitched(10, levels, cols), LANES), jnp.float32),
            pltpu.VMEM((ITERS, cols, lats), jnp.float32),
        ],
        compiler_params=pltpu.CompilerParams(vmem_limit_bytes=32 << 20),
        cost_estimate=SHORT,
        name="inner_steps",
    )(place, lam, *fields, top, region)


def slot(c, cols):
    return (LOW, c + EDGE - 1) if c < EDGE else (HIGH, c - (cols - EDGE))


def outer_kernel(parts, cols, place, coef, *refs):
    pieces, wide, entry = refs[:parts], refs[parts], refs[parts + 1]
    levels = coef.shape[2]
    per = levels // parts
    mine = lax.rem(place[0], parts)
    odd = place[1]
    for by in range(parts):
        for half, side in enumerate((1 - odd, odd)):

            @pl.loop(0, ENTRIES // 4)
            def _(i):
                for j in range(4):
                    e = i * 4 + j
                    for k in range(2):
                        at = ((side * ENTRIES + e) * 2 + k) * levels + (mine ^ by) * per
                        entry[pl.ds(at, per), :] = pieces[by][half, e, :, HALVES[k]]

    def slab(side, e):
        at = (side * ENTRIES + e) * 2 * levels
        return jnp.concatenate([entry[at + k * levels : at + (k + 1) * levels] for k in (0, 1)], 1)

    for side in (LOW, HIGH):
        for i in range(EDGE - 1):
            w, e, n, s, u = (slab(side, 5 * i + j) for j in range(5))
            if side == HIGH and i == 0:
                w = coef[cols, 2]
            for j, value in enumerate((1.0 - e - w - n - s, e, w, n, s, u)):
                wide[side, i + EDGE * side, j] = value
    first_west = slab(LOW, ENTRIES - 1)
    e, n, s, u = (coef[0, j] for j in (1, 3, 4, 5))
    for j, value in enumerate((1.0 - e - first_west - n - s, e, first_west, n, s, u)):
        wide[*slot(0, cols), j] = value


def outer_coefs(parts, cols, place, coef, pieces):
    _, _, levels, lats = coef.shape
    vmem = pl.BlockSpec(memory_space=pltpu.VMEM)
    return pl.pallas_call(
        functools.partial(outer_kernel, parts, cols),
        in_specs=[pl.BlockSpec(memory_space=pltpu.SMEM)] + [vmem] * (1 + parts),
        out_specs=vmem,
        out_shape=pltpu.VMEM((2, 2 * EDGE - 1, 6, levels, lats), jnp.float32),
        scratch_shapes=[pltpu.VMEM((2 * ENTRIES * 2 * levels, LANES), jnp.float32)],
        compiler_params=pltpu.CompilerParams(vmem_limit_bytes=24 << 20),
        cost_estimate=SHORT,
        name="outer_coefs",
    )(place, coef, *pieces)


def border_steps(
    depth, place, region, coef, wide, kept, l0, halos, halo, work, grad=None, store=None, finish=None
):
    cols, tags, levels, lats = kept[1].shape
    first_tag = place[0] * tags
    part = slice(0, depth)
    halo[1 - place[1]] = halos[0][:, part]
    halo[place[1]] = halos[1][:, part]

    def coefs_at(c):
        if 0 < c < cols:
            return [coef[c, j, part] for j in range(6)]
        return [wide[*slot(c, cols), j, part] for j in range(6)]

    def state(t, c, tag):
        if t == 0:
            if c < 0:
                return halo[LOW, tag * EDGE + c + EDGE]
            if c >= cols:
                return halo[HIGH, tag * EDGE + c - cols]
            return l0[c if c < 2 else c - (cols - 4), tag, part]
        if t <= c < cols - t:
            return kept[t][c, tag, part]
        return work[t, *slot(c, cols), tag]

    def column(t, c):
        return [state(t, c, tag) for tag in range(tags)]

    for t in range(ITERS if store is None else ITERS - 1):
        reach = EDGE - 1 - t
        for run in (range(-reach, t + 1), range(cols - t - 1, cols + reach)):
            west, mid = column(t, run[0] - 1), column(t, run[0])
            for c in run:
                east = column(t, c + 1)
                coefs = coefs_at(c)
                new = [advance(coefs, mid[k], east[k], west[k]) for k in range(tags)]
                if t < ITERS - 1:
                    for k in range(tags):
                        work[t + 1, *slot(c, cols), k] = new[k]
                if grad is not None and 0 <= c < cols:
                    grad[c : c + 1] += chosen(region[c : c + 1, :], first_tag, new)
                west, mid = mid, east
    if store is None:
        return
    t = ITERS - 1
    for k in range(tags):
        for c in [*range(EDGE), *range(cols - EDGE, cols)]:
            near = [state(t, at, k) for at in (c, c + 1, c - 1)]
            store(c, k, advance(coefs_at(c), *near))
        finish(k)


def low_kernel(place, region, coef, wide, l0, l1, l2, l3, second, first, inner_grad, grad, halo, work):
    grad[...] = inner_grad[...]
    kept = (None, l1, l2, l3)
    border_steps(8, place, region, coef, wide, kept, l0, (first, second), halo, work, grad)


def border_scratch(tags, depth, lats):
    return [
        pltpu.VMEM((2, tags * EDGE, depth, lats), jnp.float32),
        pltpu.VMEM((ITERS, 2, 2 * EDGE - 1, tags, depth, lats), jnp.float32),
    ]


def gradient(place, region, coef, wide, states, halos, inner_grad):
    cols, tags, levels, lats = states[1].shape
    vmem = pl.BlockSpec(memory_space=pltpu.VMEM)
    operands = [region, coef, wide, *states, *halos, inner_grad]
    return pl.pallas_call(
        low_kernel,
        in_specs=[pl.BlockSpec(memory_space=pltpu.SMEM)] + [vmem] * len(operands),
        out_specs=vmem,
        out_shape=pltpu.VMEM((cols, lats), jnp.float32),
        scratch_shapes=border_scratch(tags, 8, lats),
        compiler_params=pltpu.CompilerParams(vmem_limit_bytes=32 << 20),
        cost_estimate=SHORT,
        name="border_low_levels",
    )(place, *operands)


def border_kernel(place, coef, wide, l0, l1, l2, l3, second, first, *refs):
    final_in, out_in, final, out, halo, work, sides, sems = refs
    cols, tags, levels, lats = l1.shape
    pitch = cols + 1
    store = storing_rows(final, tags, levels, pitch)
    kept = (None, l1, l2, l3)
    copies = []

    def finish(tag):
        @pl.loop(0, levels // 8)
        def _(i):
            for j in range(8):
                level = i * 8 + j
                for k in range(2):
                    at = ((k * tags + tag) * levels + level) * pitch
                    for side, c in enumerate((0, cols - 8)):
                        sides[side, tag, level, :, HALVES[k]] = final[pl.ds(at + c, 8), :]

        for side, c in enumerate((0, cols - 8)):
            copies.append(
                pltpu.make_async_copy(
                    sides.at[side, tag], out.at[tag, :, pl.ds(c, 8)], sems.at[len(copies)]
                )
            )
            copies[-1].start()

    border_steps(
        levels, place, None, coef, wide, kept, l0, (first, second), halo, work, None, store, finish
    )
    for c in copies:
        c.wait()


def border(place, coef, wide, states, halos, final, out):
    cols, tags, levels, lats = states[1].shape
    vmem = pl.BlockSpec(memory_space=pltpu.VMEM)
    hbm = pl.BlockSpec(memory_space=pltpu.HBM)
    operands = [coef, wide, *states, *halos]
    n = len(operands) + 1
    return pl.pallas_call(
        border_kernel,
        in_specs=[pl.BlockSpec(memory_space=pltpu.SMEM)] + [vmem] * n + [hbm],
        out_specs=[vmem, hbm],
        out_shape=[
            pltpu.VMEM(final.shape, jnp.float32),
            pltpu.HBM(out.shape, jnp.float32),
        ],
        input_output_aliases={n: 0, n + 1: 1},
        scratch_shapes=[
            *border_scratch(tags, levels, lats),
            pltpu.VMEM((2, tags, levels, 8, lats), jnp.float32),
            pltpu.SemaphoreType.DMA((2 * tags,)),
        ],
        compiler_params=pltpu.CompilerParams(vmem_limit_bytes=32 << 20),
        cost_estimate=SHORT,
        name="border_all_levels",
    )(place, *operands, final, out)[1]


def write_kernel(final, out, block, sems):
    tags, levels, cols, _ = out.shape
    pitch = cols + 1
    copies = []
    for tag in range(tags):

        @pl.loop(0, levels)
        def _(level):
            for k in range(2):
                at = ((k * tags + tag) * levels + level) * pitch + 8
                block[tag, level, :, HALVES[k]] = final[pl.ds(at, cols - 16), :]

        copies.append(
            pltpu.make_async_copy(
                block.at[tag], out.at[tag, :, pl.ds(8, cols - 16)], sems.at[tag]
            )
        )
        copies[-1].start()
    for c in copies:
        c.wait()


def write_inner(final, shape):
    tags, levels, cols, lats = shape
    return pl.pallas_call(
        write_kernel,
        in_specs=[pl.BlockSpec(memory_space=pltpu.VMEM)],
        out_specs=pl.BlockSpec(memory_space=pltpu.HBM),
        out_shape=pltpu.HBM(shape, jnp.float32),
        scratch_shapes=[
            pltpu.VMEM((tags, levels, cols - 16, lats), jnp.float32),
            pltpu.SemaphoreType.DMA((tags,)),
        ],
        compiler_params=pltpu.CompilerParams(vmem_limit_bytes=24 << 20),
        cost_estimate=SHORT,
        name="write_inner",
    )(final)


def local(lam, east_wind, north_wind, east_diff, north_diff, mass_flux, region, top):
    groups, tiles = lax.axis_size("grp"), lax.axis_size("dom")
    parts = 4 if groups % 4 == 0 else 1
    grp, dom = lax.axis_index("grp"), lax.axis_index("dom")
    place = jnp.stack([grp, dom % 2]).astype(jnp.int32)
    own = (lam, east_wind, east_diff, north_wind, north_diff, mass_flux)
    far = [pltpu.with_memory_space_constraint(value, pltpu.HBM) for value in (*own, top)]

    pairs = lambda i: i ^ 1
    turn = lambda i: (((i - 1) % tiles ^ 1) + 1) % tiles
    coef_first, coef_second, first, second = pack(parts, place, far[0], far[1:6], far[6])
    coef_first = swapped(coef_first, "dom", pairs)
    coef_second = swapped(coef_second, "dom", turn)
    second = swapped(second, "dom", turn)
    first = swapped(first, "dom", pairs)
    pieces = [jnp.stack([coef_first, coef_second])]
    for by in range(1, parts):
        pieces.append(swapped(pieces[0], "grp", lambda i: i ^ by))
    coef, *states, final, inner_grad = inner(place, own[0], own[1:], top, region)
    wide = outer_coefs(parts, lam.shape[2], place, coef, pieces)
    out = write_inner(final, lam.shape)
    wide, out = lax.optimization_barrier((wide, out))
    grad = gradient(place, region, coef, wide, states, (second, first), inner_grad)
    grad, wide = lax.optimization_barrier((grad, wide))
    out = border(place, coef, wide, states, (second, first), final, out)
    share = grad
    for by in range(1, groups):
        grad = grad + swapped(share, "grp", lambda i: i ^ by)
    return out, grad


def solution(mesh):
    return jax.shard_map(
        local,
        mesh=mesh,
        in_specs=(
            P("grp", None, "dom", None),
            P(None, "dom", None),
            P(None, "dom", None),
            P(None, "dom", None),
            P(None, "dom", None),
            P(None, "dom", None),
            P("dom", None),
            P("dom", None),
        ),
        out_specs=(P("grp", None, "dom", None), P("dom", None)),
        check_vma=False,
    )
```

```python
import functools

import jax
import jax.numpy as jnp
from jax import lax
from jax.experimental import pallas as pl
from jax.experimental.pallas import tpu as pltpu
from jax.sharding import PartitionSpec as P

ITERS = 4
EDGE = ITERS
ENTRIES = 16
CHUNKS = 2
LANES = 128
HALVES = (slice(0, LANES), slice(LANES, 2 * LANES))
SHORT = pl.CostEstimate(flops=1000, bytes_accessed=1000, transcendentals=0)
LOW, HIGH = 0, 1

def swapped(value, axis, partner):
    return lax.ppermute(value, axis, [(i, partner(i)) for i in range(lax.axis_size(axis))])


def faces(ew, ed, nw, nd):
    lats = ew.shape[1]
    lat = lax.broadcasted_iota(jnp.int32, ew.shape, 1)
    east = jnp.maximum(ew, 0.0) + ed
    west_next = jnp.maximum(-ew, 0.0) + ed
    north = jnp.where(lat < lats - 1, jnp.maximum(nw, 0.0) + nd, 0.0)
    south = jnp.maximum(-nw, 0.0) + nd
    south = jnp.where(lat > 0, pltpu.roll(south, 1, 1), 0.0)
    return east, west_next, north, south


def updraft(mf, top_row):
    levels = mf.shape[0]
    level = lax.broadcasted_iota(jnp.int32, mf.shape, 0)
    return jnp.where((level < top_row) & (level < levels - 1), mf, 0.0)


def parity():
    return lax.rem(lax.axis_index("dom"), 2)


def level_above(h):
    if h.shape[0] == 8:
        return pltpu.roll(h, 7, 0)
    parts = [pltpu.roll(h[at : at + 8], 7, 0) for at in range(0, h.shape[0], 8)]
    inside = lax.broadcasted_iota(jnp.int32, parts[0].shape, 0) < 7
    joined = [jnp.where(inside, low, high) for low, high in zip(parts, parts[1:])]
    return jnp.concatenate([*joined, parts[-1]], axis=0)


def advance(coefs, mid, east, west):
    d, e, w, n, s, u = coefs
    h = d * mid + e * east + w * west
    lane = lax.broadcasted_iota(jnp.int32, (mid.shape[0], LANES), 1)
    north = [pltpu.roll(mid[:, part], LANES - 1, 1) for part in HALVES]
    south = [pltpu.roll(mid[:, part], 1, 1) for part in HALVES]
    north = jnp.concatenate([jnp.where(lane < LANES - 1, *north), north[1]], axis=1)
    south = jnp.concatenate([south[0], jnp.where(lane > 0, south[1], south[0])], axis=1)
    h = h + n * north + s * south
    return h + u * (level_above(h) - h)


def pitched(slabs, levels, width):
    return -(-(slabs * levels * (width + 1) + width + 8) // 8) * 8


def column_at(ref, start, levels, pitch, apart):
    parts = [ref[pl.ds(start + apart * k, levels, stride=pitch), :] for k in range(2)]
    return jnp.concatenate(parts, axis=1)


def pack_kernel(parts, lam, ew, ed, nw, nd, mf, top, *refs):
    coef_first, coef_second, lam_first, lam_second = refs[:4]
    field_s, top_s, lam_s, coef_p, lam_p, sems = refs[4:]
    tags, levels, cols, lats = lam.shape
    per = levels // parts
    base = lax.rem(lax.axis_index("grp"), parts) * per
    copies = []

    def copy(src, dst):
        copies.append(pltpu.make_async_copy(src, dst, sems.at[len(copies)]))
        copies[-1].start()

    for side, at in ((LOW, 0), (HIGH, cols - 8)):
        for f, field in enumerate((ew, ed, nw, nd, mf)):
            copy(field.at[pl.ds(base, per), pl.ds(at, 8)], field_s.at[f, side])
        copy(top.at[pl.ds(at, 8)], top_s.at[side])
    for side, at in ((LOW, 0), (HIGH, cols - 8)):
        for tag in range(tags):
            copy(lam.at[tag, :, pl.ds(at, 8)], lam_s.at[side, tag])
    for c in copies[:12]:
        c.wait()
    pitch = 9
    few = per * pitch

    @pl.loop(0, per)
    def _(i):
        level = base + i
        for side in (LOW, HIGH):
            ew, ed, nw, nd, mf = (field_s[f, side, i] for f in range(5))
            lift = jnp.where((level < top_s[side]) & (level < levels - 1), mf, 0.0)
            for j, value in enumerate((*faces(ew, ed, nw, nd), lift)):
                for k in range(2):
                    at = ((j * 2 + side) * 2 + k) * few + i * pitch
                    coef_p[pl.ds(at, 8), :] = value[:, HALVES[k]]

    odd = parity()
    start = 8 - EDGE
    for dest, side in ((coef_first, 1 - odd), (coef_second, odd)):

        def column(j, c):
            return column_at(coef_p, (j * 2 + side) * 2 * few + c, per, pitch, few)

        c = side * (start + 1)
        dest[0] = column(1, jnp.maximum(c - 1, 0))
        for i in range(EDGE - 1):
            for n, j in enumerate((0, 2, 3, 4, 1)):
                dest[5 * i + 1 + n] = column(j, c + i)

    for c in copies[12:]:
        c.wait()
    slab = levels * pitch

    @pl.loop(0, levels)
    def _(level):
        for side in (LOW, HIGH):
            for tag in range(tags):
                for k in range(2):
                    at = ((side * 2 + k) * tags + tag) * slab + level * pitch
                    lam_p[pl.ds(at, 8), :] = lam_s[side, tag, level, :, HALVES[k]]

    for dest, side in ((lam_first, 1 - odd), (lam_second, odd)):
        at = side * (2 * tags * slab + start)
        for tag in range(tags):
            for c in range(EDGE):
                dest[tag * EDGE + c] = column_at(
                    lam_p, at + tag * slab + c, levels, pitch, tags * slab
                )


def pack(parts, lam, fields, top):
    tags, levels, cols, lats = lam.shape
    per = levels // parts
    hbm = pl.BlockSpec(memory_space=pltpu.HBM)
    coef_send = pltpu.VMEM((ENTRIES, per, lats), jnp.float32)
    lam_send = pltpu.VMEM((tags * EDGE, levels, lats), jnp.float32)
    return pl.pallas_call(
        functools.partial(pack_kernel, parts),
        in_specs=[hbm] * 7,
        out_specs=[pl.BlockSpec(memory_space=pltpu.VMEM)] * 4,
        out_shape=[coef_send, coef_send, lam_send, lam_send],
        scratch_shapes=[
            pltpu.VMEM((5, 2, per, 8, lats), jnp.float32),
            pltpu.VMEM((2, 8, lats), jnp.int32),
            pltpu.VMEM((2, tags, levels, 8, lats), jnp.float32),
            pltpu.VMEM((pitched(20, per, 8), LANES), jnp.float32),
            pltpu.VMEM((pitched(4 * tags, levels, 8), LANES), jnp.float32),
            pltpu.SemaphoreType.DMA((12 + 2 * tags,)),
        ],
        compiler_params=pltpu.CompilerParams(vmem_limit_bytes=24 << 20),
        cost_estimate=SHORT,
        name="pack_edges",
    )(lam, *fields, top)


def chosen(region_row, first_tag, values):
    row = jnp.zeros(region_row.shape, jnp.float32)
    for tag, value in enumerate(values):
        row = jnp.where(region_row == first_tag + tag, value[0:1], row)
    return row


def sweep(t, shape, first_tag, region, coef, load, store, rows):
    tags, _, cols, _ = shape
    low, high = t + 1, cols - t - 1
    chunk = -(-(high - low) // CHUNKS)
    column = lambda c: [load(c, k) for k in range(tags)]

    @pl.loop(0, CHUNKS)
    def _(i):
        start = jnp.minimum(low + i * chunk, high - chunk)
        west, mid = column(start - 1), column(start)
        for j in range(chunk):
            c = start + j
            east = column(c + 1)
            coefs = [coef[c, n] for n in range(6)]
            new = [advance(coefs, mid[k], east[k], west[k]) for k in range(tags)]
            for k in range(tags):
                store(c, k, new[k])
            rows[t, pl.ds(c, 1), :] = chosen(region[pl.ds(c, 1), :], first_tag, new)
            west, mid = mid, east


def loading(ref):
    return lambda c, tag: ref[c, tag]


def storing(ref):
    def store(c, tag, value):
        ref[c, tag] = value

    return store


def storing_rows(ref, tags, levels, pitch):
    def store(c, tag, value):
        for k in range(2):
            at = (k * tags + tag) * levels * pitch + c
            ref[pl.ds(at, levels, stride=pitch), :] = value[:, HALVES[k]]

    return store


def inner_kernel(lam, ew, ed, nw, nd, mf, top, region, *refs):
    coef, l0, l1, l2, l3, final, rows, lam_p, field_p = refs
    tags, levels, cols, lats = lam.shape
    pitch = cols + 1
    slab = levels * pitch

    @pl.loop(0, levels)
    def _(level):
        row = level * pitch
        for f, field in enumerate((ew, ed, nw, nd, mf)):
            for k in range(2):
                field_p[pl.ds((f * 2 + k) * slab + row, cols), :] = field[level, :, HALVES[k]]
        for tag in range(tags):
            for k in range(2):
                at = (k * tags + tag) * slab + row
                lam_p[pl.ds(at, cols), :] = lam[tag, level, :, HALVES[k]]

    def coefficients(c, west):
        ew, ed, nw, nd, mf = (
            column_at(field_p, f * 2 * slab + c, levels, pitch, slab) for f in range(5)
        )
        e, next_west, n, s = faces(ew, ed, nw, nd)
        u = updraft(mf, top[pl.ds(c, 1), :])
        for j, value in enumerate((1.0 - e - west - n - s, e, west, n, s, u)):
            coef[c, j] = value
        return next_west

    def some(i, west):
        for j in range(8):
            west = coefficients(i * 8 + j, west)
        return west

    west = lax.fori_loop(0, cols // 8, some, jnp.zeros((levels, lats), jnp.float32))
    coef[cols, 2] = west

    def given(c, tag):
        return column_at(lam_p, tag * slab + c, levels, pitch, tags * slab)

    for at, c in enumerate((0, 1, cols - 2, cols - 1)):
        for tag in range(tags):
            l0[at, tag] = given(c, tag)
    last = storing_rows(final, tags, levels, pitch)
    loads = (given, loading(l1), loading(l2), loading(l3))
    stores = (storing(l1), storing(l2), storing(l3), last)
    for t in range(ITERS):
        sweep(t, lam.shape, lax.axis_index("grp") * tags, region, coef, loads[t], stores[t], rows)


def inner(lam, fields, top, region):
    tags, levels, cols, lats = lam.shape
    vmem = pl.BlockSpec(memory_space=pltpu.VMEM)
    state = pltpu.VMEM((cols, tags, levels, lats), jnp.float32)
    return pl.pallas_call(
        inner_kernel,
        in_specs=[vmem] * 8,
        out_specs=[vmem] * 7,
        out_shape=[
            pltpu.VMEM((cols + 1, 6, levels, lats), jnp.float32),
            pltpu.VMEM((4, tags, levels, lats), jnp.float32),
            *[state] * 3,
            pltpu.VMEM((pitched(2 * tags, levels, cols), LANES), jnp.float32),
            pltpu.VMEM((ITERS, cols, lats), jnp.float32),
        ],
        scratch_shapes=[
            pltpu.VMEM((pitched(2 * tags, levels, cols), LANES), jnp.float32),
            pltpu.VMEM((pitched(10, levels, cols), LANES), jnp.float32),
        ],
        compiler_params=pltpu.CompilerParams(vmem_limit_bytes=32 << 20),
        cost_estimate=SHORT,
        name="inner_steps",
    )(lam, *fields, top, region)


def slot(c, cols):
    return (LOW, c + EDGE - 1) if c < EDGE else (HIGH, c - (cols - EDGE))


def outer_kernel(parts, cols, coef, *refs):
    pieces, wide, entry = refs[:parts], refs[parts], refs[parts + 1]
    levels = coef.shape[2]
    per = levels // parts
    mine = lax.rem(lax.axis_index("grp"), parts)
    odd = parity()
    for by in range(parts):
        for half, side in enumerate((1 - odd, odd)):

            @pl.loop(0, ENTRIES // 4)
            def _(i):
                for j in range(4):
                    e = i * 4 + j
                    for k in range(2):
                        at = ((side * ENTRIES + e) * 2 + k) * levels + (mine ^ by) * per
                        entry[pl.ds(at, per), :] = pieces[by][half, e, :, HALVES[k]]

    def slab(side, e):
        at = (side * ENTRIES + e) * 2 * levels
        return jnp.concatenate([entry[at + k * levels : at + (k + 1) * levels] for k in (0, 1)], 1)

    for side in (LOW, HIGH):
        for i in range(EDGE - 1):
            w, e, n, s, u = (slab(side, 5 * i + j) for j in range(5))
            if side == HIGH and i == 0:
                w = coef[cols, 2]
            for j, value in enumerate((1.0 - e - w - n - s, e, w, n, s, u)):
                wide[side, i + EDGE * side, j] = value
    first_west = slab(LOW, ENTRIES - 1)
    e, n, s, u = (coef[0, j] for j in (1, 3, 4, 5))
    for j, value in enumerate((1.0 - e - first_west - n - s, e, first_west, n, s, u)):
        wide[*slot(0, cols), j] = value


def outer_coefs(parts, cols, coef, pieces):
    _, _, levels, lats = coef.shape
    vmem = pl.BlockSpec(memory_space=pltpu.VMEM)
    return pl.pallas_call(
        functools.partial(outer_kernel, parts, cols),
        in_specs=[vmem] * (1 + parts),
        out_specs=vmem,
        out_shape=pltpu.VMEM((2, 2 * EDGE - 1, 6, levels, lats), jnp.float32),
        scratch_shapes=[pltpu.VMEM((2 * ENTRIES * 2 * levels, LANES), jnp.float32)],
        compiler_params=pltpu.CompilerParams(vmem_limit_bytes=24 << 20),
        cost_estimate=SHORT,
        name="outer_coefs",
    )(coef, *pieces)


def border_steps(
    depth, region, coef, wide, kept, l0, halos, halo, work, rows=None, store=None, finish=None
):
    cols, tags, levels, lats = kept[1].shape
    first_tag = lax.axis_index("grp") * tags
    part = slice(0, depth)
    halo[1 - parity()] = halos[0][:, part]
    halo[parity()] = halos[1][:, part]

    def coefs_at(c):
        if 0 < c < cols:
            return [coef[c, j, part] for j in range(6)]
        return [wide[*slot(c, cols), j, part] for j in range(6)]

    def state(t, c, tag):
        if t == 0:
            if c < 0:
                return halo[LOW, tag * EDGE + c + EDGE]
            if c >= cols:
                return halo[HIGH, tag * EDGE + c - cols]
            return l0[c if c < 2 else c - (cols - 4), tag, part]
        if t <= c < cols - t:
            return kept[t][c, tag, part]
        return work[t, *slot(c, cols), tag]

    def column(t, c):
        return [state(t, c, tag) for tag in range(tags)]

    for t in range(ITERS if store is None else ITERS - 1):
        reach = EDGE - 1 - t
        for run in (range(-reach, t + 1), range(cols - t - 1, cols + reach)):
            west, mid = column(t, run[0] - 1), column(t, run[0])
            for c in run:
                east = column(t, c + 1)
                coefs = coefs_at(c)
                new = [advance(coefs, mid[k], east[k], west[k]) for k in range(tags)]
                if t < ITERS - 1:
                    for k in range(tags):
                        work[t + 1, *slot(c, cols), k] = new[k]
                if rows is not None and 0 <= c < cols:
                    rows[t, c : c + 1, :] = chosen(region[c : c + 1, :], first_tag, new)
                west, mid = mid, east
    if store is None:
        return
    t = ITERS - 1
    for k in range(tags):
        for c in [*range(EDGE), *range(cols - EDGE, cols)]:
            near = [state(t, at, k) for at in (c, c + 1, c - 1)]
            store(c, k, advance(coefs_at(c), *near))
        finish(k)


def low_kernel(region, coef, wide, l0, l1, l2, l3, first, second, rows_in, grad, halo, work, rows):
    rows[...] = rows_in[...]
    kept = (None, l1, l2, l3)
    border_steps(8, region, coef, wide, kept, l0, (first, second), halo, work, rows)
    total = rows[0]
    for t in range(1, ITERS):
        total = total + rows[t]
    grad[...] = total


def border_scratch(tags, depth, lats):
    return [
        pltpu.VMEM((2, tags * EDGE, depth, lats), jnp.float32),
        pltpu.VMEM((ITERS, 2, 2 * EDGE - 1, tags, depth, lats), jnp.float32),
    ]


def gradient(region, coef, wide, states, halos, rows):
    cols, tags, levels, lats = states[1].shape
    vmem = pl.BlockSpec(memory_space=pltpu.VMEM)
    operands = [region, coef, wide, *states, *halos, rows]
    return pl.pallas_call(
        low_kernel,
        in_specs=[vmem] * len(operands),
        out_specs=vmem,
        out_shape=pltpu.VMEM((cols, lats), jnp.float32),
        scratch_shapes=[
            *border_scratch(tags, 8, lats),
            pltpu.VMEM((ITERS, cols, lats), jnp.float32),
        ],
        compiler_params=pltpu.CompilerParams(vmem_limit_bytes=32 << 20),
        cost_estimate=SHORT,
        name="border_low_levels",
    )(*operands)


def border_kernel(coef, wide, l0, l1, l2, l3, first, second, *refs):
    final_in, out_in, final, out, halo, work, sides, sems = refs
    cols, tags, levels, lats = l1.shape
    pitch = cols + 1
    store = storing_rows(final, tags, levels, pitch)
    kept = (None, l1, l2, l3)
    copies = []

    def finish(tag):
        @pl.loop(0, levels // 8)
        def _(i):
            for j in range(8):
                level = i * 8 + j
                for k in range(2):
                    at = ((k * tags + tag) * levels + level) * pitch
                    for side, c in enumerate((0, cols - 8)):
                        sides[side, tag, level, :, HALVES[k]] = final[pl.ds(at + c, 8), :]

        for side, c in enumerate((0, cols - 8)):
            copies.append(
                pltpu.make_async_copy(
                    sides.at[side, tag], out.at[tag, :, pl.ds(c, 8)], sems.at[len(copies)]
                )
            )
            copies[-1].start()

    border_steps(
        levels, None, coef, wide, kept, l0, (first, second), halo, work, None, store, finish
    )
    for c in copies:
        c.wait()


def border(coef, wide, states, halos, final, out):
    cols, tags, levels, lats = states[1].shape
    vmem = pl.BlockSpec(memory_space=pltpu.VMEM)
    hbm = pl.BlockSpec(memory_space=pltpu.HBM)
    operands = [coef, wide, *states, *halos]
    n = len(operands)
    return pl.pallas_call(
        border_kernel,
        in_specs=[vmem] * (n + 1) + [hbm],
        out_specs=[vmem, hbm],
        out_shape=[
            pltpu.VMEM(final.shape, jnp.float32),
            pltpu.HBM(out.shape, jnp.float32),
        ],
        input_output_aliases={n: 0, n + 1: 1},
        scratch_shapes=[
            *border_scratch(tags, levels, lats),
            pltpu.VMEM((2, tags, levels, 8, lats), jnp.float32),
            pltpu.SemaphoreType.DMA((2 * tags,)),
        ],
        compiler_params=pltpu.CompilerParams(vmem_limit_bytes=32 << 20),
        cost_estimate=SHORT,
        name="border_all_levels",
    )(*operands, final, out)[1]


def write_kernel(final, out, block, sems):
    tags, levels, cols, _ = out.shape
    pitch = cols + 1
    copies = []
    for tag in range(tags):

        @pl.loop(0, levels)
        def _(level):
            for k in range(2):
                at = ((k * tags + tag) * levels + level) * pitch + 8
                block[tag, level, :, HALVES[k]] = final[pl.ds(at, cols - 16), :]

        copies.append(
            pltpu.make_async_copy(
                block.at[tag], out.at[tag, :, pl.ds(8, cols - 16)], sems.at[tag]
            )
        )
        copies[-1].start()
    for c in copies:
        c.wait()


def write_inner(final, shape):
    tags, levels, cols, lats = shape
    return pl.pallas_call(
        write_kernel,
        in_specs=[pl.BlockSpec(memory_space=pltpu.VMEM)],
        out_specs=pl.BlockSpec(memory_space=pltpu.HBM),
        out_shape=pltpu.HBM(shape, jnp.float32),
        scratch_shapes=[
            pltpu.VMEM((tags, levels, cols - 16, lats), jnp.float32),
            pltpu.SemaphoreType.DMA((tags,)),
        ],
        compiler_params=pltpu.CompilerParams(vmem_limit_bytes=24 << 20),
        cost_estimate=SHORT,
        name="write_inner",
    )(final)


def local(lam, east_wind, north_wind, east_diff, north_diff, mass_flux, region, top):
    groups, tiles = lax.axis_size("grp"), lax.axis_size("dom")
    parts = 4 if groups % 4 == 0 else 1
    own = (lam, east_wind, east_diff, north_wind, north_diff, mass_flux)
    far = [pltpu.with_memory_space_constraint(value, pltpu.HBM) for value in (*own, top)]

    pairs = lambda i: i ^ 1
    turn = lambda i: (((i - 1) % tiles ^ 1) + 1) % tiles
    coef_first, coef_second, first, second = pack(parts, far[0], far[1:6], far[6])
    coef_first = swapped(coef_first, "dom", pairs)
    coef_second = swapped(coef_second, "dom", turn)
    first = swapped(first, "dom", pairs)
    second = swapped(second, "dom", turn)
    pieces = [jnp.stack([coef_first, coef_second])]
    for by in range(1, parts):
        pieces.append(swapped(pieces[0], "grp", lambda i: i ^ by))
    coef, *states, final, rows = inner(own[0], own[1:], top, region)
    wide = outer_coefs(parts, lam.shape[2], coef, pieces)
    out = write_inner(final, lam.shape)
    wide, out = lax.optimization_barrier((wide, out))
    grad = gradient(region, coef, wide, states, (first, second), rows)
    grad, wide = lax.optimization_barrier((grad, wide))
    out = border(coef, wide, states, (first, second), final, out)
    share = grad
    for by in range(1, groups):
        grad = grad + swapped(share, "grp", lambda i: i ^ by)
    return out, grad


def solution(mesh):
    return jax.shard_map(
        local,
        mesh=mesh,
        in_specs=(
            P("grp", None, "dom", None),
            P(None, "dom", None),
            P(None, "dom", None),
            P(None, "dom", None),
            P(None, "dom", None),
            P(None, "dom", None),
            P("dom", None),
            P("dom", None),
        ),
        out_specs=(P("grp", None, "dom", None), P("dom", None)),
        check_vma=False,
    )
```

```python
import functools

import jax
import jax.numpy as jnp
from jax import lax
from jax.experimental import pallas as pl
from jax.experimental.pallas import tpu as pltpu
from jax.sharding import PartitionSpec as P

ITERS = 4
EDGE = ITERS
ENTRIES = 16
BLOCK = 4
CHUNKS = 2
LANES = 128
HALVES = (slice(0, LANES), slice(LANES, 2 * LANES))
SHORT = pl.CostEstimate(flops=1000, bytes_accessed=1000, transcendentals=0)
LOW, HIGH = 0, 1

def swapped(value, axis, partner):
    return lax.ppermute(value, axis, [(i, partner(i)) for i in range(lax.axis_size(axis))])


def faces(ew, ed, nw, nd):
    lats = ew.shape[1]
    lat = lax.broadcasted_iota(jnp.int32, ew.shape, 1)
    east = jnp.maximum(ew, 0.0) + ed
    west_next = jnp.maximum(-ew, 0.0) + ed
    north = jnp.where(lat < lats - 1, jnp.maximum(nw, 0.0) + nd, 0.0)
    south = jnp.maximum(-nw, 0.0) + nd
    south = jnp.where(lat > 0, pltpu.roll(south, 1, 1), 0.0)
    return east, west_next, north, south


def updraft(mf, top_row):
    levels = mf.shape[0]
    level = lax.broadcasted_iota(jnp.int32, mf.shape, 0)
    return jnp.where((level < top_row) & (level < levels - 1), mf, 0.0)


def parity():
    return lax.rem(lax.axis_index("dom"), 2)


def level_above(h):
    if h.shape[0] == 8:
        return pltpu.roll(h, 7, 0)
    parts = [pltpu.roll(h[at : at + 8], 7, 0) for at in range(0, h.shape[0], 8)]
    inside = lax.broadcasted_iota(jnp.int32, parts[0].shape, 0) < 7
    joined = [jnp.where(inside, low, high) for low, high in zip(parts, parts[1:])]
    return jnp.concatenate([*joined, parts[-1]], axis=0)


def advance(coefs, mid, east, west):
    d, e, w, n, s, u = coefs
    h = d * mid + e * east + w * west
    lane = lax.broadcasted_iota(jnp.int32, (mid.shape[0], LANES), 1)
    north = [pltpu.roll(mid[:, part], LANES - 1, 1) for part in HALVES]
    south = [pltpu.roll(mid[:, part], 1, 1) for part in HALVES]
    north = jnp.concatenate([jnp.where(lane < LANES - 1, *north), north[1]], axis=1)
    south = jnp.concatenate([south[0], jnp.where(lane > 0, south[1], south[0])], axis=1)
    h = h + n * north + s * south
    return h + u * (level_above(h) - h)


def pitched(slabs, levels, width):
    return -(-(slabs * levels * (width + 1) + width + 8) // 8) * 8


def column_at(ref, start, levels, pitch, apart):
    parts = [ref[pl.ds(start + apart * k, levels, stride=pitch), :] for k in range(2)]
    return jnp.concatenate(parts, axis=1)


def coef_side(rank):
    return lax.rem(1 - parity() + rank, 2)


def coef_half(rank):
    return lax.rem(lax.div(rank, 2), 2)


def pack_kernel(lam, ew, ed, nw, nd, mf, top, *refs):
    coef_send, lam_first, lam_second = refs[:3]
    field_s, top_s, lam_s, coef_p, lam_p, sems = refs[3:]
    tags, levels, cols, lats = lam.shape
    per = levels // 2
    rank = lax.axis_index("grp")
    base = coef_half(rank) * per
    high = coef_side(rank)
    edge = pl.ds(pl.multiple_of(high * (cols - 8), 8), 8)
    copies = []

    def copy(src, dst):
        copies.append(pltpu.make_async_copy(src, dst, sems.at[len(copies)]))
        copies[-1].start()

    for f, field in enumerate((ew, ed, nw, nd, mf)):
        copy(field.at[pl.ds(base, per), edge], field_s.at[f])
    copy(top.at[edge], top_s)
    for side, at in ((LOW, 0), (HIGH, cols - 8)):
        for tag in range(tags):
            copy(lam.at[tag, :, pl.ds(at, 8)], lam_s.at[side, tag])
    for c in copies[:6]:
        c.wait()
    pitch = 9
    few = per * pitch

    @pl.loop(0, per // 2)
    def _(pair):
        for half in range(2):
            i = pair * 2 + half
            level = base + i
            ew, ed, nw, nd, mf = (field_s[f, i] for f in range(5))
            lift = jnp.where((level < top_s[...]) & (level < levels - 1), mf, 0.0)
            for j, value in enumerate((*faces(ew, ed, nw, nd), lift)):
                for k in range(2):
                    at = (j * 2 + k) * few + i * pitch
                    coef_p[pl.ds(at, 8), :] = value[:, HALVES[k]]

    def coef_column(j, c):
        return column_at(coef_p, j * 2 * few + c, per, pitch, few)

    start = 8 - EDGE
    c = high * (start + 1)
    coef_send[0] = coef_column(1, jnp.maximum(c - 1, 0))
    for i in range(EDGE - 1):
        for n, j in enumerate((0, 2, 3, 4, 1)):
            coef_send[5 * i + 1 + n] = coef_column(j, c + i)

    odd = parity()
    for c in copies[6:]:
        c.wait()
    slab = levels * pitch

    @pl.loop(0, levels)
    def _(level):
        for side in (LOW, HIGH):
            for tag in range(tags):
                for k in range(2):
                    at = ((side * 2 + k) * tags + tag) * slab + level * pitch
                    lam_p[pl.ds(at, 8), :] = lam_s[side, tag, level, :, HALVES[k]]

    for dest, side in ((lam_first, 1 - odd), (lam_second, odd)):
        at = side * (2 * tags * slab + start)
        for tag in range(tags):
            for c in range(EDGE):
                dest[tag * EDGE + c] = column_at(
                    lam_p, at + tag * slab + c, levels, pitch, tags * slab
                )


def pack(lam, fields, top):
    tags, levels, cols, lats = lam.shape
    per = levels // 2
    hbm = pl.BlockSpec(memory_space=pltpu.HBM)
    coef_send = pltpu.VMEM((ENTRIES, per, lats), jnp.float32)
    lam_send = pltpu.VMEM((tags * EDGE, levels, lats), jnp.float32)
    return pl.pallas_call(
        pack_kernel,
        in_specs=[hbm] * 7,
        out_specs=[pl.BlockSpec(memory_space=pltpu.VMEM)] * 3,
        out_shape=[coef_send, lam_send, lam_send],
        scratch_shapes=[
            pltpu.VMEM((5, per, 8, lats), jnp.float32),
            pltpu.VMEM((8, lats), jnp.int32),
            pltpu.VMEM((2, tags, levels, 8, lats), jnp.float32),
            pltpu.VMEM((pitched(10, per, 8), LANES), jnp.float32),
            pltpu.VMEM((pitched(4 * tags, levels, 8), LANES), jnp.float32),
            pltpu.SemaphoreType.DMA((6 + 2 * tags,)),
        ],
        compiler_params=pltpu.CompilerParams(vmem_limit_bytes=24 << 20),
        cost_estimate=SHORT,
        name="pack_edges",
    )(lam, *fields, top)


def chosen(region_row, first_tag, values):
    row = jnp.zeros(region_row.shape, jnp.float32)
    for tag, value in enumerate(values):
        row = jnp.where(region_row == first_tag + tag, value[0:1], row)
    return row


def sweep(t, shape, first_tag, region, coef, load, store, rows):
    tags, _, cols, _ = shape
    low, high = t + 1, cols - t - 1
    chunk = -(-(high - low) // CHUNKS)
    column = lambda c: [load(c, k) for k in range(tags)]

    @pl.loop(0, CHUNKS)
    def _(i):
        start = jnp.minimum(low + i * chunk, high - chunk)
        west, mid = column(start - 1), column(start)
        for j in range(chunk):
            c = start + j
            east = column(c + 1)
            coefs = [coef[c, n] for n in range(6)]
            new = [advance(coefs, mid[k], east[k], west[k]) for k in range(tags)]
            for k in range(tags):
                store(c, k, new[k])
            rows[t, pl.ds(c, 1), :] = chosen(region[pl.ds(c, 1), :], first_tag, new)
            west, mid = mid, east


def loading(ref):
    return lambda c, tag: ref[c, tag]


def storing(ref):
    def store(c, tag, value):
        ref[c, tag] = value

    return store


def storing_rows(ref, tags, levels, pitch):
    def store(c, tag, value):
        for k in range(2):
            at = (k * tags + tag) * levels * pitch + c
            ref[pl.ds(at, levels, stride=pitch), :] = value[:, HALVES[k]]

    return store


def inner_kernel(lam, ew, ed, nw, nd, mf, top, region, *refs):
    coef, l0, l1, l2, l3, final, rows, lam_p, field_p = refs
    tags, levels, cols, lats = lam.shape
    pitch = cols + 1
    slab = levels * pitch

    @pl.loop(0, levels)
    def _(level):
        row = level * pitch
        for f, field in enumerate((ew, ed, nw, nd, mf)):
            for k in range(2):
                field_p[pl.ds((f * 2 + k) * slab + row, cols), :] = field[level, :, HALVES[k]]
        for tag in range(tags):
            for k in range(2):
                at = (k * tags + tag) * slab + row
                lam_p[pl.ds(at, cols), :] = lam[tag, level, :, HALVES[k]]

    def coefficients(c, west):
        ew, ed, nw, nd, mf = (
            column_at(field_p, f * 2 * slab + c, levels, pitch, slab) for f in range(5)
        )
        e, next_west, n, s = faces(ew, ed, nw, nd)
        u = updraft(mf, top[pl.ds(c, 1), :])
        for j, value in enumerate((1.0 - e - west - n - s, e, west, n, s, u)):
            coef[c, j] = value
        return next_west

    def some(i, west):
        for j in range(8):
            west = coefficients(i * 8 + j, west)
        return west

    west = lax.fori_loop(0, cols // 8, some, jnp.zeros((levels, lats), jnp.float32))
    coef[cols, 2] = west

    def given(c, tag):
        return column_at(lam_p, tag * slab + c, levels, pitch, tags * slab)

    for at, c in enumerate((0, 1, cols - 2, cols - 1)):
        for tag in range(tags):
            l0[at, tag] = given(c, tag)
    last = storing_rows(final, tags, levels, pitch)
    loads = (given, loading(l1), loading(l2), loading(l3))
    stores = (storing(l1), storing(l2), storing(l3), last)
    for t in range(ITERS):
        sweep(t, lam.shape, lax.axis_index("grp") * tags, region, coef, loads[t], stores[t], rows)


def inner(lam, fields, top, region):
    tags, levels, cols, lats = lam.shape
    vmem = pl.BlockSpec(memory_space=pltpu.VMEM)
    state = pltpu.VMEM((cols, tags, levels, lats), jnp.float32)
    return pl.pallas_call(
        inner_kernel,
        in_specs=[vmem] * 8,
        out_specs=[vmem] * 7,
        out_shape=[
            pltpu.VMEM((cols + 1, 6, levels, lats), jnp.float32),
            pltpu.VMEM((4, tags, levels, lats), jnp.float32),
            *[state] * 3,
            pltpu.VMEM((pitched(2 * tags, levels, cols), LANES), jnp.float32),
            pltpu.VMEM((ITERS, cols, lats), jnp.float32),
        ],
        scratch_shapes=[
            pltpu.VMEM((pitched(2 * tags, levels, cols), LANES), jnp.float32),
            pltpu.VMEM((pitched(10, levels, cols), LANES), jnp.float32),
        ],
        compiler_params=pltpu.CompilerParams(vmem_limit_bytes=32 << 20),
        cost_estimate=SHORT,
        name="inner_steps",
    )(lam, *fields, top, region)


def slot(c, cols):
    return (LOW, c + EDGE - 1) if c < EDGE else (HIGH, c - (cols - EDGE))


def outer_kernel(cols, coef, *refs):
    pieces, wide, entry = refs[:BLOCK], refs[BLOCK], refs[BLOCK + 1]
    per = coef.shape[2] // 2
    for by in range(BLOCK):
        rank = lax.axis_index("grp") ^ by
        rows = pl.ds(pl.multiple_of(coef_half(rank) * per, 8), per)
        entry[coef_side(rank), :, rows] = pieces[by][...]

    def slab(side, e):
        return entry[side, e]

    for side in (LOW, HIGH):
        for i in range(EDGE - 1):
            w, e, n, s, u = (slab(side, 5 * i + j) for j in range(5))
            if side == HIGH and i == 0:
                w = coef[cols, 2]
            for j, value in enumerate((1.0 - e - w - n - s, e, w, n, s, u)):
                wide[side, i + EDGE * side, j] = value
    first_west = slab(LOW, ENTRIES - 1)
    e, n, s, u = (coef[0, j] for j in (1, 3, 4, 5))
    for j, value in enumerate((1.0 - e - first_west - n - s, e, first_west, n, s, u)):
        wide[*slot(0, cols), j] = value


def outer_coefs(cols, coef, pieces):
    _, _, levels, lats = coef.shape
    vmem = pl.BlockSpec(memory_space=pltpu.VMEM)
    return pl.pallas_call(
        functools.partial(outer_kernel, cols),
        in_specs=[vmem] * (1 + BLOCK),
        out_specs=vmem,
        out_shape=pltpu.VMEM((2, 2 * EDGE - 1, 6, levels, lats), jnp.float32),
        scratch_shapes=[pltpu.VMEM((2, ENTRIES, levels, lats), jnp.float32)],
        compiler_params=pltpu.CompilerParams(vmem_limit_bytes=24 << 20),
        cost_estimate=SHORT,
        name="outer_coefs",
    )(coef, *pieces)


def border_steps(
    depth, region, coef, wide, kept, l0, halos, halo, work, rows=None, store=None, finish=None
):
    cols, tags, levels, lats = kept[1].shape
    first_tag = lax.axis_index("grp") * tags
    part = slice(0, depth)
    halo[1 - parity()] = halos[0][:, part]
    halo[parity()] = halos[1][:, part]

    def coefs_at(c):
        if 0 < c < cols:
            return [coef[c, j, part] for j in range(6)]
        return [wide[*slot(c, cols), j, part] for j in range(6)]

    def state(t, c, tag):
        if t == 0:
            if c < 0:
                return halo[LOW, tag * EDGE + c + EDGE]
            if c >= cols:
                return halo[HIGH, tag * EDGE + c - cols]
            return l0[c if c < 2 else c - (cols - 4), tag, part]
        if t <= c < cols - t:
            return kept[t][c, tag, part]
        return work[t, *slot(c, cols), tag]

    def column(t, c):
        return [state(t, c, tag) for tag in range(tags)]

    for t in range(ITERS if store is None else ITERS - 1):
        reach = EDGE - 1 - t
        for run in (range(-reach, t + 1), range(cols - t - 1, cols + reach)):
            west, mid = column(t, run[0] - 1), column(t, run[0])
            for c in run:
                east = column(t, c + 1)
                coefs = coefs_at(c)
                new = [advance(coefs, mid[k], east[k], west[k]) for k in range(tags)]
                if t < ITERS - 1:
                    for k in range(tags):
                        work[t + 1, *slot(c, cols), k] = new[k]
                if rows is not None and 0 <= c < cols:
                    rows[t, c : c + 1, :] = chosen(region[c : c + 1, :], first_tag, new)
                west, mid = mid, east
    if store is None:
        return
    t = ITERS - 1
    for k in range(tags):
        for c in [*range(EDGE), *range(cols - EDGE, cols)]:
            near = [state(t, at, k) for at in (c, c + 1, c - 1)]
            store(c, k, advance(coefs_at(c), *near))
        finish(k)


def low_kernel(region, coef, wide, l0, l1, l2, l3, first, second, rows_in, grad, halo, work, rows):
    rows[...] = rows_in[...]
    kept = (None, l1, l2, l3)
    border_steps(8, region, coef, wide, kept, l0, (first, second), halo, work, rows)
    total = rows[0]
    for t in range(1, ITERS):
        total = total + rows[t]
    grad[...] = total


def border_scratch(tags, depth, lats):
    return [
        pltpu.VMEM((2, tags * EDGE, depth, lats), jnp.float32),
        pltpu.VMEM((ITERS, 2, 2 * EDGE - 1, tags, depth, lats), jnp.float32),
    ]


def gradient(region, coef, wide, states, halos, rows):
    cols, tags, levels, lats = states[1].shape
    vmem = pl.BlockSpec(memory_space=pltpu.VMEM)
    operands = [region, coef, wide, *states, *halos, rows]
    return pl.pallas_call(
        low_kernel,
        in_specs=[vmem] * len(operands),
        out_specs=vmem,
        out_shape=pltpu.VMEM((cols, lats), jnp.float32),
        scratch_shapes=[
            *border_scratch(tags, 8, lats),
            pltpu.VMEM((ITERS, cols, lats), jnp.float32),
        ],
        compiler_params=pltpu.CompilerParams(vmem_limit_bytes=32 << 20),
        cost_estimate=SHORT,
        name="border_low_levels",
    )(*operands)


def border_kernel(coef, wide, l0, l1, l2, l3, first, second, *refs):
    final_in, out_in, final, out, halo, work, sides, sems = refs
    cols, tags, levels, lats = l1.shape
    pitch = cols + 1
    store = storing_rows(final, tags, levels, pitch)
    kept = (None, l1, l2, l3)
    copies = []

    def finish(tag):
        @pl.loop(0, levels // 8)
        def _(i):
            for j in range(8):
                level = i * 8 + j
                for k in range(2):
                    at = ((k * tags + tag) * levels + level) * pitch
                    for side, c in enumerate((0, cols - 8)):
                        sides[side, tag, level, :, HALVES[k]] = final[pl.ds(at + c, 8), :]

        for side, c in enumerate((0, cols - 8)):
            copies.append(
                pltpu.make_async_copy(
                    sides.at[side, tag], out.at[tag, :, pl.ds(c, 8)], sems.at[len(copies)]
                )
            )
            copies[-1].start()

    border_steps(
        levels, None, coef, wide, kept, l0, (first, second), halo, work, None, store, finish
    )
    for c in copies:
        c.wait()


def border(coef, wide, states, halos, final, out):
    cols, tags, levels, lats = states[1].shape
    vmem = pl.BlockSpec(memory_space=pltpu.VMEM)
    hbm = pl.BlockSpec(memory_space=pltpu.HBM)
    operands = [coef, wide, *states, *halos]
    n = len(operands)
    return pl.pallas_call(
        border_kernel,
        in_specs=[vmem] * (n + 1) + [hbm],
        out_specs=[vmem, hbm],
        out_shape=[
            pltpu.VMEM(final.shape, jnp.float32),
            pltpu.HBM(out.shape, jnp.float32),
        ],
        input_output_aliases={n: 0, n + 1: 1},
        scratch_shapes=[
            *border_scratch(tags, levels, lats),
            pltpu.VMEM((2, tags, levels, 8, lats), jnp.float32),
            pltpu.SemaphoreType.DMA((2 * tags,)),
        ],
        compiler_params=pltpu.CompilerParams(vmem_limit_bytes=32 << 20),
        cost_estimate=SHORT,
        name="border_all_levels",
    )(*operands, final, out)[1]


def write_kernel(final, out, block, sems):
    tags, levels, cols, _ = out.shape
    pitch = cols + 1
    copies = []
    for tag in range(tags):

        @pl.loop(0, levels)
        def _(level):
            for k in range(2):
                at = ((k * tags + tag) * levels + level) * pitch + 8
                block[tag, level, :, HALVES[k]] = final[pl.ds(at, cols - 16), :]

        copies.append(
            pltpu.make_async_copy(
                block.at[tag], out.at[tag, :, pl.ds(8, cols - 16)], sems.at[tag]
            )
        )
        copies[-1].start()
    for c in copies:
        c.wait()


def write_inner(final, shape):
    tags, levels, cols, lats = shape
    return pl.pallas_call(
        write_kernel,
        in_specs=[pl.BlockSpec(memory_space=pltpu.VMEM)],
        out_specs=pl.BlockSpec(memory_space=pltpu.HBM),
        out_shape=pltpu.HBM(shape, jnp.float32),
        scratch_shapes=[
            pltpu.VMEM((tags, levels, cols - 16, lats), jnp.float32),
            pltpu.SemaphoreType.DMA((tags,)),
        ],
        compiler_params=pltpu.CompilerParams(vmem_limit_bytes=24 << 20),
        cost_estimate=SHORT,
        name="write_inner",
    )(final)


def local(lam, east_wind, north_wind, east_diff, north_diff, mass_flux, region, top):
    groups, tiles = lax.axis_size("grp"), lax.axis_size("dom")
    own = (lam, east_wind, east_diff, north_wind, north_diff, mass_flux)
    far = [pltpu.with_memory_space_constraint(value, pltpu.HBM) for value in (*own, top)]

    pairs = lambda i: i ^ 1
    turn = lambda i: (((i - 1) % tiles ^ 1) + 1) % tiles
    coefs, first, second = pack(far[0], far[1:6], far[6])

    def partner(i):
        tile, rank = divmod(i, groups)
        return (turn if rank % 2 else pairs)(tile) * groups + rank

    coefs = swapped(coefs, ("dom", "grp"), partner)
    first = swapped(first, "dom", pairs)
    second = swapped(second, "dom", turn)
    pieces = [coefs]
    for by in range(1, BLOCK):
        pieces.append(swapped(coefs, "grp", lambda i: i ^ by))
    coef, *states, final, rows = inner(own[0], own[1:], top, region)
    wide = outer_coefs(lam.shape[2], coef, pieces)
    out = write_inner(final, lam.shape)
    wide, out = lax.optimization_barrier((wide, out))
    grad = gradient(region, coef, wide, states, (first, second), rows)
    grad, wide = lax.optimization_barrier((grad, wide))
    out = border(coef, wide, states, (first, second), final, out)
    share = grad
    for by in range(1, groups):
        grad = grad + swapped(share, "grp", lambda i: i ^ by)
    return out, grad


def solution(mesh):
    return jax.shard_map(
        local,
        mesh=mesh,
        in_specs=(
            P("grp", None, "dom", None),
            P(None, "dom", None),
            P(None, "dom", None),
            P(None, "dom", None),
            P(None, "dom", None),
            P(None, "dom", None),
            P("dom", None),
            P("dom", None),
        ),
        out_specs=(P("grp", None, "dom", None), P("dom", None)),
        check_vma=False,
    )
```

```python
import functools

import jax
import jax.numpy as jnp
from jax import lax
from jax.experimental import pallas as pl
from jax.experimental.pallas import tpu as pltpu
from jax.sharding import PartitionSpec as P

ITERS = 4
EDGE = ITERS
ENTRIES = 16
BLOCK = 4
CHUNKS = 2
LANES = 128
HALVES = (slice(0, LANES), slice(LANES, 2 * LANES))
SHORT = pl.CostEstimate(flops=1000, bytes_accessed=1000, transcendentals=0)
LOW, HIGH = 0, 1

def swapped(value, axis, partner):
    return lax.ppermute(value, axis, [(i, partner(i)) for i in range(lax.axis_size(axis))])


def faces(ew, ed, nw, nd):
    lats = ew.shape[1]
    lat = lax.broadcasted_iota(jnp.int32, ew.shape, 1)
    east = jnp.maximum(ew, 0.0) + ed
    west_next = jnp.maximum(-ew, 0.0) + ed
    north = jnp.where(lat < lats - 1, jnp.maximum(nw, 0.0) + nd, 0.0)
    south = jnp.maximum(-nw, 0.0) + nd
    south = jnp.where(lat > 0, pltpu.roll(south, 1, 1), 0.0)
    return east, west_next, north, south


def updraft(mf, top_row):
    levels = mf.shape[0]
    level = lax.broadcasted_iota(jnp.int32, mf.shape, 0)
    return jnp.where((level < top_row) & (level < levels - 1), mf, 0.0)


def parity():
    return lax.rem(lax.axis_index("dom"), 2)


def level_above(h):
    if h.shape[0] == 8:
        return pltpu.roll(h, 7, 0)
    parts = [pltpu.roll(h[at : at + 8], 7, 0) for at in range(0, h.shape[0], 8)]
    inside = lax.broadcasted_iota(jnp.int32, parts[0].shape, 0) < 7
    joined = [jnp.where(inside, low, high) for low, high in zip(parts, parts[1:])]
    return jnp.concatenate([*joined, parts[-1]], axis=0)


def advance(coefs, mid, east, west):
    d, e, w, n, s, u = coefs
    h = d * mid + e * east + w * west
    lane = lax.broadcasted_iota(jnp.int32, (mid.shape[0], LANES), 1)
    north = [pltpu.roll(mid[:, part], LANES - 1, 1) for part in HALVES]
    south = [pltpu.roll(mid[:, part], 1, 1) for part in HALVES]
    north = jnp.concatenate([jnp.where(lane < LANES - 1, *north), north[1]], axis=1)
    south = jnp.concatenate([south[0], jnp.where(lane > 0, south[1], south[0])], axis=1)
    h = h + n * north + s * south
    return h + u * (level_above(h) - h)


def pitched(slabs, levels, width):
    return -(-(slabs * levels * (width + 1) + width + 8) // 8) * 8


def column_at(ref, start, levels, pitch, apart):
    parts = [ref[pl.ds(start + apart * k, levels, stride=pitch), :] for k in range(2)]
    return jnp.concatenate(parts, axis=1)


def coef_side(rank):
    return lax.rem(1 - parity() + rank, 2)


def coef_half(rank):
    return lax.rem(lax.div(rank, 2), 2)


def pack_kernel(lam, ew, ed, nw, nd, mf, top, *refs):
    coef_send, lam_first, lam_second = refs[:3]
    field_s, top_s, lam_s, coef_p, lam_p, sems = refs[3:]
    tags, levels, cols, lats = lam.shape
    per = levels // 2
    rank = lax.axis_index("grp")
    base = coef_half(rank) * per
    high = coef_side(rank)
    edge = pl.ds(pl.multiple_of(high * (cols - 8), 8), 8)
    copies = []

    def copy(src, dst):
        copies.append(pltpu.make_async_copy(src, dst, sems.at[len(copies)]))
        copies[-1].start()

    for f, field in enumerate((ew, ed, nw, nd, mf)):
        copy(field.at[pl.ds(base, per), edge], field_s.at[f])
    copy(top.at[edge], top_s)
    for side, at in ((LOW, 0), (HIGH, cols - 8)):
        for tag in range(tags):
            copy(lam.at[tag, :, pl.ds(at, 8)], lam_s.at[side, tag])
    for c in copies[:6]:
        c.wait()
    pitch = 9
    few = per * pitch

    @pl.loop(0, per // 2)
    def _(pair):
        for half in range(2):
            i = pair * 2 + half
            level = base + i
            ew, ed, nw, nd, mf = (field_s[f, i] for f in range(5))
            lift = jnp.where((level < top_s[...]) & (level < levels - 1), mf, 0.0)
            for j, value in enumerate((*faces(ew, ed, nw, nd), lift)):
                for k in range(2):
                    at = (j * 2 + k) * few + i * pitch
                    coef_p[pl.ds(at, 8), :] = value[:, HALVES[k]]

    def coef_column(j, c):
        return column_at(coef_p, j * 2 * few + c, per, pitch, few)

    start = 8 - EDGE
    c = high * (start + 1)
    coef_send[0] = coef_column(1, jnp.maximum(c - 1, 0))
    for i in range(EDGE - 1):
        for n, j in enumerate((0, 2, 3, 4, 1)):
            coef_send[5 * i + 1 + n] = coef_column(j, c + i)

    odd = parity()
    for c in copies[6:]:
        c.wait()
    slab = levels * pitch

    @pl.loop(0, levels)
    def _(level):
        for side in (LOW, HIGH):
            for tag in range(tags):
                for k in range(2):
                    at = ((side * 2 + k) * tags + tag) * slab + level * pitch
                    lam_p[pl.ds(at, 8), :] = lam_s[side, tag, level, :, HALVES[k]]

    for dest, side in ((lam_first, 1 - odd), (lam_second, odd)):
        at = side * (2 * tags * slab + start)
        for tag in range(tags):
            for c in range(EDGE):
                dest[tag * EDGE + c] = column_at(
                    lam_p, at + tag * slab + c, levels, pitch, tags * slab
                )


def pack(lam, fields, top):
    tags, levels, cols, lats = lam.shape
    per = levels // 2
    hbm = pl.BlockSpec(memory_space=pltpu.HBM)
    coef_send = pltpu.VMEM((ENTRIES, per, lats), jnp.float32)
    lam_send = pltpu.VMEM((tags * EDGE, levels, lats), jnp.float32)
    return pl.pallas_call(
        pack_kernel,
        in_specs=[hbm] * 7,
        out_specs=[pl.BlockSpec(memory_space=pltpu.VMEM)] * 3,
        out_shape=[coef_send, lam_send, lam_send],
        scratch_shapes=[
            pltpu.VMEM((5, per, 8, lats), jnp.float32),
            pltpu.VMEM((8, lats), jnp.int32),
            pltpu.VMEM((2, tags, levels, 8, lats), jnp.float32),
            pltpu.VMEM((pitched(10, per, 8), LANES), jnp.float32),
            pltpu.VMEM((pitched(4 * tags, levels, 8), LANES), jnp.float32),
            pltpu.SemaphoreType.DMA((6 + 2 * tags,)),
        ],
        compiler_params=pltpu.CompilerParams(vmem_limit_bytes=24 << 20),
        cost_estimate=SHORT,
        name="pack_edges",
    )(lam, *fields, top)


def chosen(region_row, first_tag, values):
    row = jnp.zeros(region_row.shape, jnp.float32)
    for tag, value in enumerate(values):
        row = jnp.where(region_row == first_tag + tag, value[0:1], row)
    return row


def sweep(t, shape, first_tag, region, coef, load, store, rows):
    tags, _, cols, _ = shape
    low, high = t + 1, cols - t - 1
    chunk = -(-(high - low) // CHUNKS)
    column = lambda c: [load(c, k) for k in range(tags)]

    @pl.loop(0, CHUNKS)
    def _(i):
        start = jnp.minimum(low + i * chunk, high - chunk)
        west, mid = column(start - 1), column(start)
        for j in range(chunk):
            c = start + j
            east = column(c + 1)
            coefs = [coef[c, n] for n in range(6)]
            new = [advance(coefs, mid[k], east[k], west[k]) for k in range(tags)]
            for k in range(tags):
                store(c, k, new[k])
            rows[t, pl.ds(c, 1), :] = chosen(region[pl.ds(c, 1), :], first_tag, new)
            west, mid = mid, east


def loading(ref):
    return lambda c, tag: ref[c, tag]


def storing(ref):
    def store(c, tag, value):
        ref[c, tag] = value

    return store


def storing_rows(ref, tags, levels, pitch):
    def store(c, tag, value):
        for k in range(2):
            at = (k * tags + tag) * levels * pitch + c
            ref[pl.ds(at, levels, stride=pitch), :] = value[:, HALVES[k]]

    return store


def prepare_kernel(lam, ew, ed, nw, nd, mf, top, coef, l0, lam_p, field_p):
    tags, levels, cols, lats = lam.shape
    pitch = cols + 1
    slab = levels * pitch

    @pl.loop(0, levels)
    def _(level):
        row = level * pitch
        for f, field in enumerate((ew, ed, nw, nd, mf)):
            for k in range(2):
                field_p[pl.ds((f * 2 + k) * slab + row, cols), :] = field[level, :, HALVES[k]]
        for tag in range(tags):
            for k in range(2):
                at = (k * tags + tag) * slab + row
                lam_p[pl.ds(at, cols), :] = lam[tag, level, :, HALVES[k]]

    def coefficients(c, west):
        ew, ed, nw, nd, mf = (
            column_at(field_p, f * 2 * slab + c, levels, pitch, slab) for f in range(5)
        )
        e, next_west, n, s = faces(ew, ed, nw, nd)
        u = updraft(mf, top[pl.ds(c, 1), :])
        for j, value in enumerate((1.0 - e - west - n - s, e, west, n, s, u)):
            coef[c, j] = value
        return next_west

    def some(i, west):
        for j in range(8):
            west = coefficients(i * 8 + j, west)
        return west

    west = lax.fori_loop(0, cols // 8, some, jnp.zeros((levels, lats), jnp.float32))
    coef[cols, 2] = west
    for at, c in enumerate((0, 1, cols - 2, cols - 1)):
        for tag in range(tags):
            l0[at, tag] = column_at(lam_p, tag * slab + c, levels, pitch, tags * slab)


def prepare(lam, fields, top):
    tags, levels, cols, lats = lam.shape
    vmem = pl.BlockSpec(memory_space=pltpu.VMEM)
    return pl.pallas_call(
        prepare_kernel,
        in_specs=[vmem] * 7,
        out_specs=[vmem] * 3,
        out_shape=[
            pltpu.VMEM((cols + 1, 6, levels, lats), jnp.float32),
            pltpu.VMEM((4, tags, levels, lats), jnp.float32),
            pltpu.VMEM((pitched(2 * tags, levels, cols), LANES), jnp.float32),
        ],
        scratch_shapes=[pltpu.VMEM((pitched(10, levels, cols), LANES), jnp.float32)],
        compiler_params=pltpu.CompilerParams(vmem_limit_bytes=32 << 20),
        cost_estimate=SHORT,
        name="prepare",
    )(lam, *fields, top)


def inner_kernel(coef, lam_p, region, l1, l2, l3, final, rows):
    cols, tags, levels, lats = l1.shape
    pitch = cols + 1
    slab = levels * pitch

    def given(c, tag):
        return column_at(lam_p, tag * slab + c, levels, pitch, tags * slab)

    last = storing_rows(final, tags, levels, pitch)
    loads = (given, loading(l1), loading(l2), loading(l3))
    stores = (storing(l1), storing(l2), storing(l3), last)
    shape = (tags, levels, cols, lats)
    for t in range(ITERS):
        sweep(t, shape, lax.axis_index("grp") * tags, region, coef, loads[t], stores[t], rows)


def inner(shape, coef, lam_p, region):
    tags, levels, cols, lats = shape
    vmem = pl.BlockSpec(memory_space=pltpu.VMEM)
    state = pltpu.VMEM((cols, tags, levels, lats), jnp.float32)
    return pl.pallas_call(
        inner_kernel,
        in_specs=[vmem] * 3,
        out_specs=[vmem] * 5,
        out_shape=[
            *[state] * 3,
            pltpu.VMEM(lam_p.shape, jnp.float32),
            pltpu.VMEM((ITERS, cols, lats), jnp.float32),
        ],
        compiler_params=pltpu.CompilerParams(vmem_limit_bytes=32 << 20),
        cost_estimate=SHORT,
        name="inner_steps",
    )(coef, lam_p, region)


def slot(c, cols):
    return (LOW, c + EDGE - 1) if c < EDGE else (HIGH, c - (cols - EDGE))


def outer_kernel(cols, coef, *refs):
    pieces, wide, entry = refs[:BLOCK], refs[BLOCK], refs[BLOCK + 1]
    per = coef.shape[2] // 2
    for by in range(BLOCK):
        rank = lax.axis_index("grp") ^ by
        rows = pl.ds(pl.multiple_of(coef_half(rank) * per, 8), per)
        entry[coef_side(rank), :, rows] = pieces[by][...]

    def slab(side, e):
        return entry[side, e]

    for side in (LOW, HIGH):
        for i in range(EDGE - 1):
            w, e, n, s, u = (slab(side, 5 * i + j) for j in range(5))
            if side == HIGH and i == 0:
                w = coef[cols, 2]
            for j, value in enumerate((1.0 - e - w - n - s, e, w, n, s, u)):
                wide[side, i + EDGE * side, j] = value
    first_west = slab(LOW, ENTRIES - 1)
    e, n, s, u = (coef[0, j] for j in (1, 3, 4, 5))
    for j, value in enumerate((1.0 - e - first_west - n - s, e, first_west, n, s, u)):
        wide[*slot(0, cols), j] = value


def outer_coefs(cols, coef, pieces):
    _, _, levels, lats = coef.shape
    vmem = pl.BlockSpec(memory_space=pltpu.VMEM)
    return pl.pallas_call(
        functools.partial(outer_kernel, cols),
        in_specs=[vmem] * (1 + BLOCK),
        out_specs=vmem,
        out_shape=pltpu.VMEM((2, 2 * EDGE - 1, 6, levels, lats), jnp.float32),
        scratch_shapes=[pltpu.VMEM((2, ENTRIES, levels, lats), jnp.float32)],
        compiler_params=pltpu.CompilerParams(vmem_limit_bytes=24 << 20),
        cost_estimate=SHORT,
        name="outer_coefs",
    )(coef, *pieces)


def border_steps(
    depth, region, coef, wide, kept, l0, halos, halo, work, rows=None, store=None, finish=None
):
    cols, tags, levels, lats = kept[1].shape
    first_tag = lax.axis_index("grp") * tags
    part = slice(0, depth)
    halo[1 - parity()] = halos[0][:, part]
    halo[parity()] = halos[1][:, part]

    def coefs_at(c):
        if 0 < c < cols:
            return [coef[c, j, part] for j in range(6)]
        return [wide[*slot(c, cols), j, part] for j in range(6)]

    def state(t, c, tag):
        if t == 0:
            if c < 0:
                return halo[LOW, tag * EDGE + c + EDGE]
            if c >= cols:
                return halo[HIGH, tag * EDGE + c - cols]
            return l0[c if c < 2 else c - (cols - 4), tag, part]
        if t <= c < cols - t:
            return kept[t][c, tag, part]
        return work[t, *slot(c, cols), tag]

    def column(t, c):
        return [state(t, c, tag) for tag in range(tags)]

    for t in range(ITERS if store is None else ITERS - 1):
        reach = EDGE - 1 - t
        for run in (range(-reach, t + 1), range(cols - t - 1, cols + reach)):
            west, mid = column(t, run[0] - 1), column(t, run[0])
            for c in run:
                east = column(t, c + 1)
                coefs = coefs_at(c)
                new = [advance(coefs, mid[k], east[k], west[k]) for k in range(tags)]
                if t < ITERS - 1:
                    for k in range(tags):
                        work[t + 1, *slot(c, cols), k] = new[k]
                if rows is not None and 0 <= c < cols:
                    rows[t, c : c + 1, :] = chosen(region[c : c + 1, :], first_tag, new)
                west, mid = mid, east
    if store is None:
        return
    t = ITERS - 1
    for k in range(tags):
        for c in [*range(EDGE), *range(cols - EDGE, cols)]:
            near = [state(t, at, k) for at in (c, c + 1, c - 1)]
            store(c, k, advance(coefs_at(c), *near))
        finish(k)


def low_kernel(region, coef, wide, l0, l1, l2, l3, first, second, rows_in, grad, halo, work, rows):
    rows[...] = rows_in[...]
    kept = (None, l1, l2, l3)
    border_steps(8, region, coef, wide, kept, l0, (first, second), halo, work, rows)
    total = rows[0]
    for t in range(1, ITERS):
        total = total + rows[t]
    grad[...] = total


def border_scratch(tags, depth, lats):
    return [
        pltpu.VMEM((2, tags * EDGE, depth, lats), jnp.float32),
        pltpu.VMEM((ITERS, 2, 2 * EDGE - 1, tags, depth, lats), jnp.float32),
    ]


def gradient(region, coef, wide, states, halos, rows):
    cols, tags, levels, lats = states[1].shape
    vmem = pl.BlockSpec(memory_space=pltpu.VMEM)
    operands = [region, coef, wide, *states, *halos, rows]
    return pl.pallas_call(
        low_kernel,
        in_specs=[vmem] * len(operands),
        out_specs=vmem,
        out_shape=pltpu.VMEM((cols, lats), jnp.float32),
        scratch_shapes=[
            *border_scratch(tags, 8, lats),
            pltpu.VMEM((ITERS, cols, lats), jnp.float32),
        ],
        compiler_params=pltpu.CompilerParams(vmem_limit_bytes=32 << 20),
        cost_estimate=SHORT,
        name="border_low_levels",
    )(*operands)


def border_kernel(coef, wide, l0, l1, l2, l3, first, second, *refs):
    final_in, out_in, final, out, halo, work, sides, sems = refs
    cols, tags, levels, lats = l1.shape
    pitch = cols + 1
    store = storing_rows(final, tags, levels, pitch)
    kept = (None, l1, l2, l3)
    copies = []

    def finish(tag):
        @pl.loop(0, levels // 8)
        def _(i):
            for j in range(8):
                level = i * 8 + j
                for k in range(2):
                    at = ((k * tags + tag) * levels + level) * pitch
                    for side, c in enumerate((0, cols - 8)):
                        sides[side, tag, level, :, HALVES[k]] = final[pl.ds(at + c, 8), :]

        for side, c in enumerate((0, cols - 8)):
            copies.append(
                pltpu.make_async_copy(
                    sides.at[side, tag], out.at[tag, :, pl.ds(c, 8)], sems.at[len(copies)]
                )
            )
            copies[-1].start()

    border_steps(
        levels, None, coef, wide, kept, l0, (first, second), halo, work, None, store, finish
    )
    for c in copies:
        c.wait()


def border(coef, wide, states, halos, final, out):
    cols, tags, levels, lats = states[1].shape
    vmem = pl.BlockSpec(memory_space=pltpu.VMEM)
    hbm = pl.BlockSpec(memory_space=pltpu.HBM)
    operands = [coef, wide, *states, *halos]
    n = len(operands)
    return pl.pallas_call(
        border_kernel,
        in_specs=[vmem] * (n + 1) + [hbm],
        out_specs=[vmem, hbm],
        out_shape=[
            pltpu.VMEM(final.shape, jnp.float32),
            pltpu.HBM(out.shape, jnp.float32),
        ],
        input_output_aliases={n: 0, n + 1: 1},
        scratch_shapes=[
            *border_scratch(tags, levels, lats),
            pltpu.VMEM((2, tags, levels, 8, lats), jnp.float32),
            pltpu.SemaphoreType.DMA((2 * tags,)),
        ],
        compiler_params=pltpu.CompilerParams(vmem_limit_bytes=32 << 20),
        cost_estimate=SHORT,
        name="border_all_levels",
    )(*operands, final, out)[1]


def write_kernel(final, out, block, sems):
    tags, levels, cols, _ = out.shape
    pitch = cols + 1
    copies = []
    for tag in range(tags):

        @pl.loop(0, levels)
        def _(level):
            for k in range(2):
                at = ((k * tags + tag) * levels + level) * pitch + 8
                block[tag, level, :, HALVES[k]] = final[pl.ds(at, cols - 16), :]

        copies.append(
            pltpu.make_async_copy(
                block.at[tag], out.at[tag, :, pl.ds(8, cols - 16)], sems.at[tag]
            )
        )
        copies[-1].start()
    for c in copies:
        c.wait()


def write_inner(final, shape):
    tags, levels, cols, lats = shape
    return pl.pallas_call(
        write_kernel,
        in_specs=[pl.BlockSpec(memory_space=pltpu.VMEM)],
        out_specs=pl.BlockSpec(memory_space=pltpu.HBM),
        out_shape=pltpu.HBM(shape, jnp.float32),
        scratch_shapes=[
            pltpu.VMEM((tags, levels, cols - 16, lats), jnp.float32),
            pltpu.SemaphoreType.DMA((tags,)),
        ],
        compiler_params=pltpu.CompilerParams(vmem_limit_bytes=24 << 20),
        cost_estimate=SHORT,
        name="write_inner",
    )(final)


def local(lam, east_wind, north_wind, east_diff, north_diff, mass_flux, region, top):
    groups, tiles = lax.axis_size("grp"), lax.axis_size("dom")
    own = (lam, east_wind, east_diff, north_wind, north_diff, mass_flux)
    far = [pltpu.with_memory_space_constraint(value, pltpu.HBM) for value in (*own, top)]

    pairs = lambda i: i ^ 1
    turn = lambda i: (((i - 1) % tiles ^ 1) + 1) % tiles
    coefs, first, second = pack(far[0], far[1:6], far[6])

    def partner(i):
        tile, rank = divmod(i, groups)
        return (turn if rank % 2 else pairs)(tile) * groups + rank

    coefs = swapped(coefs, ("dom", "grp"), partner)
    coef, l0, lam_p = prepare(own[0], own[1:], top)
    first, second, coef = lax.optimization_barrier((first, second, coef))
    first = swapped(first, "dom", pairs)
    second = swapped(second, "dom", turn)
    pieces = [coefs]
    for by in range(1, BLOCK):
        pieces.append(swapped(coefs, "grp", lambda i: i ^ by))
    *states, final, rows = inner(lam.shape, coef, lam_p, region)
    states = [l0, *states]
    wide = outer_coefs(lam.shape[2], coef, pieces)
    out = write_inner(final, lam.shape)
    wide, out = lax.optimization_barrier((wide, out))
    grad = gradient(region, coef, wide, states, (first, second), rows)
    grad, wide = lax.optimization_barrier((grad, wide))
    out = border(coef, wide, states, (first, second), final, out)
    share = grad
    for by in range(1, groups):
        grad = grad + swapped(share, "grp", lambda i: i ^ by)
    return out, grad


def solution(mesh):
    return jax.shard_map(
        local,
        mesh=mesh,
        in_specs=(
            P("grp", None, "dom", None),
            P(None, "dom", None),
            P(None, "dom", None),
            P(None, "dom", None),
            P(None, "dom", None),
            P(None, "dom", None),
            P("dom", None),
            P("dom", None),
        ),
        out_specs=(P("grp", None, "dom", None), P("dom", None)),
        check_vma=False,
    )
```

```python
import functools

import jax
import jax.numpy as jnp
from jax import lax
from jax.experimental import pallas as pl
from jax.experimental.pallas import tpu as pltpu
from jax.sharding import PartitionSpec as P

ITERS = 4
EDGE = ITERS
ENTRIES = 16
CHUNKS = 2
LANES = 128
HALVES = (slice(0, LANES), slice(LANES, 2 * LANES))
SHORT = pl.CostEstimate(flops=1000, bytes_accessed=1000, transcendentals=0)
LOW, HIGH = 0, 1

def swapped(value, axis, partner):
    return lax.ppermute(value, axis, [(i, partner(i)) for i in range(lax.axis_size(axis))])


def faces(ew, ed, nw, nd):
    lats = ew.shape[1]
    lat = lax.broadcasted_iota(jnp.int32, ew.shape, 1)
    east = jnp.maximum(ew, 0.0) + ed
    west_next = jnp.maximum(-ew, 0.0) + ed
    north = jnp.where(lat < lats - 1, jnp.maximum(nw, 0.0) + nd, 0.0)
    south = jnp.maximum(-nw, 0.0) + nd
    south = jnp.where(lat > 0, pltpu.roll(south, 1, 1), 0.0)
    return east, west_next, north, south


def updraft(mf, top_row):
    levels = mf.shape[0]
    level = lax.broadcasted_iota(jnp.int32, mf.shape, 0)
    return jnp.where((level < top_row) & (level < levels - 1), mf, 0.0)


def parity():
    return lax.rem(lax.axis_index("dom"), 2)


def level_above(h):
    if h.shape[0] == 8:
        return pltpu.roll(h, 7, 0)
    parts = [pltpu.roll(h[at : at + 8], 7, 0) for at in range(0, h.shape[0], 8)]
    inside = lax.broadcasted_iota(jnp.int32, parts[0].shape, 0) < 7
    joined = [jnp.where(inside, low, high) for low, high in zip(parts, parts[1:])]
    return jnp.concatenate([*joined, parts[-1]], axis=0)


def advance(coefs, mid, east, west):
    d, e, w, n, s, u = coefs
    h = d * mid + e * east + w * west
    lane = lax.broadcasted_iota(jnp.int32, (mid.shape[0], LANES), 1)
    north = [pltpu.roll(mid[:, part], LANES - 1, 1) for part in HALVES]
    south = [pltpu.roll(mid[:, part], 1, 1) for part in HALVES]
    north = jnp.concatenate([jnp.where(lane < LANES - 1, *north), north[1]], axis=1)
    south = jnp.concatenate([south[0], jnp.where(lane > 0, south[1], south[0])], axis=1)
    h = h + n * north + s * south
    return h + u * (level_above(h) - h)


def pitched(slabs, levels, width):
    return -(-(slabs * levels * (width + 1) + width + 8) // 8) * 8


def column_at(ref, start, levels, pitch, apart):
    parts = [ref[pl.ds(start + apart * k, levels, stride=pitch), :] for k in range(2)]
    return jnp.concatenate(parts, axis=1)


def coef_side(half):
    return lax.rem(1 - parity() + half, 2)


def coef_half():
    return lax.rem(lax.div(lax.axis_index("grp"), 2), 2)


def pack_kernel(lam, ew, ed, nw, nd, mf, top, *refs):
    coef_send, lam_first, lam_second = refs[:3]
    field_s, top_s, lam_s, coef_p, lam_p, sems = refs[3:]
    tags, levels, cols, lats = lam.shape
    high = coef_side(coef_half())
    edge = pl.ds(pl.multiple_of(high * (cols - 8), 8), 8)
    copies = []

    def copy(src, dst):
        copies.append(pltpu.make_async_copy(src, dst, sems.at[len(copies)]))
        copies[-1].start()

    for f, field in enumerate((ew, ed, nw, nd, mf)):
        copy(field.at[:, edge], field_s.at[f])
    copy(top.at[edge], top_s)
    for side, at in ((LOW, 0), (HIGH, cols - 8)):
        for tag in range(tags):
            copy(lam.at[tag, :, pl.ds(at, 8)], lam_s.at[side, tag])
    for c in copies[:6]:
        c.wait()
    pitch = 9
    few = levels * pitch

    @pl.loop(0, levels // 4)
    def _(i):
        for step in range(4):
            level = i * 4 + step
            ew, ed, nw, nd, mf = (field_s[f, level] for f in range(5))
            lift = jnp.where((level < top_s[...]) & (level < levels - 1), mf, 0.0)
            for j, value in enumerate((*faces(ew, ed, nw, nd), lift)):
                for k in range(2):
                    at = (j * 2 + k) * few + level * pitch
                    coef_p[pl.ds(at, 8), :] = value[:, HALVES[k]]

    def coef_column(j, c):
        return column_at(coef_p, j * 2 * few + c, levels, pitch, few)

    start = 8 - EDGE
    c = high * (start + 1)
    coef_send[0] = coef_column(1, jnp.maximum(c - 1, 0))
    for i in range(EDGE - 1):
        for n, j in enumerate((0, 2, 3, 4, 1)):
            coef_send[5 * i + 1 + n] = coef_column(j, c + i)

    odd = parity()
    for c in copies[6:]:
        c.wait()
    slab = levels * pitch

    @pl.loop(0, levels)
    def _(level):
        for side in (LOW, HIGH):
            for tag in range(tags):
                for k in range(2):
                    at = ((side * 2 + k) * tags + tag) * slab + level * pitch
                    lam_p[pl.ds(at, 8), :] = lam_s[side, tag, level, :, HALVES[k]]

    for dest, side in ((lam_first, 1 - odd), (lam_second, odd)):
        at = side * (2 * tags * slab + start)
        for tag in range(tags):
            for c in range(EDGE):
                dest[tag * EDGE + c] = column_at(
                    lam_p, at + tag * slab + c, levels, pitch, tags * slab
                )


def pack(lam, fields, top):
    tags, levels, cols, lats = lam.shape
    hbm = pl.BlockSpec(memory_space=pltpu.HBM)
    coef_send = pltpu.VMEM((ENTRIES, levels, lats), jnp.float32)
    lam_send = pltpu.VMEM((tags * EDGE, levels, lats), jnp.float32)
    return pl.pallas_call(
        pack_kernel,
        in_specs=[hbm] * 7,
        out_specs=[pl.BlockSpec(memory_space=pltpu.VMEM)] * 3,
        out_shape=[coef_send, lam_send, lam_send],
        scratch_shapes=[
            pltpu.VMEM((5, levels, 8, lats), jnp.float32),
            pltpu.VMEM((8, lats), jnp.int32),
            pltpu.VMEM((2, tags, levels, 8, lats), jnp.float32),
            pltpu.VMEM((pitched(10, levels, 8), LANES), jnp.float32),
            pltpu.VMEM((pitched(4 * tags, levels, 8), LANES), jnp.float32),
            pltpu.SemaphoreType.DMA((6 + 2 * tags,)),
        ],
        compiler_params=pltpu.CompilerParams(vmem_limit_bytes=24 << 20),
        cost_estimate=SHORT,
        name="pack_edges",
    )(lam, *fields, top)


def chosen(region_row, first_tag, values):
    row = jnp.zeros(region_row.shape, jnp.float32)
    for tag, value in enumerate(values):
        row = jnp.where(region_row == first_tag + tag, value[0:1], row)
    return row


def sweep(t, shape, first_tag, region, coef, load, store, rows):
    tags, _, cols, _ = shape
    low, high = t + 1, cols - t - 1
    chunk = -(-(high - low) // CHUNKS)
    column = lambda c: [load(c, k) for k in range(tags)]

    @pl.loop(0, CHUNKS)
    def _(i):
        start = jnp.minimum(low + i * chunk, high - chunk)
        west, mid = column(start - 1), column(start)
        for j in range(chunk):
            c = start + j
            east = column(c + 1)
            coefs = [coef[c, n] for n in range(6)]
            new = [advance(coefs, mid[k], east[k], west[k]) for k in range(tags)]
            for k in range(tags):
                store(c, k, new[k])
            rows[t, pl.ds(c, 1), :] = chosen(region[pl.ds(c, 1), :], first_tag, new)
            west, mid = mid, east


def loading(ref):
    return lambda c, tag: ref[c, tag]


def storing(ref):
    def store(c, tag, value):
        ref[c, tag] = value

    return store


def storing_rows(ref, tags, levels, pitch):
    def store(c, tag, value):
        for k in range(2):
            at = (k * tags + tag) * levels * pitch + c
            ref[pl.ds(at, levels, stride=pitch), :] = value[:, HALVES[k]]

    return store


def inner_kernel(lam, ew, ed, nw, nd, mf, top, region, *refs):
    coef, l0, l1, l2, l3, final, rows, lam_p, field_p = refs
    tags, levels, cols, lats = lam.shape
    pitch = cols + 1
    slab = levels * pitch

    @pl.loop(0, levels)
    def _(level):
        row = level * pitch
        for f, field in enumerate((ew, ed, nw, nd, mf)):
            for k in range(2):
                field_p[pl.ds((f * 2 + k) * slab + row, cols), :] = field[level, :, HALVES[k]]
        for tag in range(tags):
            for k in range(2):
                at = (k * tags + tag) * slab + row
                lam_p[pl.ds(at, cols), :] = lam[tag, level, :, HALVES[k]]

    def coefficients(c, west):
        ew, ed, nw, nd, mf = (
            column_at(field_p, f * 2 * slab + c, levels, pitch, slab) for f in range(5)
        )
        e, next_west, n, s = faces(ew, ed, nw, nd)
        u = updraft(mf, top[pl.ds(c, 1), :])
        for j, value in enumerate((1.0 - e - west - n - s, e, west, n, s, u)):
            coef[c, j] = value
        return next_west

    def some(i, west):
        for j in range(8):
            west = coefficients(i * 8 + j, west)
        return west

    west = lax.fori_loop(0, cols // 8, some, jnp.zeros((levels, lats), jnp.float32))
    coef[cols, 2] = west

    def given(c, tag):
        return column_at(lam_p, tag * slab + c, levels, pitch, tags * slab)

    for at, c in enumerate((0, 1, cols - 2, cols - 1)):
        for tag in range(tags):
            l0[at, tag] = given(c, tag)
    last = storing_rows(final, tags, levels, pitch)
    loads = (given, loading(l1), loading(l2), loading(l3))
    stores = (storing(l1), storing(l2), storing(l3), last)
    for t in range(ITERS):
        sweep(t, lam.shape, lax.axis_index("grp") * tags, region, coef, loads[t], stores[t], rows)


def inner(lam, fields, top, region):
    tags, levels, cols, lats = lam.shape
    vmem = pl.BlockSpec(memory_space=pltpu.VMEM)
    state = pltpu.VMEM((cols, tags, levels, lats), jnp.float32)
    return pl.pallas_call(
        inner_kernel,
        in_specs=[vmem] * 8,
        out_specs=[vmem] * 7,
        out_shape=[
            pltpu.VMEM((cols + 1, 6, levels, lats), jnp.float32),
            pltpu.VMEM((4, tags, levels, lats), jnp.float32),
            *[state] * 3,
            pltpu.VMEM((pitched(2 * tags, levels, cols), LANES), jnp.float32),
            pltpu.VMEM((ITERS, cols, lats), jnp.float32),
        ],
        scratch_shapes=[
            pltpu.VMEM((pitched(2 * tags, levels, cols), LANES), jnp.float32),
            pltpu.VMEM((pitched(10, levels, cols), LANES), jnp.float32),
        ],
        compiler_params=pltpu.CompilerParams(vmem_limit_bytes=32 << 20),
        cost_estimate=SHORT,
        name="inner_steps",
    )(lam, *fields, top, region)


def slot(c, cols):
    return (LOW, c + EDGE - 1) if c < EDGE else (HIGH, c - (cols - EDGE))


def outer_kernel(cols, first, second, coef, own, mate, across, aslant, wide, halo, entry):
    halo[1 - parity()] = first[...]
    halo[parity()] = second[...]
    half = coef_half()
    odd_rank = lax.rem(lax.axis_index("grp"), 2)
    for rank, near, far in ((0, mate, aslant), (1, own, across)):

        @pl.when(odd_rank == rank)
        def _():
            entry[coef_side(half)] = near[...]
            entry[coef_side(1 - half)] = far[...]

    def slab(side, e):
        return entry[side, e]

    for side in (LOW, HIGH):
        for i in range(EDGE - 1):
            w, e, n, s, u = (slab(side, 5 * i + j) for j in range(5))
            if side == HIGH and i == 0:
                w = coef[cols, 2]
            for j, value in enumerate((1.0 - e - w - n - s, e, w, n, s, u)):
                wide[side, i + EDGE * side, j] = value
    first_west = slab(LOW, ENTRIES - 1)
    e, n, s, u = (coef[0, j] for j in (1, 3, 4, 5))
    for j, value in enumerate((1.0 - e - first_west - n - s, e, first_west, n, s, u)):
        wide[*slot(0, cols), j] = value


def outer_parts(first, second, coef, pieces):
    levels, lats = coef.shape[2:]
    vmem = pl.BlockSpec(memory_space=pltpu.VMEM)
    return pl.pallas_call(
        functools.partial(outer_kernel, coef.shape[0] - 1),
        in_specs=[vmem] * 7,
        out_specs=[vmem] * 2,
        out_shape=[
            pltpu.VMEM((2, 2 * EDGE - 1, 6, levels, lats), jnp.float32),
            pltpu.VMEM((2, *first.shape), jnp.float32),
        ],
        scratch_shapes=[pltpu.VMEM((2, ENTRIES, levels, lats), jnp.float32)],
        compiler_params=pltpu.CompilerParams(vmem_limit_bytes=24 << 20),
        cost_estimate=SHORT,
        name="outer_parts",
    )(first, second, coef, *pieces)


def border_steps(
    depth, region, coef, wide, kept, l0, halo, work, rows=None, store=None, finish=None
):
    cols, tags, levels, lats = kept[1].shape
    first_tag = lax.axis_index("grp") * tags
    part = slice(0, depth)

    def coefs_at(c):
        if 0 < c < cols:
            return [coef[c, j, part] for j in range(6)]
        return [wide[*slot(c, cols), j, part] for j in range(6)]

    def state(t, c, tag):
        if t == 0:
            if c < 0:
                return halo[LOW, tag * EDGE + c + EDGE, part]
            if c >= cols:
                return halo[HIGH, tag * EDGE + c - cols, part]
            return l0[c if c < 2 else c - (cols - 4), tag, part]
        if t <= c < cols - t:
            return kept[t][c, tag, part]
        return work[t, *slot(c, cols), tag]

    def column(t, c):
        return [state(t, c, tag) for tag in range(tags)]

    for t in range(ITERS if store is None else ITERS - 1):
        reach = EDGE - 1 - t
        for run in (range(-reach, t + 1), range(cols - t - 1, cols + reach)):
            west, mid = column(t, run[0] - 1), column(t, run[0])
            for c in run:
                east = column(t, c + 1)
                coefs = coefs_at(c)
                new = [advance(coefs, mid[k], east[k], west[k]) for k in range(tags)]
                if t < ITERS - 1:
                    for k in range(tags):
                        work[t + 1, *slot(c, cols), k] = new[k]
                if rows is not None and 0 <= c < cols:
                    rows[t, c : c + 1, :] = chosen(region[c : c + 1, :], first_tag, new)
                west, mid = mid, east
    if store is None:
        return
    t = ITERS - 1
    for k in range(tags):
        for c in [*range(EDGE), *range(cols - EDGE, cols)]:
            near = [state(t, at, k) for at in (c, c + 1, c - 1)]
            store(c, k, advance(coefs_at(c), *near))
        finish(k)


def low_kernel(region, coef, wide, halo, l0, l1, l2, l3, rows_in, grad, work, rows):
    rows[...] = rows_in[...]
    kept = (None, l1, l2, l3)
    border_steps(8, region, coef, wide, kept, l0, halo, work, rows)
    total = rows[0]
    for t in range(1, ITERS):
        total = total + rows[t]
    grad[...] = total


def border_scratch(tags, depth, lats):
    return pltpu.VMEM((ITERS, 2, 2 * EDGE - 1, tags, depth, lats), jnp.float32)


def gradient(region, coef, wide, halo, states, rows):
    cols, tags, levels, lats = states[1].shape
    vmem = pl.BlockSpec(memory_space=pltpu.VMEM)
    operands = [region, coef, wide, halo, *states, rows]
    return pl.pallas_call(
        low_kernel,
        in_specs=[vmem] * len(operands),
        out_specs=vmem,
        out_shape=pltpu.VMEM((cols, lats), jnp.float32),
        scratch_shapes=[
            border_scratch(tags, 8, lats),
            pltpu.VMEM((ITERS, cols, lats), jnp.float32),
        ],
        compiler_params=pltpu.CompilerParams(vmem_limit_bytes=32 << 20),
        cost_estimate=SHORT,
        name="border_low_levels",
    )(*operands)


def border_kernel(coef, wide, halo, l0, l1, l2, l3, *refs):
    final_in, out_in, final, out, work, sides, sems = refs
    cols, tags, levels, lats = l1.shape
    pitch = cols + 1
    store = storing_rows(final, tags, levels, pitch)
    kept = (None, l1, l2, l3)
    copies = []

    def finish(tag):
        @pl.loop(0, levels // 8)
        def _(i):
            for j in range(8):
                level = i * 8 + j
                for k in range(2):
                    at = ((k * tags + tag) * levels + level) * pitch
                    for side, c in enumerate((0, cols - 8)):
                        sides[side, tag, level, :, HALVES[k]] = final[pl.ds(at + c, 8), :]

        for side, c in enumerate((0, cols - 8)):
            copies.append(
                pltpu.make_async_copy(
                    sides.at[side, tag], out.at[tag, :, pl.ds(c, 8)], sems.at[len(copies)]
                )
            )
            copies[-1].start()

    border_steps(levels, None, coef, wide, kept, l0, halo, work, None, store, finish)
    for c in copies:
        c.wait()


def border(coef, wide, halo, states, final, out):
    cols, tags, levels, lats = states[1].shape
    vmem = pl.BlockSpec(memory_space=pltpu.VMEM)
    hbm = pl.BlockSpec(memory_space=pltpu.HBM)
    operands = [coef, wide, halo, *states]
    n = len(operands)
    return pl.pallas_call(
        border_kernel,
        in_specs=[vmem] * (n + 1) + [hbm],
        out_specs=[vmem, hbm],
        out_shape=[
            pltpu.VMEM(final.shape, jnp.float32),
            pltpu.HBM(out.shape, jnp.float32),
        ],
        input_output_aliases={n: 0, n + 1: 1},
        scratch_shapes=[
            border_scratch(tags, levels, lats),
            pltpu.VMEM((2, tags, levels, 8, lats), jnp.float32),
            pltpu.SemaphoreType.DMA((2 * tags,)),
        ],
        compiler_params=pltpu.CompilerParams(vmem_limit_bytes=32 << 20),
        cost_estimate=SHORT,
        name="border_all_levels",
    )(*operands, final, out)[1]


def write_kernel(final, out, block, sems):
    tags, levels, cols, _ = out.shape
    pitch = cols + 1
    copies = []
    for tag in range(tags):

        @pl.loop(0, levels)
        def _(level):
            for k in range(2):
                at = ((k * tags + tag) * levels + level) * pitch + 8
                block[tag, level, :, HALVES[k]] = final[pl.ds(at, cols - 16), :]

        copies.append(
            pltpu.make_async_copy(
                block.at[tag], out.at[tag, :, pl.ds(8, cols - 16)], sems.at[tag]
            )
        )
        copies[-1].start()
    for c in copies:
        c.wait()


def write_inner(final, shape):
    tags, levels, cols, lats = shape
    return pl.pallas_call(
        write_kernel,
        in_specs=[pl.BlockSpec(memory_space=pltpu.VMEM)],
        out_specs=pl.BlockSpec(memory_space=pltpu.HBM),
        out_shape=pltpu.HBM(shape, jnp.float32),
        scratch_shapes=[
            pltpu.VMEM((tags, levels, cols - 16, lats), jnp.float32),
            pltpu.SemaphoreType.DMA((tags,)),
        ],
        compiler_params=pltpu.CompilerParams(vmem_limit_bytes=24 << 20),
        cost_estimate=SHORT,
        name="write_inner",
    )(final)


def local(lam, east_wind, north_wind, east_diff, north_diff, mass_flux, region, top):
    groups, tiles = lax.axis_size("grp"), lax.axis_size("dom")
    own = (lam, east_wind, east_diff, north_wind, north_diff, mass_flux)
    far = [pltpu.with_memory_space_constraint(value, pltpu.HBM) for value in (*own, top)]

    pairs = lambda i: i ^ 1
    turn = lambda i: (((i - 1) % tiles ^ 1) + 1) % tiles
    coefs, first, second = pack(far[0], far[1:6], far[6])

    senders = [i for i in range(tiles * groups) if i % 2]

    def partner(i):
        tile, rank = divmod(i, groups)
        return (turn if rank % 4 // 2 else pairs)(tile) * groups + rank

    coefs = lax.ppermute(coefs, ("dom", "grp"), [(i, partner(i)) for i in senders])
    first = swapped(first, "dom", pairs)
    second = swapped(second, "dom", turn)
    odd_ranks = range(1, groups, 2)
    pieces = [coefs] + [
        lax.ppermute(coefs, "grp", [(i, i ^ by) for i in odd_ranks]) for by in (1, 2, 3)
    ]
    coef, *states, final, rows = inner(own[0], own[1:], top, region)
    out = write_inner(final, lam.shape)
    coef, out = lax.optimization_barrier((coef, out))
    wide, halo = outer_parts(first, second, coef, pieces)
    grad = gradient(region, coef, wide, halo, states, rows)
    grad, wide = lax.optimization_barrier((grad, wide))
    out = border(coef, wide, halo, states, final, out)
    share = grad
    for by in range(1, groups):
        grad = grad + swapped(share, "grp", lambda i: i ^ by)
    return out, grad


def solution(mesh):
    return jax.shard_map(
        local,
        mesh=mesh,
        in_specs=(
            P("grp", None, "dom", None),
            P(None, "dom", None),
            P(None, "dom", None),
            P(None, "dom", None),
            P(None, "dom", None),
            P(None, "dom", None),
            P("dom", None),
            P("dom", None),
        ),
        out_specs=(P("grp", None, "dom", None), P("dom", None)),
        check_vma=False,
    )
```

```python
import functools

import jax
import jax.numpy as jnp
from jax import lax
from jax.experimental import pallas as pl
from jax.experimental.pallas import tpu as pltpu
from jax.sharding import PartitionSpec as P

ITERS = 4
EDGE = ITERS
ENTRIES = 16
BLOCK = 4
CHUNKS = 2
LANES = 128
HALVES = (slice(0, LANES), slice(LANES, 2 * LANES))
SHORT = pl.CostEstimate(flops=1000, bytes_accessed=1000, transcendentals=0)
LOW, HIGH = 0, 1

def swapped(value, axis, partner):
    return lax.ppermute(value, axis, [(i, partner(i)) for i in range(lax.axis_size(axis))])


def faces(ew, ed, nw, nd):
    lats = ew.shape[1]
    lat = lax.broadcasted_iota(jnp.int32, ew.shape, 1)
    east = jnp.maximum(ew, 0.0) + ed
    west_next = jnp.maximum(-ew, 0.0) + ed
    north = jnp.where(lat < lats - 1, jnp.maximum(nw, 0.0) + nd, 0.0)
    south = jnp.maximum(-nw, 0.0) + nd
    south = jnp.where(lat > 0, pltpu.roll(south, 1, 1), 0.0)
    return east, west_next, north, south


def updraft(mf, top_row):
    levels = mf.shape[0]
    level = lax.broadcasted_iota(jnp.int32, mf.shape, 0)
    return jnp.where((level < top_row) & (level < levels - 1), mf, 0.0)


def parity():
    return lax.rem(lax.axis_index("dom"), 2)


def level_above(h):
    if h.shape[0] == 8:
        return pltpu.roll(h, 7, 0)
    parts = [pltpu.roll(h[at : at + 8], 7, 0) for at in range(0, h.shape[0], 8)]
    inside = lax.broadcasted_iota(jnp.int32, parts[0].shape, 0) < 7
    joined = [jnp.where(inside, low, high) for low, high in zip(parts, parts[1:])]
    return jnp.concatenate([*joined, parts[-1]], axis=0)


def advance(coefs, mid, east, west):
    d, e, w, n, s, u = coefs
    h = d * mid + e * east + w * west
    lane = lax.broadcasted_iota(jnp.int32, (mid.shape[0], LANES), 1)
    north = [pltpu.roll(mid[:, part], LANES - 1, 1) for part in HALVES]
    south = [pltpu.roll(mid[:, part], 1, 1) for part in HALVES]
    north = jnp.concatenate([jnp.where(lane < LANES - 1, *north), north[1]], axis=1)
    south = jnp.concatenate([south[0], jnp.where(lane > 0, south[1], south[0])], axis=1)
    h = h + n * north + s * south
    return h + u * (level_above(h) - h)


def pitched(slabs, levels, width):
    return -(-(slabs * levels * (width + 1) + width + 8) // 8) * 8


def column_at(ref, start, levels, pitch, apart):
    parts = [ref[pl.ds(start + apart * k, levels, stride=pitch), :] for k in range(2)]
    return jnp.concatenate(parts, axis=1)


def coef_side(rank):
    return lax.rem(1 - parity() + rank, 2)


def coef_half(rank):
    return lax.rem(lax.div(rank, 2), 2)


def pack_kernel(lam, ew, ed, nw, nd, mf, top, *refs):
    coef_send, lam_first, lam_second = refs[:3]
    field_s, top_s, lam_s, coef_p, lam_p, sems = refs[3:]
    tags, levels, cols, lats = lam.shape
    per = levels // 2
    rank = lax.axis_index("grp")
    base = coef_half(rank) * per
    high = coef_side(rank)
    edge = pl.ds(pl.multiple_of(high * (cols - 8), 8), 8)
    copies = []

    def copy(src, dst):
        copies.append(pltpu.make_async_copy(src, dst, sems.at[len(copies)]))
        copies[-1].start()

    for f, field in enumerate((ew, ed, nw, nd, mf)):
        copy(field.at[pl.ds(base, per), edge], field_s.at[f])
    copy(top.at[edge], top_s)
    for side, at in ((LOW, 0), (HIGH, cols - 8)):
        for tag in range(tags):
            copy(lam.at[tag, :, pl.ds(at, 8)], lam_s.at[side, tag])
    for c in copies[:6]:
        c.wait()
    pitch = 9
    few = per * pitch

    @pl.loop(0, per // 2)
    def _(pair):
        for half in range(2):
            i = pair * 2 + half
            level = base + i
            ew, ed, nw, nd, mf = (field_s[f, i] for f in range(5))
            lift = jnp.where((level < top_s[...]) & (level < levels - 1), mf, 0.0)
            for j, value in enumerate((*faces(ew, ed, nw, nd), lift)):
                for k in range(2):
                    at = (j * 2 + k) * few + i * pitch
                    coef_p[pl.ds(at, 8), :] = value[:, HALVES[k]]

    def coef_column(j, c):
        return column_at(coef_p, j * 2 * few + c, per, pitch, few)

    start = 8 - EDGE
    c = high * (start + 1)
    coef_send[0] = coef_column(1, jnp.maximum(c - 1, 0))
    for i in range(EDGE - 1):
        for n, j in enumerate((0, 2, 3, 4, 1)):
            coef_send[5 * i + 1 + n] = coef_column(j, c + i)

    odd = parity()
    for c in copies[6:]:
        c.wait()
    slab = levels * pitch

    @pl.loop(0, levels)
    def _(level):
        for side in (LOW, HIGH):
            for tag in range(tags):
                for k in range(2):
                    at = ((side * 2 + k) * tags + tag) * slab + level * pitch
                    lam_p[pl.ds(at, 8), :] = lam_s[side, tag, level, :, HALVES[k]]

    for dest, side in ((lam_first, 1 - odd), (lam_second, odd)):
        at = side * (2 * tags * slab + start)
        for tag in range(tags):
            for c in range(EDGE):
                dest[tag * EDGE + c] = column_at(
                    lam_p, at + tag * slab + c, levels, pitch, tags * slab
                )


def pack(lam, fields, top):
    tags, levels, cols, lats = lam.shape
    per = levels // 2
    hbm = pl.BlockSpec(memory_space=pltpu.HBM)
    coef_send = pltpu.VMEM((ENTRIES, per, lats), jnp.float32)
    lam_send = pltpu.VMEM((tags * EDGE, levels, lats), jnp.float32)
    return pl.pallas_call(
        pack_kernel,
        in_specs=[hbm] * 7,
        out_specs=[pl.BlockSpec(memory_space=pltpu.VMEM)] * 3,
        out_shape=[coef_send, lam_send, lam_send],
        scratch_shapes=[
            pltpu.VMEM((5, per, 8, lats), jnp.float32),
            pltpu.VMEM((8, lats), jnp.int32),
            pltpu.VMEM((2, tags, levels, 8, lats), jnp.float32),
            pltpu.VMEM((pitched(10, per, 8), LANES), jnp.float32),
            pltpu.VMEM((pitched(4 * tags, levels, 8), LANES), jnp.float32),
            pltpu.SemaphoreType.DMA((6 + 2 * tags,)),
        ],
        compiler_params=pltpu.CompilerParams(vmem_limit_bytes=24 << 20),
        cost_estimate=SHORT,
        name="pack_edges",
    )(lam, *fields, top)


def chosen(region_row, first_tag, values):
    row = jnp.zeros(region_row.shape, jnp.float32)
    for tag, value in enumerate(values):
        row = jnp.where(region_row == first_tag + tag, value[0:1], row)
    return row


def sweep(t, shape, first_tag, region, coef, load, store, rows):
    tags, _, cols, _ = shape
    low, high = t + 1, cols - t - 1
    chunk = -(-(high - low) // CHUNKS)
    column = lambda c: [load(c, k) for k in range(tags)]

    @pl.loop(0, CHUNKS)
    def _(i):
        start = jnp.minimum(low + i * chunk, high - chunk)
        west, mid = column(start - 1), column(start)
        for j in range(chunk):
            c = start + j
            east = column(c + 1)
            coefs = [coef[c, n] for n in range(6)]
            new = [advance(coefs, mid[k], east[k], west[k]) for k in range(tags)]
            for k in range(tags):
                store(c, k, new[k])
            rows[t, pl.ds(c, 1), :] = chosen(region[pl.ds(c, 1), :], first_tag, new)
            west, mid = mid, east


def loading(ref):
    return lambda c, tag: ref[c, tag]


def storing(ref):
    def store(c, tag, value):
        ref[c, tag] = value

    return store


def storing_rows(ref, tags, levels, pitch):
    def store(c, tag, value):
        for k in range(2):
            at = (k * tags + tag) * levels * pitch + c
            ref[pl.ds(at, levels, stride=pitch), :] = value[:, HALVES[k]]

    return store


def prepare_kernel(lam, ew, ed, nw, nd, mf, top, region, coef, l0, l1, l2, rows, lam_p, field_p):
    tags, levels, cols, lats = lam.shape
    pitch = cols + 1
    slab = levels * pitch

    @pl.loop(0, levels)
    def _(level):
        row = level * pitch
        for f, field in enumerate((ew, ed, nw, nd, mf)):
            for k in range(2):
                field_p[pl.ds((f * 2 + k) * slab + row, cols), :] = field[level, :, HALVES[k]]
        for tag in range(tags):
            for k in range(2):
                at = (k * tags + tag) * slab + row
                lam_p[pl.ds(at, cols), :] = lam[tag, level, :, HALVES[k]]

    def coefficients(c, west):
        ew, ed, nw, nd, mf = (
            column_at(field_p, f * 2 * slab + c, levels, pitch, slab) for f in range(5)
        )
        e, next_west, n, s = faces(ew, ed, nw, nd)
        u = updraft(mf, top[pl.ds(c, 1), :])
        for j, value in enumerate((1.0 - e - west - n - s, e, west, n, s, u)):
            coef[c, j] = value
        return next_west

    def some(i, west):
        for j in range(8):
            west = coefficients(i * 8 + j, west)
        return west

    west = lax.fori_loop(0, cols // 8, some, jnp.zeros((levels, lats), jnp.float32))
    coef[cols, 2] = west
    for at, c in enumerate((0, 1, cols - 2, cols - 1)):
        for tag in range(tags):
            l0[at, tag] = column_at(lam_p, tag * slab + c, levels, pitch, tags * slab)

    def given(c, tag):
        return column_at(lam_p, tag * slab + c, levels, pitch, tags * slab)

    first_tag = lax.axis_index("grp") * tags
    sweep(0, lam.shape, first_tag, region, coef, given, storing(l1), rows)
    sweep(1, lam.shape, first_tag, region, coef, loading(l1), storing(l2), rows)


def prepare(lam, fields, top, region):
    tags, levels, cols, lats = lam.shape
    vmem = pl.BlockSpec(memory_space=pltpu.VMEM)
    state = pltpu.VMEM((cols, tags, levels, lats), jnp.float32)
    return pl.pallas_call(
        prepare_kernel,
        in_specs=[vmem] * 8,
        out_specs=[vmem] * 5,
        out_shape=[
            pltpu.VMEM((cols + 1, 6, levels, lats), jnp.float32),
            pltpu.VMEM((4, tags, levels, lats), jnp.float32),
            state,
            state,
            pltpu.VMEM((2, cols, lats), jnp.float32),
        ],
        scratch_shapes=[
            pltpu.VMEM((pitched(2 * tags, levels, cols), LANES), jnp.float32),
            pltpu.VMEM((pitched(10, levels, cols), LANES), jnp.float32),
        ],
        compiler_params=pltpu.CompilerParams(vmem_limit_bytes=32 << 20),
        cost_estimate=SHORT,
        name="first_steps",
    )(lam, *fields, top, region)


def inner_kernel(coef, l2, region, rows_in, l3, final, rows):
    cols, tags, levels, lats = l2.shape
    rows[0:2] = rows_in[...]
    shape = (tags, levels, cols, lats)
    first_tag = lax.axis_index("grp") * tags
    last = storing_rows(final, tags, levels, cols + 1)
    sweep(2, shape, first_tag, region, coef, loading(l2), storing(l3), rows)
    sweep(3, shape, first_tag, region, coef, loading(l3), last, rows)


def inner(coef, l2, region, rows):
    cols, tags, levels, lats = l2.shape
    vmem = pl.BlockSpec(memory_space=pltpu.VMEM)
    return pl.pallas_call(
        inner_kernel,
        in_specs=[vmem] * 4,
        out_specs=[vmem] * 3,
        out_shape=[
            pltpu.VMEM(l2.shape, jnp.float32),
            pltpu.VMEM((pitched(2 * tags, levels, cols), LANES), jnp.float32),
            pltpu.VMEM((ITERS, cols, lats), jnp.float32),
        ],
        compiler_params=pltpu.CompilerParams(vmem_limit_bytes=32 << 20),
        cost_estimate=SHORT,
        name="inner_steps",
    )(coef, l2, region, rows)


def slot(c, cols):
    return (LOW, c + EDGE - 1) if c < EDGE else (HIGH, c - (cols - EDGE))


def outer_kernel(cols, coef, *refs):
    pieces, wide, entry = refs[:BLOCK], refs[BLOCK], refs[BLOCK + 1]
    per = coef.shape[2] // 2
    for by in range(BLOCK):
        rank = lax.axis_index("grp") ^ by
        rows = pl.ds(pl.multiple_of(coef_half(rank) * per, 8), per)
        entry[coef_side(rank), :, rows] = pieces[by][...]

    def slab(side, e):
        return entry[side, e]

    for side in (LOW, HIGH):
        for i in range(EDGE - 1):
            w, e, n, s, u = (slab(side, 5 * i + j) for j in range(5))
            if side == HIGH and i == 0:
                w = coef[cols, 2]
            for j, value in enumerate((1.0 - e - w - n - s, e, w, n, s, u)):
                wide[side, i + EDGE * side, j] = value
    first_west = slab(LOW, ENTRIES - 1)
    e, n, s, u = (coef[0, j] for j in (1, 3, 4, 5))
    for j, value in enumerate((1.0 - e - first_west - n - s, e, first_west, n, s, u)):
        wide[*slot(0, cols), j] = value


def outer_coefs(cols, coef, pieces):
    _, _, levels, lats = coef.shape
    vmem = pl.BlockSpec(memory_space=pltpu.VMEM)
    return pl.pallas_call(
        functools.partial(outer_kernel, cols),
        in_specs=[vmem] * (1 + BLOCK),
        out_specs=vmem,
        out_shape=pltpu.VMEM((2, 2 * EDGE - 1, 6, levels, lats), jnp.float32),
        scratch_shapes=[pltpu.VMEM((2, ENTRIES, levels, lats), jnp.float32)],
        compiler_params=pltpu.CompilerParams(vmem_limit_bytes=24 << 20),
        cost_estimate=SHORT,
        name="outer_coefs",
    )(coef, *pieces)


def border_steps(
    depth, region, coef, wide, kept, l0, halos, halo, work, rows=None, store=None, finish=None
):
    cols, tags, levels, lats = kept[1].shape
    first_tag = lax.axis_index("grp") * tags
    part = slice(0, depth)
    halo[1 - parity()] = halos[0][:, part]
    halo[parity()] = halos[1][:, part]

    def coefs_at(c):
        if 0 < c < cols:
            return [coef[c, j, part] for j in range(6)]
        return [wide[*slot(c, cols), j, part] for j in range(6)]

    def state(t, c, tag):
        if t == 0:
            if c < 0:
                return halo[LOW, tag * EDGE + c + EDGE]
            if c >= cols:
                return halo[HIGH, tag * EDGE + c - cols]
            return l0[c if c < 2 else c - (cols - 4), tag, part]
        if t <= c < cols - t:
            return kept[t][c, tag, part]
        return work[t, *slot(c, cols), tag]

    def column(t, c):
        return [state(t, c, tag) for tag in range(tags)]

    for t in range(ITERS if store is None else ITERS - 1):
        reach = EDGE - 1 - t
        for run in (range(-reach, t + 1), range(cols - t - 1, cols + reach)):
            west, mid = column(t, run[0] - 1), column(t, run[0])
            for c in run:
                east = column(t, c + 1)
                coefs = coefs_at(c)
                new = [advance(coefs, mid[k], east[k], west[k]) for k in range(tags)]
                if t < ITERS - 1:
                    for k in range(tags):
                        work[t + 1, *slot(c, cols), k] = new[k]
                if rows is not None and 0 <= c < cols:
                    rows[t, c : c + 1, :] = chosen(region[c : c + 1, :], first_tag, new)
                west, mid = mid, east
    if store is None:
        return
    t = ITERS - 1
    for k in range(tags):
        for c in [*range(EDGE), *range(cols - EDGE, cols)]:
            near = [state(t, at, k) for at in (c, c + 1, c - 1)]
            store(c, k, advance(coefs_at(c), *near))
        finish(k)


def low_kernel(region, coef, wide, l0, l1, l2, l3, first, second, rows_in, grad, halo, work, rows):
    rows[...] = rows_in[...]
    kept = (None, l1, l2, l3)
    border_steps(8, region, coef, wide, kept, l0, (first, second), halo, work, rows)
    total = rows[0]
    for t in range(1, ITERS):
        total = total + rows[t]
    grad[...] = total


def border_scratch(tags, depth, lats):
    return [
        pltpu.VMEM((2, tags * EDGE, depth, lats), jnp.float32),
        pltpu.VMEM((ITERS, 2, 2 * EDGE - 1, tags, depth, lats), jnp.float32),
    ]


def gradient(region, coef, wide, states, halos, rows):
    cols, tags, levels, lats = states[1].shape
    vmem = pl.BlockSpec(memory_space=pltpu.VMEM)
    operands = [region, coef, wide, *states, *halos, rows]
    return pl.pallas_call(
        low_kernel,
        in_specs=[vmem] * len(operands),
        out_specs=vmem,
        out_shape=pltpu.VMEM((cols, lats), jnp.float32),
        scratch_shapes=[
            *border_scratch(tags, 8, lats),
            pltpu.VMEM((ITERS, cols, lats), jnp.float32),
        ],
        compiler_params=pltpu.CompilerParams(vmem_limit_bytes=32 << 20),
        cost_estimate=SHORT,
        name="border_low_levels",
    )(*operands)


def border_kernel(coef, wide, l0, l1, l2, l3, first, second, *refs):
    final_in, out_in, final, out, halo, work, sides, sems = refs
    cols, tags, levels, lats = l1.shape
    pitch = cols + 1
    store = storing_rows(final, tags, levels, pitch)
    kept = (None, l1, l2, l3)
    copies = []

    def finish(tag):
        @pl.loop(0, levels // 8)
        def _(i):
            for j in range(8):
                level = i * 8 + j
                for k in range(2):
                    at = ((k * tags + tag) * levels + level) * pitch
                    for side, c in enumerate((0, cols - 8)):
                        sides[side, tag, level, :, HALVES[k]] = final[pl.ds(at + c, 8), :]

        for side, c in enumerate((0, cols - 8)):
            copies.append(
                pltpu.make_async_copy(
                    sides.at[side, tag], out.at[tag, :, pl.ds(c, 8)], sems.at[len(copies)]
                )
            )
            copies[-1].start()

    border_steps(
        levels, None, coef, wide, kept, l0, (first, second), halo, work, None, store, finish
    )
    for c in copies:
        c.wait()


def border(coef, wide, states, halos, final, out):
    cols, tags, levels, lats = states[1].shape
    vmem = pl.BlockSpec(memory_space=pltpu.VMEM)
    hbm = pl.BlockSpec(memory_space=pltpu.HBM)
    operands = [coef, wide, *states, *halos]
    n = len(operands)
    return pl.pallas_call(
        border_kernel,
        in_specs=[vmem] * (n + 1) + [hbm],
        out_specs=[vmem, hbm],
        out_shape=[
            pltpu.VMEM(final.shape, jnp.float32),
            pltpu.HBM(out.shape, jnp.float32),
        ],
        input_output_aliases={n: 0, n + 1: 1},
        scratch_shapes=[
            *border_scratch(tags, levels, lats),
            pltpu.VMEM((2, tags, levels, 8, lats), jnp.float32),
            pltpu.SemaphoreType.DMA((2 * tags,)),
        ],
        compiler_params=pltpu.CompilerParams(vmem_limit_bytes=32 << 20),
        cost_estimate=SHORT,
        name="border_all_levels",
    )(*operands, final, out)[1]


def write_kernel(final, out, block, sems):
    tags, levels, cols, _ = out.shape
    pitch = cols + 1
    copies = []
    for tag in range(tags):

        @pl.loop(0, levels)
        def _(level):
            for k in range(2):
                at = ((k * tags + tag) * levels + level) * pitch + 8
                block[tag, level, :, HALVES[k]] = final[pl.ds(at, cols - 16), :]

        copies.append(
            pltpu.make_async_copy(
                block.at[tag], out.at[tag, :, pl.ds(8, cols - 16)], sems.at[tag]
            )
        )
        copies[-1].start()
    for c in copies:
        c.wait()


def write_inner(final, shape):
    tags, levels, cols, lats = shape
    return pl.pallas_call(
        write_kernel,
        in_specs=[pl.BlockSpec(memory_space=pltpu.VMEM)],
        out_specs=pl.BlockSpec(memory_space=pltpu.HBM),
        out_shape=pltpu.HBM(shape, jnp.float32),
        scratch_shapes=[
            pltpu.VMEM((tags, levels, cols - 16, lats), jnp.float32),
            pltpu.SemaphoreType.DMA((tags,)),
        ],
        compiler_params=pltpu.CompilerParams(vmem_limit_bytes=24 << 20),
        cost_estimate=SHORT,
        name="write_inner",
    )(final)


def local(lam, east_wind, north_wind, east_diff, north_diff, mass_flux, region, top):
    groups, tiles = lax.axis_size("grp"), lax.axis_size("dom")
    own = (lam, east_wind, east_diff, north_wind, north_diff, mass_flux)
    far = [pltpu.with_memory_space_constraint(value, pltpu.HBM) for value in (*own, top)]

    pairs = lambda i: i ^ 1
    turn = lambda i: (((i - 1) % tiles ^ 1) + 1) % tiles
    coefs, first, second = pack(far[0], far[1:6], far[6])

    def partner(i):
        tile, rank = divmod(i, groups)
        return (turn if rank % 2 else pairs)(tile) * groups + rank

    coefs = swapped(coefs, ("dom", "grp"), partner)
    coef, l0, l1, l2, rows = prepare(own[0], own[1:], top, region)
    second, coef = lax.optimization_barrier((second, coef))
    first = swapped(first, "dom", pairs)
    second = swapped(second, "dom", turn)
    pieces = [coefs]
    for by in range(1, BLOCK):
        pieces.append(swapped(coefs, "grp", lambda i: i ^ by))
    l3, final, rows = inner(coef, l2, region, rows)
    states = [l0, l1, l2, l3]
    wide = outer_coefs(lam.shape[2], coef, pieces)
    out = write_inner(final, lam.shape)
    wide, out = lax.optimization_barrier((wide, out))
    grad = gradient(region, coef, wide, states, (first, second), rows)
    grad, wide = lax.optimization_barrier((grad, wide))
    out = border(coef, wide, states, (first, second), final, out)
    share = grad
    for by in range(1, groups):
        grad = grad + swapped(share, "grp", lambda i: i ^ by)
    return out, grad


def solution(mesh):
    return jax.shard_map(
        local,
        mesh=mesh,
        in_specs=(
            P("grp", None, "dom", None),
            P(None, "dom", None),
            P(None, "dom", None),
            P(None, "dom", None),
            P(None, "dom", None),
            P(None, "dom", None),
            P("dom", None),
            P("dom", None),
        ),
        out_specs=(P("grp", None, "dom", None), P("dom", None)),
        check_vma=False,
    )
```

```python
import functools

import jax
import jax.numpy as jnp
from jax import lax
from jax.experimental import pallas as pl
from jax.experimental.pallas import tpu as pltpu
from jax.sharding import PartitionSpec as P

ITERS = 4
EDGE = ITERS
ENTRIES = 16
BLOCK = 4
CHUNKS = 2
LANES = 128
HALVES = (slice(0, LANES), slice(LANES, 2 * LANES))
SHORT = pl.CostEstimate(flops=1000, bytes_accessed=1000, transcendentals=0)
LOW, HIGH = 0, 1

def swapped(value, axis, partner):
    return lax.ppermute(value, axis, [(i, partner(i)) for i in range(lax.axis_size(axis))])


def faces(ew, ed, nw, nd):
    lats = ew.shape[1]
    lat = lax.broadcasted_iota(jnp.int32, ew.shape, 1)
    east = jnp.maximum(ew, 0.0) + ed
    west_next = jnp.maximum(-ew, 0.0) + ed
    north = jnp.where(lat < lats - 1, jnp.maximum(nw, 0.0) + nd, 0.0)
    south = jnp.maximum(-nw, 0.0) + nd
    south = jnp.where(lat > 0, pltpu.roll(south, 1, 1), 0.0)
    return east, west_next, north, south


def updraft(mf, top_row):
    levels = mf.shape[0]
    level = lax.broadcasted_iota(jnp.int32, mf.shape, 0)
    return jnp.where((level < top_row) & (level < levels - 1), mf, 0.0)


def parity():
    return lax.rem(lax.axis_index("dom"), 2)


def level_above(h):
    if h.shape[0] == 8:
        return pltpu.roll(h, 7, 0)
    parts = [pltpu.roll(h[at : at + 8], 7, 0) for at in range(0, h.shape[0], 8)]
    inside = lax.broadcasted_iota(jnp.int32, parts[0].shape, 0) < 7
    joined = [jnp.where(inside, low, high) for low, high in zip(parts, parts[1:])]
    return jnp.concatenate([*joined, parts[-1]], axis=0)


def advance(coefs, mid, east, west):
    d, e, w, n, s, u = coefs
    h = d * mid + e * east + w * west
    lane = lax.broadcasted_iota(jnp.int32, (mid.shape[0], LANES), 1)
    north = [pltpu.roll(mid[:, part], LANES - 1, 1) for part in HALVES]
    south = [pltpu.roll(mid[:, part], 1, 1) for part in HALVES]
    north = jnp.concatenate([jnp.where(lane < LANES - 1, *north), north[1]], axis=1)
    south = jnp.concatenate([south[0], jnp.where(lane > 0, south[1], south[0])], axis=1)
    h = h + n * north + s * south
    return h + u * (level_above(h) - h)


def pitched(slabs, levels, width):
    return -(-(slabs * levels * (width + 1) + width + 8) // 8) * 8


def column_at(ref, start, levels, pitch, apart):
    parts = [ref[pl.ds(start + apart * k, levels, stride=pitch), :] for k in range(2)]
    return jnp.concatenate(parts, axis=1)


def coef_side(rank):
    return lax.rem(1 - parity() + rank, 2)


def coef_half(rank):
    return lax.rem(lax.div(rank, 2), 2)


def pack_kernel(lam, ew, ed, nw, nd, mf, top, *refs):
    coef_send, lam_first, lam_second = refs[:3]
    field_s, top_s, lam_s, coef_p, lam_p, sems = refs[3:]
    tags, levels, cols, lats = lam.shape
    per = levels // 2
    rank = lax.axis_index("grp")
    base = coef_half(rank) * per
    high = coef_side(rank)
    edge = pl.ds(pl.multiple_of(high * (cols - 8), 8), 8)
    copies = []

    def copy(src, dst):
        copies.append(pltpu.make_async_copy(src, dst, sems.at[len(copies)]))
        copies[-1].start()

    for f, field in enumerate((ew, ed, nw, nd, mf)):
        copy(field.at[pl.ds(base, per), edge], field_s.at[f])
    copy(top.at[edge], top_s)
    for side, at in ((LOW, 0), (HIGH, cols - 8)):
        for tag in range(tags):
            copy(lam.at[tag, :, pl.ds(at, 8)], lam_s.at[side, tag])
    for c in copies[:6]:
        c.wait()
    pitch = 9
    few = per * pitch

    @pl.loop(0, per // 2)
    def _(pair):
        for half in range(2):
            i = pair * 2 + half
            level = base + i
            ew, ed, nw, nd, mf = (field_s[f, i] for f in range(5))
            lift = jnp.where((level < top_s[...]) & (level < levels - 1), mf, 0.0)
            for j, value in enumerate((*faces(ew, ed, nw, nd), lift)):
                for k in range(2):
                    at = (j * 2 + k) * few + i * pitch
                    coef_p[pl.ds(at, 8), :] = value[:, HALVES[k]]

    def coef_column(j, c):
        return column_at(coef_p, j * 2 * few + c, per, pitch, few)

    start = 8 - EDGE
    c = high * (start + 1)
    coef_send[0] = coef_column(1, jnp.maximum(c - 1, 0))
    for i in range(EDGE - 1):
        for n, j in enumerate((0, 2, 3, 4, 1)):
            coef_send[5 * i + 1 + n] = coef_column(j, c + i)

    odd = parity()
    for c in copies[6:]:
        c.wait()
    slab = levels * pitch

    @pl.loop(0, levels)
    def _(level):
        for side in (LOW, HIGH):
            for tag in range(tags):
                for k in range(2):
                    at = ((side * 2 + k) * tags + tag) * slab + level * pitch
                    lam_p[pl.ds(at, 8), :] = lam_s[side, tag, level, :, HALVES[k]]

    for dest, side in ((lam_first, 1 - odd), (lam_second, odd)):
        at = side * (2 * tags * slab + start)
        for tag in range(tags):
            for c in range(EDGE):
                dest[tag * EDGE + c] = column_at(
                    lam_p, at + tag * slab + c, levels, pitch, tags * slab
                )


def pack(lam, fields, top):
    tags, levels, cols, lats = lam.shape
    per = levels // 2
    hbm = pl.BlockSpec(memory_space=pltpu.HBM)
    coef_send = pltpu.VMEM((ENTRIES, per, lats), jnp.float32)
    lam_send = pltpu.VMEM((tags * EDGE, levels, lats), jnp.float32)
    return pl.pallas_call(
        pack_kernel,
        in_specs=[hbm] * 7,
        out_specs=[pl.BlockSpec(memory_space=pltpu.VMEM)] * 3,
        out_shape=[coef_send, lam_send, lam_send],
        scratch_shapes=[
            pltpu.VMEM((5, per, 8, lats), jnp.float32),
            pltpu.VMEM((8, lats), jnp.int32),
            pltpu.VMEM((2, tags, levels, 8, lats), jnp.float32),
            pltpu.VMEM((pitched(10, per, 8), LANES), jnp.float32),
            pltpu.VMEM((pitched(4 * tags, levels, 8), LANES), jnp.float32),
            pltpu.SemaphoreType.DMA((6 + 2 * tags,)),
        ],
        compiler_params=pltpu.CompilerParams(vmem_limit_bytes=24 << 20),
        cost_estimate=SHORT,
        name="pack_edges",
    )(lam, *fields, top)


def chosen(region_row, first_tag, values):
    row = jnp.zeros(region_row.shape, jnp.float32)
    for tag, value in enumerate(values):
        row = jnp.where(region_row == first_tag + tag, value[0:1], row)
    return row


def sweep(t, shape, first_tag, region, coef, load, store, rows):
    tags, _, cols, _ = shape
    low, high = t + 1, cols - t - 1
    chunk = -(-(high - low) // CHUNKS)
    column = lambda c: [load(c, k) for k in range(tags)]

    @pl.loop(0, CHUNKS)
    def _(i):
        start = jnp.minimum(low + i * chunk, high - chunk)
        west, mid = column(start - 1), column(start)
        for j in range(chunk):
            c = start + j
            east = column(c + 1)
            coefs = [coef[c, n] for n in range(6)]
            new = [advance(coefs, mid[k], east[k], west[k]) for k in range(tags)]
            for k in range(tags):
                store(c, k, new[k])
            rows[t, pl.ds(c, 1), :] = chosen(region[pl.ds(c, 1), :], first_tag, new)
            west, mid = mid, east


def loading(ref):
    return lambda c, tag: ref[c, tag]


def storing(ref):
    def store(c, tag, value):
        ref[c, tag] = value

    return store


def storing_rows(ref, tags, levels, pitch):
    def store(c, tag, value):
        for k in range(2):
            at = (k * tags + tag) * levels * pitch + c
            ref[pl.ds(at, levels, stride=pitch), :] = value[:, HALVES[k]]

    return store


def prepare_kernel(lam, ew, ed, nw, nd, mf, top, region, coef, l0, l1, rows, lam_p, field_p):
    tags, levels, cols, lats = lam.shape
    pitch = cols + 1
    slab = levels * pitch

    @pl.loop(0, levels)
    def _(level):
        row = level * pitch
        for f, field in enumerate((ew, ed, nw, nd, mf)):
            for k in range(2):
                field_p[pl.ds((f * 2 + k) * slab + row, cols), :] = field[level, :, HALVES[k]]
        for tag in range(tags):
            for k in range(2):
                at = (k * tags + tag) * slab + row
                lam_p[pl.ds(at, cols), :] = lam[tag, level, :, HALVES[k]]

    def coefficients(c, west):
        ew, ed, nw, nd, mf = (
            column_at(field_p, f * 2 * slab + c, levels, pitch, slab) for f in range(5)
        )
        e, next_west, n, s = faces(ew, ed, nw, nd)
        u = updraft(mf, top[pl.ds(c, 1), :])
        for j, value in enumerate((1.0 - e - west - n - s, e, west, n, s, u)):
            coef[c, j] = value
        return next_west

    def some(i, west):
        for j in range(8):
            west = coefficients(i * 8 + j, west)
        return west

    west = lax.fori_loop(0, cols // 8, some, jnp.zeros((levels, lats), jnp.float32))
    coef[cols, 2] = west
    for at, c in enumerate((0, 1, cols - 2, cols - 1)):
        for tag in range(tags):
            l0[at, tag] = column_at(lam_p, tag * slab + c, levels, pitch, tags * slab)

    def given(c, tag):
        return column_at(lam_p, tag * slab + c, levels, pitch, tags * slab)

    first_tag = lax.axis_index("grp") * tags
    sweep(0, lam.shape, first_tag, region, coef, given, storing(l1), rows)


def prepare(lam, fields, top, region):
    tags, levels, cols, lats = lam.shape
    vmem = pl.BlockSpec(memory_space=pltpu.VMEM)
    state = pltpu.VMEM((cols, tags, levels, lats), jnp.float32)
    return pl.pallas_call(
        prepare_kernel,
        in_specs=[vmem] * 8,
        out_specs=[vmem] * 4,
        out_shape=[
            pltpu.VMEM((cols + 1, 6, levels, lats), jnp.float32),
            pltpu.VMEM((4, tags, levels, lats), jnp.float32),
            state,
            pltpu.VMEM((1, cols, lats), jnp.float32),
        ],
        scratch_shapes=[
            pltpu.VMEM((pitched(2 * tags, levels, cols), LANES), jnp.float32),
            pltpu.VMEM((pitched(10, levels, cols), LANES), jnp.float32),
        ],
        compiler_params=pltpu.CompilerParams(vmem_limit_bytes=32 << 20),
        cost_estimate=SHORT,
        name="first_steps",
    )(lam, *fields, top, region)


def inner_kernel(coef, l1, region, rows_in, l2, l3, final, rows):
    cols, tags, levels, lats = l1.shape
    rows[0] = rows_in[0]
    shape = (tags, levels, cols, lats)
    first_tag = lax.axis_index("grp") * tags
    last = storing_rows(final, tags, levels, cols + 1)
    sweep(1, shape, first_tag, region, coef, loading(l1), storing(l2), rows)
    sweep(2, shape, first_tag, region, coef, loading(l2), storing(l3), rows)
    sweep(3, shape, first_tag, region, coef, loading(l3), last, rows)


def inner(coef, l1, region, rows):
    cols, tags, levels, lats = l1.shape
    vmem = pl.BlockSpec(memory_space=pltpu.VMEM)
    return pl.pallas_call(
        inner_kernel,
        in_specs=[vmem] * 4,
        out_specs=[vmem] * 4,
        out_shape=[
            pltpu.VMEM(l1.shape, jnp.float32),
            pltpu.VMEM(l1.shape, jnp.float32),
            pltpu.VMEM((pitched(2 * tags, levels, cols), LANES), jnp.float32),
            pltpu.VMEM((ITERS, cols, lats), jnp.float32),
        ],
        compiler_params=pltpu.CompilerParams(vmem_limit_bytes=32 << 20),
        cost_estimate=SHORT,
        name="inner_steps",
    )(coef, l1, region, rows)


def slot(c, cols):
    return (LOW, c + EDGE - 1) if c < EDGE else (HIGH, c - (cols - EDGE))


def outer_kernel(cols, coef, *refs):
    pieces, wide, entry = refs[:BLOCK], refs[BLOCK], refs[BLOCK + 1]
    per = coef.shape[2] // 2
    for by in range(BLOCK):
        rank = lax.axis_index("grp") ^ by
        rows = pl.ds(pl.multiple_of(coef_half(rank) * per, 8), per)
        entry[coef_side(rank), :, rows] = pieces[by][...]

    def slab(side, e):
        return entry[side, e]

    for side in (LOW, HIGH):
        for i in range(EDGE - 1):
            w, e, n, s, u = (slab(side, 5 * i + j) for j in range(5))
            if side == HIGH and i == 0:
                w = coef[cols, 2]
            for j, value in enumerate((1.0 - e - w - n - s, e, w, n, s, u)):
                wide[side, i + EDGE * side, j] = value
    first_west = slab(LOW, ENTRIES - 1)
    e, n, s, u = (coef[0, j] for j in (1, 3, 4, 5))
    for j, value in enumerate((1.0 - e - first_west - n - s, e, first_west, n, s, u)):
        wide[*slot(0, cols), j] = value


def outer_coefs(cols, coef, pieces):
    _, _, levels, lats = coef.shape
    vmem = pl.BlockSpec(memory_space=pltpu.VMEM)
    return pl.pallas_call(
        functools.partial(outer_kernel, cols),
        in_specs=[vmem] * (1 + BLOCK),
        out_specs=vmem,
        out_shape=pltpu.VMEM((2, 2 * EDGE - 1, 6, levels, lats), jnp.float32),
        scratch_shapes=[pltpu.VMEM((2, ENTRIES, levels, lats), jnp.float32)],
        compiler_params=pltpu.CompilerParams(vmem_limit_bytes=24 << 20),
        cost_estimate=SHORT,
        name="outer_coefs",
    )(coef, *pieces)


def border_steps(
    depth, region, coef, wide, kept, l0, halos, halo, work, rows=None, store=None, finish=None
):
    cols, tags, levels, lats = kept[1].shape
    first_tag = lax.axis_index("grp") * tags
    part = slice(0, depth)
    halo[1 - parity()] = halos[0][:, part]
    halo[parity()] = halos[1][:, part]

    def coefs_at(c):
        if 0 < c < cols:
            return [coef[c, j, part] for j in range(6)]
        return [wide[*slot(c, cols), j, part] for j in range(6)]

    def state(t, c, tag):
        if t == 0:
            if c < 0:
                return halo[LOW, tag * EDGE + c + EDGE]
            if c >= cols:
                return halo[HIGH, tag * EDGE + c - cols]
            return l0[c if c < 2 else c - (cols - 4), tag, part]
        if t <= c < cols - t:
            return kept[t][c, tag, part]
        return work[t, *slot(c, cols), tag]

    def column(t, c):
        return [state(t, c, tag) for tag in range(tags)]

    for t in range(ITERS if store is None else ITERS - 1):
        reach = EDGE - 1 - t
        for run in (range(-reach, t + 1), range(cols - t - 1, cols + reach)):
            west, mid = column(t, run[0] - 1), column(t, run[0])
            for c in run:
                east = column(t, c + 1)
                coefs = coefs_at(c)
                new = [advance(coefs, mid[k], east[k], west[k]) for k in range(tags)]
                if t < ITERS - 1:
                    for k in range(tags):
                        work[t + 1, *slot(c, cols), k] = new[k]
                if rows is not None and 0 <= c < cols:
                    rows[t, c : c + 1, :] = chosen(region[c : c + 1, :], first_tag, new)
                west, mid = mid, east
    if store is None:
        return
    t = ITERS - 1
    for k in range(tags):
        for c in [*range(EDGE), *range(cols - EDGE, cols)]:
            near = [state(t, at, k) for at in (c, c + 1, c - 1)]
            store(c, k, advance(coefs_at(c), *near))
        finish(k)


def low_kernel(region, coef, wide, l0, l1, l2, l3, first, second, rows_in, grad, halo, work, rows):
    rows[...] = rows_in[...]
    kept = (None, l1, l2, l3)
    border_steps(8, region, coef, wide, kept, l0, (first, second), halo, work, rows)
    total = rows[0]
    for t in range(1, ITERS):
        total = total + rows[t]
    grad[...] = total


def border_scratch(tags, depth, lats):
    return [
        pltpu.VMEM((2, tags * EDGE, depth, lats), jnp.float32),
        pltpu.VMEM((ITERS, 2, 2 * EDGE - 1, tags, depth, lats), jnp.float32),
    ]


def gradient(region, coef, wide, states, halos, rows):
    cols, tags, levels, lats = states[1].shape
    vmem = pl.BlockSpec(memory_space=pltpu.VMEM)
    operands = [region, coef, wide, *states, *halos, rows]
    return pl.pallas_call(
        low_kernel,
        in_specs=[vmem] * len(operands),
        out_specs=vmem,
        out_shape=pltpu.VMEM((cols, lats), jnp.float32),
        scratch_shapes=[
            *border_scratch(tags, 8, lats),
            pltpu.VMEM((ITERS, cols, lats), jnp.float32),
        ],
        compiler_params=pltpu.CompilerParams(vmem_limit_bytes=32 << 20),
        cost_estimate=SHORT,
        name="border_low_levels",
    )(*operands)


def border_kernel(coef, wide, l0, l1, l2, l3, first, second, *refs):
    final_in, out_in, final, out, halo, work, sides, sems = refs
    cols, tags, levels, lats = l1.shape
    pitch = cols + 1
    store = storing_rows(final, tags, levels, pitch)
    kept = (None, l1, l2, l3)
    copies = []

    def finish(tag):
        @pl.loop(0, levels // 8)
        def _(i):
            for j in range(8):
                level = i * 8 + j
                for k in range(2):
                    at = ((k * tags + tag) * levels + level) * pitch
                    for side, c in enumerate((0, cols - 8)):
                        sides[side, tag, level, :, HALVES[k]] = final[pl.ds(at + c, 8), :]

        for side, c in enumerate((0, cols - 8)):
            copies.append(
                pltpu.make_async_copy(
                    sides.at[side, tag], out.at[tag, :, pl.ds(c, 8)], sems.at[len(copies)]
                )
            )
            copies[-1].start()

    border_steps(
        levels, None, coef, wide, kept, l0, (first, second), halo, work, None, store, finish
    )
    for c in copies:
        c.wait()


def border(coef, wide, states, halos, final, out):
    cols, tags, levels, lats = states[1].shape
    vmem = pl.BlockSpec(memory_space=pltpu.VMEM)
    hbm = pl.BlockSpec(memory_space=pltpu.HBM)
    operands = [coef, wide, *states, *halos]
    n = len(operands)
    return pl.pallas_call(
        border_kernel,
        in_specs=[vmem] * (n + 1) + [hbm],
        out_specs=[vmem, hbm],
        out_shape=[
            pltpu.VMEM(final.shape, jnp.float32),
            pltpu.HBM(out.shape, jnp.float32),
        ],
        input_output_aliases={n: 0, n + 1: 1},
        scratch_shapes=[
            *border_scratch(tags, levels, lats),
            pltpu.VMEM((2, tags, levels, 8, lats), jnp.float32),
            pltpu.SemaphoreType.DMA((2 * tags,)),
        ],
        compiler_params=pltpu.CompilerParams(vmem_limit_bytes=32 << 20),
        cost_estimate=SHORT,
        name="border_all_levels",
    )(*operands, final, out)[1]


def write_kernel(final, out, block, sems):
    tags, levels, cols, _ = out.shape
    pitch = cols + 1
    copies = []
    for tag in range(tags):

        @pl.loop(0, levels)
        def _(level):
            for k in range(2):
                at = ((k * tags + tag) * levels + level) * pitch + 8
                block[tag, level, :, HALVES[k]] = final[pl.ds(at, cols - 16), :]

        copies.append(
            pltpu.make_async_copy(
                block.at[tag], out.at[tag, :, pl.ds(8, cols - 16)], sems.at[tag]
            )
        )
        copies[-1].start()
    for c in copies:
        c.wait()


def write_inner(final, shape):
    tags, levels, cols, lats = shape
    return pl.pallas_call(
        write_kernel,
        in_specs=[pl.BlockSpec(memory_space=pltpu.VMEM)],
        out_specs=pl.BlockSpec(memory_space=pltpu.HBM),
        out_shape=pltpu.HBM(shape, jnp.float32),
        scratch_shapes=[
            pltpu.VMEM((tags, levels, cols - 16, lats), jnp.float32),
            pltpu.SemaphoreType.DMA((tags,)),
        ],
        compiler_params=pltpu.CompilerParams(vmem_limit_bytes=24 << 20),
        cost_estimate=SHORT,
        name="write_inner",
    )(final)


def local(lam, east_wind, north_wind, east_diff, north_diff, mass_flux, region, top):
    groups, tiles = lax.axis_size("grp"), lax.axis_size("dom")
    own = (lam, east_wind, east_diff, north_wind, north_diff, mass_flux)
    far = [pltpu.with_memory_space_constraint(value, pltpu.HBM) for value in (*own, top)]

    pairs = lambda i: i ^ 1
    turn = lambda i: (((i - 1) % tiles ^ 1) + 1) % tiles
    coefs, first, second = pack(far[0], far[1:6], far[6])

    def partner(i):
        tile, rank = divmod(i, groups)
        return (turn if rank % 2 else pairs)(tile) * groups + rank

    coefs = swapped(coefs, ("dom", "grp"), partner)
    coef, l0, l1, rows = prepare(own[0], own[1:], top, region)
    second, coef = lax.optimization_barrier((second, coef))
    first = swapped(first, "dom", pairs)
    second = swapped(second, "dom", turn)
    pieces = [coefs]
    for by in range(1, BLOCK):
        pieces.append(swapped(coefs, "grp", lambda i: i ^ by))
    l2, l3, final, rows = inner(coef, l1, region, rows)
    states = [l0, l1, l2, l3]
    wide = outer_coefs(lam.shape[2], coef, pieces)
    out = write_inner(final, lam.shape)
    wide, out = lax.optimization_barrier((wide, out))
    grad = gradient(region, coef, wide, states, (first, second), rows)
    grad, wide = lax.optimization_barrier((grad, wide))
    out = border(coef, wide, states, (first, second), final, out)
    share = grad
    for by in range(1, groups):
        grad = grad + swapped(share, "grp", lambda i: i ^ by)
    return out, grad


def solution(mesh):
    return jax.shard_map(
        local,
        mesh=mesh,
        in_specs=(
            P("grp", None, "dom", None),
            P(None, "dom", None),
            P(None, "dom", None),
            P(None, "dom", None),
            P(None, "dom", None),
            P(None, "dom", None),
            P("dom", None),
            P("dom", None),
        ),
        out_specs=(P("grp", None, "dom", None), P("dom", None)),
        check_vma=False,
    )
```

```python
import functools

import jax
import jax.numpy as jnp
from jax import lax
from jax.experimental import pallas as pl
from jax.experimental.pallas import tpu as pltpu
from jax.sharding import PartitionSpec as P

ITERS = 4
EDGE = ITERS
ENTRIES = 16
BLOCK = 4
CHUNKS = 2
LANES = 128
HALVES = (slice(0, LANES), slice(LANES, 2 * LANES))
SHORT = pl.CostEstimate(flops=1000, bytes_accessed=1000, transcendentals=0)
LOW, HIGH = 0, 1

def swapped(value, axis, partner):
    return lax.ppermute(value, axis, [(i, partner(i)) for i in range(lax.axis_size(axis))])


def faces(ew, ed, nw, nd):
    lats = ew.shape[1]
    lat = lax.broadcasted_iota(jnp.int32, ew.shape, 1)
    east = jnp.maximum(ew, 0.0) + ed
    west_next = jnp.maximum(-ew, 0.0) + ed
    north = jnp.where(lat < lats - 1, jnp.maximum(nw, 0.0) + nd, 0.0)
    south = jnp.maximum(-nw, 0.0) + nd
    south = jnp.where(lat > 0, pltpu.roll(south, 1, 1), 0.0)
    return east, west_next, north, south


def updraft(mf, top_row):
    levels = mf.shape[0]
    level = lax.broadcasted_iota(jnp.int32, mf.shape, 0)
    return jnp.where((level < top_row) & (level < levels - 1), mf, 0.0)


def parity():
    return lax.rem(lax.axis_index("dom"), 2)


def level_above(h):
    if h.shape[0] == 8:
        return pltpu.roll(h, 7, 0)
    parts = [pltpu.roll(h[at : at + 8], 7, 0) for at in range(0, h.shape[0], 8)]
    inside = lax.broadcasted_iota(jnp.int32, parts[0].shape, 0) < 7
    joined = [jnp.where(inside, low, high) for low, high in zip(parts, parts[1:])]
    return jnp.concatenate([*joined, parts[-1]], axis=0)


def advance(coefs, mid, east, west):
    d, e, w, n, s, u = coefs
    h = d * mid + e * east + w * west
    lane = lax.broadcasted_iota(jnp.int32, (mid.shape[0], LANES), 1)
    north = [pltpu.roll(mid[:, part], LANES - 1, 1) for part in HALVES]
    south = [pltpu.roll(mid[:, part], 1, 1) for part in HALVES]
    north = jnp.concatenate([jnp.where(lane < LANES - 1, *north), north[1]], axis=1)
    south = jnp.concatenate([south[0], jnp.where(lane > 0, south[1], south[0])], axis=1)
    h = h + n * north + s * south
    return h + u * (level_above(h) - h)


def pitched(slabs, levels, width):
    return -(-(slabs * levels * (width + 1) + width + 8) // 8) * 8


def column_at(ref, start, levels, pitch, apart):
    parts = [ref[pl.ds(start + apart * k, levels, stride=pitch), :] for k in range(2)]
    return jnp.concatenate(parts, axis=1)


def coef_side(rank):
    return lax.rem(1 - parity() + rank, 2)


def coef_half(rank):
    return lax.rem(lax.div(rank, 2), 2)


def pack_kernel(lam, ew, ed, nw, nd, mf, top, *refs):
    coef_send, lam_first, lam_second, top_v = refs[:4]
    field_s, lam_s, coef_p, lam_p, sems = refs[4:]
    tags, levels, cols, lats = lam.shape
    per = levels // 2
    rank = lax.axis_index("grp")
    base = coef_half(rank) * per
    high = coef_side(rank)
    edge = pl.ds(pl.multiple_of(high * (cols - 8), 8), 8)
    copies = []

    def copy(src, dst):
        copies.append(pltpu.make_async_copy(src, dst, sems.at[len(copies)]))
        copies[-1].start()

    for f, field in enumerate((ew, ed, nw, nd, mf)):
        copy(field.at[pl.ds(base, per), edge], field_s.at[f])
    copy(top, top_v)
    for side, at in ((LOW, 0), (HIGH, cols - 8)):
        for tag in range(tags):
            copy(lam.at[tag, :, pl.ds(at, 8)], lam_s.at[side, tag])
    for c in copies[:6]:
        c.wait()
    pitch = 9
    few = per * pitch

    @pl.loop(0, per // 2)
    def _(pair):
        for half in range(2):
            i = pair * 2 + half
            level = base + i
            ew, ed, nw, nd, mf = (field_s[f, i] for f in range(5))
            lift = jnp.where((level < top_v[edge]) & (level < levels - 1), mf, 0.0)
            for j, value in enumerate((*faces(ew, ed, nw, nd), lift)):
                for k in range(2):
                    at = (j * 2 + k) * few + i * pitch
                    coef_p[pl.ds(at, 8), :] = value[:, HALVES[k]]

    def coef_column(j, c):
        return column_at(coef_p, j * 2 * few + c, per, pitch, few)

    start = 8 - EDGE
    c = high * (start + 1)
    coef_send[0] = coef_column(1, jnp.maximum(c - 1, 0))
    for i in range(EDGE - 1):
        for n, j in enumerate((0, 2, 3, 4, 1)):
            coef_send[5 * i + 1 + n] = coef_column(j, c + i)

    odd = parity()
    for c in copies[6:]:
        c.wait()
    slab = levels * pitch

    @pl.loop(0, levels)
    def _(level):
        for side in (LOW, HIGH):
            for tag in range(tags):
                for k in range(2):
                    at = ((side * 2 + k) * tags + tag) * slab + level * pitch
                    lam_p[pl.ds(at, 8), :] = lam_s[side, tag, level, :, HALVES[k]]

    for dest, side in ((lam_first, 1 - odd), (lam_second, odd)):
        at = side * (2 * tags * slab + start)
        for tag in range(tags):
            for c in range(EDGE):
                dest[tag * EDGE + c] = column_at(
                    lam_p, at + tag * slab + c, levels, pitch, tags * slab
                )


def pack(lam, fields, top):
    tags, levels, cols, lats = lam.shape
    per = levels // 2
    hbm = pl.BlockSpec(memory_space=pltpu.HBM)
    coef_send = pltpu.VMEM((ENTRIES, per, lats), jnp.float32)
    lam_send = pltpu.VMEM((tags * EDGE, levels, lats), jnp.float32)
    return pl.pallas_call(
        pack_kernel,
        in_specs=[hbm] * 7,
        out_specs=[pl.BlockSpec(memory_space=pltpu.VMEM)] * 4,
        out_shape=[coef_send, lam_send, lam_send, pltpu.VMEM((cols, lats), jnp.int32)],
        scratch_shapes=[
            pltpu.VMEM((5, per, 8, lats), jnp.float32),
            pltpu.VMEM((2, tags, levels, 8, lats), jnp.float32),
            pltpu.VMEM((pitched(10, per, 8), LANES), jnp.float32),
            pltpu.VMEM((pitched(4 * tags, levels, 8), LANES), jnp.float32),
            pltpu.SemaphoreType.DMA((6 + 2 * tags,)),
        ],
        compiler_params=pltpu.CompilerParams(vmem_limit_bytes=24 << 20),
        cost_estimate=SHORT,
        name="pack_edges",
    )(lam, *fields, top)


def chosen(region_row, first_tag, values):
    row = jnp.zeros(region_row.shape, jnp.float32)
    for tag, value in enumerate(values):
        row = jnp.where(region_row == first_tag + tag, value[0:1], row)
    return row


def sweep(t, shape, first_tag, region, coef, load, store, rows):
    tags, _, cols, _ = shape
    low, high = t + 1, cols - t - 1
    chunk = -(-(high - low) // CHUNKS)
    column = lambda c: [load(c, k) for k in range(tags)]

    @pl.loop(0, CHUNKS)
    def _(i):
        start = jnp.minimum(low + i * chunk, high - chunk)
        west, mid = column(start - 1), column(start)
        for j in range(chunk):
            c = start + j
            east = column(c + 1)
            coefs = [coef[c, n] for n in range(6)]
            new = [advance(coefs, mid[k], east[k], west[k]) for k in range(tags)]
            for k in range(tags):
                store(c, k, new[k])
            rows[t, pl.ds(c, 1), :] = chosen(region[pl.ds(c, 1), :], first_tag, new)
            west, mid = mid, east


def loading(ref):
    return lambda c, tag: ref[c, tag]


def storing(ref):
    def store(c, tag, value):
        ref[c, tag] = value

    return store


def storing_rows(ref, tags, levels, pitch):
    def store(c, tag, value):
        for k in range(2):
            at = (k * tags + tag) * levels * pitch + c
            ref[pl.ds(at, levels, stride=pitch), :] = value[:, HALVES[k]]

    return store


def prepare_kernel(lam, ew, ed, nw, nd, mf, top, region, coef, l0, l1, rows, lam_p, field_p):
    tags, levels, cols, lats = lam.shape
    pitch = cols + 1
    slab = levels * pitch

    @pl.loop(0, levels)
    def _(level):
        row = level * pitch
        for f, field in enumerate((ew, ed, nw, nd, mf)):
            for k in range(2):
                field_p[pl.ds((f * 2 + k) * slab + row, cols), :] = field[level, :, HALVES[k]]
        for tag in range(tags):
            for k in range(2):
                at = (k * tags + tag) * slab + row
                lam_p[pl.ds(at, cols), :] = lam[tag, level, :, HALVES[k]]

    def coefficients(c, west):
        ew, ed, nw, nd, mf = (
            column_at(field_p, f * 2 * slab + c, levels, pitch, slab) for f in range(5)
        )
        e, next_west, n, s = faces(ew, ed, nw, nd)
        u = updraft(mf, top[pl.ds(c, 1), :])
        for j, value in enumerate((1.0 - e - west - n - s, e, west, n, s, u)):
            coef[c, j] = value
        return next_west

    def some(i, west):
        for j in range(8):
            west = coefficients(i * 8 + j, west)
        return west

    west = lax.fori_loop(0, cols // 8, some, jnp.zeros((levels, lats), jnp.float32))
    coef[cols, 2] = west
    for at, c in enumerate((0, 1, cols - 2, cols - 1)):
        for tag in range(tags):
            l0[at, tag] = column_at(lam_p, tag * slab + c, levels, pitch, tags * slab)

    def given(c, tag):
        return column_at(lam_p, tag * slab + c, levels, pitch, tags * slab)

    first_tag = lax.axis_index("grp") * tags
    sweep(0, lam.shape, first_tag, region, coef, given, storing(l1), rows)


def prepare(lam, fields, top, region):
    tags, levels, cols, lats = lam.shape
    vmem = pl.BlockSpec(memory_space=pltpu.VMEM)
    state = pltpu.VMEM((cols, tags, levels, lats), jnp.float32)
    return pl.pallas_call(
        prepare_kernel,
        in_specs=[vmem] * 8,
        out_specs=[vmem] * 4,
        out_shape=[
            pltpu.VMEM((cols + 1, 6, levels, lats), jnp.float32),
            pltpu.VMEM((4, tags, levels, lats), jnp.float32),
            state,
            pltpu.VMEM((1, cols, lats), jnp.float32),
        ],
        scratch_shapes=[
            pltpu.VMEM((pitched(2 * tags, levels, cols), LANES), jnp.float32),
            pltpu.VMEM((pitched(10, levels, cols), LANES), jnp.float32),
        ],
        compiler_params=pltpu.CompilerParams(vmem_limit_bytes=32 << 20),
        cost_estimate=SHORT,
        name="first_steps",
    )(lam, *fields, top, region)


def inner_kernel(coef, l1, region, rows_in, l2, l3, final, rows):
    cols, tags, levels, lats = l1.shape
    rows[0] = rows_in[0]
    shape = (tags, levels, cols, lats)
    first_tag = lax.axis_index("grp") * tags
    last = storing_rows(final, tags, levels, cols + 1)
    sweep(1, shape, first_tag, region, coef, loading(l1), storing(l2), rows)
    sweep(2, shape, first_tag, region, coef, loading(l2), storing(l3), rows)
    sweep(3, shape, first_tag, region, coef, loading(l3), last, rows)


def inner(coef, l1, region, rows):
    cols, tags, levels, lats = l1.shape
    vmem = pl.BlockSpec(memory_space=pltpu.VMEM)
    return pl.pallas_call(
        inner_kernel,
        in_specs=[vmem] * 4,
        out_specs=[vmem] * 4,
        out_shape=[
            pltpu.VMEM(l1.shape, jnp.float32),
            pltpu.VMEM(l1.shape, jnp.float32),
            pltpu.VMEM((pitched(2 * tags, levels, cols), LANES), jnp.float32),
            pltpu.VMEM((ITERS, cols, lats), jnp.float32),
        ],
        compiler_params=pltpu.CompilerParams(vmem_limit_bytes=32 << 20),
        cost_estimate=SHORT,
        name="inner_steps",
    )(coef, l1, region, rows)


def slot(c, cols):
    return (LOW, c + EDGE - 1) if c < EDGE else (HIGH, c - (cols - EDGE))


def outer_kernel(cols, coef, *refs):
    pieces, wide, entry = refs[:BLOCK], refs[BLOCK], refs[BLOCK + 1]
    per = coef.shape[2] // 2
    for by in range(BLOCK):
        rank = lax.axis_index("grp") ^ by
        rows = pl.ds(pl.multiple_of(coef_half(rank) * per, 8), per)
        entry[coef_side(rank), :, rows] = pieces[by][...]

    def slab(side, e):
        return entry[side, e]

    for side in (LOW, HIGH):
        for i in range(EDGE - 1):
            w, e, n, s, u = (slab(side, 5 * i + j) for j in range(5))
            if side == HIGH and i == 0:
                w = coef[cols, 2]
            for j, value in enumerate((1.0 - e - w - n - s, e, w, n, s, u)):
                wide[side, i + EDGE * side, j] = value
    first_west = slab(LOW, ENTRIES - 1)
    e, n, s, u = (coef[0, j] for j in (1, 3, 4, 5))
    for j, value in enumerate((1.0 - e - first_west - n - s, e, first_west, n, s, u)):
        wide[*slot(0, cols), j] = value


def outer_coefs(cols, coef, pieces):
    _, _, levels, lats = coef.shape
    vmem = pl.BlockSpec(memory_space=pltpu.VMEM)
    return pl.pallas_call(
        functools.partial(outer_kernel, cols),
        in_specs=[vmem] * (1 + BLOCK),
        out_specs=vmem,
        out_shape=pltpu.VMEM((2, 2 * EDGE - 1, 6, levels, lats), jnp.float32),
        scratch_shapes=[pltpu.VMEM((2, ENTRIES, levels, lats), jnp.float32)],
        compiler_params=pltpu.CompilerParams(vmem_limit_bytes=24 << 20),
        cost_estimate=SHORT,
        name="outer_coefs",
    )(coef, *pieces)


def border_steps(
    depth, region, coef, wide, kept, l0, halos, halo, work, rows=None, store=None, finish=None
):
    cols, tags, levels, lats = kept[1].shape
    first_tag = lax.axis_index("grp") * tags
    part = slice(0, depth)
    halo[1 - parity()] = halos[0][:, part]
    halo[parity()] = halos[1][:, part]

    def coefs_at(c):
        if 0 < c < cols:
            return [coef[c, j, part] for j in range(6)]
        return [wide[*slot(c, cols), j, part] for j in range(6)]

    def state(t, c, tag):
        if t == 0:
            if c < 0:
                return halo[LOW, tag * EDGE + c + EDGE]
            if c >= cols:
                return halo[HIGH, tag * EDGE + c - cols]
            return l0[c if c < 2 else c - (cols - 4), tag, part]
        if t <= c < cols - t:
            return kept[t][c, tag, part]
        return work[t, *slot(c, cols), tag]

    def column(t, c):
        return [state(t, c, tag) for tag in range(tags)]

    for t in range(ITERS if store is None else ITERS - 1):
        reach = EDGE - 1 - t
        for run in (range(-reach, t + 1), range(cols - t - 1, cols + reach)):
            west, mid = column(t, run[0] - 1), column(t, run[0])
            for c in run:
                east = column(t, c + 1)
                coefs = coefs_at(c)
                new = [advance(coefs, mid[k], east[k], west[k]) for k in range(tags)]
                if t < ITERS - 1:
                    for k in range(tags):
                        work[t + 1, *slot(c, cols), k] = new[k]
                if rows is not None and 0 <= c < cols:
                    rows[t, c : c + 1, :] = chosen(region[c : c + 1, :], first_tag, new)
                west, mid = mid, east
    if store is None:
        return
    t = ITERS - 1
    for k in range(tags):
        for c in [*range(EDGE), *range(cols - EDGE, cols)]:
            near = [state(t, at, k) for at in (c, c + 1, c - 1)]
            store(c, k, advance(coefs_at(c), *near))
        finish(k)


def low_kernel(region, coef, wide, l0, l1, l2, l3, first, second, rows_in, grad, halo, work, rows):
    rows[...] = rows_in[...]
    kept = (None, l1, l2, l3)
    border_steps(8, region, coef, wide, kept, l0, (first, second), halo, work, rows)
    total = rows[0]
    for t in range(1, ITERS):
        total = total + rows[t]
    grad[...] = total


def border_scratch(tags, depth, lats):
    return [
        pltpu.VMEM((2, tags * EDGE, depth, lats), jnp.float32),
        pltpu.VMEM((ITERS, 2, 2 * EDGE - 1, tags, depth, lats), jnp.float32),
    ]


def gradient(region, coef, wide, states, halos, rows):
    cols, tags, levels, lats = states[1].shape
    vmem = pl.BlockSpec(memory_space=pltpu.VMEM)
    operands = [region, coef, wide, *states, *halos, rows]
    return pl.pallas_call(
        low_kernel,
        in_specs=[vmem] * len(operands),
        out_specs=vmem,
        out_shape=pltpu.VMEM((cols, lats), jnp.float32),
        scratch_shapes=[
            *border_scratch(tags, 8, lats),
            pltpu.VMEM((ITERS, cols, lats), jnp.float32),
        ],
        compiler_params=pltpu.CompilerParams(vmem_limit_bytes=32 << 20),
        cost_estimate=SHORT,
        name="border_low_levels",
    )(*operands)


def border_kernel(coef, wide, l0, l1, l2, l3, first, second, *refs):
    final_in, out_in, final, out, halo, work, sides, sems = refs
    cols, tags, levels, lats = l1.shape
    pitch = cols + 1
    store = storing_rows(final, tags, levels, pitch)
    kept = (None, l1, l2, l3)
    copies = []

    def finish(tag):
        @pl.loop(0, levels // 8)
        def _(i):
            for j in range(8):
                level = i * 8 + j
                for k in range(2):
                    at = ((k * tags + tag) * levels + level) * pitch
                    for side, c in enumerate((0, cols - 8)):
                        sides[side, tag, level, :, HALVES[k]] = final[pl.ds(at + c, 8), :]

        for side, c in enumerate((0, cols - 8)):
            copies.append(
                pltpu.make_async_copy(
                    sides.at[side, tag], out.at[tag, :, pl.ds(c, 8)], sems.at[len(copies)]
                )
            )
            copies[-1].start()

    border_steps(
        levels, None, coef, wide, kept, l0, (first, second), halo, work, None, store, finish
    )
    for c in copies:
        c.wait()


def border(coef, wide, states, halos, final, out):
    cols, tags, levels, lats = states[1].shape
    vmem = pl.BlockSpec(memory_space=pltpu.VMEM)
    hbm = pl.BlockSpec(memory_space=pltpu.HBM)
    operands = [coef, wide, *states, *halos]
    n = len(operands)
    return pl.pallas_call(
        border_kernel,
        in_specs=[vmem] * (n + 1) + [hbm],
        out_specs=[vmem, hbm],
        out_shape=[
            pltpu.VMEM(final.shape, jnp.float32),
            pltpu.HBM(out.shape, jnp.float32),
        ],
        input_output_aliases={n: 0, n + 1: 1},
        scratch_shapes=[
            *border_scratch(tags, levels, lats),
            pltpu.VMEM((2, tags, levels, 8, lats), jnp.float32),
            pltpu.SemaphoreType.DMA((2 * tags,)),
        ],
        compiler_params=pltpu.CompilerParams(vmem_limit_bytes=32 << 20),
        cost_estimate=SHORT,
        name="border_all_levels",
    )(*operands, final, out)[1]


def write_kernel(final, out, block, sems):
    tags, levels, cols, _ = out.shape
    pitch = cols + 1
    copies = []
    for tag in range(tags):

        @pl.loop(0, levels)
        def _(level):
            for k in range(2):
                at = ((k * tags + tag) * levels + level) * pitch + 8
                block[tag, level, :, HALVES[k]] = final[pl.ds(at, cols - 16), :]

        copies.append(
            pltpu.make_async_copy(
                block.at[tag], out.at[tag, :, pl.ds(8, cols - 16)], sems.at[tag]
            )
        )
        copies[-1].start()
    for c in copies:
        c.wait()


def write_inner(final, shape):
    tags, levels, cols, lats = shape
    return pl.pallas_call(
        write_kernel,
        in_specs=[pl.BlockSpec(memory_space=pltpu.VMEM)],
        out_specs=pl.BlockSpec(memory_space=pltpu.HBM),
        out_shape=pltpu.HBM(shape, jnp.float32),
        scratch_shapes=[
            pltpu.VMEM((tags, levels, cols - 16, lats), jnp.float32),
            pltpu.SemaphoreType.DMA((tags,)),
        ],
        compiler_params=pltpu.CompilerParams(vmem_limit_bytes=24 << 20),
        cost_estimate=SHORT,
        name="write_inner",
    )(final)


def local(lam, east_wind, north_wind, east_diff, north_diff, mass_flux, region, top):
    groups, tiles = lax.axis_size("grp"), lax.axis_size("dom")
    own = (lam, east_wind, east_diff, north_wind, north_diff, mass_flux)
    far = [pltpu.with_memory_space_constraint(value, pltpu.HBM) for value in (*own, top)]

    pairs = lambda i: i ^ 1
    turn = lambda i: (((i - 1) % tiles ^ 1) + 1) % tiles
    coefs, first, second, top = pack(far[0], far[1:6], far[6])

    def partner(i):
        tile, rank = divmod(i, groups)
        return (turn if rank % 2 else pairs)(tile) * groups + rank

    coefs = swapped(coefs, ("dom", "grp"), partner)
    coef, l0, l1, rows = prepare(own[0], own[1:], top, region)
    second, coef = lax.optimization_barrier((second, coef))
    first = swapped(first, "dom", pairs)
    second = swapped(second, "dom", turn)
    pieces = [coefs]
    for by in range(1, BLOCK):
        pieces.append(swapped(coefs, "grp", lambda i: i ^ by))
    l2, l3, final, rows = inner(coef, l1, region, rows)
    states = [l0, l1, l2, l3]
    wide = outer_coefs(lam.shape[2], coef, pieces)
    out = write_inner(final, lam.shape)
    wide, out = lax.optimization_barrier((wide, out))
    grad = gradient(region, coef, wide, states, (first, second), rows)
    grad, wide = lax.optimization_barrier((grad, wide))
    out = border(coef, wide, states, (first, second), final, out)
    share = grad
    for by in range(1, groups):
        grad = grad + swapped(share, "grp", lambda i: i ^ by)
    return out, grad


def solution(mesh):
    return jax.shard_map(
        local,
        mesh=mesh,
        in_specs=(
            P("grp", None, "dom", None),
            P(None, "dom", None),
            P(None, "dom", None),
            P(None, "dom", None),
            P(None, "dom", None),
            P(None, "dom", None),
            P("dom", None),
            P("dom", None),
        ),
        out_specs=(P("grp", None, "dom", None), P("dom", None)),
        check_vma=False,
    )
```

```python
import functools

import jax
import jax.numpy as jnp
from jax import lax
from jax.experimental import pallas as pl
from jax.experimental.pallas import tpu as pltpu
from jax.sharding import PartitionSpec as P

ITERS = 4
EDGE = ITERS
ENTRIES = 16
BLOCK = 4
CHUNKS = 1
LANES = 128
HALVES = (slice(0, LANES), slice(LANES, 2 * LANES))
SHORT = pl.CostEstimate(flops=1000, bytes_accessed=1000, transcendentals=0)
LOW, HIGH = 0, 1

def swapped(value, axis, partner):
    return lax.ppermute(value, axis, [(i, partner(i)) for i in range(lax.axis_size(axis))])


def faces(ew, ed, nw, nd):
    lats = ew.shape[1]
    lat = lax.broadcasted_iota(jnp.int32, ew.shape, 1)
    east = jnp.maximum(ew, 0.0) + ed
    west_next = jnp.maximum(-ew, 0.0) + ed
    north = jnp.where(lat < lats - 1, jnp.maximum(nw, 0.0) + nd, 0.0)
    south = jnp.maximum(-nw, 0.0) + nd
    south = jnp.where(lat > 0, pltpu.roll(south, 1, 1), 0.0)
    return east, west_next, north, south


def updraft(mf, top_row):
    levels = mf.shape[0]
    level = lax.broadcasted_iota(jnp.int32, mf.shape, 0)
    return jnp.where((level < top_row) & (level < levels - 1), mf, 0.0)


def parity():
    return lax.rem(lax.axis_index("dom"), 2)


def level_above(h):
    if h.shape[0] == 8:
        return pltpu.roll(h, 7, 0)
    parts = [pltpu.roll(h[at : at + 8], 7, 0) for at in range(0, h.shape[0], 8)]
    inside = lax.broadcasted_iota(jnp.int32, parts[0].shape, 0) < 7
    joined = [jnp.where(inside, low, high) for low, high in zip(parts, parts[1:])]
    return jnp.concatenate([*joined, parts[-1]], axis=0)


def advance(coefs, mid, east, west):
    d, e, w, n, s, u = coefs
    h = d * mid + e * east + w * west
    lane = lax.broadcasted_iota(jnp.int32, (mid.shape[0], LANES), 1)
    north = [pltpu.roll(mid[:, part], LANES - 1, 1) for part in HALVES]
    south = [pltpu.roll(mid[:, part], 1, 1) for part in HALVES]
    north = jnp.concatenate([jnp.where(lane < LANES - 1, *north), north[1]], axis=1)
    south = jnp.concatenate([south[0], jnp.where(lane > 0, south[1], south[0])], axis=1)
    h = h + n * north + s * south
    return h + u * (level_above(h) - h)


def pitched(slabs, levels, width):
    return -(-(slabs * levels * (width + 1) + width + 8) // 8) * 8


def column_at(ref, start, levels, pitch, apart):
    parts = [ref[pl.ds(start + apart * k, levels, stride=pitch), :] for k in range(2)]
    return jnp.concatenate(parts, axis=1)


def coef_side(rank):
    return lax.rem(1 - parity() + rank, 2)


def coef_half(rank):
    return lax.rem(lax.div(rank, 2), 2)


def pack_kernel(lam, ew, ed, nw, nd, mf, top, *refs):
    coef_send, lam_first, lam_second, top_v = refs[:4]
    field_s, lam_s, coef_p, lam_p, sems = refs[4:]
    tags, levels, cols, lats = lam.shape
    per = levels // 2
    rank = lax.axis_index("grp")
    base = coef_half(rank) * per
    high = coef_side(rank)
    edge = pl.ds(pl.multiple_of(high * (cols - 8), 8), 8)
    copies = []

    def copy(src, dst):
        copies.append(pltpu.make_async_copy(src, dst, sems.at[len(copies)]))
        copies[-1].start()

    for f, field in enumerate((ew, ed, nw, nd, mf)):
        copy(field.at[pl.ds(base, per), edge], field_s.at[f])
    copy(top, top_v)
    for side, at in ((LOW, 0), (HIGH, cols - 8)):
        for tag in range(tags):
            copy(lam.at[tag, :, pl.ds(at, 8)], lam_s.at[side, tag])
    for c in copies[:6]:
        c.wait()
    pitch = 9
    few = per * pitch

    @pl.loop(0, per // 2)
    def _(pair):
        for half in range(2):
            i = pair * 2 + half
            level = base + i
            ew, ed, nw, nd, mf = (field_s[f, i] for f in range(5))
            lift = jnp.where((level < top_v[edge]) & (level < levels - 1), mf, 0.0)
            for j, value in enumerate((*faces(ew, ed, nw, nd), lift)):
                for k in range(2):
                    at = (j * 2 + k) * few + i * pitch
                    coef_p[pl.ds(at, 8), :] = value[:, HALVES[k]]

    def coef_column(j, c):
        return column_at(coef_p, j * 2 * few + c, per, pitch, few)

    start = 8 - EDGE
    c = high * (start + 1)
    coef_send[0] = coef_column(1, jnp.maximum(c - 1, 0))
    for i in range(EDGE - 1):
        for n, j in enumerate((0, 2, 3, 4, 1)):
            coef_send[5 * i + 1 + n] = coef_column(j, c + i)

    odd = parity()
    for c in copies[6:]:
        c.wait()
    slab = levels * pitch

    @pl.loop(0, levels)
    def _(level):
        for side in (LOW, HIGH):
            for tag in range(tags):
                for k in range(2):
                    at = ((side * 2 + k) * tags + tag) * slab + level * pitch
                    lam_p[pl.ds(at, 8), :] = lam_s[side, tag, level, :, HALVES[k]]

    for dest, side in ((lam_first, 1 - odd), (lam_second, odd)):
        at = side * (2 * tags * slab + start)
        for tag in range(tags):
            for c in range(EDGE):
                dest[tag * EDGE + c] = column_at(
                    lam_p, at + tag * slab + c, levels, pitch, tags * slab
                )


def pack(lam, fields, top):
    tags, levels, cols, lats = lam.shape
    per = levels // 2
    hbm = pl.BlockSpec(memory_space=pltpu.HBM)
    coef_send = pltpu.VMEM((ENTRIES, per, lats), jnp.float32)
    lam_send = pltpu.VMEM((tags * EDGE, levels, lats), jnp.float32)
    return pl.pallas_call(
        pack_kernel,
        in_specs=[hbm] * 7,
        out_specs=[pl.BlockSpec(memory_space=pltpu.VMEM)] * 4,
        out_shape=[coef_send, lam_send, lam_send, pltpu.VMEM((cols, lats), jnp.int32)],
        scratch_shapes=[
            pltpu.VMEM((5, per, 8, lats), jnp.float32),
            pltpu.VMEM((2, tags, levels, 8, lats), jnp.float32),
            pltpu.VMEM((pitched(10, per, 8), LANES), jnp.float32),
            pltpu.VMEM((pitched(4 * tags, levels, 8), LANES), jnp.float32),
            pltpu.SemaphoreType.DMA((6 + 2 * tags,)),
        ],
        compiler_params=pltpu.CompilerParams(vmem_limit_bytes=24 << 20),
        cost_estimate=SHORT,
        name="pack_edges",
    )(lam, *fields, top)


def chosen(region_row, first_tag, values):
    row = jnp.zeros(region_row.shape, jnp.float32)
    for tag, value in enumerate(values):
        row = jnp.where(region_row == first_tag + tag, value[0:1], row)
    return row


def sweep(t, shape, first_tag, region, coef, load, store, rows):
    tags, _, cols, _ = shape
    low, high = t + 1, cols - t - 1
    chunk = -(-(high - low) // CHUNKS)
    column = lambda c: [load(c, k) for k in range(tags)]

    @pl.loop(0, CHUNKS)
    def _(i):
        start = jnp.minimum(low + i * chunk, high - chunk)
        west, mid = column(start - 1), column(start)
        for j in range(chunk):
            c = start + j
            east = column(c + 1)
            coefs = [coef[c, n] for n in range(6)]
            new = [advance(coefs, mid[k], east[k], west[k]) for k in range(tags)]
            for k in range(tags):
                store(c, k, new[k])
            rows[t, pl.ds(c, 1), :] = chosen(region[pl.ds(c, 1), :], first_tag, new)
            west, mid = mid, east


def loading(ref):
    return lambda c, tag: ref[c, tag]


def storing(ref):
    def store(c, tag, value):
        ref[c, tag] = value

    return store


def storing_rows(ref, tags, levels, pitch):
    def store(c, tag, value):
        for k in range(2):
            at = (k * tags + tag) * levels * pitch + c
            ref[pl.ds(at, levels, stride=pitch), :] = value[:, HALVES[k]]

    return store


def prepare_kernel(lam, ew, ed, nw, nd, mf, top, region, coef, l0, l1, l2, rows, lam_p, field_p):
    tags, levels, cols, lats = lam.shape
    pitch = cols + 1
    slab = levels * pitch

    @pl.loop(0, levels)
    def _(level):
        row = level * pitch
        for f, field in enumerate((ew, ed, nw, nd, mf)):
            for k in range(2):
                field_p[pl.ds((f * 2 + k) * slab + row, cols), :] = field[level, :, HALVES[k]]
        for tag in range(tags):
            for k in range(2):
                at = (k * tags + tag) * slab + row
                lam_p[pl.ds(at, cols), :] = lam[tag, level, :, HALVES[k]]

    def coefficients(c, west):
        ew, ed, nw, nd, mf = (
            column_at(field_p, f * 2 * slab + c, levels, pitch, slab) for f in range(5)
        )
        e, next_west, n, s = faces(ew, ed, nw, nd)
        u = updraft(mf, top[pl.ds(c, 1), :])
        for j, value in enumerate((1.0 - e - west - n - s, e, west, n, s, u)):
            coef[c, j] = value
        return next_west

    def some(i, west):
        for j in range(8):
            west = coefficients(i * 8 + j, west)
        return west

    west = lax.fori_loop(0, cols // 8, some, jnp.zeros((levels, lats), jnp.float32))
    coef[cols, 2] = west
    for at, c in enumerate((0, 1, cols - 2, cols - 1)):
        for tag in range(tags):
            l0[at, tag] = column_at(lam_p, tag * slab + c, levels, pitch, tags * slab)

    def given(c, tag):
        return column_at(lam_p, tag * slab + c, levels, pitch, tags * slab)

    first_tag = lax.axis_index("grp") * tags
    sweep(0, lam.shape, first_tag, region, coef, given, storing(l1), rows)
    sweep(1, lam.shape, first_tag, region, coef, loading(l1), storing(l2), rows)


def prepare(lam, fields, top, region):
    tags, levels, cols, lats = lam.shape
    vmem = pl.BlockSpec(memory_space=pltpu.VMEM)
    state = pltpu.VMEM((cols, tags, levels, lats), jnp.float32)
    return pl.pallas_call(
        prepare_kernel,
        in_specs=[vmem] * 8,
        out_specs=[vmem] * 5,
        out_shape=[
            pltpu.VMEM((cols + 1, 6, levels, lats), jnp.float32),
            pltpu.VMEM((4, tags, levels, lats), jnp.float32),
            state,
            state,
            pltpu.VMEM((2, cols, lats), jnp.float32),
        ],
        scratch_shapes=[
            pltpu.VMEM((pitched(2 * tags, levels, cols), LANES), jnp.float32),
            pltpu.VMEM((pitched(10, levels, cols), LANES), jnp.float32),
        ],
        compiler_params=pltpu.CompilerParams(vmem_limit_bytes=32 << 20),
        cost_estimate=SHORT,
        name="first_steps",
    )(lam, *fields, top, region)


def inner_kernel(coef, l2, region, rows_in, l3, final, rows):
    cols, tags, levels, lats = l2.shape
    rows[0:2] = rows_in[...]
    shape = (tags, levels, cols, lats)
    first_tag = lax.axis_index("grp") * tags
    last = storing_rows(final, tags, levels, cols + 1)
    sweep(2, shape, first_tag, region, coef, loading(l2), storing(l3), rows)
    sweep(3, shape, first_tag, region, coef, loading(l3), last, rows)


def inner(coef, l2, region, rows):
    cols, tags, levels, lats = l2.shape
    vmem = pl.BlockSpec(memory_space=pltpu.VMEM)
    return pl.pallas_call(
        inner_kernel,
        in_specs=[vmem] * 4,
        out_specs=[vmem] * 3,
        out_shape=[
            pltpu.VMEM(l2.shape, jnp.float32),
            pltpu.VMEM((pitched(2 * tags, levels, cols), LANES), jnp.float32),
            pltpu.VMEM((ITERS, cols, lats), jnp.float32),
        ],
        compiler_params=pltpu.CompilerParams(vmem_limit_bytes=32 << 20),
        cost_estimate=SHORT,
        name="inner_steps",
    )(coef, l2, region, rows)


def slot(c, cols):
    return (LOW, c + EDGE - 1) if c < EDGE else (HIGH, c - (cols - EDGE))


def outer_kernel(cols, coef, *refs):
    pieces, wide, entry = refs[:BLOCK], refs[BLOCK], refs[BLOCK + 1]
    per = coef.shape[2] // 2
    for by in range(BLOCK):
        rank = lax.axis_index("grp") ^ by
        rows = pl.ds(pl.multiple_of(coef_half(rank) * per, 8), per)
        entry[coef_side(rank), :, rows] = pieces[by][...]

    def slab(side, e):
        return entry[side, e]

    for side in (LOW, HIGH):
        for i in range(EDGE - 1):
            w, e, n, s, u = (slab(side, 5 * i + j) for j in range(5))
            if side == HIGH and i == 0:
                w = coef[cols, 2]
            for j, value in enumerate((1.0 - e - w - n - s, e, w, n, s, u)):
                wide[side, i + EDGE * side, j] = value
    first_west = slab(LOW, ENTRIES - 1)
    e, n, s, u = (coef[0, j] for j in (1, 3, 4, 5))
    for j, value in enumerate((1.0 - e - first_west - n - s, e, first_west, n, s, u)):
        wide[*slot(0, cols), j] = value


def outer_coefs(cols, coef, pieces):
    _, _, levels, lats = coef.shape
    vmem = pl.BlockSpec(memory_space=pltpu.VMEM)
    return pl.pallas_call(
        functools.partial(outer_kernel, cols),
        in_specs=[vmem] * (1 + BLOCK),
        out_specs=vmem,
        out_shape=pltpu.VMEM((2, 2 * EDGE - 1, 6, levels, lats), jnp.float32),
        scratch_shapes=[pltpu.VMEM((2, ENTRIES, levels, lats), jnp.float32)],
        compiler_params=pltpu.CompilerParams(vmem_limit_bytes=24 << 20),
        cost_estimate=SHORT,
        name="outer_coefs",
    )(coef, *pieces)


def border_steps(
    depth, region, coef, wide, kept, l0, halos, halo, work, rows=None, store=None, finish=None
):
    cols, tags, levels, lats = kept[1].shape
    first_tag = lax.axis_index("grp") * tags
    part = slice(0, depth)
    halo[1 - parity()] = halos[0][:, part]
    halo[parity()] = halos[1][:, part]

    def coefs_at(c):
        if 0 < c < cols:
            return [coef[c, j, part] for j in range(6)]
        return [wide[*slot(c, cols), j, part] for j in range(6)]

    def state(t, c, tag):
        if t == 0:
            if c < 0:
                return halo[LOW, tag * EDGE + c + EDGE]
            if c >= cols:
                return halo[HIGH, tag * EDGE + c - cols]
            return l0[c if c < 2 else c - (cols - 4), tag, part]
        if t <= c < cols - t:
            return kept[t][c, tag, part]
        return work[t, *slot(c, cols), tag]

    def column(t, c):
        return [state(t, c, tag) for tag in range(tags)]

    for t in range(ITERS if store is None else ITERS - 1):
        reach = EDGE - 1 - t
        for run in (range(-reach, t + 1), range(cols - t - 1, cols + reach)):
            west, mid = column(t, run[0] - 1), column(t, run[0])
            for c in run:
                east = column(t, c + 1)
                coefs = coefs_at(c)
                new = [advance(coefs, mid[k], east[k], west[k]) for k in range(tags)]
                if t < ITERS - 1:
                    for k in range(tags):
                        work[t + 1, *slot(c, cols), k] = new[k]
                if rows is not None and 0 <= c < cols:
                    rows[t, c : c + 1, :] = chosen(region[c : c + 1, :], first_tag, new)
                west, mid = mid, east
    if store is None:
        return
    t = ITERS - 1
    for k in range(tags):
        for c in [*range(EDGE), *range(cols - EDGE, cols)]:
            near = [state(t, at, k) for at in (c, c + 1, c - 1)]
            store(c, k, advance(coefs_at(c), *near))
        finish(k)


def low_kernel(region, coef, wide, l0, l1, l2, l3, first, second, rows_in, grad, halo, work, rows):
    rows[...] = rows_in[...]
    kept = (None, l1, l2, l3)
    border_steps(8, region, coef, wide, kept, l0, (first, second), halo, work, rows)
    total = rows[0]
    for t in range(1, ITERS):
        total = total + rows[t]
    grad[...] = total


def border_scratch(tags, depth, lats):
    return [
        pltpu.VMEM((2, tags * EDGE, depth, lats), jnp.float32),
        pltpu.VMEM((ITERS, 2, 2 * EDGE - 1, tags, depth, lats), jnp.float32),
    ]


def gradient(region, coef, wide, states, halos, rows):
    cols, tags, levels, lats = states[1].shape
    vmem = pl.BlockSpec(memory_space=pltpu.VMEM)
    operands = [region, coef, wide, *states, *halos, rows]
    return pl.pallas_call(
        low_kernel,
        in_specs=[vmem] * len(operands),
        out_specs=vmem,
        out_shape=pltpu.VMEM((cols, lats), jnp.float32),
        scratch_shapes=[
            *border_scratch(tags, 8, lats),
            pltpu.VMEM((ITERS, cols, lats), jnp.float32),
        ],
        compiler_params=pltpu.CompilerParams(vmem_limit_bytes=32 << 20),
        cost_estimate=SHORT,
        name="border_low_levels",
    )(*operands)


def border_kernel(coef, wide, l0, l1, l2, l3, first, second, *refs):
    final_in, out_in, final, out, halo, work, sides, sems = refs
    cols, tags, levels, lats = l1.shape
    pitch = cols + 1
    store = storing_rows(final, tags, levels, pitch)
    kept = (None, l1, l2, l3)
    copies = []

    def finish(tag):
        @pl.loop(0, levels // 8)
        def _(i):
            for j in range(8):
                level = i * 8 + j
                for k in range(2):
                    at = ((k * tags + tag) * levels + level) * pitch
                    for side, c in enumerate((0, cols - 8)):
                        sides[side, tag, level, :, HALVES[k]] = final[pl.ds(at + c, 8), :]

        for side, c in enumerate((0, cols - 8)):
            copies.append(
                pltpu.make_async_copy(
                    sides.at[side, tag], out.at[tag, :, pl.ds(c, 8)], sems.at[len(copies)]
                )
            )
            copies[-1].start()

    border_steps(
        levels, None, coef, wide, kept, l0, (first, second), halo, work, None, store, finish
    )
    for c in copies:
        c.wait()


def border(coef, wide, states, halos, final, out):
    cols, tags, levels, lats = states[1].shape
    vmem = pl.BlockSpec(memory_space=pltpu.VMEM)
    hbm = pl.BlockSpec(memory_space=pltpu.HBM)
    operands = [coef, wide, *states, *halos]
    n = len(operands)
    return pl.pallas_call(
        border_kernel,
        in_specs=[vmem] * (n + 1) + [hbm],
        out_specs=[vmem, hbm],
        out_shape=[
            pltpu.VMEM(final.shape, jnp.float32),
            pltpu.HBM(out.shape, jnp.float32),
        ],
        input_output_aliases={n: 0, n + 1: 1},
        scratch_shapes=[
            *border_scratch(tags, levels, lats),
            pltpu.VMEM((2, tags, levels, 8, lats), jnp.float32),
            pltpu.SemaphoreType.DMA((2 * tags,)),
        ],
        compiler_params=pltpu.CompilerParams(vmem_limit_bytes=32 << 20),
        cost_estimate=SHORT,
        name="border_all_levels",
    )(*operands, final, out)[1]


def write_kernel(final, out, block, sems):
    tags, levels, cols, _ = out.shape
    pitch = cols + 1
    copies = []
    for tag in range(tags):

        @pl.loop(0, levels)
        def _(level):
            for k in range(2):
                at = ((k * tags + tag) * levels + level) * pitch + 8
                block[tag, level, :, HALVES[k]] = final[pl.ds(at, cols - 16), :]

        copies.append(
            pltpu.make_async_copy(
                block.at[tag], out.at[tag, :, pl.ds(8, cols - 16)], sems.at[tag]
            )
        )
        copies[-1].start()
    for c in copies:
        c.wait()


def write_inner(final, shape):
    tags, levels, cols, lats = shape
    return pl.pallas_call(
        write_kernel,
        in_specs=[pl.BlockSpec(memory_space=pltpu.VMEM)],
        out_specs=pl.BlockSpec(memory_space=pltpu.HBM),
        out_shape=pltpu.HBM(shape, jnp.float32),
        scratch_shapes=[
            pltpu.VMEM((tags, levels, cols - 16, lats), jnp.float32),
            pltpu.SemaphoreType.DMA((tags,)),
        ],
        compiler_params=pltpu.CompilerParams(vmem_limit_bytes=24 << 20),
        cost_estimate=SHORT,
        name="write_inner",
    )(final)


def local(lam, east_wind, north_wind, east_diff, north_diff, mass_flux, region, top):
    groups, tiles = lax.axis_size("grp"), lax.axis_size("dom")
    own = (lam, east_wind, east_diff, north_wind, north_diff, mass_flux)
    far = [pltpu.with_memory_space_constraint(value, pltpu.HBM) for value in (*own, top)]

    pairs = lambda i: i ^ 1
    turn = lambda i: (((i - 1) % tiles ^ 1) + 1) % tiles
    coefs, first, second, top = pack(far[0], far[1:6], far[6])

    def partner(i):
        tile, rank = divmod(i, groups)
        return (turn if rank % 2 else pairs)(tile) * groups + rank

    coefs = swapped(coefs, ("dom", "grp"), partner)
    coef, l0, l1, l2, rows = prepare(own[0], own[1:], top, region)
    second, coef = lax.optimization_barrier((second, coef))
    first = swapped(first, "dom", pairs)
    second = swapped(second, "dom", turn)
    pieces = [coefs]
    for by in range(1, BLOCK):
        pieces.append(swapped(coefs, "grp", lambda i: i ^ by))
    l3, final, rows = inner(coef, l2, region, rows)
    states = [l0, l1, l2, l3]
    wide = outer_coefs(lam.shape[2], coef, pieces)
    out = write_inner(final, lam.shape)
    wide, out = lax.optimization_barrier((wide, out))
    grad = gradient(region, coef, wide, states, (first, second), rows)
    grad, wide = lax.optimization_barrier((grad, wide))
    out = border(coef, wide, states, (first, second), final, out)
    share = grad
    for by in range(1, groups):
        grad = grad + swapped(share, "grp", lambda i: i ^ by)
    return out, grad


def solution(mesh):
    return jax.shard_map(
        local,
        mesh=mesh,
        in_specs=(
            P("grp", None, "dom", None),
            P(None, "dom", None),
            P(None, "dom", None),
            P(None, "dom", None),
            P(None, "dom", None),
            P(None, "dom", None),
            P("dom", None),
            P("dom", None),
        ),
        out_specs=(P("grp", None, "dom", None), P("dom", None)),
        check_vma=False,
    )
```
